32 devices in a mesh: ty: 4 (over x, core), tx: 8 (over z, y).
Axes of the slice: x: 2, y: 2, z: 4, core: 2. Of those that a mesh axis runs over, the one named last changes fastest.
Arguments:
- pixels: bfloat16 [2, 3, 288, 288], P(None, None, 'ty', 'tx'), may hold values from -6 to 6
- pixel_mask: int32 [2, 288, 288], P(None, 'ty', 'tx'), may hold values 0 or 1
- image_sizes: int32 [2], replicated, may hold values from 160 to 288, as said below
- latents: bfloat16 [2, 512, 1024], P(None, 'tx'), may hold values from -6 to 6
- cotangent: bfloat16 [2, 512, 1024], P(None, 'tx'), may hold values from -6 to 6
- feature_gain: float32 [261], replicated, may hold values from 0.5 to 1.5
- query_gain: float32 [1024], replicated, may hold values from 0.5 to 1.5
- query_proj: bfloat16 [1024, 1024], replicated, may hold values from -0.375 to 0.375
- key_proj: bfloat16 [261, 1024], replicated, may hold values from -0.375 to 0.375
- value_proj: bfloat16 [261, 1024], replicated, may hold values from -0.375 to 0.375
- cross_proj: bfloat16 [1024, 1024], replicated, may hold values from -6 to 6
- hidden_gain: float32 [1024], replicated, may hold values from 0.5 to 1.5
- hidden_up: bfloat16 [1024, 1024], replicated, may hold values from -0.1875 to 0.1875
- hidden_down: bfloat16 [1024, 1024], replicated, may hold values from -0.1875 to 0.1875
- tower_gain: float32 [1024], replicated, may hold values from 0.5 to 1.5
- tower_query: bfloat16 [1024, 1024], replicated, may hold values from -0.375 to 0.375
- tower_key: bfloat16 [1024, 1024], replicated, may hold values from -0.1875 to 0.1875
- tower_value: bfloat16 [1024, 1024], replicated, may hold values from -0.1875 to 0.1875
- tower_proj: bfloat16 [1024, 1024], replicated, may hold values from -0.5 to 0.5
- final_gain: float32 [1024], replicated, may hold values from 0.5 to 1.5
- final_up: bfloat16 [1024, 1024], replicated, may hold values from -0.1875 to 0.1875
- final_down: bfloat16 [1024, 1024], replicated, may hold values from -0.1875 to 0.1875
Outputs:
- result: bfloat16 [2, 512, 1024], P(None, 'tx')
- latent_grad: float32 [2, 512, 1024], P(None, 'tx')
- feature_gain_grad: float32 [261], replicated
- query_gain_grad: float32 [1024], P('tx')
- query_proj_grad: float32 [1024, 1024], P('tx')
- key_proj_grad: float32 [261, 1024], replicated
- value_proj_grad: float32 [261, 1024], replicated
- cross_proj_grad: float32 [1024, 1024], P('tx')
- hidden_gain_grad: float32 [1024], P('tx')
- hidden_up_grad: float32 [1024, 1024], P('tx')
- hidden_down_grad: float32 [1024, 1024], P('tx')
- tower_gain_grad: float32 [1024], P('tx')
- tower_query_grad: float32 [1024, 1024], P('tx')
- tower_key_grad: float32 [1024, 1024], P('tx')
- tower_value_grad: float32 [1024, 1024], P('tx')
- tower_proj_grad: float32 [1024, 1024], P('tx')
- final_gain_grad: float32 [1024], P('tx')
- final_up_grad: float32 [1024, 1024], P('tx')
- final_down_grad: float32 [1024, 1024], P('tx')
The draws below stay inside these ranges and needn't reach their ends.
Inputs may be any that keep to these rules, and one draw needn't show every extreme that they name: `image_sizes`: each image is square, with 160, 224 or 288 pixels on a side, and some image has each of the two ends.
All inputs are finite; a program needn't handle non-finite values. No bound on the sum of `pixel_mask` on one device may be relied on, other than what follows from the above.
Results may differ from the reference program's by a relative error of at most 0.025.
Values may be sent and summed in bfloat16 or wider, within the bound.
A program may use at most 192 MiB of HBM per device.

```python
import math
import jax
import jax.numpy as jnp
from jax import lax

B = 2
IMG = 288
BANDS = 64
FEAT = 261
LAT = 512
C = 1024
FF = 1024
HEADS = 8


def draw_image_sizes(key, part):
    pick_key, first_key, second_key = jax.random.split(key, 3)
    levels = jnp.array([IMG * 5 // 9, IMG * 7 // 9, IMG], dtype=jnp.int32)
    picked = jax.random.randint(pick_key, (B,), 0, 3)
    chosen = levels[picked]
    largest = jax.random.randint(first_key, (), 0, B)
    offset = jax.random.randint(second_key, (), 1, B)
    smallest = (largest + offset) % B
    position = jnp.arange(B, dtype=jnp.int32)
    chosen = jnp.where(position == largest, IMG, chosen)
    chosen = jnp.where(position == smallest, IMG * 5 // 9, chosen)
    return chosen.astype(jnp.int32)


def touch_ends(entries, own_key, least, high):
    spot = [jax.random.randint(jax.random.fold_in(own_key, axis), (), 0, length) for axis, length in enumerate(entries.shape)]
    widest = entries.shape.index(max(entries.shape))
    next_to = spot[:widest] + [(spot[widest] + 1) % entries.shape[widest]] + spot[widest + 1:]
    return entries.at[tuple(spot)].set(least).at[tuple(next_to)].set(high)


def block_scale(stream_key, extent, shards, low, high):
    def one(dim, blocks):
        heights = jax.random.uniform(jax.random.fold_in(jax.random.fold_in(stream_key, 6), dim), (blocks,), jnp.float32, low / len(shards), high / len(shards))
        return jnp.repeat(jnp.exp(heights), extent[dim] // blocks).reshape((-1,) + (1,) * (len(extent) - dim - 1))

    loudness = one(*shards[0])
    for cut in shards[1:]:
        loudness = loudness * one(*cut)
    return loudness


def scatter_about(own_key, extent, width, limit, shards=(), held_as=jnp.bfloat16):
    level = block_scale(own_key, extent, shards, -0.22, 0.18) if shards else 1.0
    values = jax.random.normal(own_key, extent, jnp.float32) * width * level
    return jnp.minimum(jnp.maximum(values, -limit), limit).astype(held_as)


def setup_inputs(seed: int = 0) -> dict:
    splits = jax.random.split(jax.random.key(seed), 23)
    pixels = scatter_about(splits[0], (B, 3, IMG, IMG), 1.0, 6.0, ((2, 4), (3, 8)))
    pixel_mask = touch_ends((jax.random.randint(splits[1], (B, IMG, IMG), 0, 8) < 7).astype(jnp.int32), jax.random.fold_in(splits[1], 1), 0, 1)
    image_sizes = draw_image_sizes(jax.random.fold_in(splits[22], 71), 0)
    latents = scatter_about(splits[3], (B, LAT, C), 1.0, 6.0, ((1, 8),))
    cotangent = scatter_about(splits[4], (B, LAT, C), 1.0, 6.0, ((1, 8),))
    feature_gain = jnp.clip(1.0 + 0.1 * jax.random.normal(splits[5], (FEAT,), jnp.float32), 0.5, 1.5)
    query_gain = jnp.clip(1.0 + 0.1 * jax.random.normal(splits[6], (C,), jnp.float32), 0.5, 1.5)
    query_proj = scatter_about(splits[7], (C, C), (C // 4) ** -0.5, 0.375)
    key_proj = scatter_about(splits[8], (FEAT, C), FEAT ** -0.5, 0.375)
    value_proj = scatter_about(splits[9], (FEAT, C), FEAT ** -0.5, 0.375)
    cross_proj = scatter_about(splits[10], (C, C), 1.0, 6.0)
    hidden_gain = jnp.clip(1.0 + 0.1 * jax.random.normal(splits[11], (C,), jnp.float32), 0.5, 1.5)
    hidden_up = scatter_about(splits[12], (C, FF), C ** -0.5, 0.1875)
    hidden_down = scatter_about(splits[13], (FF, C), FF ** -0.5, 0.1875)
    tower_gain = jnp.clip(1.0 + 0.1 * jax.random.normal(splits[14], (C,), jnp.float32), 0.5, 1.5)
    tower_query = scatter_about(splits[15], (C, C), (C // 4) ** -0.5, 0.375)
    tower_key = scatter_about(splits[16], (C, C), C ** -0.5, 0.1875)
    tower_value = scatter_about(splits[17], (C, C), C ** -0.5, 0.1875)
    tower_proj = scatter_about(splits[18], (C, C), (C * 55 // LAT) ** -0.5, 0.5)
    final_gain = jnp.clip(1.0 + 0.1 * jax.random.normal(splits[19], (C,), jnp.float32), 0.5, 1.5)
    final_up = scatter_about(splits[20], (C, FF), C ** -0.5, 0.1875)
    final_down = scatter_about(splits[21], (FF, C), FF ** -0.5, 0.1875)
    return dict(pixels=pixels, pixel_mask=pixel_mask, image_sizes=image_sizes, latents=latents, cotangent=cotangent, feature_gain=feature_gain, query_gain=query_gain, query_proj=query_proj, key_proj=key_proj, value_proj=value_proj, cross_proj=cross_proj, hidden_gain=hidden_gain, hidden_up=hidden_up, hidden_down=hidden_down, tower_gain=tower_gain, tower_query=tower_query, tower_key=tower_key, tower_value=tower_value, tower_proj=tower_proj, final_gain=final_gain, final_up=final_up, final_down=final_down)


@jax.custom_vjp
def low(v):
    return lax.optimization_barrier(v.astype(jnp.bfloat16)).astype(jnp.float32)

@jax.custom_vjp
def low_back(v):
    return v

def low_keep(v):
    return (low(v), None)

def low_pass(kept, grad):
    return (grad,)

def back_keep(v):
    return (v, None)

def back_low(kept, grad):
    return (low(grad),)
low.defvjp(low_keep, low_pass)
low_back.defvjp(back_keep, back_low)
EPSILON = 1e-05

def layer_norm(values, scales):
    centre = lax.optimization_barrier(jnp.mean(values, axis=-1, keepdims=True))
    shifted = values - centre
    spread = lax.optimization_barrier(jnp.mean(shifted * shifted, axis=-1, keepdims=True))
    return shifted * lax.rsqrt(spread + EPSILON) * scales

def gelu_tanh(values):
    cubic = values + 0.044715 * values * values * values
    return 0.5 * values * (1.0 + jnp.tanh(0.7978845608028654 * cubic))

def dense(inputs, weight):
    return jnp.einsum('...k,kn->...n', inputs, weight, precision=lax.Precision.HIGHEST)

def pixel_features(image, image_side):
    positions = jnp.arange(IMG, dtype=jnp.int32).astype(jnp.float32)
    side_value = image_side.astype(jnp.float32)
    coords = -1.0 + 2.0 * positions / (side_value - 1.0)
    band_index = jnp.arange(BANDS, dtype=jnp.int32).astype(jnp.float32)
    frequency = 1.0 + band_index * (side_value * 0.5 - 1.0) / (BANDS - 1)
    angles = math.pi * coords[:, None] * frequency[None, :]
    grid_shape = (IMG, IMG)
    pieces = [jnp.transpose(image, (1, 2, 0)), jnp.broadcast_to(coords[:, None, None], grid_shape + (1,)), jnp.broadcast_to(coords[None, :, None], grid_shape + (1,)), jnp.broadcast_to(jnp.sin(angles)[:, None, :], grid_shape + (BANDS,)), jnp.broadcast_to(jnp.cos(angles)[:, None, :], grid_shape + (BANDS,)), jnp.broadcast_to(jnp.sin(angles)[None, :, :], grid_shape + (BANDS,)), jnp.broadcast_to(jnp.cos(angles)[None, :, :], grid_shape + (BANDS,))]
    return jnp.concatenate(pieces, axis=2).reshape(IMG * IMG, FEAT)

def cross_item(query_block, image, valid_item, image_side, feature_gain, key_proj, value_proj):
    features = pixel_features(image, image_side)
    normed = low(layer_norm(features, feature_gain))
    pixel_keys = low_back(low(dense(normed, key_proj)))
    pixel_values = low_back(low(dense(normed, value_proj)))
    scores = low_back(dense(query_block, jnp.transpose(pixel_keys)) * (1.0 / math.sqrt(C)))
    live_mask = valid_item.reshape(1, IMG * IMG) > 0.5
    row_top = lax.optimization_barrier(jnp.max(jnp.where(live_mask, scores, -1e+30), axis=1, keepdims=True))
    exponent = jnp.where(live_mask, jnp.exp(jnp.where(live_mask, scores, row_top) - row_top), 0.0)
    row_total = lax.optimization_barrier(jnp.sum(exponent, axis=1, keepdims=True))
    probabilities = low(exponent / row_total)
    return dense(probabilities, pixel_values)

def reference(pixels, pixel_mask, image_sizes, latents, cotangent, feature_gain, query_gain, query_proj, key_proj, value_proj, cross_proj, hidden_gain, hidden_up, hidden_down, tower_gain, tower_query, tower_key, tower_value, tower_proj, final_gain, final_up, final_down):
    pixels_float = pixels.astype(jnp.float32)
    grid_rows = jnp.arange(IMG, dtype=jnp.int32)
    inside = (pixel_mask > 0) & (grid_rows[None, :, None] < image_sizes[:, None, None]) & (grid_rows[None, None, :] < image_sizes[:, None, None])
    valid = inside.astype(jnp.float32)
    checkpointed = jax.checkpoint(cross_item)
    head_size = C // HEADS
    tower_scale = 1.0 / math.sqrt(head_size)

    def forward(latent_rows, feature_gain, query_gain, query_proj, key_proj, value_proj, cross_proj, hidden_gain, hidden_up, hidden_down, tower_gain, tower_query, tower_key, tower_value, tower_proj, final_gain, final_up, final_down):
        query_rows = low(layer_norm(latent_rows, query_gain))
        queries = low_back(low(dense(query_rows, query_proj)))

        def one_item(inputs):
            return checkpointed(inputs[0], inputs[1], inputs[2], inputs[3], feature_gain, key_proj, value_proj)
        attended = lax.map(one_item, (queries, pixels_float, valid, image_sizes))
        attended = low_back(low(attended))
        resid_one = latent_rows + low_back(dense(attended, cross_proj))
        hidden = low(layer_norm(resid_one, hidden_gain))
        lifted = low_back(dense(hidden, hidden_up))
        resid_two = resid_one + low_back(dense(low(gelu_tanh(lifted)), hidden_down))
        tower_rows = low(layer_norm(resid_two, tower_gain))
        split_q = low_back(low(dense(tower_rows, tower_query))).reshape(B, LAT, HEADS, head_size)
        split_k = low_back(low(dense(tower_rows, tower_key))).reshape(B, LAT, HEADS, head_size)
        split_v = low_back(low(dense(tower_rows, tower_value))).reshape(B, LAT, HEADS, head_size)
        tower_scores = low_back(jnp.einsum('bqhd,bkhd->bhqk', split_q, split_k, precision=lax.Precision.HIGHEST) * tower_scale)
        tower_top = lax.optimization_barrier(jnp.max(tower_scores, axis=3, keepdims=True))
        tower_exp = jnp.exp(tower_scores - tower_top)
        tower_probs = low(tower_exp / lax.optimization_barrier(jnp.sum(tower_exp, axis=3, keepdims=True)))
        mixed_heads = jnp.einsum('bhqk,bkhd->bqhd', tower_probs, split_v, precision=lax.Precision.HIGHEST).reshape(B, LAT, C)
        mixed_heads = low_back(low(mixed_heads))
        resid_three = resid_two + low_back(dense(mixed_heads, tower_proj))
        final_rows = low(layer_norm(resid_three, final_gain))
        final_lifted = low_back(dense(final_rows, final_up))
        return resid_three + low_back(dense(low(gelu_tanh(final_lifted)), final_down))
    params = (latents.astype(jnp.float32), feature_gain, query_gain, query_proj.astype(jnp.float32), key_proj.astype(jnp.float32), value_proj.astype(jnp.float32), cross_proj.astype(jnp.float32), hidden_gain, hidden_up.astype(jnp.float32), hidden_down.astype(jnp.float32), tower_gain, tower_query.astype(jnp.float32), tower_key.astype(jnp.float32), tower_value.astype(jnp.float32), tower_proj.astype(jnp.float32), final_gain, final_up.astype(jnp.float32), final_down.astype(jnp.float32))
    output, pullback = jax.vjp(forward, *params)
    grads = pullback(cotangent.astype(jnp.float32))
    return (output.astype(jnp.bfloat16), grads[0], grads[1], grads[2], grads[3], grads[4], grads[5], grads[6], grads[7], grads[8], grads[9], grads[10], grads[11], grads[12], grads[13], grads[14], grads[15], grads[16], grads[17])
```

```python
import math

import jax
import jax.numpy as jnp
from jax import lax
from jax.experimental import pallas as pl
from jax.experimental.pallas import tpu as pltpu
from jax.sharding import PartitionSpec as P

BANDS = 64
FEAT = 261
HEADS = 8


EPSILON = 1e-05
FLOAT = jnp.float32
BFLOAT = jnp.bfloat16


def layer_norm(values, scales):
    centre = jnp.mean(values, axis=-1, keepdims=True)
    shifted = values - centre
    spread = jnp.mean(shifted * shifted, axis=-1, keepdims=True)
    return shifted * lax.rsqrt(spread + EPSILON) * scales


def gelu_tanh(values):
    cubic = values + 0.044715 * values * values * values
    return 0.5 * values * (1.0 + jnp.tanh(0.7978845608028654 * cubic))


def linear(inputs, weight):
    return lax.dot_general(
        inputs, weight, (((inputs.ndim - 1,), (0,)), ((), ())), preferred_element_type=FLOAT
    )


def linear_back(upstream, weight):
    return lax.dot_general(
        upstream, weight, (((upstream.ndim - 1,), (1,)), ((), ())), preferred_element_type=FLOAT
    )


def weight_grad(inputs, upstream):
    flat_inputs = inputs.reshape(-1, inputs.shape[-1])
    flat_upstream = upstream.reshape(-1, upstream.shape[-1])
    return lax.dot_general(
        flat_inputs, flat_upstream, (((0,), (0,)), ((), ())), preferred_element_type=FLOAT
    )


def axis_tables(image_sizes, ids, coord_lane, first_lane):
    side = image_sizes.astype(FLOAT)[:, None]
    coord = -1.0 + 2.0 * ids.astype(FLOAT)[None, :] / (side - 1.0)
    band = jnp.arange(BANDS, dtype=jnp.int32).astype(FLOAT)
    frequency = 1.0 + band[None, :] * (side * 0.5 - 1.0) / (BANDS - 1)
    angle = math.pi * coord[:, :, None] * frequency[:, None, :]
    waves = jnp.concatenate([jnp.sin(angle), jnp.cos(angle)], axis=2)
    count, length = coord.shape
    lead = jnp.zeros((count, length, coord_lane), FLOAT)
    gap = jnp.zeros((count, length, first_lane - coord_lane - 1), FLOAT)
    tail = jnp.zeros((count, length, FEAT - first_lane - 2 * BANDS), FLOAT)
    table = jnp.concatenate([lead, coord[:, :, None], gap, waves, tail], axis=2)
    return table, coord, jnp.sum(waves, axis=2) + coord


MESH = pl.DeviceIdType.MESH


def peer_ty(ty, d):
    return lax.rem(ty + d, lax.axis_size("ty"))


def send(src, dst, send_sem, recv_sem, where):
    copy = pltpu.make_async_remote_copy(
        src_ref=src, dst_ref=dst, send_sem=send_sem, recv_sem=recv_sem,
        device_id=where, device_id_type=MESH,
    )
    copy.start()
    return copy


def greet(places):
    barrier = pltpu.get_barrier_semaphore()
    for place in places:
        pl.semaphore_signal(barrier, inc=1, device_id=place, device_id_type=MESH)
    pl.semaphore_wait(barrier, len(places))


def column_chunk(ref, index, width):
    return ref[:, pl.ds(pl.multiple_of(index * width, width), width)]


def outer(left, right):
    return lax.dot_general(left, right, (((0,), (0,)), ((), ())), preferred_element_type=FLOAT)


def weight_sums_kernel(
    x_ref, g_ref, out_ref,
    xs, gs, ysend, yrecv, own, zsend, zrecv, last,
    local_sem, xg_send, xg_recv, y_send, y_recv, z_send, z_recv, o_send, o_recv,
):
    ty, tx = lax.axis_index("ty"), lax.axis_index("tx")
    z, y = tx // 2, lax.rem(tx, 2)
    tys = [{"ty": lax.rem(ty + d, 4), "tx": tx} for d in (1, 2, 3)]
    beside = {"ty": ty, "tx": 2 * z + 1 - y}
    zs = [{"ty": ty, "tx": 2 * lax.rem(z + d, 4) + y} for d in (1, 2, 3)]
    greet(tys + [beside] + zs)
    rows = x_ref.shape[1]
    started = []
    gathers = [[], []]
    for k in range(2):
        for s, (src, dst) in enumerate(((x_ref, xs), (g_ref, gs))):
            for d in (1, 2, 3):
                gathers[k].append(send(
                    src.at[4 * k + lax.rem(ty + d, 4)], dst.at[k, ty],
                    xg_send.at[k, s, d - 1], xg_recv.at[k, s, d - 1], tys[d - 1],
                ))
            mine = pltpu.make_async_copy(src.at[4 * k + ty], dst.at[k, ty], local_sem.at[k, s])
            mine.start()
            gathers[k].append(mine)
    ycopies = [[], []]
    for k in range(2):
        for copy in gathers[k]:
            copy.wait()
        gk = gs[k].reshape(4 * rows, -1)
        for c in range(4):
            part = xs[k, :, :, pl.ds(pl.multiple_of((2 * c + 1 - y) * 128, 128), 128)]
            ysend[k, c] = outer(part.reshape(4 * rows, 128), gk).astype(BFLOAT)
            ycopies[k].append(send(
                ysend.at[k, c], yrecv.at[k, c], y_send.at[k, c], y_recv.at[k, c], beside
            ))
        for c in range(4):
            at = lax.rem(z + c, 4)
            part = xs[k, :, :, pl.ds(pl.multiple_of((2 * at + y) * 128, 128), 128)]
            own[k, c] = outer(part.reshape(4 * rows, 128), gk)
    zcopies = [[], []]
    for k in range(2):
        for copy in ycopies[k]:
            copy.wait()
        for c in (1, 2, 3, 0):
            at = lax.rem(z + c, 4)
            total = own[k, c] + yrecv[k, at].astype(FLOAT)
            if c == 0:
                own[k, c] = total
            else:
                zsend[k, c - 1] = total.astype(BFLOAT)
                zcopies[k].append(send(
                    zsend.at[k, c - 1], zrecv.at[k, c - 1],
                    z_send.at[k, c - 1], z_recv.at[k, c - 1], zs[c - 1],
                ))
    for k in range(2):
        for copy in zcopies[k]:
            copy.wait()
        total = own[k, 0]
        for c in range(3):
            total = total + zrecv[k, c].astype(FLOAT)
        last[k] = total.astype(BFLOAT)
        for d in (1, 2, 3):
            started.append(send(
                last.at[k], out_ref.at[4 * k + ty], o_send.at[k, d - 1], o_recv.at[k, d - 1],
                tys[d - 1],
            ))
        mine = pltpu.make_async_copy(last.at[k], out_ref.at[4 * k + ty], local_sem.at[k, 0])
        mine.start()
        started.append(mine)
    for copy in started:
        copy.wait()


def weight_sums(x, g):
    count, rows, width = x.shape
    dma = pltpu.SemaphoreType.DMA
    block = (width // 8, width)
    return pl.pallas_call(
        weight_sums_kernel,
        out_shape=jax.ShapeDtypeStruct((count,) + block, BFLOAT),
        in_specs=[pl.BlockSpec(memory_space=pl.ANY)] * 2,
        out_specs=pl.BlockSpec(memory_space=pl.ANY),
        scratch_shapes=[
            pltpu.VMEM((2, 4, rows, width), BFLOAT),
            pltpu.VMEM((2, 4, rows, width), BFLOAT),
            pltpu.VMEM((2, 4) + block, BFLOAT),
            pltpu.VMEM((2, 4) + block, BFLOAT),
            pltpu.VMEM((2, 4) + block, FLOAT),
            pltpu.VMEM((2, 3) + block, BFLOAT),
            pltpu.VMEM((2, 3) + block, BFLOAT),
            pltpu.VMEM((2,) + block, BFLOAT),
            dma((2, 2)), dma((2, 2, 3)), dma((2, 2, 3)), dma((2, 4)), dma((2, 4)),
            dma((2, 3)), dma((2, 3)), dma((2, 3)), dma((2, 3)),
        ],
        compiler_params=pltpu.CompilerParams(
            collective_id=1, has_side_effects=True, vmem_limit_bytes=48 << 20
        ),
        name="weight_sums",
    )(x, g)


def all_sum_kernel(
    v_ref, out_ref, recv1, quarter, recv2, recv3, s1, r1, s2, r2, s3, r3, s4, r4, local_sem
):
    ty, tx = lax.axis_index("ty"), lax.axis_index("tx")
    tys = [{"ty": lax.rem(ty + d, 4), "tx": tx} for d in (1, 2, 3)]
    txs = [{"ty": ty, "tx": lax.rem(tx + d, 8)} for d in range(1, 8)]
    greet(tys + txs)
    copies = [
        send(v_ref.at[lax.rem(ty + d, 4)], recv1.at[d - 1], s1.at[d - 1], r1.at[d - 1], tys[d - 1])
        for d in (1, 2, 3)
    ]
    total = v_ref[ty].astype(FLOAT)
    for d, copy in enumerate(copies):
        copy.wait()
        total = total + recv1[d].astype(FLOAT)
    for c in range(8):
        quarter[c] = total[:, c * 128 : c * 128 + 128].astype(BFLOAT)
    copies = [
        send(quarter.at[lax.rem(tx + d, 8)], recv2.at[d - 1], s2.at[d - 1], r2.at[d - 1], txs[d - 1])
        for d in range(1, 8)
    ]
    total = quarter[tx].astype(FLOAT)
    for d, copy in enumerate(copies):
        copy.wait()
        total = total + recv2[d].astype(FLOAT)
    recv3[tx] = total.astype(BFLOAT)
    copies = [
        send(recv3.at[tx], recv3.at[tx], s3.at[d - 1], r3.at[d - 1], txs[d - 1])
        for d in range(1, 8)
    ]
    for copy in copies:
        copy.wait()
    copies = [
        send(recv3, out_ref.at[ty], s4.at[d - 1], r4.at[d - 1], tys[d - 1]) for d in (1, 2, 3)
    ]
    mine = pltpu.make_async_copy(recv3, out_ref.at[ty], local_sem)
    mine.start()
    for copy in copies + [mine]:
        copy.wait()


def all_sum(v):
    rows, width = v.shape
    part = rows // 4
    dma = pltpu.SemaphoreType.DMA
    out = pl.pallas_call(
        all_sum_kernel,
        out_shape=jax.ShapeDtypeStruct((4, 8, part, 128), BFLOAT),
        in_specs=[pl.BlockSpec(memory_space=pltpu.VMEM)],
        out_specs=pl.BlockSpec(memory_space=pl.ANY),
        scratch_shapes=[
            pltpu.VMEM((3, part, width), BFLOAT),
            pltpu.VMEM((8, part, 128), BFLOAT),
            pltpu.VMEM((7, part, 128), BFLOAT),
            pltpu.VMEM((8, part, 128), BFLOAT),
            dma((3,)), dma((3,)), dma((7,)), dma((7,)), dma((7,)), dma((7,)), dma((3,)), dma((3,)),
            dma(()),
        ],
        compiler_params=pltpu.CompilerParams(
            collective_id=2, has_side_effects=True, vmem_limit_bytes=32 << 20
        ),
        name="all_sum",
    )(v.reshape(4, part, width))
    return jnp.transpose(out, (0, 2, 1, 3)).reshape(rows, width)


def on_device_fast(
    pixels,
    pixel_mask,
    image_sizes,
    latents,
    cotangent,
    feature_gain,
    query_gain,
    query_proj,
    key_proj,
    value_proj,
    cross_proj,
    hidden_gain,
    hidden_up,
    hidden_down,
    tower_gain,
    tower_query,
    tower_key,
    tower_value,
    tower_proj,
    final_gain,
    final_up,
    final_down,
):
    item_count = pixels.shape[0]
    tile_height = pixels.shape[2]
    tile_width = pixels.shape[3]
    model_width = latents.shape[2]
    rows_here = latents.shape[1]
    head_count = HEADS
    head_size = model_width // head_count
    cross_scale = 1.0 / math.sqrt(model_width)
    tower_scale = 1.0 / math.sqrt(head_size)
    row_ids = lax.axis_index("ty") * tile_height + jnp.arange(tile_height, dtype=jnp.int32)
    col_ids = lax.axis_index("tx") * tile_width + jnp.arange(tile_width, dtype=jnp.int32)
    all_cols = jnp.arange(tile_width * lax.axis_size("tx"), dtype=jnp.int32)
    wide_pixels = lax.all_gather(pixels, "tx", axis=3, tiled=True).astype(FLOAT)
    wide_mask = lax.all_gather(pixel_mask, "tx", axis=2, tiled=True)
    side_sizes = image_sizes[:, None, None]
    live = (
        (wide_mask > 0)
        & (row_ids[None, :, None] < side_sizes)
        & (all_cols[None, None, :] < side_sizes)
    )[:, None]
    row_table, row_coord, row_sum = axis_tables(image_sizes, row_ids, 3, 5)
    col_table, col_coord, col_sum = axis_tables(image_sizes, all_cols, 4, 5 + 2 * BANDS)
    pixel_mean = (
        jnp.sum(wide_pixels, axis=1) + row_sum[:, :, None] + col_sum[:, None, :]
    ) / FEAT
    pixel_square = (
        jnp.sum(wide_pixels * wide_pixels, axis=1)
        + (row_coord * row_coord)[:, :, None]
        + (col_coord * col_coord)[:, None, :]
        + 2.0 * BANDS
    ) / FEAT
    pixel_rate = lax.rsqrt(pixel_square - pixel_mean * pixel_mean + EPSILON)
    exact = lax.Precision.HIGHEST

    def against_pixels(coefs):
        by_row = jnp.einsum("blf,bif->bli", coefs, row_table, precision=exact)
        by_col = jnp.einsum("blf,bjf->blj", coefs, col_table, precision=exact)
        total = by_row[:, :, :, None] + by_col[:, :, None, :]
        for c in range(3):
            total = total + coefs[:, :, c][:, :, None, None] * wide_pixels[:, None, c]
        total = total - jnp.sum(coefs, axis=2)[:, :, None, None] * pixel_mean[:, None]
        return total * pixel_rate[:, None]

    def over_pixels(weights):
        scaled = weights * pixel_rate[:, None]
        by_row = jnp.sum(scaled, axis=3)
        by_col = jnp.sum(scaled, axis=2)
        total = jnp.einsum("bli,bif->blf", by_row, row_table, precision=exact)
        total = total + jnp.einsum("blj,bjf->blf", by_col, col_table, precision=exact)
        colour = jnp.stack(
            [jnp.sum(scaled * wide_pixels[:, None, c], axis=(2, 3)) for c in range(3)], axis=2
        )
        total = total + jnp.pad(colour, ((0, 0), (0, 0), (0, FEAT - 3)))
        return total - jnp.sum(scaled * pixel_mean[:, None], axis=(2, 3))[:, :, None]

    latent_rows = latents.astype(FLOAT)
    query_normed, back_query_norm = jax.vjp(layer_norm, latent_rows, query_gain)
    query_input = query_normed.astype(BFLOAT)
    own_queries = linear(query_input, query_proj).astype(BFLOAT)
    raw_query = linear_back(own_queries, key_proj) * cross_scale
    scores = against_pixels(raw_query * feature_gain)
    row_top = jnp.max(jnp.where(live, scores, -1e30), axis=(2, 3))
    all_top = lax.pmax(row_top, "ty")
    row_exp = jnp.where(live, jnp.exp(scores - all_top[:, :, None, None]), 0.0)
    row_total = lax.psum(jnp.sum(row_exp, axis=(2, 3)), "ty")
    cross_exact = row_exp / row_total[:, :, None, None]
    raw_mix = lax.psum(over_pixels(cross_exact), "ty")
    mix = raw_mix * feature_gain
    attended = linear(mix.astype(BFLOAT), value_proj)
    attended_input = attended.astype(BFLOAT)
    resid_one = latent_rows + linear(attended_input, cross_proj)
    hidden_normed, back_hidden_norm = jax.vjp(layer_norm, resid_one, hidden_gain)
    hidden_input = hidden_normed.astype(BFLOAT)
    hidden_lifted, back_hidden_gelu = jax.vjp(gelu_tanh, linear(hidden_input, hidden_up))
    hidden_act = hidden_lifted.astype(BFLOAT)
    resid_two = resid_one + linear(hidden_act, hidden_down)
    tower_normed, back_tower_norm = jax.vjp(layer_norm, resid_two, tower_gain)
    tower_input = tower_normed.astype(BFLOAT)
    tower_q = linear(tower_input, tower_query).astype(BFLOAT)
    tower_k = linear(tower_input, tower_key).astype(BFLOAT)
    tower_v = linear(tower_input, tower_value).astype(BFLOAT)
    all_keys, all_values = (
        lax.all_gather(tower_k, "tx", axis=1, tiled=True),
        lax.all_gather(tower_v, "tx", axis=1, tiled=True),
    )
    split_q = tower_q.reshape(item_count, rows_here, head_count, head_size)
    split_k = all_keys.reshape(item_count, -1, head_count, head_size)
    split_v = all_values.reshape(item_count, -1, head_count, head_size)
    tower_scores = (
        jnp.einsum("bqhd,bkhd->bhqk", split_q, split_k, preferred_element_type=FLOAT) * tower_scale
    )
    tower_top = jnp.max(tower_scores, axis=3, keepdims=True)
    tower_exp = jnp.exp(tower_scores - tower_top)
    tower_total = jnp.sum(tower_exp, axis=3, keepdims=True)
    tower_exact = tower_exp / tower_total
    tower_probs = tower_exact.astype(BFLOAT)
    mixed = jnp.einsum(
        "bhqk,bkhd->bqhd", tower_probs, split_v, preferred_element_type=FLOAT
    ).reshape(item_count, rows_here, model_width)
    mixed_input = mixed.astype(BFLOAT)
    resid_three = resid_two + linear(mixed_input, tower_proj)
    final_normed, back_final_norm = jax.vjp(layer_norm, resid_three, final_gain)
    final_input = final_normed.astype(BFLOAT)
    final_lifted, back_final_gelu = jax.vjp(gelu_tanh, linear(final_input, final_up))
    final_act = final_lifted.astype(BFLOAT)
    resid_four = resid_three + linear(final_act, final_down)
    grad_four = cotangent.astype(FLOAT)
    grad_final_lift = back_final_gelu(linear_back(cotangent, final_down))[0].astype(BFLOAT)
    grad_rows_three, final_gain_grad = back_final_norm(linear_back(grad_final_lift, final_up))
    grad_three = grad_four + grad_rows_three
    grad_tower_out = grad_three.astype(BFLOAT)
    grad_mixed_flat = linear_back(grad_tower_out, tower_proj).astype(BFLOAT)
    grad_mixed = grad_mixed_flat.reshape(item_count, rows_here, head_count, head_size)
    grad_tower_p = jnp.einsum("bqhd,bkhd->bhqk", grad_mixed, split_v, preferred_element_type=FLOAT)
    tower_delta = jnp.sum(tower_exact * grad_tower_p, axis=3, keepdims=True)
    grad_tower_scores = (tower_exact * (grad_tower_p - tower_delta)).astype(BFLOAT)
    grad_tower_q = (
        (
            jnp.einsum("bhqk,bkhd->bqhd", grad_tower_scores, split_k, preferred_element_type=FLOAT)
            * tower_scale
        )
        .astype(BFLOAT)
        .reshape(item_count, rows_here, model_width)
    )
    value_part = jnp.einsum(
        "bhqk,bqhd->bkhd", tower_probs, grad_mixed, preferred_element_type=FLOAT
    )
    key_part = (
        jnp.einsum("bhqk,bqhd->bkhd", grad_tower_scores, split_q, preferred_element_type=FLOAT)
        * tower_scale
    )
    key_sums, value_sums = (
        lax.psum_scatter(
            key_part.reshape(item_count, -1, model_width), "tx", scatter_dimension=1, tiled=True
        ),
        lax.psum_scatter(
            value_part.reshape(item_count, -1, model_width), "tx", scatter_dimension=1, tiled=True
        ),
    )
    grad_tower_k = key_sums.astype(BFLOAT)
    grad_tower_v = value_sums.astype(BFLOAT)
    grad_tower_rows = (
        linear_back(grad_tower_q, tower_query)
        + linear_back(grad_tower_k, tower_key)
        + linear_back(grad_tower_v, tower_value)
    )
    grad_rows_two, tower_gain_grad = back_tower_norm(grad_tower_rows)
    grad_two = grad_three + grad_rows_two
    grad_hidden_out = grad_two.astype(BFLOAT)
    grad_hidden_lift = back_hidden_gelu(linear_back(grad_hidden_out, hidden_down))[0].astype(BFLOAT)
    grad_rows_one, hidden_gain_grad = back_hidden_norm(linear_back(grad_hidden_lift, hidden_up))
    grad_one = grad_two + grad_rows_one
    grad_cross_out = grad_one.astype(BFLOAT)
    grad_attended = linear_back(grad_cross_out, cross_proj).astype(BFLOAT)
    raw_up = linear_back(grad_attended, value_proj)
    grad_probs = against_pixels(raw_up * feature_gain)
    cross_delta = jnp.sum(grad_attended.astype(FLOAT) * attended, axis=2)
    grad_scores = cross_exact * (grad_probs - cross_delta[:, :, None, None])
    raw_grad_mix = lax.psum(over_pixels(grad_scores), "ty")
    grad_mix = (raw_grad_mix * feature_gain).astype(BFLOAT)
    grad_queries = (linear(grad_mix, key_proj) * cross_scale).astype(BFLOAT)
    feature_part = jnp.sum(raw_grad_mix * raw_query + raw_mix * raw_up, axis=(0, 1))
    grad_latent_rows, query_gain_grad = back_query_norm(linear_back(grad_queries, query_proj))
    latent_grad = grad_one + grad_latent_rows
    share = item_count * rows_here // lax.axis_size("ty")
    ty_index = lax.axis_index("ty")

    def own_rows(rows):
        return lax.dynamic_slice_in_dim(
            rows.reshape(item_count * rows_here, -1), ty_index * share, share, 0
        )

    pairs = [
        (final_act, cotangent),
        (final_input, grad_final_lift),
        (mixed_input, grad_tower_out),
        (tower_input, grad_tower_q),
        (tower_input, grad_tower_k),
        (tower_input, grad_tower_v),
        (hidden_act, grad_hidden_out),
        (hidden_input, grad_hidden_lift),
    ]
    sums = weight_sums(
        jnp.stack([own_rows(x) for x, _ in pairs]), jnp.stack([own_rows(g) for _, g in pairs])
    ).astype(FLOAT)
    quarter = 1.0 / lax.axis_size("ty")
    lanes = ((0, 11), (0, 0))
    gains = jnp.stack(
        [query_gain_grad, hidden_gain_grad, tower_gain_grad, final_gain_grad,
         jnp.pad(feature_part, (0, model_width - FEAT))]
    ) * quarter
    joined = jnp.concatenate(
        [
            jnp.pad(weight_grad(own_rows(mix).astype(BFLOAT), own_rows(grad_cross_out)), lanes),
            jnp.pad(weight_grad(own_rows(grad_mix), own_rows(query_input)), lanes),
            jnp.pad(gains, ((0, 27), (0, 0))),
        ]
    )
    joined = all_sum(joined.astype(BFLOAT))
    cross_core = joined[:FEAT]
    query_core = joined[272 : 272 + FEAT]
    value_proj_grad = linear_back(cross_core, cross_proj)
    key_proj_grad = linear(query_core, query_proj) * cross_scale
    wide = model_width // lax.axis_size("tx")
    tx_from = lax.axis_index("tx") * wide
    cross_proj_grad = weight_grad(
        lax.dynamic_slice_in_dim(value_proj, tx_from, wide, 1), cross_core
    )
    query_proj_grad = weight_grad(
        lax.dynamic_slice_in_dim(query_core, tx_from, wide, 1), key_proj
    ) * cross_scale
    gain_sums = joined[544:549].astype(FLOAT)
    gain_here = lax.dynamic_slice_in_dim(gain_sums, tx_from, wide, 1)
    return (
        resid_four.astype(BFLOAT),
        latent_grad,
        gain_sums[4, :FEAT],
        gain_here[0],
        query_proj_grad,
        key_proj_grad,
        value_proj_grad,
        cross_proj_grad,
        gain_here[1],
        sums[7],
        sums[6],
        gain_here[2],
        sums[3],
        sums[4],
        sums[5],
        sums[2],
        gain_here[3],
        sums[1],
        sums[0],
    )


def on_device(
    pixels,
    pixel_mask,
    image_sizes,
    latents,
    cotangent,
    feature_gain,
    query_gain,
    query_proj,
    key_proj,
    value_proj,
    cross_proj,
    hidden_gain,
    hidden_up,
    hidden_down,
    tower_gain,
    tower_query,
    tower_key,
    tower_value,
    tower_proj,
    final_gain,
    final_up,
    final_down,
):
    item_count = pixels.shape[0]
    tile_height = pixels.shape[2]
    tile_width = pixels.shape[3]
    model_width = latents.shape[2]
    rows_here = latents.shape[1]
    head_count = HEADS
    head_size = model_width // head_count
    cross_scale = 1.0 / math.sqrt(model_width)
    tower_scale = 1.0 / math.sqrt(head_size)
    row_ids = lax.axis_index("ty") * tile_height + jnp.arange(tile_height, dtype=jnp.int32)
    col_ids = lax.axis_index("tx") * tile_width + jnp.arange(tile_width, dtype=jnp.int32)
    all_cols = jnp.arange(tile_width * lax.axis_size("tx"), dtype=jnp.int32)
    wide_pixels = lax.all_gather(pixels, "tx", axis=3, tiled=True).astype(FLOAT)
    wide_mask = lax.all_gather(pixel_mask, "tx", axis=2, tiled=True)
    side_sizes = image_sizes[:, None, None]
    live = (
        (wide_mask > 0)
        & (row_ids[None, :, None] < side_sizes)
        & (all_cols[None, None, :] < side_sizes)
    )[:, None]
    row_table, row_coord, row_sum = axis_tables(image_sizes, row_ids, 3, 5)
    col_table, col_coord, col_sum = axis_tables(image_sizes, all_cols, 4, 5 + 2 * BANDS)
    pixel_mean = (
        jnp.sum(wide_pixels, axis=1) + row_sum[:, :, None] + col_sum[:, None, :]
    ) / FEAT
    pixel_square = (
        jnp.sum(wide_pixels * wide_pixels, axis=1)
        + (row_coord * row_coord)[:, :, None]
        + (col_coord * col_coord)[:, None, :]
        + 2.0 * BANDS
    ) / FEAT
    pixel_rate = lax.rsqrt(pixel_square - pixel_mean * pixel_mean + EPSILON)
    exact = lax.Precision.HIGHEST

    def against_pixels(coefs):
        by_row = jnp.einsum("blf,bif->bli", coefs, row_table, precision=exact)
        by_col = jnp.einsum("blf,bjf->blj", coefs, col_table, precision=exact)
        total = by_row[:, :, :, None] + by_col[:, :, None, :]
        for c in range(3):
            total = total + coefs[:, :, c][:, :, None, None] * wide_pixels[:, None, c]
        total = total - jnp.sum(coefs, axis=2)[:, :, None, None] * pixel_mean[:, None]
        return total * pixel_rate[:, None]

    def over_pixels(weights):
        scaled = weights * pixel_rate[:, None]
        by_row = jnp.sum(scaled, axis=3)
        by_col = jnp.sum(scaled, axis=2)
        total = jnp.einsum("bli,bif->blf", by_row, row_table, precision=exact)
        total = total + jnp.einsum("blj,bjf->blf", by_col, col_table, precision=exact)
        colour = jnp.stack(
            [jnp.sum(scaled * wide_pixels[:, None, c], axis=(2, 3)) for c in range(3)], axis=2
        )
        total = total + jnp.pad(colour, ((0, 0), (0, 0), (0, FEAT - 3)))
        return total - jnp.sum(scaled * pixel_mean[:, None], axis=(2, 3))[:, :, None]

    latent_rows = latents.astype(FLOAT)
    query_normed, back_query_norm = jax.vjp(layer_norm, latent_rows, query_gain)
    query_input = query_normed.astype(BFLOAT)
    own_queries = linear(query_input, query_proj).astype(BFLOAT)
    raw_query = linear_back(own_queries, key_proj) * cross_scale
    scores = against_pixels(raw_query * feature_gain)
    row_top = jnp.max(jnp.where(live, scores, -1e30), axis=(2, 3))
    all_top = lax.pmax(row_top, "ty")
    row_exp = jnp.where(live, jnp.exp(scores - all_top[:, :, None, None]), 0.0)
    row_total = lax.psum(jnp.sum(row_exp, axis=(2, 3)), "ty")
    cross_exact = row_exp / row_total[:, :, None, None]
    raw_mix = lax.psum(over_pixels(cross_exact), "ty")
    mix = raw_mix * feature_gain
    attended = linear(mix.astype(BFLOAT), value_proj)
    attended_input = attended.astype(BFLOAT)
    resid_one = latent_rows + linear(attended_input, cross_proj)
    hidden_normed, back_hidden_norm = jax.vjp(layer_norm, resid_one, hidden_gain)
    hidden_input = hidden_normed.astype(BFLOAT)
    hidden_lifted, back_hidden_gelu = jax.vjp(gelu_tanh, linear(hidden_input, hidden_up))
    hidden_act = hidden_lifted.astype(BFLOAT)
    resid_two = resid_one + linear(hidden_act, hidden_down)
    tower_normed, back_tower_norm = jax.vjp(layer_norm, resid_two, tower_gain)
    tower_input = tower_normed.astype(BFLOAT)
    tower_q = linear(tower_input, tower_query).astype(BFLOAT)
    tower_k = linear(tower_input, tower_key).astype(BFLOAT)
    tower_v = linear(tower_input, tower_value).astype(BFLOAT)
    all_keys, all_values = (
        lax.all_gather(tower_k, "tx", axis=1, tiled=True),
        lax.all_gather(tower_v, "tx", axis=1, tiled=True),
    )
    split_q = tower_q.reshape(item_count, rows_here, head_count, head_size)
    split_k = all_keys.reshape(item_count, -1, head_count, head_size)
    split_v = all_values.reshape(item_count, -1, head_count, head_size)
    tower_scores = (
        jnp.einsum("bqhd,bkhd->bhqk", split_q, split_k, preferred_element_type=FLOAT) * tower_scale
    )
    tower_top = jnp.max(tower_scores, axis=3, keepdims=True)
    tower_exp = jnp.exp(tower_scores - tower_top)
    tower_total = jnp.sum(tower_exp, axis=3, keepdims=True)
    tower_exact = tower_exp / tower_total
    tower_probs = tower_exact.astype(BFLOAT)
    mixed = jnp.einsum(
        "bhqk,bkhd->bqhd", tower_probs, split_v, preferred_element_type=FLOAT
    ).reshape(item_count, rows_here, model_width)
    mixed_input = mixed.astype(BFLOAT)
    resid_three = resid_two + linear(mixed_input, tower_proj)
    final_normed, back_final_norm = jax.vjp(layer_norm, resid_three, final_gain)
    final_input = final_normed.astype(BFLOAT)
    final_lifted, back_final_gelu = jax.vjp(gelu_tanh, linear(final_input, final_up))
    final_act = final_lifted.astype(BFLOAT)
    resid_four = resid_three + linear(final_act, final_down)
    grad_four = cotangent.astype(FLOAT)
    final_down_grad = weight_grad(final_act, cotangent)
    grad_final_lift = back_final_gelu(linear_back(cotangent, final_down))[0].astype(BFLOAT)
    final_up_grad = weight_grad(final_input, grad_final_lift)
    grad_rows_three, final_gain_grad = back_final_norm(linear_back(grad_final_lift, final_up))
    grad_three = grad_four + grad_rows_three
    grad_tower_out = grad_three.astype(BFLOAT)
    tower_proj_grad = weight_grad(mixed_input, grad_tower_out)
    grad_mixed_flat = linear_back(grad_tower_out, tower_proj).astype(BFLOAT)
    grad_mixed = grad_mixed_flat.reshape(item_count, rows_here, head_count, head_size)
    grad_tower_p = jnp.einsum("bqhd,bkhd->bhqk", grad_mixed, split_v, preferred_element_type=FLOAT)
    tower_delta = jnp.sum(tower_exact * grad_tower_p, axis=3, keepdims=True)
    grad_tower_scores = (tower_exact * (grad_tower_p - tower_delta)).astype(BFLOAT)
    grad_tower_q = (
        (
            jnp.einsum("bhqk,bkhd->bqhd", grad_tower_scores, split_k, preferred_element_type=FLOAT)
            * tower_scale
        )
        .astype(BFLOAT)
        .reshape(item_count, rows_here, model_width)
    )
    value_part = jnp.einsum(
        "bhqk,bqhd->bkhd", tower_probs, grad_mixed, preferred_element_type=FLOAT
    )
    key_part = (
        jnp.einsum("bhqk,bqhd->bkhd", grad_tower_scores, split_q, preferred_element_type=FLOAT)
        * tower_scale
    )
    key_sums, value_sums = (
        lax.psum_scatter(
            key_part.reshape(item_count, -1, model_width), "tx", scatter_dimension=1, tiled=True
        ),
        lax.psum_scatter(
            value_part.reshape(item_count, -1, model_width), "tx", scatter_dimension=1, tiled=True
        ),
    )
    grad_tower_k = key_sums.astype(BFLOAT)
    grad_tower_v = value_sums.astype(BFLOAT)
    tower_query_grad = weight_grad(tower_input, grad_tower_q)
    tower_key_grad = weight_grad(tower_input, grad_tower_k)
    tower_value_grad = weight_grad(tower_input, grad_tower_v)
    grad_tower_rows = (
        linear_back(grad_tower_q, tower_query)
        + linear_back(grad_tower_k, tower_key)
        + linear_back(grad_tower_v, tower_value)
    )
    grad_rows_two, tower_gain_grad = back_tower_norm(grad_tower_rows)
    grad_two = grad_three + grad_rows_two
    grad_hidden_out = grad_two.astype(BFLOAT)
    hidden_down_grad = weight_grad(hidden_act, grad_hidden_out)
    grad_hidden_lift = back_hidden_gelu(linear_back(grad_hidden_out, hidden_down))[0].astype(BFLOAT)
    hidden_up_grad = weight_grad(hidden_input, grad_hidden_lift)
    grad_rows_one, hidden_gain_grad = back_hidden_norm(linear_back(grad_hidden_lift, hidden_up))
    grad_one = grad_two + grad_rows_one
    grad_cross_out = grad_one.astype(BFLOAT)
    cross_proj_grad = weight_grad(attended_input, grad_cross_out)
    grad_attended = linear_back(grad_cross_out, cross_proj).astype(BFLOAT)
    raw_up = linear_back(grad_attended, value_proj)
    grad_probs = against_pixels(raw_up * feature_gain)
    cross_delta = jnp.sum(grad_attended.astype(FLOAT) * attended, axis=2)
    grad_scores = cross_exact * (grad_probs - cross_delta[:, :, None, None])
    raw_grad_mix = lax.psum(over_pixels(grad_scores), "ty")
    grad_mix = (raw_grad_mix * feature_gain).astype(BFLOAT)
    grad_queries = (linear(grad_mix, key_proj) * cross_scale).astype(BFLOAT)
    key_proj_grad = weight_grad(grad_mix, own_queries) * cross_scale
    value_proj_grad = weight_grad(mix.astype(BFLOAT), grad_attended)
    feature_part = jnp.sum(raw_grad_mix * raw_query + raw_mix * raw_up, axis=(0, 1))
    pixel_sums = lax.psum((key_proj_grad, value_proj_grad, feature_part), "tx")
    query_proj_grad = weight_grad(query_input, grad_queries)
    grad_latent_rows, query_gain_grad = back_query_norm(linear_back(grad_queries, query_proj))
    latent_grad = grad_one + grad_latent_rows
    summed = (
        lax.psum_scatter(query_gain_grad, "tx", scatter_dimension=0, tiled=True),
        lax.psum_scatter(query_proj_grad, "tx", scatter_dimension=0, tiled=True),
        lax.psum_scatter(cross_proj_grad, "tx", scatter_dimension=0, tiled=True),
        lax.psum_scatter(hidden_gain_grad, "tx", scatter_dimension=0, tiled=True),
        lax.psum_scatter(hidden_up_grad, "tx", scatter_dimension=0, tiled=True),
        lax.psum_scatter(hidden_down_grad, "tx", scatter_dimension=0, tiled=True),
        lax.psum_scatter(tower_gain_grad, "tx", scatter_dimension=0, tiled=True),
        lax.psum_scatter(tower_query_grad, "tx", scatter_dimension=0, tiled=True),
        lax.psum_scatter(tower_key_grad, "tx", scatter_dimension=0, tiled=True),
        lax.psum_scatter(tower_value_grad, "tx", scatter_dimension=0, tiled=True),
        lax.psum_scatter(tower_proj_grad, "tx", scatter_dimension=0, tiled=True),
        lax.psum_scatter(final_gain_grad, "tx", scatter_dimension=0, tiled=True),
        lax.psum_scatter(final_up_grad, "tx", scatter_dimension=0, tiled=True),
        lax.psum_scatter(final_down_grad, "tx", scatter_dimension=0, tiled=True),
    )
    return (
        resid_four.astype(BFLOAT),
        latent_grad,
        pixel_sums[2],
        summed[0],
        summed[1],
        pixel_sums[0],
        pixel_sums[1],
        summed[2],
        summed[3],
        summed[4],
        summed[5],
        summed[6],
        summed[7],
        summed[8],
        summed[9],
        summed[10],
        summed[11],
        summed[12],
        summed[13],
    )


def solution(mesh):
    in_specs = (
        P(None, None, "ty", "tx"),
        P(None, "ty", "tx"),
        P(),
        P(None, "tx", None),
        P(None, "tx", None),
        P(),
        P(),
        P(),
        P(),
        P(),
        P(),
        P(),
        P(),
        P(),
        P(),
        P(),
        P(),
        P(),
        P(),
        P(),
        P(),
        P(),
    )
    out_specs = (
        P(None, "tx", None),
        P(None, "tx", None),
        P(),
        P("tx"),
        P("tx", None),
        P(),
        P(),
        P("tx", None),
        P("tx"),
        P("tx", None),
        P("tx", None),
        P("tx"),
        P("tx", None),
        P("tx", None),
        P("tx", None),
        P("tx", None),
        P("tx"),
        P("tx", None),
        P("tx", None),
    )
    fits = mesh.shape["ty"] == 4 and mesh.shape["tx"] == HEADS
    plan = on_device_fast if fits else on_device
    return jax.shard_map(
        plan, mesh=mesh, in_specs=in_specs, out_specs=out_specs, check_vma=False
    )
```

```python
import math

import jax
import jax.numpy as jnp
from jax import lax
from jax.experimental import pallas as pl
from jax.experimental.pallas import tpu as pltpu
from jax.sharding import PartitionSpec as P

BANDS = 64
FEAT = 261
HEADS = 8


EPSILON = 1e-05
FLOAT = jnp.float32
BFLOAT = jnp.bfloat16


def layer_norm(values, scales):
    centre = jnp.mean(values, axis=-1, keepdims=True)
    shifted = values - centre
    spread = jnp.mean(shifted * shifted, axis=-1, keepdims=True)
    return shifted * lax.rsqrt(spread + EPSILON) * scales


def gelu_tanh(values):
    cubic = values + 0.044715 * values * values * values
    return 0.5 * values * (1.0 + jnp.tanh(0.7978845608028654 * cubic))


def linear(inputs, weight):
    return lax.dot_general(
        inputs, weight, (((inputs.ndim - 1,), (0,)), ((), ())), preferred_element_type=FLOAT
    )


def linear_back(upstream, weight):
    return lax.dot_general(
        upstream, weight, (((upstream.ndim - 1,), (1,)), ((), ())), preferred_element_type=FLOAT
    )


def weight_grad(inputs, upstream):
    flat_inputs = inputs.reshape(-1, inputs.shape[-1])
    flat_upstream = upstream.reshape(-1, upstream.shape[-1])
    return lax.dot_general(
        flat_inputs, flat_upstream, (((0,), (0,)), ((), ())), preferred_element_type=FLOAT
    )


def axis_tables(image_sizes, ids, coord_lane, first_lane):
    side = image_sizes.astype(FLOAT)[:, None]
    coord = -1.0 + 2.0 * ids.astype(FLOAT)[None, :] / (side - 1.0)
    band = jnp.arange(BANDS, dtype=jnp.int32).astype(FLOAT)
    frequency = 1.0 + band[None, :] * (side * 0.5 - 1.0) / (BANDS - 1)
    angle = math.pi * coord[:, :, None] * frequency[:, None, :]
    waves = jnp.concatenate([jnp.sin(angle), jnp.cos(angle)], axis=2)
    count, length = coord.shape
    lead = jnp.zeros((count, length, coord_lane), FLOAT)
    gap = jnp.zeros((count, length, first_lane - coord_lane - 1), FLOAT)
    tail = jnp.zeros((count, length, FEAT - first_lane - 2 * BANDS), FLOAT)
    table = jnp.concatenate([lead, coord[:, :, None], gap, waves, tail], axis=2)
    return table, coord, jnp.sum(waves, axis=2) + coord


MESH = pl.DeviceIdType.MESH


def peer_ty(ty, d):
    return lax.rem(ty + d, lax.axis_size("ty"))


def send(src, dst, send_sem, recv_sem, where):
    copy = pltpu.make_async_remote_copy(
        src_ref=src, dst_ref=dst, send_sem=send_sem, recv_sem=recv_sem,
        device_id=where, device_id_type=MESH,
    )
    copy.start()
    return copy


def greet(places):
    barrier = pltpu.get_barrier_semaphore()
    for place in places:
        pl.semaphore_signal(barrier, inc=1, device_id=place, device_id_type=MESH)
    pl.semaphore_wait(barrier, len(places))


def column_chunk(ref, index, width):
    return ref[:, pl.ds(pl.multiple_of(index * width, width), width)]


def outer(left, right):
    return lax.dot_general(left, right, (((0,), (0,)), ((), ())), preferred_element_type=FLOAT)


def weight_sums_kernel(
    x_ref, g_ref, out_ref,
    xs, gs, ysend, yrecv, own, zsend, zrecv, last,
    local_sem, xg_send, xg_recv, y_send, y_recv, z_send, z_recv, o_send, o_recv,
):
    ty, tx = lax.axis_index("ty"), lax.axis_index("tx")
    z, y = tx // 2, lax.rem(tx, 2)
    tys = [{"ty": lax.rem(ty + d, 4), "tx": tx} for d in (1, 2, 3)]
    beside = {"ty": ty, "tx": 2 * z + 1 - y}
    zs = [{"ty": ty, "tx": 2 * lax.rem(z + d, 4) + y} for d in (1, 2, 3)]
    greet(tys + [beside] + zs)
    rows = x_ref.shape[1]
    started = []
    gathers = [[], []]
    for k in range(2):
        for s, (src, dst) in enumerate(((x_ref, xs), (g_ref, gs))):
            for d in (1, 2, 3):
                gathers[k].append(send(
                    src.at[4 * k + lax.rem(ty + d, 4)], dst.at[k, ty],
                    xg_send.at[k, s, d - 1], xg_recv.at[k, s, d - 1], tys[d - 1],
                ))
            mine = pltpu.make_async_copy(src.at[4 * k + ty], dst.at[k, ty], local_sem.at[k, s])
            mine.start()
            gathers[k].append(mine)
    ycopies = [[], []]
    for k in range(2):
        for copy in gathers[k]:
            copy.wait()
        gk = gs[k].reshape(4 * rows, -1)
        for c in range(4):
            part = xs[k, :, :, pl.ds(pl.multiple_of((2 * c + 1 - y) * 128, 128), 128)]
            ysend[k, c] = outer(part.reshape(4 * rows, 128), gk).astype(BFLOAT)
            ycopies[k].append(send(
                ysend.at[k, c], yrecv.at[k, c], y_send.at[k, c], y_recv.at[k, c], beside
            ))
        for c in range(4):
            at = lax.rem(z + c, 4)
            part = xs[k, :, :, pl.ds(pl.multiple_of((2 * at + y) * 128, 128), 128)]
            own[k, c] = outer(part.reshape(4 * rows, 128), gk)
    zcopies = [[], []]
    for k in range(2):
        for copy in ycopies[k]:
            copy.wait()
        for c in (1, 2, 3, 0):
            at = lax.rem(z + c, 4)
            total = own[k, c] + yrecv[k, at].astype(FLOAT)
            if c == 0:
                own[k, c] = total
            else:
                zsend[k, c - 1] = total.astype(BFLOAT)
                zcopies[k].append(send(
                    zsend.at[k, c - 1], zrecv.at[k, c - 1],
                    z_send.at[k, c - 1], z_recv.at[k, c - 1], zs[c - 1],
                ))
    for k in range(2):
        for copy in zcopies[k]:
            copy.wait()
        total = own[k, 0]
        for c in range(3):
            total = total + zrecv[k, c].astype(FLOAT)
        last[k] = total.astype(BFLOAT)
        for d in (1, 2, 3):
            started.append(send(
                last.at[k], out_ref.at[4 * k + ty], o_send.at[k, d - 1], o_recv.at[k, d - 1],
                tys[d - 1],
            ))
        mine = pltpu.make_async_copy(last.at[k], out_ref.at[4 * k + ty], local_sem.at[k, 0])
        mine.start()
        started.append(mine)
    for copy in started:
        copy.wait()


def weight_sums(x, g):
    count, rows, width = x.shape
    dma = pltpu.SemaphoreType.DMA
    block = (width // 8, width)
    return pl.pallas_call(
        weight_sums_kernel,
        out_shape=jax.ShapeDtypeStruct((count,) + block, BFLOAT),
        in_specs=[pl.BlockSpec(memory_space=pl.ANY)] * 2,
        out_specs=pl.BlockSpec(memory_space=pl.ANY),
        scratch_shapes=[
            pltpu.VMEM((2, 4, rows, width), BFLOAT),
            pltpu.VMEM((2, 4, rows, width), BFLOAT),
            pltpu.VMEM((2, 4) + block, BFLOAT),
            pltpu.VMEM((2, 4) + block, BFLOAT),
            pltpu.VMEM((2, 4) + block, FLOAT),
            pltpu.VMEM((2, 3) + block, BFLOAT),
            pltpu.VMEM((2, 3) + block, BFLOAT),
            pltpu.VMEM((2,) + block, BFLOAT),
            dma((2, 2)), dma((2, 2, 3)), dma((2, 2, 3)), dma((2, 4)), dma((2, 4)),
            dma((2, 3)), dma((2, 3)), dma((2, 3)), dma((2, 3)),
        ],
        compiler_params=pltpu.CompilerParams(
            collective_id=1, has_side_effects=True, vmem_limit_bytes=48 << 20
        ),
        name="weight_sums",
    )(x, g)


def all_sum_kernel(
    v_ref, out_ref, recv1, quarter, recv2, recv3, s1, r1, s2, r2, s3, r3, s4, r4, local_sem
):
    ty, tx = lax.axis_index("ty"), lax.axis_index("tx")
    tys = [{"ty": lax.rem(ty + d, 4), "tx": tx} for d in (1, 2, 3)]
    txs = [{"ty": ty, "tx": lax.rem(tx + d, 8)} for d in range(1, 8)]
    greet(tys + txs)
    copies = [
        send(v_ref.at[lax.rem(ty + d, 4)], recv1.at[d - 1], s1.at[d - 1], r1.at[d - 1], tys[d - 1])
        for d in (1, 2, 3)
    ]
    total = v_ref[ty].astype(FLOAT)
    for d, copy in enumerate(copies):
        copy.wait()
        total = total + recv1[d].astype(FLOAT)
    for c in range(8):
        quarter[c] = total[:, c * 128 : c * 128 + 128].astype(BFLOAT)
    copies = [
        send(quarter.at[lax.rem(tx + d, 8)], recv2.at[d - 1], s2.at[d - 1], r2.at[d - 1], txs[d - 1])
        for d in range(1, 8)
    ]
    total = quarter[tx].astype(FLOAT)
    for d, copy in enumerate(copies):
        copy.wait()
        total = total + recv2[d].astype(FLOAT)
    recv3[tx] = total.astype(BFLOAT)
    copies = [
        send(recv3.at[tx], recv3.at[tx], s3.at[d - 1], r3.at[d - 1], txs[d - 1])
        for d in range(1, 8)
    ]
    for copy in copies:
        copy.wait()
    copies = [
        send(recv3, out_ref.at[ty], s4.at[d - 1], r4.at[d - 1], tys[d - 1]) for d in (1, 2, 3)
    ]
    mine = pltpu.make_async_copy(recv3, out_ref.at[ty], local_sem)
    mine.start()
    for copy in copies + [mine]:
        copy.wait()


def all_sum(v):
    rows, width = v.shape
    part = rows // 4
    dma = pltpu.SemaphoreType.DMA
    out = pl.pallas_call(
        all_sum_kernel,
        out_shape=jax.ShapeDtypeStruct((4, 8, part, 128), BFLOAT),
        in_specs=[pl.BlockSpec(memory_space=pltpu.VMEM)],
        out_specs=pl.BlockSpec(memory_space=pl.ANY),
        scratch_shapes=[
            pltpu.VMEM((3, part, width), BFLOAT),
            pltpu.VMEM((8, part, 128), BFLOAT),
            pltpu.VMEM((7, part, 128), BFLOAT),
            pltpu.VMEM((8, part, 128), BFLOAT),
            dma((3,)), dma((3,)), dma((7,)), dma((7,)), dma((7,)), dma((7,)), dma((3,)), dma((3,)),
            dma(()),
        ],
        compiler_params=pltpu.CompilerParams(
            collective_id=2, has_side_effects=True, vmem_limit_bytes=32 << 20
        ),
        name="all_sum",
    )(v.reshape(4, part, width))
    return jnp.transpose(out, (0, 2, 1, 3)).reshape(rows, width)


LANES = 384
CUBE = 0.044715
SLOPE = 0.7978845608028654


def norm_rows(rows):
    shifted = rows - jnp.mean(rows, axis=-1, keepdims=True)
    rate = lax.rsqrt(jnp.mean(shifted * shifted, axis=-1, keepdims=True) + EPSILON)
    return shifted * rate, rate


def norm_rows_back(upstream, gain, unit, rate):
    scaled = upstream * gain
    along = jnp.mean(scaled * unit, axis=-1, keepdims=True)
    grad = rate * (scaled - jnp.mean(scaled, axis=-1, keepdims=True) - unit * along)
    return grad, jnp.sum(upstream * unit, axis=0, keepdims=True)


def gelu_pair(values):
    square = values * values
    bend = jnp.tanh(SLOPE * (values + CUBE * values * square))
    half = 0.5 * (1.0 + bend)
    slope = half + 0.5 * values * (1.0 - bend * bend) * (SLOPE * (1.0 + 3.0 * CUBE * square))
    return values * half, slope


def dot_nt(left, right):
    return lax.dot_general(left, right, (((1,), (1,)), ((), ())), preferred_element_type=FLOAT)


def dot_nn(left, right):
    return lax.dot_general(left, right, (((1,), (0,)), ((), ())), preferred_element_type=FLOAT)


def tower_kernel(
    part_ref, lat_ref, cot_ref, fgain_ref, hgain_ref, tgain_ref, ogain_ref, vproj_ref,
    w0, w1, w2, w3, w4, w5, w6, w7, w8,
    result_ref, x_ref, g_ref, mix_ref, gcross_ref, one_ref, gains_ref, feat_ref, coef_ref,
    ws, part_in, qkv_out, qkv_in, kv_in, probs, mixed_out, mixed_in, gm_out, gm_in,
    kvx_out, kvx_in, gqkv_out, gqkv_in,
    w_sem, a_s, a_r, q_s, q_r, k_s, k_r, m_s, m_r, g_s, g_r, e_s, e_r, b_s, b_r, c_s, c_r, o_s, o_r,
):
    ty, tx = lax.axis_index("ty"), lax.axis_index("tx")
    tys = [{"ty": lax.rem(ty + d, 4), "tx": tx} for d in (1, 2, 3)]
    txs = [{"ty": ty, "tx": lax.rem(tx + d, 8)} for d in range(1, 8)]
    mate = {"ty": 2 * (ty // 2) + 1 - lax.rem(ty, 2), "tx": tx}
    weights = (w0, w1, w2, w3, w4, w5, w6, w7, w8)
    loads = []
    for i, w in enumerate(weights):
        loads.append(pltpu.make_async_copy(w, ws.at[i], w_sem.at[i]))
        loads[i].start()
    greet(tys + txs)
    cross, up, down, tq, tk, tv, tproj, fup, fdown = range(9)

    def times(rows, i):
        return dot_nn(rows, ws[i])

    def times_back(rows, i):
        return dot_nt(rows, ws[i])

    def spread(out, into, s_sem, r_sem):
        copies = [
            send(out.at[lax.rem(tx + d, 8)], into.at[tx], s_sem.at[d - 1], r_sem.at[d - 1], txs[d - 1])
            for d in range(1, 8)
        ]
        into[tx] = out[tx]
        return copies

    def finish(copies):
        for copy in copies:
            copy.wait()

    copies = [
        send(part_ref.at[lax.rem(ty + d, 4)], part_in.at[d - 1], a_s.at[d - 1], a_r.at[d - 1], tys[d - 1])
        for d in (1, 2, 3)
    ]
    parts = [part_ref[ty]]
    finish(copies)
    parts += [part_in[d] for d in range(3)]
    tops = [p[:, FEAT + 1 : FEAT + 2] for p in parts]
    top = jnp.maximum(jnp.maximum(tops[0], tops[1]), jnp.maximum(tops[2], tops[3]))
    joined = sum(p * jnp.exp2(t - top) for p, t in zip(parts, tops))
    total = joined[:, FEAT : FEAT + 1]
    fgain = fgain_ref[...]
    raw_mix = joined / total
    shift = top + jnp.log2(total)
    mix = (raw_mix * fgain).astype(BFLOAT)
    mix_ref[...] = mix
    attended = dot_nn(mix, vproj_ref[...])
    finish(loads[:1])
    one = lat_ref[ty].astype(FLOAT) + times(attended.astype(BFLOAT), cross)
    h_unit, h_rate = norm_rows(one)
    hidden = (h_unit * hgain_ref[...]).astype(BFLOAT)
    x_ref[7] = hidden
    finish(loads[1:2])
    act, act_slope = gelu_pair(times(hidden, up))
    act = act.astype(BFLOAT)
    x_ref[6] = act
    finish(loads[2:3])
    two = one + times(act, down)
    t_unit, t_rate = norm_rows(two)
    trows = (t_unit * tgain_ref[...]).astype(BFLOAT)
    x_ref[3] = trows
    x_ref[4] = trows
    x_ref[5] = trows
    for s, i in enumerate((tq, tk, tv)):
        finish(loads[i : i + 1])
        value = times(trows, i).astype(BFLOAT)
        for h in range(8):
            qkv_out[h, 32 * s : 32 * s + 32] = value[:, 128 * h : 128 * h + 128]
    finish(spread(qkv_out, qkv_in, q_s, q_r))
    copies = [send(qkv_in.at[:, 32:96], kv_in, k_s, k_r, mate)]
    q = qkv_in[:, 0:32].reshape(256, 128)
    k1 = qkv_in[:, 32:64].reshape(256, 128)
    v1 = qkv_in[:, 64:96].reshape(256, 128)
    scale = 1.0 / math.sqrt(128)
    s1 = dot_nt(q, k1) * scale
    finish(copies)
    k2 = kv_in[:, 0:32].reshape(256, 128)
    v2 = kv_in[:, 32:64].reshape(256, 128)
    s2 = dot_nt(q, k2) * scale
    stop = jnp.maximum(
        jnp.max(s1, axis=1, keepdims=True), jnp.max(s2, axis=1, keepdims=True)
    )
    e1, e2 = jnp.exp(s1 - stop), jnp.exp(s2 - stop)
    rate = 1.0 / (jnp.sum(e1, axis=1, keepdims=True) + jnp.sum(e2, axis=1, keepdims=True))
    p1, p2 = e1 * rate, e2 * rate
    probs[0] = p1
    probs[1] = p2
    mixed_out[...] = (
        (dot_nn(p1.astype(BFLOAT), v1) + dot_nn(p2.astype(BFLOAT), v2))
        .astype(BFLOAT)
        .reshape(8, 32, 128)
    )
    copies = spread(mixed_out, mixed_in, m_s, m_r)
    finish(loads[6:9])
    cot = cot_ref[ty]
    g_ref[0] = cot
    back_four = times_back(cot, fdown)
    finish(copies)
    mixed = jnp.concatenate([mixed_in[h] for h in range(8)], axis=1)
    x_ref[2] = mixed
    three = two + times(mixed, tproj)
    o_unit, o_rate = norm_rows(three)
    ogain = ogain_ref[...]
    frows = (o_unit * ogain).astype(BFLOAT)
    x_ref[1] = frows
    fact, fact_slope = gelu_pair(times(frows, fup))
    fact = fact.astype(BFLOAT)
    x_ref[0] = fact
    g_lift = (back_four * fact_slope).astype(BFLOAT)
    g_ref[1] = g_lift
    g_three, o_grad = norm_rows_back(times_back(g_lift, fup), ogain, o_unit, o_rate)
    gains_ref[2:3] = o_grad
    g_three = cot.astype(FLOAT) + g_three
    g_tower = g_three.astype(BFLOAT)
    g_ref[2] = g_tower
    g_mixed = times_back(g_tower, tproj).astype(BFLOAT)
    for h in range(8):
        gm_out[h] = g_mixed[:, 128 * h : 128 * h + 128]
    copies = spread(gm_out, gm_in, g_s, g_r)
    result_ref[ty] = (three + times(fact, fdown)).astype(BFLOAT)
    copies_out = [
        send(result_ref.at[ty], result_ref.at[ty], o_s.at[d - 1], o_r.at[d - 1], tys[d - 1])
        for d in (1, 2, 3)
    ]
    finish(copies)
    gm = gm_in[...].reshape(256, 128)
    q = qkv_in[:, 0:32].reshape(256, 128)
    k1 = qkv_in[:, 32:64].reshape(256, 128)
    v1 = qkv_in[:, 64:96].reshape(256, 128)
    k2 = kv_in[:, 0:32].reshape(256, 128)
    v2 = kv_in[:, 32:64].reshape(256, 128)
    p1, p2 = probs[0], probs[1]
    gp1, gp2 = dot_nt(gm, v1), dot_nt(gm, v2)
    away = jnp.sum(p1 * gp1, axis=1, keepdims=True) + jnp.sum(p2 * gp2, axis=1, keepdims=True)
    gs1 = (p1 * (gp1 - away)).astype(BFLOAT)
    gs2 = (p2 * (gp2 - away)).astype(BFLOAT)
    kvx_out[0] = (outer(gs2, q) * scale).astype(BFLOAT)
    kvx_out[1] = outer(p2.astype(BFLOAT), gm).astype(BFLOAT)
    copies = [send(kvx_out, kvx_in, e_s, e_r, mate)]
    gq = (dot_nn(gs1, k1) + dot_nn(gs2, k2)) * scale
    gk = outer(gs1, q) * scale
    gv = outer(p1.astype(BFLOAT), gm)
    gqkv_out[:, 0:32] = gq.astype(BFLOAT).reshape(8, 32, 128)
    finish(copies)
    gqkv_out[:, 32:64] = (gk + kvx_in[0].astype(FLOAT)).astype(BFLOAT).reshape(8, 32, 128)
    gqkv_out[:, 64:96] = (gv + kvx_in[1].astype(FLOAT)).astype(BFLOAT).reshape(8, 32, 128)
    finish(spread(gqkv_out, gqkv_in, b_s, b_r))
    g_trows = None
    for s, i in enumerate((tq, tk, tv)):
        value = jnp.concatenate([gqkv_in[h, 32 * s : 32 * s + 32] for h in range(8)], axis=1)
        g_ref[3 + s] = value
        term = times_back(value, i)
        g_trows = term if g_trows is None else g_trows + term
    g_two, t_grad = norm_rows_back(g_trows, tgain_ref[...], t_unit, t_rate)
    gains_ref[1:2] = t_grad
    g_two = g_three + g_two
    g_hidden = g_two.astype(BFLOAT)
    g_ref[6] = g_hidden
    g_hlift = (times_back(g_hidden, down) * act_slope).astype(BFLOAT)
    g_ref[7] = g_hlift
    g_one, h_grad = norm_rows_back(times_back(g_hlift, up), hgain_ref[...], h_unit, h_rate)
    gains_ref[0:1] = h_grad
    g_one = g_two + g_one
    one_ref[...] = g_one
    g_cross = g_one.astype(BFLOAT)
    gcross_ref[...] = g_cross
    g_att = times_back(g_cross, cross).astype(BFLOAT)
    raw_up = dot_nt(g_att, vproj_ref[...])
    feat_ref[...] = jnp.sum(raw_mix * raw_up, axis=0, keepdims=True)
    delta = jnp.sum(g_att.astype(FLOAT) * attended, axis=1, keepdims=True)
    lane = lax.broadcasted_iota(jnp.int32, raw_up.shape, 1)
    coef_ref[ty] = jnp.where(
        lane < FEAT, raw_up * fgain, jnp.where(lane == FEAT, delta, shift)
    )
    copies_out += [
        send(coef_ref.at[ty], coef_ref.at[ty], c_s.at[d - 1], c_r.at[d - 1], tys[d - 1])
        for d in (1, 2, 3)
    ]
    finish(copies_out)


def tower(part, lat, cot, fgain, hgain, tgain, ogain, vproj, weights):
    _, rows, width = lat.shape
    dma = pltpu.SemaphoreType.DMA
    vmem = pl.BlockSpec(memory_space=pltpu.VMEM)
    shape = jax.ShapeDtypeStruct
    head = (8, rows, 128)
    three = (8, 3 * rows, 128)
    return pl.pallas_call(
        tower_kernel,
        out_shape=(
            shape((4, rows, width), BFLOAT),
            shape((8, rows, width), BFLOAT),
            shape((8, rows, width), BFLOAT),
            shape((rows, LANES), BFLOAT),
            shape((rows, width), BFLOAT),
            shape((rows, width), FLOAT),
            shape((3, width), FLOAT),
            shape((1, LANES), FLOAT),
            shape((4, rows, LANES), FLOAT),
        ),
        in_specs=[vmem] * 8 + [pl.BlockSpec(memory_space=pl.ANY)] * 9,
        out_specs=(vmem,) * 9,
        scratch_shapes=[
            pltpu.VMEM((9, width, width), BFLOAT),
            pltpu.VMEM((3, rows, LANES), FLOAT),
            pltpu.VMEM(three, BFLOAT),
            pltpu.VMEM(three, BFLOAT),
            pltpu.VMEM((8, 2 * rows, 128), BFLOAT),
            pltpu.VMEM((2, 8 * rows, 8 * rows), FLOAT),
            pltpu.VMEM(head, BFLOAT), pltpu.VMEM(head, BFLOAT),
            pltpu.VMEM(head, BFLOAT), pltpu.VMEM(head, BFLOAT),
            pltpu.VMEM((2, 8 * rows, 128), BFLOAT), pltpu.VMEM((2, 8 * rows, 128), BFLOAT),
            pltpu.VMEM(three, BFLOAT), pltpu.VMEM(three, BFLOAT),
            dma((9,)),
            dma((3,)), dma((3,)), dma((7,)), dma((7,)), dma(()), dma(()), dma((7,)), dma((7,)),
            dma((7,)), dma((7,)), dma(()), dma(()), dma((7,)), dma((7,)), dma((3,)), dma((3,)),
            dma((3,)), dma((3,)),
        ],
        compiler_params=pltpu.CompilerParams(
            collective_id=3, has_side_effects=True, vmem_limit_bytes=56 << 20
        ),
        name="tower",
    )(part, lat, cot, fgain, hgain, tgain, ogain, vproj, *weights)


def on_device_fast(
    pixels,
    pixel_mask,
    image_sizes,
    latents,
    cotangent,
    feature_gain,
    query_gain,
    query_proj,
    key_proj,
    value_proj,
    cross_proj,
    hidden_gain,
    hidden_up,
    hidden_down,
    tower_gain,
    tower_query,
    tower_key,
    tower_value,
    tower_proj,
    final_gain,
    final_up,
    final_down,
):
    item_count = pixels.shape[0]
    tile_height = pixels.shape[2]
    tile_width = pixels.shape[3]
    model_width = latents.shape[2]
    rows_here = latents.shape[1]
    head_count = HEADS
    head_size = model_width // head_count
    cross_scale = 1.0 / math.sqrt(model_width)
    tower_scale = 1.0 / math.sqrt(head_size)
    row_ids = lax.axis_index("ty") * tile_height + jnp.arange(tile_height, dtype=jnp.int32)
    col_ids = lax.axis_index("tx") * tile_width + jnp.arange(tile_width, dtype=jnp.int32)
    all_cols = jnp.arange(tile_width * lax.axis_size("tx"), dtype=jnp.int32)
    wide_pixels = lax.all_gather(pixels, "tx", axis=3, tiled=True).astype(FLOAT)
    wide_mask = lax.all_gather(pixel_mask, "tx", axis=2, tiled=True)
    side_sizes = image_sizes[:, None, None]
    live = (
        (wide_mask > 0)
        & (row_ids[None, :, None] < side_sizes)
        & (all_cols[None, None, :] < side_sizes)
    )[:, None]
    row_table, row_coord, row_sum = axis_tables(image_sizes, row_ids, 3, 5)
    col_table, col_coord, col_sum = axis_tables(image_sizes, all_cols, 4, 5 + 2 * BANDS)
    pixel_mean = (
        jnp.sum(wide_pixels, axis=1) + row_sum[:, :, None] + col_sum[:, None, :]
    ) / FEAT
    pixel_square = (
        jnp.sum(wide_pixels * wide_pixels, axis=1)
        + (row_coord * row_coord)[:, :, None]
        + (col_coord * col_coord)[:, None, :]
        + 2.0 * BANDS
    ) / FEAT
    pixel_rate = lax.rsqrt(pixel_square - pixel_mean * pixel_mean + EPSILON)
    exact = lax.Precision.HIGHEST

    def against_pixels(coefs):
        by_row = jnp.einsum("blf,bif->bli", coefs, row_table, precision=exact)
        by_col = jnp.einsum("blf,bjf->blj", coefs, col_table, precision=exact)
        total = by_row[:, :, :, None] + by_col[:, :, None, :]
        for c in range(3):
            total = total + coefs[:, :, c][:, :, None, None] * wide_pixels[:, None, c]
        total = total - jnp.sum(coefs, axis=2)[:, :, None, None] * pixel_mean[:, None]
        return total * pixel_rate[:, None]

    def over_pixels(weights):
        scaled = weights * pixel_rate[:, None]
        by_row = jnp.sum(scaled, axis=3)
        by_col = jnp.sum(scaled, axis=2)
        total = jnp.einsum("bli,bif->blf", by_row, row_table, precision=exact)
        total = total + jnp.einsum("blj,bjf->blf", by_col, col_table, precision=exact)
        colour = jnp.stack(
            [jnp.sum(scaled * wide_pixels[:, None, c], axis=(2, 3)) for c in range(3)], axis=2
        )
        total = total + jnp.pad(colour, ((0, 0), (0, 0), (0, FEAT - 3)))
        return total - jnp.sum(scaled * pixel_mean[:, None], axis=(2, 3))[:, :, None]

    latent_rows = latents.astype(FLOAT)
    query_normed, back_query_norm = jax.vjp(layer_norm, latent_rows, query_gain)
    query_input = query_normed.astype(BFLOAT)
    own_queries = linear(query_input, query_proj).astype(BFLOAT)
    raw_query = linear_back(own_queries, key_proj) * cross_scale
    query_coefs = raw_query * (feature_gain * (1.0 / math.log(2.0)))
    scores = against_pixels(query_coefs)
    row_top = jnp.max(jnp.where(live, scores, -1e30), axis=(2, 3))
    row_exp = jnp.where(live, jnp.exp2(scores - row_top[:, :, None, None]), 0.0)
    row_total = jnp.sum(row_exp, axis=(2, 3))
    part = jnp.concatenate(
        [over_pixels(row_exp), row_total[:, :, None], row_top[:, :, None],
         jnp.zeros((item_count, rows_here, LANES - FEAT - 2), FLOAT)], axis=2
    )
    share = item_count * rows_here // lax.axis_size("ty")
    ty_index = lax.axis_index("ty")

    def in_shares(rows):
        return rows.reshape(lax.axis_size("ty"), share, rows.shape[-1])

    def own_share(rows):
        return lax.dynamic_index_in_dim(in_shares(rows), ty_index, 0, keepdims=False)

    def wide_lanes(rows):
        return jnp.pad(rows, ((0, 0), (0, LANES - FEAT)))

    gain_lanes = jnp.pad(feature_gain, (0, LANES - FEAT))[None]
    value_rows = jnp.pad(value_proj, ((0, LANES - FEAT), (0, 0)))
    result, lefts, rights, mix, g_cross, grad_one, gain_parts, feat_part, coefs = tower(
        in_shares(part), in_shares(latents), in_shares(cotangent), gain_lanes,
        hidden_gain[None], tower_gain[None], final_gain[None], value_rows,
        (cross_proj, hidden_up, hidden_down, tower_query, tower_key, tower_value, tower_proj,
         final_up, final_down),
    )
    coefs = coefs.reshape(item_count, rows_here, LANES)
    grad_probs = against_pixels(coefs[:, :, :FEAT])
    probs = jnp.where(live, jnp.exp2(scores - coefs[:, :, FEAT + 1][:, :, None, None]), 0.0)
    grad_scores = probs * (grad_probs - coefs[:, :, FEAT][:, :, None, None])
    raw_grad_mix = lax.psum(over_pixels(grad_scores), "ty")
    raw_grad_mix = own_share(raw_grad_mix)
    grad_mix = (raw_grad_mix * feature_gain).astype(BFLOAT)
    grad_queries = (linear(grad_mix, key_proj) * cross_scale).astype(BFLOAT)
    feature_part = jnp.sum(raw_grad_mix * own_share(raw_query), axis=0) + feat_part[0, :FEAT]
    own_latents, own_query_input = own_share(latent_rows), own_share(query_input)
    unit, rate = norm_rows(own_latents)
    grad_latent_rows, query_gain_grad = norm_rows_back(
        linear_back(grad_queries, query_proj), query_gain[None], unit, rate
    )
    latent_grad = lax.all_gather(grad_one + grad_latent_rows, "ty", axis=0)
    latent_grad = latent_grad.reshape(latents.shape)
    sums = weight_sums(lefts, rights).astype(FLOAT)
    lanes = ((0, 11), (0, 0))
    gains = jnp.concatenate(
        [query_gain_grad, gain_parts, jnp.pad(feature_part, (0, model_width - FEAT))[None]]
    )
    joined = jnp.concatenate(
        [
            weight_grad(mix, g_cross)[:272],
            jnp.pad(weight_grad(grad_mix, own_query_input), lanes),
            jnp.pad(gains, ((0, 27), (0, 0))),
        ]
    )
    joined = all_sum(joined.astype(BFLOAT))
    cross_core = joined[:FEAT]
    query_core = joined[272 : 272 + FEAT]
    value_proj_grad = linear_back(cross_core, cross_proj)
    key_proj_grad = linear(query_core, query_proj) * cross_scale
    wide = model_width // lax.axis_size("tx")
    tx_from = lax.axis_index("tx") * wide
    cross_proj_grad = weight_grad(
        lax.dynamic_slice_in_dim(value_proj, tx_from, wide, 1), cross_core
    )
    query_proj_grad = weight_grad(
        lax.dynamic_slice_in_dim(query_core, tx_from, wide, 1), key_proj
    ) * cross_scale
    gain_sums = joined[544:549].astype(FLOAT)
    gain_here = lax.dynamic_slice_in_dim(gain_sums, tx_from, wide, 1)
    return (
        result.reshape(latents.shape),
        latent_grad,
        gain_sums[4, :FEAT],
        gain_here[0],
        query_proj_grad,
        key_proj_grad,
        value_proj_grad,
        cross_proj_grad,
        gain_here[1],
        sums[7],
        sums[6],
        gain_here[2],
        sums[3],
        sums[4],
        sums[5],
        sums[2],
        gain_here[3],
        sums[1],
        sums[0],
    )


def on_device(
    pixels,
    pixel_mask,
    image_sizes,
    latents,
    cotangent,
    feature_gain,
    query_gain,
    query_proj,
    key_proj,
    value_proj,
    cross_proj,
    hidden_gain,
    hidden_up,
    hidden_down,
    tower_gain,
    tower_query,
    tower_key,
    tower_value,
    tower_proj,
    final_gain,
    final_up,
    final_down,
):
    item_count = pixels.shape[0]
    tile_height = pixels.shape[2]
    tile_width = pixels.shape[3]
    model_width = latents.shape[2]
    rows_here = latents.shape[1]
    head_count = HEADS
    head_size = model_width // head_count
    cross_scale = 1.0 / math.sqrt(model_width)
    tower_scale = 1.0 / math.sqrt(head_size)
    row_ids = lax.axis_index("ty") * tile_height + jnp.arange(tile_height, dtype=jnp.int32)
    col_ids = lax.axis_index("tx") * tile_width + jnp.arange(tile_width, dtype=jnp.int32)
    all_cols = jnp.arange(tile_width * lax.axis_size("tx"), dtype=jnp.int32)
    wide_pixels = lax.all_gather(pixels, "tx", axis=3, tiled=True).astype(FLOAT)
    wide_mask = lax.all_gather(pixel_mask, "tx", axis=2, tiled=True)
    side_sizes = image_sizes[:, None, None]
    live = (
        (wide_mask > 0)
        & (row_ids[None, :, None] < side_sizes)
        & (all_cols[None, None, :] < side_sizes)
    )[:, None]
    row_table, row_coord, row_sum = axis_tables(image_sizes, row_ids, 3, 5)
    col_table, col_coord, col_sum = axis_tables(image_sizes, all_cols, 4, 5 + 2 * BANDS)
    pixel_mean = (
        jnp.sum(wide_pixels, axis=1) + row_sum[:, :, None] + col_sum[:, None, :]
    ) / FEAT
    pixel_square = (
        jnp.sum(wide_pixels * wide_pixels, axis=1)
        + (row_coord * row_coord)[:, :, None]
        + (col_coord * col_coord)[:, None, :]
        + 2.0 * BANDS
    ) / FEAT
    pixel_rate = lax.rsqrt(pixel_square - pixel_mean * pixel_mean + EPSILON)
    exact = lax.Precision.HIGHEST

    def against_pixels(coefs):
        by_row = jnp.einsum("blf,bif->bli", coefs, row_table, precision=exact)
        by_col = jnp.einsum("blf,bjf->blj", coefs, col_table, precision=exact)
        total = by_row[:, :, :, None] + by_col[:, :, None, :]
        for c in range(3):
            total = total + coefs[:, :, c][:, :, None, None] * wide_pixels[:, None, c]
        total = total - jnp.sum(coefs, axis=2)[:, :, None, None] * pixel_mean[:, None]
        return total * pixel_rate[:, None]

    def over_pixels(weights):
        scaled = weights * pixel_rate[:, None]
        by_row = jnp.sum(scaled, axis=3)
        by_col = jnp.sum(scaled, axis=2)
        total = jnp.einsum("bli,bif->blf", by_row, row_table, precision=exact)
        total = total + jnp.einsum("blj,bjf->blf", by_col, col_table, precision=exact)
        colour = jnp.stack(
            [jnp.sum(scaled * wide_pixels[:, None, c], axis=(2, 3)) for c in range(3)], axis=2
        )
        total = total + jnp.pad(colour, ((0, 0), (0, 0), (0, FEAT - 3)))
        return total - jnp.sum(scaled * pixel_mean[:, None], axis=(2, 3))[:, :, None]

    latent_rows = latents.astype(FLOAT)
    query_normed, back_query_norm = jax.vjp(layer_norm, latent_rows, query_gain)
    query_input = query_normed.astype(BFLOAT)
    own_queries = linear(query_input, query_proj).astype(BFLOAT)
    raw_query = linear_back(own_queries, key_proj) * cross_scale
    scores = against_pixels(raw_query * feature_gain)
    row_top = jnp.max(jnp.where(live, scores, -1e30), axis=(2, 3))
    all_top = lax.pmax(row_top, "ty")
    row_exp = jnp.where(live, jnp.exp(scores - all_top[:, :, None, None]), 0.0)
    row_total = lax.psum(jnp.sum(row_exp, axis=(2, 3)), "ty")
    cross_exact = row_exp / row_total[:, :, None, None]
    raw_mix = lax.psum(over_pixels(cross_exact), "ty")
    mix = raw_mix * feature_gain
    attended = linear(mix.astype(BFLOAT), value_proj)
    attended_input = attended.astype(BFLOAT)
    resid_one = latent_rows + linear(attended_input, cross_proj)
    hidden_normed, back_hidden_norm = jax.vjp(layer_norm, resid_one, hidden_gain)
    hidden_input = hidden_normed.astype(BFLOAT)
    hidden_lifted, back_hidden_gelu = jax.vjp(gelu_tanh, linear(hidden_input, hidden_up))
    hidden_act = hidden_lifted.astype(BFLOAT)
    resid_two = resid_one + linear(hidden_act, hidden_down)
    tower_normed, back_tower_norm = jax.vjp(layer_norm, resid_two, tower_gain)
    tower_input = tower_normed.astype(BFLOAT)
    tower_q = linear(tower_input, tower_query).astype(BFLOAT)
    tower_k = linear(tower_input, tower_key).astype(BFLOAT)
    tower_v = linear(tower_input, tower_value).astype(BFLOAT)
    all_keys, all_values = (
        lax.all_gather(tower_k, "tx", axis=1, tiled=True),
        lax.all_gather(tower_v, "tx", axis=1, tiled=True),
    )
    split_q = tower_q.reshape(item_count, rows_here, head_count, head_size)
    split_k = all_keys.reshape(item_count, -1, head_count, head_size)
    split_v = all_values.reshape(item_count, -1, head_count, head_size)
    tower_scores = (
        jnp.einsum("bqhd,bkhd->bhqk", split_q, split_k, preferred_element_type=FLOAT) * tower_scale
    )
    tower_top = jnp.max(tower_scores, axis=3, keepdims=True)
    tower_exp = jnp.exp(tower_scores - tower_top)
    tower_total = jnp.sum(tower_exp, axis=3, keepdims=True)
    tower_exact = tower_exp / tower_total
    tower_probs = tower_exact.astype(BFLOAT)
    mixed = jnp.einsum(
        "bhqk,bkhd->bqhd", tower_probs, split_v, preferred_element_type=FLOAT
    ).reshape(item_count, rows_here, model_width)
    mixed_input = mixed.astype(BFLOAT)
    resid_three = resid_two + linear(mixed_input, tower_proj)
    final_normed, back_final_norm = jax.vjp(layer_norm, resid_three, final_gain)
    final_input = final_normed.astype(BFLOAT)
    final_lifted, back_final_gelu = jax.vjp(gelu_tanh, linear(final_input, final_up))
    final_act = final_lifted.astype(BFLOAT)
    resid_four = resid_three + linear(final_act, final_down)
    grad_four = cotangent.astype(FLOAT)
    final_down_grad = weight_grad(final_act, cotangent)
    grad_final_lift = back_final_gelu(linear_back(cotangent, final_down))[0].astype(BFLOAT)
    final_up_grad = weight_grad(final_input, grad_final_lift)
    grad_rows_three, final_gain_grad = back_final_norm(linear_back(grad_final_lift, final_up))
    grad_three = grad_four + grad_rows_three
    grad_tower_out = grad_three.astype(BFLOAT)
    tower_proj_grad = weight_grad(mixed_input, grad_tower_out)
    grad_mixed_flat = linear_back(grad_tower_out, tower_proj).astype(BFLOAT)
    grad_mixed = grad_mixed_flat.reshape(item_count, rows_here, head_count, head_size)
    grad_tower_p = jnp.einsum("bqhd,bkhd->bhqk", grad_mixed, split_v, preferred_element_type=FLOAT)
    tower_delta = jnp.sum(tower_exact * grad_tower_p, axis=3, keepdims=True)
    grad_tower_scores = (tower_exact * (grad_tower_p - tower_delta)).astype(BFLOAT)
    grad_tower_q = (
        (
            jnp.einsum("bhqk,bkhd->bqhd", grad_tower_scores, split_k, preferred_element_type=FLOAT)
            * tower_scale
        )
        .astype(BFLOAT)
        .reshape(item_count, rows_here, model_width)
    )
    value_part = jnp.einsum(
        "bhqk,bqhd->bkhd", tower_probs, grad_mixed, preferred_element_type=FLOAT
    )
    key_part = (
        jnp.einsum("bhqk,bqhd->bkhd", grad_tower_scores, split_q, preferred_element_type=FLOAT)
        * tower_scale
    )
    key_sums, value_sums = (
        lax.psum_scatter(
            key_part.reshape(item_count, -1, model_width), "tx", scatter_dimension=1, tiled=True
        ),
        lax.psum_scatter(
            value_part.reshape(item_count, -1, model_width), "tx", scatter_dimension=1, tiled=True
        ),
    )
    grad_tower_k = key_sums.astype(BFLOAT)
    grad_tower_v = value_sums.astype(BFLOAT)
    tower_query_grad = weight_grad(tower_input, grad_tower_q)
    tower_key_grad = weight_grad(tower_input, grad_tower_k)
    tower_value_grad = weight_grad(tower_input, grad_tower_v)
    grad_tower_rows = (
        linear_back(grad_tower_q, tower_query)
        + linear_back(grad_tower_k, tower_key)
        + linear_back(grad_tower_v, tower_value)
    )
    grad_rows_two, tower_gain_grad = back_tower_norm(grad_tower_rows)
    grad_two = grad_three + grad_rows_two
    grad_hidden_out = grad_two.astype(BFLOAT)
    hidden_down_grad = weight_grad(hidden_act, grad_hidden_out)
    grad_hidden_lift = back_hidden_gelu(linear_back(grad_hidden_out, hidden_down))[0].astype(BFLOAT)
    hidden_up_grad = weight_grad(hidden_input, grad_hidden_lift)
    grad_rows_one, hidden_gain_grad = back_hidden_norm(linear_back(grad_hidden_lift, hidden_up))
    grad_one = grad_two + grad_rows_one
    grad_cross_out = grad_one.astype(BFLOAT)
    cross_proj_grad = weight_grad(attended_input, grad_cross_out)
    grad_attended = linear_back(grad_cross_out, cross_proj).astype(BFLOAT)
    raw_up = linear_back(grad_attended, value_proj)
    grad_probs = against_pixels(raw_up * feature_gain)
    cross_delta = jnp.sum(grad_attended.astype(FLOAT) * attended, axis=2)
    grad_scores = cross_exact * (grad_probs - cross_delta[:, :, None, None])
    raw_grad_mix = lax.psum(over_pixels(grad_scores), "ty")
    grad_mix = (raw_grad_mix * feature_gain).astype(BFLOAT)
    grad_queries = (linear(grad_mix, key_proj) * cross_scale).astype(BFLOAT)
    key_proj_grad = weight_grad(grad_mix, own_queries) * cross_scale
    value_proj_grad = weight_grad(mix.astype(BFLOAT), grad_attended)
    feature_part = jnp.sum(raw_grad_mix * raw_query + raw_mix * raw_up, axis=(0, 1))
    pixel_sums = lax.psum((key_proj_grad, value_proj_grad, feature_part), "tx")
    query_proj_grad = weight_grad(query_input, grad_queries)
    grad_latent_rows, query_gain_grad = back_query_norm(linear_back(grad_queries, query_proj))
    latent_grad = grad_one + grad_latent_rows
    summed = (
        lax.psum_scatter(query_gain_grad, "tx", scatter_dimension=0, tiled=True),
        lax.psum_scatter(query_proj_grad, "tx", scatter_dimension=0, tiled=True),
        lax.psum_scatter(cross_proj_grad, "tx", scatter_dimension=0, tiled=True),
        lax.psum_scatter(hidden_gain_grad, "tx", scatter_dimension=0, tiled=True),
        lax.psum_scatter(hidden_up_grad, "tx", scatter_dimension=0, tiled=True),
        lax.psum_scatter(hidden_down_grad, "tx", scatter_dimension=0, tiled=True),
        lax.psum_scatter(tower_gain_grad, "tx", scatter_dimension=0, tiled=True),
        lax.psum_scatter(tower_query_grad, "tx", scatter_dimension=0, tiled=True),
        lax.psum_scatter(tower_key_grad, "tx", scatter_dimension=0, tiled=True),
        lax.psum_scatter(tower_value_grad, "tx", scatter_dimension=0, tiled=True),
        lax.psum_scatter(tower_proj_grad, "tx", scatter_dimension=0, tiled=True),
        lax.psum_scatter(final_gain_grad, "tx", scatter_dimension=0, tiled=True),
        lax.psum_scatter(final_up_grad, "tx", scatter_dimension=0, tiled=True),
        lax.psum_scatter(final_down_grad, "tx", scatter_dimension=0, tiled=True),
    )
    return (
        resid_four.astype(BFLOAT),
        latent_grad,
        pixel_sums[2],
        summed[0],
        summed[1],
        pixel_sums[0],
        pixel_sums[1],
        summed[2],
        summed[3],
        summed[4],
        summed[5],
        summed[6],
        summed[7],
        summed[8],
        summed[9],
        summed[10],
        summed[11],
        summed[12],
        summed[13],
    )


def solution(mesh):
    in_specs = (
        P(None, None, "ty", "tx"),
        P(None, "ty", "tx"),
        P(),
        P(None, "tx", None),
        P(None, "tx", None),
        P(),
        P(),
        P(),
        P(),
        P(),
        P(),
        P(),
        P(),
        P(),
        P(),
        P(),
        P(),
        P(),
        P(),
        P(),
        P(),
        P(),
    )
    out_specs = (
        P(None, "tx", None),
        P(None, "tx", None),
        P(),
        P("tx"),
        P("tx", None),
        P(),
        P(),
        P("tx", None),
        P("tx"),
        P("tx", None),
        P("tx", None),
        P("tx"),
        P("tx", None),
        P("tx", None),
        P("tx", None),
        P("tx", None),
        P("tx"),
        P("tx", None),
        P("tx", None),
    )
    fits = mesh.shape["ty"] == 4 and mesh.shape["tx"] == HEADS
    plan = on_device_fast if fits else on_device
    return jax.shard_map(
        plan, mesh=mesh, in_specs=in_specs, out_specs=out_specs, check_vma=False
    )
```

```python
import math

import jax
import jax.numpy as jnp
import numpy as np
from jax import lax
from jax.experimental import pallas as pl
from jax.experimental.pallas import tpu as pltpu
from jax.sharding import PartitionSpec as P

BANDS = 64
FEAT = 261
HEADS = 8


EPSILON = 1e-05
FLOAT = jnp.float32
BFLOAT = jnp.bfloat16


def layer_norm(values, scales):
    centre = jnp.mean(values, axis=-1, keepdims=True)
    shifted = values - centre
    spread = jnp.mean(shifted * shifted, axis=-1, keepdims=True)
    return shifted * lax.rsqrt(spread + EPSILON) * scales


def gelu_tanh(values):
    cubic = values + 0.044715 * values * values * values
    return 0.5 * values * (1.0 + jnp.tanh(0.7978845608028654 * cubic))


def linear(inputs, weight):
    return lax.dot_general(
        inputs, weight, (((inputs.ndim - 1,), (0,)), ((), ())), preferred_element_type=FLOAT
    )


def linear_back(upstream, weight):
    return lax.dot_general(
        upstream, weight, (((upstream.ndim - 1,), (1,)), ((), ())), preferred_element_type=FLOAT
    )


def weight_grad(inputs, upstream):
    flat_inputs = inputs.reshape(-1, inputs.shape[-1])
    flat_upstream = upstream.reshape(-1, upstream.shape[-1])
    return lax.dot_general(
        flat_inputs, flat_upstream, (((0,), (0,)), ((), ())), preferred_element_type=FLOAT
    )


def axis_tables(image_sizes, ids, coord_lane, first_lane):
    side = image_sizes.astype(FLOAT)[:, None]
    coord = -1.0 + 2.0 * ids.astype(FLOAT)[None, :] / (side - 1.0)
    band = jnp.arange(BANDS, dtype=jnp.int32).astype(FLOAT)
    frequency = 1.0 + band[None, :] * (side * 0.5 - 1.0) / (BANDS - 1)
    angle = math.pi * coord[:, :, None] * frequency[:, None, :]
    waves = jnp.concatenate([jnp.sin(angle), jnp.cos(angle)], axis=2)
    count, length = coord.shape
    lead = jnp.zeros((count, length, coord_lane), FLOAT)
    gap = jnp.zeros((count, length, first_lane - coord_lane - 1), FLOAT)
    tail = jnp.zeros((count, length, FEAT - first_lane - 2 * BANDS), FLOAT)
    table = jnp.concatenate([lead, coord[:, :, None], gap, waves, tail], axis=2)
    return table, coord, jnp.sum(waves, axis=2) + coord


MESH = pl.DeviceIdType.MESH


def send(src, dst, send_sem, recv_sem, where):
    copy = pltpu.make_async_remote_copy(
        src_ref=src, dst_ref=dst, send_sem=send_sem, recv_sem=recv_sem,
        device_id=where, device_id_type=MESH,
    )
    copy.start()
    return copy


def greet(places):
    barrier = pltpu.get_barrier_semaphore()
    for place in places:
        pl.semaphore_signal(barrier, inc=1, device_id=place, device_id_type=MESH)
    pl.semaphore_wait(barrier, len(places))


def outer(left, right):
    return lax.dot_general(left, right, (((0,), (0,)), ((), ())), preferred_element_type=FLOAT)


LANES = 384
CUBE = 0.044715
SLOPE = 0.7978845608028654


def norm_rows(rows):
    shifted = rows - jnp.mean(rows, axis=-1, keepdims=True)
    rate = lax.rsqrt(jnp.mean(shifted * shifted, axis=-1, keepdims=True) + EPSILON)
    return shifted * rate, rate


def norm_rows_back(upstream, gain, unit, rate):
    scaled = upstream * gain
    along = jnp.mean(scaled * unit, axis=-1, keepdims=True)
    grad = rate * (scaled - jnp.mean(scaled, axis=-1, keepdims=True) - unit * along)
    return grad, jnp.sum(upstream * unit, axis=0, keepdims=True)


def gelu_pair(values):
    square = values * values
    bend = jnp.tanh(SLOPE * (values + CUBE * values * square))
    half = 0.5 * (1.0 + bend)
    slope = half + 0.5 * values * (1.0 - bend * bend) * (SLOPE * (1.0 + 3.0 * CUBE * square))
    return values * half, slope


def dot_nt(left, right):
    return lax.dot_general(left, right, (((1,), (1,)), ((), ())), preferred_element_type=FLOAT)


def dot_nn(left, right):
    return lax.dot_general(left, right, (((1,), (0,)), ((), ())), preferred_element_type=FLOAT)


def tower_kernel(
    part_ref, lat_ref, cot_ref, fgain_ref, hgain_ref, tgain_ref, ogain_ref, vproj_ref,
    w0, w1, w2, w3, w4, w5, w6, w7, w8,
    result_ref, xs_ref, gs_ref, mix_ref, gcross_ref, one_ref, gains_ref, feat_ref, coef_ref,
    x_ref, g_ref, gcross_out, gains_out, ws, part_in, qkv_out, qkv_in, kv_in, probs, mixed_out, mixed_in, gm_out, gm_in,
    kvx_out, kvx_in, gqkv_out, gqkv_in,
    w_sem, a_s, a_r, q_s, q_r, k_s, k_r, m_s, m_r, g_s, g_r, e_s, e_r, b_s, b_r, c_s, c_r, o_s, o_r, h_s, h_r, n_s, n_r,
):
    ty, tx = lax.axis_index("ty"), lax.axis_index("tx")
    tys = [{"ty": lax.rem(ty + d, 4), "tx": tx} for d in (1, 2, 3)]
    txs = [{"ty": ty, "tx": lax.rem(tx + d, 8)} for d in range(1, 8)]
    mate = {"ty": 2 * (ty // 2) + 1 - lax.rem(ty, 2), "tx": tx}
    weights = (w0, w1, w2, w3, w4, w5, w6, w7, w8)
    loads = []
    for i, w in enumerate(weights):
        loads.append(pltpu.make_async_copy(w, ws.at[i], w_sem.at[i]))
        loads[i].start()
    greet(tys + txs)
    cross, up, down, tq, tk, tv, tproj, fup, fdown = range(9)

    def times(rows, i):
        return dot_nn(rows, ws[i])

    def times_back(rows, i):
        return dot_nt(rows, ws[i])

    def spread(out, into, s_sem, r_sem):
        copies = [
            send(out.at[lax.rem(tx + d, 8)], into.at[tx], s_sem.at[d - 1], r_sem.at[d - 1], txs[d - 1])
            for d in range(1, 8)
        ]
        into[tx] = out[tx]
        return copies

    def finish(copies):
        for copy in copies:
            copy.wait()

    handed = []
    gains_out[...] = jnp.zeros_like(gains_out)

    def put_gain(row, grad):
        for h in range(4):
            gains_out[h, row : row + 1] = grad[:, 256 * h : 256 * h + 256]

    def hand_over(stack, into, k, s):
        for d in (1, 2, 3):
            handed.append(send(
                stack.at[4 * k + lax.rem(ty + d, 4)], into.at[k, ty],
                h_s.at[k, s, d - 1], h_r.at[k, s, d - 1], tys[d - 1],
            ))
        into[k, ty] = stack[4 * k + ty]

    def hand_to_all(out, into, i, by_place):
        for d in (1, 2, 3):
            src = out.at[lax.rem(ty + d, 4)] if by_place else into.at[ty]
            handed.append(send(src, into.at[ty], n_s.at[i, d - 1], n_r.at[i, d - 1], tys[d - 1]))

    copies = [
        send(part_ref.at[lax.rem(ty + d, 4)], part_in.at[d - 1], a_s.at[d - 1], a_r.at[d - 1], tys[d - 1])
        for d in (1, 2, 3)
    ]
    parts = [part_ref[ty]]
    finish(copies)
    parts += [part_in[d] for d in range(3)]
    tops = [p[:, FEAT + 1 : FEAT + 2] for p in parts]
    top = jnp.maximum(jnp.maximum(tops[0], tops[1]), jnp.maximum(tops[2], tops[3]))
    joined = sum(p * jnp.exp2(t - top) for p, t in zip(parts, tops))
    total = joined[:, FEAT : FEAT + 1]
    fgain = fgain_ref[...]
    raw_mix = joined / total
    shift = top + jnp.log2(total)
    mix = (raw_mix * fgain).astype(BFLOAT)
    mix_ref[ty] = mix
    hand_to_all(None, mix_ref, 0, False)
    attended = dot_nn(mix, vproj_ref[...])
    finish(loads[:1])
    one = lat_ref[ty].astype(FLOAT) + times(attended.astype(BFLOAT), cross)
    h_unit, h_rate = norm_rows(one)
    hidden = (h_unit * hgain_ref[...]).astype(BFLOAT)
    x_ref[7] = hidden
    finish(loads[1:2])
    act, act_slope = gelu_pair(times(hidden, up))
    act = act.astype(BFLOAT)
    x_ref[5] = act
    finish(loads[2:3])
    two = one + times(act, down)
    t_unit, t_rate = norm_rows(two)
    trows = (t_unit * tgain_ref[...]).astype(BFLOAT)
    x_ref[3] = trows
    x_ref[4] = trows
    x_ref[6] = trows
    for s, i in enumerate((tq, tk, tv)):
        finish(loads[i : i + 1])
        value = times(trows, i).astype(BFLOAT)
        for h in range(8):
            qkv_out[h, 32 * s : 32 * s + 32] = value[:, 128 * h : 128 * h + 128]
    copies = spread(qkv_out, qkv_in, q_s, q_r)
    hand_over(x_ref, xs_ref, 1, 0)
    finish(copies)
    copies = [send(qkv_in.at[:, 32:96], kv_in, k_s, k_r, mate)]
    q = qkv_in[:, 0:32].reshape(256, 128)
    k1 = qkv_in[:, 32:64].reshape(256, 128)
    v1 = qkv_in[:, 64:96].reshape(256, 128)
    scale = 1.0 / math.sqrt(128)
    s1 = dot_nt(q, k1) * scale
    finish(copies)
    k2 = kv_in[:, 0:32].reshape(256, 128)
    v2 = kv_in[:, 32:64].reshape(256, 128)
    s2 = dot_nt(q, k2) * scale
    stop = jnp.maximum(
        jnp.max(s1, axis=1, keepdims=True), jnp.max(s2, axis=1, keepdims=True)
    )
    e1, e2 = jnp.exp(s1 - stop), jnp.exp(s2 - stop)
    rate = 1.0 / (jnp.sum(e1, axis=1, keepdims=True) + jnp.sum(e2, axis=1, keepdims=True))
    p1, p2 = e1 * rate, e2 * rate
    probs[0] = p1
    probs[1] = p2
    mixed_out[...] = (
        (dot_nn(p1.astype(BFLOAT), v1) + dot_nn(p2.astype(BFLOAT), v2))
        .astype(BFLOAT)
        .reshape(8, 32, 128)
    )
    copies = spread(mixed_out, mixed_in, m_s, m_r)
    finish(loads[6:9])
    cot = cot_ref[ty]
    g_ref[0] = cot
    back_four = times_back(cot, fdown)
    finish(copies)
    mixed = jnp.concatenate([mixed_in[h] for h in range(8)], axis=1)
    x_ref[1] = mixed
    three = two + times(mixed, tproj)
    o_unit, o_rate = norm_rows(three)
    ogain = ogain_ref[...]
    frows = (o_unit * ogain).astype(BFLOAT)
    x_ref[2] = frows
    fact, fact_slope = gelu_pair(times(frows, fup))
    fact = fact.astype(BFLOAT)
    x_ref[0] = fact
    g_lift = (back_four * fact_slope).astype(BFLOAT)
    g_ref[2] = g_lift
    g_three, o_grad = norm_rows_back(times_back(g_lift, fup), ogain, o_unit, o_rate)
    put_gain(2, o_grad)
    g_three = cot.astype(FLOAT) + g_three
    g_tower = g_three.astype(BFLOAT)
    g_ref[1] = g_tower
    g_mixed = times_back(g_tower, tproj).astype(BFLOAT)
    for h in range(8):
        gm_out[h] = g_mixed[:, 128 * h : 128 * h + 128]
    copies = spread(gm_out, gm_in, g_s, g_r)
    hand_over(x_ref, xs_ref, 0, 0)
    result_ref[ty] = (three + times(fact, fdown)).astype(BFLOAT)
    copies_out = [
        send(result_ref.at[ty], result_ref.at[ty], o_s.at[d - 1], o_r.at[d - 1], tys[d - 1])
        for d in (1, 2, 3)
    ]
    finish(copies)
    gm = gm_in[...].reshape(256, 128)
    q = qkv_in[:, 0:32].reshape(256, 128)
    k1 = qkv_in[:, 32:64].reshape(256, 128)
    v1 = qkv_in[:, 64:96].reshape(256, 128)
    k2 = kv_in[:, 0:32].reshape(256, 128)
    v2 = kv_in[:, 32:64].reshape(256, 128)
    p1, p2 = probs[0], probs[1]
    gp1, gp2 = dot_nt(gm, v1), dot_nt(gm, v2)
    away = jnp.sum(p1 * gp1, axis=1, keepdims=True) + jnp.sum(p2 * gp2, axis=1, keepdims=True)
    gs1 = (p1 * (gp1 - away)).astype(BFLOAT)
    gs2 = (p2 * (gp2 - away)).astype(BFLOAT)
    kvx_out[0] = (outer(gs2, q) * scale).astype(BFLOAT)
    kvx_out[1] = outer(p2.astype(BFLOAT), gm).astype(BFLOAT)
    copies = [send(kvx_out, kvx_in, e_s, e_r, mate)]
    gq = (dot_nn(gs1, k1) + dot_nn(gs2, k2)) * scale
    gk = outer(gs1, q) * scale
    gv = outer(p1.astype(BFLOAT), gm)
    gqkv_out[:, 0:32] = gq.astype(BFLOAT).reshape(8, 32, 128)
    finish(copies)
    gqkv_out[:, 32:64] = (gk + kvx_in[0].astype(FLOAT)).astype(BFLOAT).reshape(8, 32, 128)
    gqkv_out[:, 64:96] = (gv + kvx_in[1].astype(FLOAT)).astype(BFLOAT).reshape(8, 32, 128)
    finish(spread(gqkv_out, gqkv_in, b_s, b_r))
    g_trows = None
    for s, i in enumerate((tq, tk, tv)):
        value = jnp.concatenate([gqkv_in[h, 32 * s : 32 * s + 32] for h in range(8)], axis=1)
        g_ref[(3, 4, 6)[s]] = value
        term = times_back(value, i)
        g_trows = term if g_trows is None else g_trows + term
    hand_over(g_ref, gs_ref, 0, 1)
    g_two, t_grad = norm_rows_back(g_trows, tgain_ref[...], t_unit, t_rate)
    put_gain(1, t_grad)
    g_two = g_three + g_two
    g_hidden = g_two.astype(BFLOAT)
    g_ref[5] = g_hidden
    g_hlift = (times_back(g_hidden, down) * act_slope).astype(BFLOAT)
    g_ref[7] = g_hlift
    hand_over(g_ref, gs_ref, 1, 1)
    g_one, h_grad = norm_rows_back(times_back(g_hlift, up), hgain_ref[...], h_unit, h_rate)
    put_gain(0, h_grad)
    gains_ref[ty] = gains_out[ty]
    hand_to_all(gains_out, gains_ref, 1, True)
    g_one = g_two + g_one
    one_ref[...] = g_one
    g_cross = g_one.astype(BFLOAT)
    for h in range(4):
        gcross_out[h] = g_cross[:, 256 * h : 256 * h + 256]
    gcross_ref[ty] = gcross_out[ty]
    hand_to_all(gcross_out, gcross_ref, 2, True)
    g_att = times_back(g_cross, cross).astype(BFLOAT)
    raw_up = dot_nt(g_att, vproj_ref[...])
    feat_ref[...] = jnp.sum(raw_mix * raw_up, axis=0, keepdims=True)
    delta = jnp.sum(g_att.astype(FLOAT) * attended, axis=1, keepdims=True)
    lane = lax.broadcasted_iota(jnp.int32, raw_up.shape, 1)
    coef_ref[ty] = jnp.where(
        lane < FEAT, raw_up * fgain, jnp.where(lane == FEAT, delta, shift)
    )
    copies_out += [
        send(coef_ref.at[ty], coef_ref.at[ty], c_s.at[d - 1], c_r.at[d - 1], tys[d - 1])
        for d in (1, 2, 3)
    ]
    finish(copies_out)
    finish(handed)


def tower(part, lat, cot, fgain, hgain, tgain, ogain, vproj, weights):
    _, rows, width = lat.shape
    dma = pltpu.SemaphoreType.DMA
    vmem = pl.BlockSpec(memory_space=pltpu.VMEM)
    shape = jax.ShapeDtypeStruct
    head = (8, rows, 128)
    three = (8, 3 * rows, 128)
    return pl.pallas_call(
        tower_kernel,
        out_shape=(
            shape((4, rows, width), BFLOAT),
            shape((2, 4, rows, width), BFLOAT),
            shape((2, 4, rows, width), BFLOAT),
            shape((4, rows, LANES), BFLOAT),
            shape((4, rows, width // 4), BFLOAT),
            shape((rows, width), FLOAT),
            shape((4, 8, width // 4), FLOAT),
            shape((1, LANES), FLOAT),
            shape((4, rows, LANES), FLOAT),
        ),
        in_specs=[vmem] * 8 + [pl.BlockSpec(memory_space=pl.ANY)] * 9,
        out_specs=(vmem,) * 9,
        scratch_shapes=[
            pltpu.VMEM((8, rows, width), BFLOAT),
            pltpu.VMEM((8, rows, width), BFLOAT),
            pltpu.VMEM((4, rows, width // 4), BFLOAT),
            pltpu.VMEM((4, 8, width // 4), FLOAT),
            pltpu.VMEM((9, width, width), BFLOAT),
            pltpu.VMEM((3, rows, LANES), FLOAT),
            pltpu.VMEM(three, BFLOAT),
            pltpu.VMEM(three, BFLOAT),
            pltpu.VMEM((8, 2 * rows, 128), BFLOAT),
            pltpu.VMEM((2, 8 * rows, 8 * rows), FLOAT),
            pltpu.VMEM(head, BFLOAT), pltpu.VMEM(head, BFLOAT),
            pltpu.VMEM(head, BFLOAT), pltpu.VMEM(head, BFLOAT),
            pltpu.VMEM((2, 8 * rows, 128), BFLOAT), pltpu.VMEM((2, 8 * rows, 128), BFLOAT),
            pltpu.VMEM(three, BFLOAT), pltpu.VMEM(three, BFLOAT),
            dma((9,)),
            dma((3,)), dma((3,)), dma((7,)), dma((7,)), dma(()), dma(()), dma((7,)), dma((7,)),
            dma((7,)), dma((7,)), dma(()), dma(()), dma((7,)), dma((7,)), dma((3,)), dma((3,)),
            dma((3,)), dma((3,)), dma((2, 2, 3)), dma((2, 2, 3)), dma((3, 3)), dma((3, 3)),
        ],
        compiler_params=pltpu.CompilerParams(
            collective_id=3, has_side_effects=True, vmem_limit_bytes=56 << 20
        ),
        name="tower",
    )(part, lat, cot, fgain, hgain, tgain, ogain, vproj, *weights)


HALVES = 2
GROUP = 128
LOG2E = 1.0 / math.log(2.0)


def split_two(values):
    high = values.astype(BFLOAT)
    return high, (values - high.astype(FLOAT)).astype(BFLOAT)


def dot_wide(dot, values, high, low):
    first, second = split_two(values)
    return dot(first, high) + (dot(first, low) + dot(second, high))


def coefs_by_pixel(coefs, thigh_ref, tlow_ref, into):
    count = coefs.shape[0] // 2
    for b in range(2):
        wide = dot_wide(dot_nt, coefs[b * count : (b + 1) * count], thigh_ref[b], tlow_ref[b])
        for half in range(HALVES):
            at = pl.ds((half * 2 + b) * count, count)
            rows = wide[:, half * GROUP : (half + 1) * GROUP]
            for t in range(8):
                high, low = split_two(rows + wide[:, (2 + t) * GROUP : (3 + t) * GROUP])
                into[t, at, 0:GROUP] = high
                into[t, at, GROUP : 2 * GROUP] = low


def features_of(sums, scales, thigh_ref, tlow_ref):
    count = sums.shape[1] // 4
    blocks = [sums[t] if scales is None else sums[t] * scales[t] for t in range(8)]
    joined = blocks[0]
    for block in blocks[1:]:
        joined = joined + block
    outs = []
    for b in range(2):
        first, second = pl.ds(b * count, count), (2 + b) * count
        lo, hi = slice(b * count, (b + 1) * count), slice((2 + b) * count, (3 + b) * count)
        wide = jnp.concatenate(
            [joined[lo], joined[hi]] + [block[lo] + block[hi] for block in blocks], axis=1
        )
        outs.append(dot_wide(dot_nn, wide, thigh_ref[b], tlow_ref[b]))
    return jnp.concatenate(outs, axis=0)


def rate_and_bias(block, group):
    rate = block[group % 2 * 4 + group // 2 * 8 + 3 :][:1].astype(FLOAT)
    return rate, jnp.where(rate == 0.0, -1e30, 0.0)


def front_kernel(
    msg_ref, lat_ref, qgain_ref, fgain_ref, qproj_ref, kproj_ref, thigh_ref, tlow_ref, hot_ref,
    msgs_ref, coef_ref, part_ref, qrows_ref, raw_ref,
    pixels, scores, weights, sums, tops, totals, rows_all, raw_all, s_sem, r_sem,
):
    ty, tx = lax.axis_index("ty"), lax.axis_index("tx")
    txs = [{"ty": ty, "tx": lax.rem(tx + d, 8)} for d in range(1, 8)]
    greet(txs)
    copies = [
        send(msg_ref, msgs_ref.at[tx], s_sem.at[d - 1], r_sem.at[d - 1], txs[d - 1])
        for d in range(1, 8)
    ]
    msgs_ref[tx] = msg_ref[...]
    pixels[0:GROUP] = hot_ref[...]
    pixels[GROUP : 2 * GROUP] = hot_ref[...]
    share = raw_ref.shape[0]
    count = 2 * share
    unit, _ = norm_rows(lat_ref[...].astype(FLOAT))
    rows = (unit * qgain_ref[...]).astype(BFLOAT)
    rows_all[...] = rows
    queries = dot_nn(rows, qproj_ref[...]).astype(BFLOAT)
    raw = dot_nt(queries, kproj_ref[...]) * (1.0 / math.sqrt(rows.shape[1]))
    raw_all[...] = raw
    mine = pl.ds(pl.multiple_of(ty * share, share), share)
    qrows_ref[...] = rows_all[:, pl.ds(pl.multiple_of(ty * qrows_ref.shape[1], 128), qrows_ref.shape[1])]
    raw_ref[...] = raw_all[mine]
    coefs_by_pixel(raw * (fgain_ref[...] * LOG2E), thigh_ref, tlow_ref, coef_ref)
    for copy in copies:
        copy.wait()

    def block_step(t, _):
        block = msgs_ref[t]
        pixels[0:16] = block
        pixels[GROUP : GROUP + 16] = block
        scores[...] = dot_nn(coef_ref[t], pixels[...])
        for group in range(4):
            at = pl.ds(group * count, count)
            rate, bias = rate_and_bias(block, group)
            s = scores[at] * rate + bias
            top = jnp.max(s, axis=1, keepdims=True)
            e = jnp.exp2(s - top)
            tops[t, at] = top
            totals[t, at] = jnp.sum(e, axis=1, keepdims=True)
            weights[at] = (e * rate).astype(BFLOAT)
        sums[t] = dot_nt(weights[...], pixels[0:GROUP])
        return 0

    lax.fori_loop(0, 8, block_step, 0)
    top = tops[0]
    for t in range(1, 8):
        top = jnp.maximum(top, tops[t])
    top = jnp.maximum(top[: 2 * count], top[2 * count :])
    both = jnp.concatenate([top, top], axis=0)
    scales = [jnp.exp2(tops[t] - both) for t in range(8)]
    total = sum(totals[t] * scales[t] for t in range(8))
    total = total[: 2 * count] + total[2 * count :]
    feats = features_of(sums, scales, thigh_ref, tlow_ref)
    lane = lax.broadcasted_iota(jnp.int32, feats.shape, 1)
    part_ref[...] = jnp.where(
        lane < FEAT, feats, jnp.where(lane == FEAT, total, top)
    ).reshape(part_ref.shape)


def front(msg, latents, query_gain, gain_lanes, query_proj, key_rows, thigh, tlow, hot):
    count, here, width = latents.shape
    share, length = count * here // 4, msg.shape[1]
    rows = 4 * here
    dma = pltpu.SemaphoreType.DMA
    vmem = pl.BlockSpec(memory_space=pltpu.VMEM)
    shape = jax.ShapeDtypeStruct
    return pl.pallas_call(
        front_kernel,
        out_shape=(
            shape((8, 16, length), BFLOAT),
            shape((8, rows, 2 * GROUP), BFLOAT),
            shape((4, share, LANES), FLOAT),
            shape((4 * share, width // 4), BFLOAT),
            shape((share, LANES), FLOAT),
        ),
        in_specs=[vmem] * 9,
        out_specs=(vmem,) * 5,
        scratch_shapes=[
            pltpu.VMEM((2 * GROUP, length), BFLOAT),
            pltpu.VMEM((rows, length), FLOAT),
            pltpu.VMEM((rows, length), BFLOAT),
            pltpu.VMEM((8, rows, GROUP), FLOAT),
            pltpu.VMEM((8, rows, 1), FLOAT),
            pltpu.VMEM((8, rows, 1), FLOAT),
            pltpu.VMEM((4 * share, width), BFLOAT),
            pltpu.VMEM((4 * share, LANES), FLOAT),
            dma((7,)), dma((7,)),
        ],
        compiler_params=pltpu.CompilerParams(
            collective_id=4, has_side_effects=True, vmem_limit_bytes=48 << 20
        ),
        name="front",
    )(msg, latents.reshape(count * here, width), query_gain, gain_lanes, query_proj, key_rows, thigh, tlow, hot)


def back_kernel(
    msgs_ref, coef_ref, up_ref, one_ref, lat_ref, raw_ref, qgain_ref, fgain_ref, qproj_ref, kproj_ref,
    thigh_ref, tlow_ref, hot_ref, xs_ref, gs_ref, mix_ref, gcross_ref, gains_ref, feat_ref, qrows_ref,
    grad_ref, value_ref, key_ref, sums_ref,
    pixels, upcoefs, scores, ups, weights, sums, part_out, part_in, gmix, qgains_out, qgains_in,
    nsend, nextra, nrecv, nmore, ysend, yrecv, own, zsend, zrecv, last,
    a_s, a_r, o_s, o_r, m_s, m_r, n_s, n_r, e_s, e_r, c_s, c_r, t_s, t_r,
    y_s, y_r, z_s, z_r, w_s, w_r, l_s,
):
    ty, tx = lax.axis_index("ty"), lax.axis_index("tx")
    z, y = tx // 2, lax.rem(tx, 2)
    tys = [{"ty": lax.rem(ty + d, 4), "tx": tx} for d in (1, 2, 3)]
    txs = [{"ty": ty, "tx": lax.rem(tx + d, 8)} for d in range(1, 8)]
    beside = {"ty": ty, "tx": 2 * z + 1 - y}
    zs = [{"ty": ty, "tx": 2 * lax.rem(z + d, 4) + y} for d in (1, 2, 3)]
    greet(tys + txs)

    def finish(copies):
        for copy in copies:
            copy.wait()

    def to_tys(src, into, s_sem, r_sem, by_place=False):
        return [
            send(
                src.at[lax.rem(ty + d, 4)] if by_place else src, into(d),
                s_sem.at[d - 1], r_sem.at[d - 1], tys[d - 1],
            )
            for d in (1, 2, 3)
        ]

    share = raw_ref.shape[0]
    count = 2 * share

    def product_start(i, left, right, gains):
        product = outer(left, right)
        nsend[i] = product[0:256].astype(BFLOAT).reshape(8, 32, 256)
        row = lax.broadcasted_iota(jnp.int32, (16, 256), 0)
        more = product[256:272] + jnp.where(row < 8, 0.0, jnp.concatenate([gains, gains], axis=0))
        nextra[i] = more.astype(BFLOAT)
        main = [
            send(nsend.at[i, lax.rem(tx + d, 8)], nrecv.at[i, d - 1], n_s.at[i, d - 1], n_r.at[i, d - 1], txs[d - 1])
            for d in range(1, 8)
        ]
        return main + [
            send(nextra.at[i], nmore.at[i, d - 1], e_s.at[i, d - 1], e_r.at[i, d - 1], txs[d - 1])
            for d in range(1, 8)
        ]

    def product_join(i, copies, into):
        finish(copies)
        main = nsend[i, tx].astype(FLOAT)
        more = nextra[i].astype(FLOAT)
        for d in range(7):
            main = main + nrecv[i, d].astype(FLOAT)
            more = more + nmore[i, d].astype(FLOAT)
        into[ty, pl.ds(pl.multiple_of(tx * 32, 32), 32)] = main.astype(BFLOAT)
        into[ty, 256:272] = more.astype(BFLOAT)
        here = into.at[ty, pl.ds(pl.multiple_of(tx * 32, 32), 32)]
        return [send(here, here, c_s.at[i, d - 1], c_r.at[i, d - 1], txs[d - 1]) for d in range(1, 8)]

    def product_end(i, copies, into):
        finish(copies)
        return to_tys(into.at[ty], lambda d: into.at[ty], t_s.at[i], t_r.at[i])

    gain_rows = gains_ref[0] + gains_ref[1] + gains_ref[2] + gains_ref[3]
    ncopies = product_start(
        0, mix_ref[...].reshape(4 * share, LANES), gcross_ref[...].reshape(4 * share, 256), gain_rows
    )
    pixels[0:GROUP] = hot_ref[...]
    pixels[GROUP : 2 * GROUP] = hot_ref[...]
    coefs_by_pixel(up_ref[...].reshape(4 * share, LANES), thigh_ref, tlow_ref, upcoefs)

    def block_step(t):
        block = msgs_ref[t]
        pixels[0:16] = block
        pixels[GROUP : GROUP + 16] = block
        scores[...] = dot_nn(coef_ref[t], pixels[...])
        ups[...] = dot_nn(upcoefs[t], pixels[...])
        for group in range(4):
            at = pl.ds(group * count, count)
            rate, bias = rate_and_bias(block, group)
            b = group % 2
            mine = up_ref[2 * b : 2 * b + 2].reshape(count, LANES)
            p = jnp.exp2(scores[at] * rate + (bias - mine[:, FEAT + 1 : FEAT + 2]))
            g = p * (ups[at] * rate - mine[:, FEAT : FEAT + 1])
            weights[at] = (g * rate).astype(BFLOAT)
        sums[t] = dot_nt(weights[...], pixels[0:GROUP])

    def weight_block(k, chunk):
        left = xs_ref[k, :, :, pl.ds(pl.multiple_of(chunk * 128, 128), 128)]
        return outer(left.reshape(4 * share, 128), gs_ref[k].reshape(4 * share, -1))

    def ycopy(k, c):
        return pltpu.make_async_remote_copy(
            src_ref=ysend.at[k, c], dst_ref=yrecv.at[k, c], send_sem=y_s.at[k, c],
            recv_sem=y_r.at[k, c], device_id=beside, device_id_type=MESH,
        )

    def zcopy(k, c, where):
        return pltpu.make_async_remote_copy(
            src_ref=zsend.at[k, c], dst_ref=zrecv.at[k, c], send_sem=z_s.at[k, c],
            recv_sem=z_r.at[k, c], device_id=where, device_id_type=MESH,
        )

    def first_steps(c, _):
        block_step(c)
        for k in range(2):
            ysend[k, c] = weight_block(k, 2 * c + 1 - y).astype(BFLOAT)
            ycopy(k, c).start()
        return 0

    def second_steps(c, _):
        block_step(4 + c)
        at = lax.rem(z + c + 1, 4)
        for k in range(2):
            ycopy(k, at).wait()
            total = weight_block(k, 2 * at + y) + yrecv[k, at].astype(FLOAT)
            zsend[k, c] = total.astype(BFLOAT)
            zcopy(k, c, {"ty": ty, "tx": 2 * at + y}).start()
        return 0

    lax.fori_loop(0, 4, first_steps, 0)
    ncopies = product_join(0, ncopies, value_ref)
    lax.fori_loop(0, 3, second_steps, 0)
    block_step(7)
    part_out[...] = features_of(sums, None, thigh_ref, tlow_ref).reshape(part_out.shape)
    tcopies = to_tys(part_out, lambda d: part_in.at[d - 1], a_s, a_r, True)
    ncopies = product_end(0, ncopies, value_ref)
    for k in range(2):
        ycopy(k, z).wait()
        own[k] = weight_block(k, 2 * z + y) + yrecv[k, z].astype(FLOAT)
    unit, rate = norm_rows(lat_ref[ty].astype(FLOAT))
    raw_mix = part_out[ty]
    finish(tcopies)
    for d in range(3):
        raw_mix = raw_mix + part_in[d]
    mix = (raw_mix * fgain_ref[...]).astype(BFLOAT)
    gmix[ty] = mix
    mcopies = to_tys(gmix.at[ty], lambda d: gmix.at[ty], m_s.at[0], m_r.at[0])
    grad_q = (dot_nn(mix, kproj_ref[...]) * (1.0 / math.sqrt(qproj_ref.shape[0]))).astype(BFLOAT)
    grad, qgain_grad = norm_rows_back(dot_nt(grad_q, qproj_ref[...]), qgain_ref[...], unit, rate)
    qgains_out[...] = jnp.zeros_like(qgains_out)
    features = feat_ref[...] + jnp.sum(raw_mix * raw_ref[...], axis=0, keepdims=True)
    for h in range(4):
        qgains_out[h, 0:1] = qgain_grad[:, 256 * h : 256 * h + 256]
    qgains_out[0, 1:2] = features[:, 0:256]
    qgains_out[1, 1:2, 0:128] = features[:, 256:384]
    qgains_in[ty] = qgains_out[ty]
    mcopies += to_tys(qgains_out, lambda d: qgains_in.at[ty], m_s.at[1], m_r.at[1], True)
    grad_ref[ty] = (one_ref[...] + grad).astype(BFLOAT)
    ncopies += to_tys(grad_ref.at[ty], lambda d: grad_ref.at[ty], o_s, o_r)
    finish(mcopies)
    gain_rows = qgains_in[0] + qgains_in[1] + qgains_in[2] + qgains_in[3]
    mcopies = product_start(1, gmix[...].reshape(4 * share, LANES), qrows_ref[...], gain_rows)
    for k in range(2):
        total = own[k]
        for c in range(3):
            zcopy(k, c, zs[c]).wait()
            total = total + zrecv[k, c].astype(FLOAT)
        last[k] = total.astype(BFLOAT)
        place = sums_ref.at[4 * k + ty]
        ncopies += to_tys(last.at[k], lambda d: place, w_s.at[k], w_r.at[k])
        mine = pltpu.make_async_copy(last.at[k], place, l_s.at[k])
        mine.start()
        ncopies.append(mine)
    mcopies = product_join(1, mcopies, key_ref)
    ncopies += product_end(1, mcopies, key_ref)
    finish(ncopies)


def back(msgs, coefs, up, one, lat, raw, query_gain, gain_lanes, query_proj, key_rows, thigh, tlow, hot,
         xs, gs, mix, gcross, gains, feats, qrows):
    _, share, width = lat.shape
    rows, length = coefs.shape[1], msgs.shape[2]
    dma = pltpu.SemaphoreType.DMA
    vmem = pl.BlockSpec(memory_space=pltpu.VMEM)
    shape = jax.ShapeDtypeStruct
    block = (width // 8, width)
    return pl.pallas_call(
        back_kernel,
        out_shape=(
            shape((4, share, width), BFLOAT),
            shape((4, 272, 256), BFLOAT),
            shape((4, 272, 256), BFLOAT),
            shape((8,) + block, BFLOAT),
        ),
        in_specs=[vmem] * 20,
        out_specs=(vmem, vmem, vmem, pl.BlockSpec(memory_space=pl.ANY)),
        scratch_shapes=[
            pltpu.VMEM((2 * GROUP, length), BFLOAT),
            pltpu.VMEM(coefs.shape, BFLOAT),
            pltpu.VMEM((rows, length), FLOAT),
            pltpu.VMEM((rows, length), FLOAT),
            pltpu.VMEM((rows, length), BFLOAT),
            pltpu.VMEM((8, rows, GROUP), FLOAT),
            pltpu.VMEM((4, share, LANES), FLOAT),
            pltpu.VMEM((3, share, LANES), FLOAT),
            pltpu.VMEM((4, share, LANES), BFLOAT),
            pltpu.VMEM((4, 8, 256), FLOAT),
            pltpu.VMEM((4, 8, 256), FLOAT),
            pltpu.VMEM((2, 8, 32, 256), BFLOAT),
            pltpu.VMEM((2, 16, 256), BFLOAT),
            pltpu.VMEM((2, 7, 32, 256), BFLOAT),
            pltpu.VMEM((2, 7, 16, 256), BFLOAT),
            pltpu.VMEM((2, 4) + block, BFLOAT),
            pltpu.VMEM((2, 4) + block, BFLOAT),
            pltpu.VMEM((2,) + block, FLOAT),
            pltpu.VMEM((2, 3) + block, BFLOAT),
            pltpu.VMEM((2, 3) + block, BFLOAT),
            pltpu.VMEM((2,) + block, BFLOAT),
            dma((3,)), dma((3,)), dma((3,)), dma((3,)), dma((2, 3)), dma((2, 3)),
            dma((2, 7)), dma((2, 7)), dma((2, 7)), dma((2, 7)), dma((2, 7)), dma((2, 7)),
            dma((2, 3)), dma((2, 3)), dma((2, 4)), dma((2, 4)), dma((2, 3)), dma((2, 3)),
            dma((2, 3)), dma((2, 3)), dma((2,)),
        ],
        compiler_params=pltpu.CompilerParams(
            collective_id=5, has_side_effects=True, vmem_limit_bytes=56 << 20
        ),
        name="back",
    )(msgs, coefs, up, one, lat, raw, query_gain, gain_lanes, query_proj, key_rows, thigh, tlow, hot,
      xs, gs, mix, gcross, gains, feats, qrows)


def pixel_tables(image_sizes, row_ids, tile_width):
    high = len(row_ids) // HALVES
    all_cols = jnp.arange(8 * tile_width, dtype=jnp.int32)
    row_table, row_coord, row_sum = axis_tables(image_sizes, row_ids, 3, 5)
    col_table, col_coord, col_sum = axis_tables(image_sizes, all_cols, 4, 5 + 2 * BANDS)
    row_table = row_table - row_sum[:, :, None] * (1.0 / FEAT)
    col_table = col_table - col_sum[:, :, None] * (1.0 / FEAT)
    row_table = row_table.reshape(2, HALVES, high, FEAT)
    col_table = col_table.reshape(2, 8, tile_width, FEAT)
    colours = np.zeros((2, HALVES, 16, FEAT), np.float32)
    for b in range(2):
        for half in range(HALVES):
            for c in range(3):
                colours[b, half, half * 8 + b * 4 + c] = -1.0 / FEAT
                colours[b, half, half * 8 + b * 4 + c, c] += 1.0
    first = jnp.concatenate(
        [jnp.asarray(colours), row_table, jnp.zeros((2, HALVES, GROUP - 16 - high, FEAT), FLOAT)], axis=2
    )
    col_from = 16 + -(-high // 8) * 8
    second = jnp.pad(col_table, ((0, 0), (0, 0), (col_from, GROUP - col_from - tile_width), (0, 0)))
    table = jnp.concatenate([first, second], axis=1).reshape(2, 10 * GROUP, FEAT)
    table = jnp.pad(table, ((0, 0), (0, 0), (0, LANES - FEAT)))
    hot = np.zeros((GROUP, -(-high * tile_width // 128) * 128), np.float32)
    for i in range(high):
        for j in range(tile_width):
            hot[16 + i, i * tile_width + j] = 1.0
            hot[col_from + j, i * tile_width + j] = 1.0
    here = lax.dynamic_slice_in_dim
    at = lax.axis_index("tx") * tile_width
    return (
        split_two(table), jnp.asarray(hot, BFLOAT),
        (row_coord, row_sum), (here(col_coord, at, tile_width, 1), here(col_sum, at, tile_width, 1)),
    )


def pixel_message(pixels, live, rows, cols, length):
    (row_coord, row_sum), (col_coord, col_sum) = rows, cols
    _, _, height, width = pixels.shape
    wide = pixels.astype(FLOAT)
    mean = (jnp.sum(wide, axis=1) + row_sum[:, :, None] + col_sum[:, None, :]) * (1.0 / FEAT)
    square = (
        jnp.sum(wide * wide, axis=1)
        + (row_coord * row_coord)[:, :, None]
        + (col_coord * col_coord)[:, None, :]
        + 2.0 * BANDS
    ) * (1.0 / FEAT)
    rate = jnp.where(live, lax.rsqrt(square - mean * mean + EPSILON), 0.0)
    rows = jnp.concatenate([pixels, rate.astype(BFLOAT)[:, None]], axis=1)
    rows = rows.reshape(2, 4, HALVES, height // HALVES * width)
    rows = jnp.transpose(rows, (2, 0, 1, 3)).reshape(16, -1)
    return jnp.pad(rows, ((0, 0), (0, length - rows.shape[1])))


def on_device_fast(
    pixels,
    pixel_mask,
    image_sizes,
    latents,
    cotangent,
    feature_gain,
    query_gain,
    query_proj,
    key_proj,
    value_proj,
    cross_proj,
    hidden_gain,
    hidden_up,
    hidden_down,
    tower_gain,
    tower_query,
    tower_key,
    tower_value,
    tower_proj,
    final_gain,
    final_up,
    final_down,
):
    item_count = pixels.shape[0]
    tile_height = pixels.shape[2]
    tile_width = pixels.shape[3]
    model_width = latents.shape[2]
    rows_here = latents.shape[1]
    cross_scale = 1.0 / math.sqrt(model_width)
    row_ids = lax.axis_index("ty") * tile_height + jnp.arange(tile_height, dtype=jnp.int32)
    col_ids = lax.axis_index("tx") * tile_width + jnp.arange(tile_width, dtype=jnp.int32)
    side_sizes = image_sizes[:, None, None]
    live = (
        (pixel_mask > 0)
        & (row_ids[None, :, None] < side_sizes)
        & (col_ids[None, None, :] < side_sizes)
    )
    (thigh, tlow), hot, rows, cols = pixel_tables(image_sizes, row_ids, tile_width)
    message = pixel_message(pixels, live, rows, cols, hot.shape[1])
    share = item_count * rows_here // 4

    def in_shares(rows):
        return rows.reshape(4, share, rows.shape[-1])

    gain_lanes = jnp.pad(feature_gain, (0, LANES - FEAT))[None]
    value_rows = jnp.pad(value_proj, ((0, LANES - FEAT), (0, 0)))
    key_rows = jnp.pad(key_proj, ((0, LANES - FEAT), (0, 0)))
    messages, pixel_coefs, part, query_rows, raw_query = front(
        message, latents, query_gain[None], gain_lanes, query_proj, key_rows, thigh, tlow, hot
    )
    result, lefts, rights, mix, g_cross, grad_one, gain_parts, feat_part, coefs = tower(
        part, in_shares(latents), in_shares(cotangent), gain_lanes,
        hidden_gain[None], tower_gain[None], final_gain[None], value_rows,
        (cross_proj, hidden_up, hidden_down, tower_query, tower_key, tower_value, tower_proj,
         final_up, final_down),
    )
    latent_grad, cross_core, query_core, sums = back(
        messages, pixel_coefs, coefs, grad_one, in_shares(latents), raw_query, query_gain[None],
        gain_lanes, query_proj, key_rows, thigh, tlow, hot, lefts, rights, mix, g_cross, gain_parts,
        feat_part, query_rows
    )
    latent_grad = latent_grad.astype(FLOAT).reshape(latents.shape)
    sums = sums.astype(FLOAT)
    cross_core = jnp.transpose(cross_core, (1, 0, 2)).reshape(-1, model_width)
    query_core = jnp.transpose(query_core, (1, 0, 2)).reshape(-1, model_width)
    gain_sums = jnp.concatenate([query_core[264:266], cross_core[264:267]]).astype(FLOAT)
    cross_core, query_core = cross_core[:FEAT], query_core[:FEAT]
    value_proj_grad = linear_back(cross_core, cross_proj)
    key_proj_grad = linear(query_core, query_proj) * cross_scale
    wide = model_width // 8
    tx_from = lax.axis_index("tx") * wide
    cross_proj_grad = weight_grad(
        lax.dynamic_slice_in_dim(value_proj, tx_from, wide, 1), cross_core
    )
    query_proj_grad = weight_grad(
        lax.dynamic_slice_in_dim(query_core, tx_from, wide, 1), key_proj
    ) * cross_scale
    gain_here = lax.dynamic_slice_in_dim(gain_sums, tx_from, wide, 1)
    return (
        result.reshape(latents.shape),
        latent_grad,
        gain_sums[1, :FEAT],
        gain_here[0],
        query_proj_grad,
        key_proj_grad,
        value_proj_grad,
        cross_proj_grad,
        gain_here[2],
        sums[7],
        sums[5],
        gain_here[3],
        sums[3],
        sums[4],
        sums[6],
        sums[1],
        gain_here[4],
        sums[2],
        sums[0],
    )


def on_device(
    pixels,
    pixel_mask,
    image_sizes,
    latents,
    cotangent,
    feature_gain,
    query_gain,
    query_proj,
    key_proj,
    value_proj,
    cross_proj,
    hidden_gain,
    hidden_up,
    hidden_down,
    tower_gain,
    tower_query,
    tower_key,
    tower_value,
    tower_proj,
    final_gain,
    final_up,
    final_down,
):
    item_count = pixels.shape[0]
    tile_height = pixels.shape[2]
    tile_width = pixels.shape[3]
    model_width = latents.shape[2]
    rows_here = latents.shape[1]
    head_count = HEADS
    head_size = model_width // head_count
    cross_scale = 1.0 / math.sqrt(model_width)
    tower_scale = 1.0 / math.sqrt(head_size)
    row_ids = lax.axis_index("ty") * tile_height + jnp.arange(tile_height, dtype=jnp.int32)
    col_ids = lax.axis_index("tx") * tile_width + jnp.arange(tile_width, dtype=jnp.int32)
    all_cols = jnp.arange(tile_width * lax.axis_size("tx"), dtype=jnp.int32)
    wide_pixels = lax.all_gather(pixels, "tx", axis=3, tiled=True).astype(FLOAT)
    wide_mask = lax.all_gather(pixel_mask, "tx", axis=2, tiled=True)
    side_sizes = image_sizes[:, None, None]
    live = (
        (wide_mask > 0)
        & (row_ids[None, :, None] < side_sizes)
        & (all_cols[None, None, :] < side_sizes)
    )[:, None]
    row_table, row_coord, row_sum = axis_tables(image_sizes, row_ids, 3, 5)
    col_table, col_coord, col_sum = axis_tables(image_sizes, all_cols, 4, 5 + 2 * BANDS)
    pixel_mean = (
        jnp.sum(wide_pixels, axis=1) + row_sum[:, :, None] + col_sum[:, None, :]
    ) / FEAT
    pixel_square = (
        jnp.sum(wide_pixels * wide_pixels, axis=1)
        + (row_coord * row_coord)[:, :, None]
        + (col_coord * col_coord)[:, None, :]
        + 2.0 * BANDS
    ) / FEAT
    pixel_rate = lax.rsqrt(pixel_square - pixel_mean * pixel_mean + EPSILON)
    exact = lax.Precision.HIGHEST

    def against_pixels(coefs):
        by_row = jnp.einsum("blf,bif->bli", coefs, row_table, precision=exact)
        by_col = jnp.einsum("blf,bjf->blj", coefs, col_table, precision=exact)
        total = by_row[:, :, :, None] + by_col[:, :, None, :]
        for c in range(3):
            total = total + coefs[:, :, c][:, :, None, None] * wide_pixels[:, None, c]
        total = total - jnp.sum(coefs, axis=2)[:, :, None, None] * pixel_mean[:, None]
        return total * pixel_rate[:, None]

    def over_pixels(weights):
        scaled = weights * pixel_rate[:, None]
        by_row = jnp.sum(scaled, axis=3)
        by_col = jnp.sum(scaled, axis=2)
        total = jnp.einsum("bli,bif->blf", by_row, row_table, precision=exact)
        total = total + jnp.einsum("blj,bjf->blf", by_col, col_table, precision=exact)
        colour = jnp.stack(
            [jnp.sum(scaled * wide_pixels[:, None, c], axis=(2, 3)) for c in range(3)], axis=2
        )
        total = total + jnp.pad(colour, ((0, 0), (0, 0), (0, FEAT - 3)))
        return total - jnp.sum(scaled * pixel_mean[:, None], axis=(2, 3))[:, :, None]

    latent_rows = latents.astype(FLOAT)
    query_normed, back_query_norm = jax.vjp(layer_norm, latent_rows, query_gain)
    query_input = query_normed.astype(BFLOAT)
    own_queries = linear(query_input, query_proj).astype(BFLOAT)
    raw_query = linear_back(own_queries, key_proj) * cross_scale
    scores = against_pixels(raw_query * feature_gain)
    row_top = jnp.max(jnp.where(live, scores, -1e30), axis=(2, 3))
    all_top = lax.pmax(row_top, "ty")
    row_exp = jnp.where(live, jnp.exp(scores - all_top[:, :, None, None]), 0.0)
    row_total = lax.psum(jnp.sum(row_exp, axis=(2, 3)), "ty")
    cross_exact = row_exp / row_total[:, :, None, None]
    raw_mix = lax.psum(over_pixels(cross_exact), "ty")
    mix = raw_mix * feature_gain
    attended = linear(mix.astype(BFLOAT), value_proj)
    attended_input = attended.astype(BFLOAT)
    resid_one = latent_rows + linear(attended_input, cross_proj)
    hidden_normed, back_hidden_norm = jax.vjp(layer_norm, resid_one, hidden_gain)
    hidden_input = hidden_normed.astype(BFLOAT)
    hidden_lifted, back_hidden_gelu = jax.vjp(gelu_tanh, linear(hidden_input, hidden_up))
    hidden_act = hidden_lifted.astype(BFLOAT)
    resid_two = resid_one + linear(hidden_act, hidden_down)
    tower_normed, back_tower_norm = jax.vjp(layer_norm, resid_two, tower_gain)
    tower_input = tower_normed.astype(BFLOAT)
    tower_q = linear(tower_input, tower_query).astype(BFLOAT)
    tower_k = linear(tower_input, tower_key).astype(BFLOAT)
    tower_v = linear(tower_input, tower_value).astype(BFLOAT)
    all_keys, all_values = (
        lax.all_gather(tower_k, "tx", axis=1, tiled=True),
        lax.all_gather(tower_v, "tx", axis=1, tiled=True),
    )
    split_q = tower_q.reshape(item_count, rows_here, head_count, head_size)
    split_k = all_keys.reshape(item_count, -1, head_count, head_size)
    split_v = all_values.reshape(item_count, -1, head_count, head_size)
    tower_scores = (
        jnp.einsum("bqhd,bkhd->bhqk", split_q, split_k, preferred_element_type=FLOAT) * tower_scale
    )
    tower_top = jnp.max(tower_scores, axis=3, keepdims=True)
    tower_exp = jnp.exp(tower_scores - tower_top)
    tower_total = jnp.sum(tower_exp, axis=3, keepdims=True)
    tower_exact = tower_exp / tower_total
    tower_probs = tower_exact.astype(BFLOAT)
    mixed = jnp.einsum(
        "bhqk,bkhd->bqhd", tower_probs, split_v, preferred_element_type=FLOAT
    ).reshape(item_count, rows_here, model_width)
    mixed_input = mixed.astype(BFLOAT)
    resid_three = resid_two + linear(mixed_input, tower_proj)
    final_normed, back_final_norm = jax.vjp(layer_norm, resid_three, final_gain)
    final_input = final_normed.astype(BFLOAT)
    final_lifted, back_final_gelu = jax.vjp(gelu_tanh, linear(final_input, final_up))
    final_act = final_lifted.astype(BFLOAT)
    resid_four = resid_three + linear(final_act, final_down)
    grad_four = cotangent.astype(FLOAT)
    final_down_grad = weight_grad(final_act, cotangent)
    grad_final_lift = back_final_gelu(linear_back(cotangent, final_down))[0].astype(BFLOAT)
    final_up_grad = weight_grad(final_input, grad_final_lift)
    grad_rows_three, final_gain_grad = back_final_norm(linear_back(grad_final_lift, final_up))
    grad_three = grad_four + grad_rows_three
    grad_tower_out = grad_three.astype(BFLOAT)
    tower_proj_grad = weight_grad(mixed_input, grad_tower_out)
    grad_mixed_flat = linear_back(grad_tower_out, tower_proj).astype(BFLOAT)
    grad_mixed = grad_mixed_flat.reshape(item_count, rows_here, head_count, head_size)
    grad_tower_p = jnp.einsum("bqhd,bkhd->bhqk", grad_mixed, split_v, preferred_element_type=FLOAT)
    tower_delta = jnp.sum(tower_exact * grad_tower_p, axis=3, keepdims=True)
    grad_tower_scores = (tower_exact * (grad_tower_p - tower_delta)).astype(BFLOAT)
    grad_tower_q = (
        (
            jnp.einsum("bhqk,bkhd->bqhd", grad_tower_scores, split_k, preferred_element_type=FLOAT)
            * tower_scale
        )
        .astype(BFLOAT)
        .reshape(item_count, rows_here, model_width)
    )
    value_part = jnp.einsum(
        "bhqk,bqhd->bkhd", tower_probs, grad_mixed, preferred_element_type=FLOAT
    )
    key_part = (
        jnp.einsum("bhqk,bqhd->bkhd", grad_tower_scores, split_q, preferred_element_type=FLOAT)
        * tower_scale
    )
    key_sums, value_sums = (
        lax.psum_scatter(
            key_part.reshape(item_count, -1, model_width), "tx", scatter_dimension=1, tiled=True
        ),
        lax.psum_scatter(
            value_part.reshape(item_count, -1, model_width), "tx", scatter_dimension=1, tiled=True
        ),
    )
    grad_tower_k = key_sums.astype(BFLOAT)
    grad_tower_v = value_sums.astype(BFLOAT)
    tower_query_grad = weight_grad(tower_input, grad_tower_q)
    tower_key_grad = weight_grad(tower_input, grad_tower_k)
    tower_value_grad = weight_grad(tower_input, grad_tower_v)
    grad_tower_rows = (
        linear_back(grad_tower_q, tower_query)
        + linear_back(grad_tower_k, tower_key)
        + linear_back(grad_tower_v, tower_value)
    )
    grad_rows_two, tower_gain_grad = back_tower_norm(grad_tower_rows)
    grad_two = grad_three + grad_rows_two
    grad_hidden_out = grad_two.astype(BFLOAT)
    hidden_down_grad = weight_grad(hidden_act, grad_hidden_out)
    grad_hidden_lift = back_hidden_gelu(linear_back(grad_hidden_out, hidden_down))[0].astype(BFLOAT)
    hidden_up_grad = weight_grad(hidden_input, grad_hidden_lift)
    grad_rows_one, hidden_gain_grad = back_hidden_norm(linear_back(grad_hidden_lift, hidden_up))
    grad_one = grad_two + grad_rows_one
    grad_cross_out = grad_one.astype(BFLOAT)
    cross_proj_grad = weight_grad(attended_input, grad_cross_out)
    grad_attended = linear_back(grad_cross_out, cross_proj).astype(BFLOAT)
    raw_up = linear_back(grad_attended, value_proj)
    grad_probs = against_pixels(raw_up * feature_gain)
    cross_delta = jnp.sum(grad_attended.astype(FLOAT) * attended, axis=2)
    grad_scores = cross_exact * (grad_probs - cross_delta[:, :, None, None])
    raw_grad_mix = lax.psum(over_pixels(grad_scores), "ty")
    grad_mix = (raw_grad_mix * feature_gain).astype(BFLOAT)
    grad_queries = (linear(grad_mix, key_proj) * cross_scale).astype(BFLOAT)
    key_proj_grad = weight_grad(grad_mix, own_queries) * cross_scale
    value_proj_grad = weight_grad(mix.astype(BFLOAT), grad_attended)
    feature_part = jnp.sum(raw_grad_mix * raw_query + raw_mix * raw_up, axis=(0, 1))
    pixel_sums = lax.psum((key_proj_grad, value_proj_grad, feature_part), "tx")
    query_proj_grad = weight_grad(query_input, grad_queries)
    grad_latent_rows, query_gain_grad = back_query_norm(linear_back(grad_queries, query_proj))
    latent_grad = grad_one + grad_latent_rows
    summed = (
        lax.psum_scatter(query_gain_grad, "tx", scatter_dimension=0, tiled=True),
        lax.psum_scatter(query_proj_grad, "tx", scatter_dimension=0, tiled=True),
        lax.psum_scatter(cross_proj_grad, "tx", scatter_dimension=0, tiled=True),
        lax.psum_scatter(hidden_gain_grad, "tx", scatter_dimension=0, tiled=True),
        lax.psum_scatter(hidden_up_grad, "tx", scatter_dimension=0, tiled=True),
        lax.psum_scatter(hidden_down_grad, "tx", scatter_dimension=0, tiled=True),
        lax.psum_scatter(tower_gain_grad, "tx", scatter_dimension=0, tiled=True),
        lax.psum_scatter(tower_query_grad, "tx", scatter_dimension=0, tiled=True),
        lax.psum_scatter(tower_key_grad, "tx", scatter_dimension=0, tiled=True),
        lax.psum_scatter(tower_value_grad, "tx", scatter_dimension=0, tiled=True),
        lax.psum_scatter(tower_proj_grad, "tx", scatter_dimension=0, tiled=True),
        lax.psum_scatter(final_gain_grad, "tx", scatter_dimension=0, tiled=True),
        lax.psum_scatter(final_up_grad, "tx", scatter_dimension=0, tiled=True),
        lax.psum_scatter(final_down_grad, "tx", scatter_dimension=0, tiled=True),
    )
    return (
        resid_four.astype(BFLOAT),
        latent_grad,
        pixel_sums[2],
        summed[0],
        summed[1],
        pixel_sums[0],
        pixel_sums[1],
        summed[2],
        summed[3],
        summed[4],
        summed[5],
        summed[6],
        summed[7],
        summed[8],
        summed[9],
        summed[10],
        summed[11],
        summed[12],
        summed[13],
    )


def solution(mesh):
    in_specs = (
        P(None, None, "ty", "tx"),
        P(None, "ty", "tx"),
        P(),
        P(None, "tx", None),
        P(None, "tx", None),
        P(),
        P(),
        P(),
        P(),
        P(),
        P(),
        P(),
        P(),
        P(),
        P(),
        P(),
        P(),
        P(),
        P(),
        P(),
        P(),
        P(),
    )
    out_specs = (
        P(None, "tx", None),
        P(None, "tx", None),
        P(),
        P("tx"),
        P("tx", None),
        P(),
        P(),
        P("tx", None),
        P("tx"),
        P("tx", None),
        P("tx", None),
        P("tx"),
        P("tx", None),
        P("tx", None),
        P("tx", None),
        P("tx", None),
        P("tx"),
        P("tx", None),
        P("tx", None),
    )
    fits = mesh.shape["ty"] == 4 and mesh.shape["tx"] == HEADS
    plan = on_device_fast if fits else on_device
    return jax.shard_map(
        plan, mesh=mesh, in_specs=in_specs, out_specs=out_specs, check_vma=False
    )
```

```python
import math

import jax
import jax.numpy as jnp
import numpy as np
from jax import lax
from jax.experimental import pallas as pl
from jax.experimental.pallas import tpu as pltpu
from jax.sharding import PartitionSpec as P

BANDS = 64
FEAT = 261
HEADS = 8


EPSILON = 1e-05
FLOAT = jnp.float32
BFLOAT = jnp.bfloat16


def layer_norm(values, scales):
    centre = jnp.mean(values, axis=-1, keepdims=True)
    shifted = values - centre
    spread = jnp.mean(shifted * shifted, axis=-1, keepdims=True)
    return shifted * lax.rsqrt(spread + EPSILON) * scales


def gelu_tanh(values):
    cubic = values + 0.044715 * values * values * values
    return 0.5 * values * (1.0 + jnp.tanh(0.7978845608028654 * cubic))


def linear(inputs, weight):
    return lax.dot_general(
        inputs, weight, (((inputs.ndim - 1,), (0,)), ((), ())), preferred_element_type=FLOAT
    )


def linear_back(upstream, weight):
    return lax.dot_general(
        upstream, weight, (((upstream.ndim - 1,), (1,)), ((), ())), preferred_element_type=FLOAT
    )


def weight_grad(inputs, upstream):
    flat_inputs = inputs.reshape(-1, inputs.shape[-1])
    flat_upstream = upstream.reshape(-1, upstream.shape[-1])
    return lax.dot_general(
        flat_inputs, flat_upstream, (((0,), (0,)), ((), ())), preferred_element_type=FLOAT
    )


def axis_tables(image_sizes, ids, coord_lane, first_lane):
    side = image_sizes.astype(FLOAT)[:, None]
    coord = -1.0 + 2.0 * ids.astype(FLOAT)[None, :] / (side - 1.0)
    band = jnp.arange(BANDS, dtype=jnp.int32).astype(FLOAT)
    frequency = 1.0 + band[None, :] * (side * 0.5 - 1.0) / (BANDS - 1)
    angle = math.pi * coord[:, :, None] * frequency[:, None, :]
    waves = jnp.concatenate([jnp.sin(angle), jnp.cos(angle)], axis=2)
    count, length = coord.shape
    lead = jnp.zeros((count, length, coord_lane), FLOAT)
    gap = jnp.zeros((count, length, first_lane - coord_lane - 1), FLOAT)
    tail = jnp.zeros((count, length, FEAT - first_lane - 2 * BANDS), FLOAT)
    table = jnp.concatenate([lead, coord[:, :, None], gap, waves, tail], axis=2)
    return table, coord, jnp.sum(waves, axis=2) + coord


MESH = pl.DeviceIdType.MESH


def send(src, dst, send_sem, recv_sem, where):
    copy = pltpu.make_async_remote_copy(
        src_ref=src, dst_ref=dst, send_sem=send_sem, recv_sem=recv_sem,
        device_id=where, device_id_type=MESH,
    )
    copy.start()
    return copy


def greet(places):
    barrier = pltpu.get_barrier_semaphore()
    for place in places:
        pl.semaphore_signal(barrier, inc=1, device_id=place, device_id_type=MESH)
    pl.semaphore_wait(barrier, len(places))


def outer(left, right):
    return lax.dot_general(left, right, (((0,), (0,)), ((), ())), preferred_element_type=FLOAT)


LANES = 384
CUBE = 0.044715
SLOPE = 0.7978845608028654


def norm_rows(rows):
    shifted = rows - jnp.mean(rows, axis=-1, keepdims=True)
    rate = lax.rsqrt(jnp.mean(shifted * shifted, axis=-1, keepdims=True) + EPSILON)
    return shifted * rate, rate


def norm_rows_back(upstream, gain, unit, rate):
    scaled = upstream * gain
    along = jnp.mean(scaled * unit, axis=-1, keepdims=True)
    grad = rate * (scaled - jnp.mean(scaled, axis=-1, keepdims=True) - unit * along)
    return grad, jnp.sum(upstream * unit, axis=0, keepdims=True)


def gelu_pair(values):
    square = values * values
    bend = jnp.tanh(SLOPE * (values + CUBE * values * square))
    half = 0.5 * (1.0 + bend)
    slope = half + 0.5 * values * (1.0 - bend * bend) * (SLOPE * (1.0 + 3.0 * CUBE * square))
    return values * half, slope


def dot_nt(left, right):
    return lax.dot_general(left, right, (((1,), (1,)), ((), ())), preferred_element_type=FLOAT)


def dot_nn(left, right):
    return lax.dot_general(left, right, (((1,), (0,)), ((), ())), preferred_element_type=FLOAT)


HALVES = 2
GROUP = 128
LOG2E = 1.0 / math.log(2.0)


def split_two(values):
    high = values.astype(BFLOAT)
    return high, (values - high.astype(FLOAT)).astype(BFLOAT)


def dot_wide(dot, values, high, low):
    first, second = split_two(values)
    return dot(first, high) + (dot(first, low) + dot(second, high))


def coefs_by_pixel(coefs, thigh_ref, tlow_ref, into):
    count = coefs.shape[0] // 2
    for b in range(2):
        wide = dot_wide(dot_nt, coefs[b * count : (b + 1) * count], thigh_ref[b], tlow_ref[b])
        for half in range(HALVES):
            at = pl.ds((half * 2 + b) * count, count)
            rows = wide[:, half * GROUP : (half + 1) * GROUP]
            for t in range(8):
                high, low = split_two(rows + wide[:, (2 + t) * GROUP : (3 + t) * GROUP])
                into[t, at, 0:GROUP] = high
                into[t, at, GROUP : 2 * GROUP] = low


def features_of(sums, scales, thigh_ref, tlow_ref):
    count = sums.shape[1] // 4
    blocks = [sums[t] if scales is None else sums[t] * scales[t] for t in range(8)]
    joined = blocks[0]
    for block in blocks[1:]:
        joined = joined + block
    outs = []
    for b in range(2):
        first, second = pl.ds(b * count, count), (2 + b) * count
        lo, hi = slice(b * count, (b + 1) * count), slice((2 + b) * count, (3 + b) * count)
        wide = jnp.concatenate(
            [joined[lo], joined[hi]] + [block[lo] + block[hi] for block in blocks], axis=1
        )
        outs.append(dot_wide(dot_nn, wide, thigh_ref[b], tlow_ref[b]))
    return jnp.concatenate(outs, axis=0)


def rate_and_bias(block, group):
    rate = block[group % 2 * 4 + group // 2 * 8 + 3 :][:1].astype(FLOAT)
    return rate, jnp.where(rate == 0.0, -1e30, 0.0)


class Ring:
    def __init__(self, places, send_sems, recv_sems):
        self.places, self.sems = places, (send_sems, recv_sems)

    def copy(self, i, d, src, dst):
        return pltpu.make_async_remote_copy(
            src_ref=src, dst_ref=dst, send_sem=self.sems[0].at[i, d], recv_sem=self.sems[1].at[i, d],
            device_id=self.places[d], device_id_type=MESH,
        )

    def start(self, i, sources, into):
        copies = [self.copy(i, d, sources(d), into(d)) for d in range(len(self.places))]
        for copy in copies:
            copy.start()
        return copies


def finish(*groups):
    for copies in groups:
        for copy in copies:
            copy.wait()


def main_kernel(
    msg_ref, lat_ref, cot_ref, fgain_ref, qgain_ref, hgain_ref, tgain_ref, ogain_ref,
    kproj_ref, vproj_ref, thigh_ref, tlow_ref, hot_ref,
    w0, w1, w2, w3, w4, w5, w6, w7, w8, w9,
    result_ref, grad_ref, value_ref, key_ref, sums_ref,
    ws, msgs, pixcoefs, upcoefs, pixels, scores, ups, weights, sums, tops, totals, raw_all, qrows,
    part_out, part_in, q_out, q_in, kv_out, kv_in, kv_more, probs, mixed_out, mixed_in, gm_out, gm_in,
    kvx_out, kvx_in, gq_in, gkv_in, up_ref, mix_all, gcross_out, gcross_all, gains_out, gains_all, gmix,
    x_out, x_pass, x_all, g_out, g_all, own, zsend, zrecv, last, nsend, nextra, nrecv, nmore,
    w_sem, l_sem, ty_s, ty_r, tx_s, tx_r, mate_s, mate_r, xg_s, xg_r, y_s, y_r, z_s, z_r, o_s, o_r,
):
    ty, tx = lax.axis_index("ty"), lax.axis_index("tx")
    z, y = tx // 2, lax.rem(tx, 2)
    tys = [{"ty": lax.rem(ty + d, 4), "tx": tx} for d in (1, 2, 3)]
    txs = [{"ty": ty, "tx": lax.rem(tx + d, 8)} for d in range(1, 8)]
    mate = {"ty": 2 * (ty // 2) + 1 - lax.rem(ty, 2), "tx": tx}
    beside = {"ty": ty, "tx": 2 * z + 1 - y}
    on_ty, on_tx = Ring(tys, ty_s, ty_r), Ring(txs, tx_s, tx_r)
    on_mate = Ring([mate], mate_s, mate_r)
    handing, passing = Ring(tys, xg_s, xg_r), Ring([beside], y_s, y_r)
    giving = Ring(tys, o_s, o_r)
    loads = []
    for i, w in enumerate((w0, w1, w2, w3, w4, w5, w6, w7, w8, w9)):
        loads.append(pltpu.make_async_copy(w, ws.at[i], w_sem.at[i]))
        loads[i].start()
    cross, up, down, tq, tk, tv, tproj, fup, fdown = range(1, 10)
    greet(tys + txs)
    ty_at = lambda d: lax.rem(ty + d + 1, 4)
    tx_at = lambda d: lax.rem(tx + d + 1, 8)

    def times(rows, i):
        return dot_nn(rows, ws[i])

    def times_back(rows, i):
        return dot_nt(rows, ws[i])

    def to_ty(i, src, into):
        return on_ty.start(i, lambda d: src, lambda d: into)

    def spread(i, out, into):
        copies = on_tx.start(i, lambda d: out.at[tx_at(d)], lambda d: into.at[tx])
        into[tx] = out[tx]
        return copies

    def over_ty(i, out, into):
        copies = on_ty.start(i, lambda d: out.at[ty_at(d)], lambda d: into.at[ty])
        into[ty] = out[ty]
        return copies

    xg = {}

    def give_x(i, rows):
        for c in range(8):
            x_out[i, c % 2, c // 2] = rows[:, 128 * c : 128 * c + 128]
        x_all[i, :, 0, ty] = x_out[i, y]
        x_pass[i, :, ty] = x_out[i, 1 - y]
        xg["x", i] = handing.start(
            i, lambda d: x_out.at[i, y], lambda d: x_all.at[i, :, 0, ty]
        ) + handing.start(14 + i, lambda d: x_out.at[i, 1 - y], lambda d: x_pass.at[i, :, ty])

    def give_g(w, rows):
        for h in range(4):
            g_out[w, h] = rows[:, 256 * h : 256 * h + 256]
        g_all[w, 0, ty] = g_out[w, ty]
        xg["g", w] = handing.start(6 + w, lambda d: g_out.at[w, ty_at(d)], lambda d: g_all.at[w, 0, ty])

    def pass_x(i):
        finish(xg.pop(("x", i)))
        xg["px", i] = passing.start(i, lambda d: x_pass.at[i], lambda d: x_all.at[i, :, 1])

    def pass_g(w):
        finish(xg.pop(("g", w)))
        xg["pg", w] = passing.start(6 + w, lambda d: g_all.at[w, 0], lambda d: g_all.at[w, 1])

    def slot_x(w):
        return min(w, 3) + max(w - 5, 0) if isinstance(w, int) else jnp.minimum(w, 3) + jnp.maximum(w - 5, 0)

    def zcopy(w, c):
        return pltpu.make_async_remote_copy(
            src_ref=zsend.at[w, c], dst_ref=zrecv.at[w, c], send_sem=z_s.at[w, c],
            recv_sem=z_r.at[w, c], device_id={"ty": ty, "tx": 2 * lax.rem(z + c + 1, 4) + y},
            device_id_type=MESH,
        )

    def stage_one(w):
        i = slot_x(w)
        if isinstance(w, int):
            finish(xg.pop(("px", i), ()), xg.pop(("pg", w)))
        else:
            finish([passing.copy(6 + w, 0, g_all.at[w, 0], g_all.at[w, 1])])
        right = g_all[w].reshape(256, 256)
        for c in range(4):
            at = lax.rem(z + c + 1, 4)
            total = outer(x_all[i, at].reshape(256, 128), right)
            if c == 3:
                own[w] = total
            else:
                zsend[w, c] = total.astype(BFLOAT)
                zcopy(w, c).start()

    def out_copies(w):
        return [giving.copy(w, d, last.at[w], sums_ref.at[w, ty]) for d in range(3)] + [
            pltpu.make_async_copy(last.at[w], sums_ref.at[w, ty], l_sem.at[w])
        ]

    def stage_three(w):
        total = own[w]
        for c in range(3):
            zcopy(w, c).wait()
            total = total + zrecv[w, c].astype(FLOAT)
        last[w] = total.astype(BFLOAT)
        for copy in out_copies(w):
            copy.start()

    def product_start(i, left, right, gains):
        product = outer(left, right)
        nsend[i] = product[0:256].astype(BFLOAT).reshape(8, 32, 256)
        row = lax.broadcasted_iota(jnp.int32, (16, 256), 0)
        more = product[256:272] + jnp.where(row < 8, 0.0, jnp.concatenate([gains, gains], axis=0))
        nextra[i] = more.astype(BFLOAT)
        return on_tx.start(
            6 + 3 * i, lambda d: nsend.at[i, tx_at(d)], lambda d: nrecv.at[i, d]
        ) + on_tx.start(7 + 3 * i, lambda d: nextra.at[i], lambda d: nmore.at[i, d])

    def product_join(i, copies, into):
        finish(copies)
        main = nsend[i, tx].astype(FLOAT)
        more = nextra[i].astype(FLOAT)
        for d in range(7):
            main = main + nrecv[i, d].astype(FLOAT)
            more = more + nmore[i, d].astype(FLOAT)
        mine = pl.ds(pl.multiple_of(tx * 32, 32), 32)
        into[ty, mine] = main.astype(BFLOAT)
        into[ty, 256:272] = more.astype(BFLOAT)
        return on_tx.start(8 + 3 * i, lambda d: into.at[ty, mine], lambda d: into.at[ty, mine])

    def product_end(i, copies, into):
        finish(copies)
        return to_ty(7 + i, into.at[ty], into.at[ty])

    def message(d):
        return on_tx.copy(0, d, msg_ref, msgs.at[tx])

    for d in range(7):
        message(d).start()
    msgs[tx] = msg_ref[...]
    pixels[0:GROUP] = hot_ref[...]
    pixels[GROUP : 2 * GROUP] = hot_ref[...]
    gains_out[...] = jnp.zeros_like(gains_out)
    share = lat_ref.shape[1]
    count, width = 2 * share, lat_ref.shape[2]
    cot = cot_ref[ty]
    give_g(0, cot)
    fgain = fgain_ref[...]
    unit, _ = norm_rows(lat_ref[...].reshape(4 * share, width).astype(FLOAT))
    rows = (unit * qgain_ref[...]).astype(BFLOAT)
    qrows[...] = rows
    finish(loads[:1])
    queries = times(rows, 0).astype(BFLOAT)
    cross_scale = 1.0 / math.sqrt(width)
    raw = dot_nt(queries, kproj_ref[...]) * cross_scale
    raw_all[...] = raw.reshape(raw_all.shape)
    coefs_by_pixel(raw * (fgain * LOG2E), thigh_ref, tlow_ref, pixcoefs)

    def take_block(t):
        block = msgs[t]
        pixels[0:16] = block
        pixels[GROUP : GROUP + 16] = block
        scores[...] = dot_nn(pixcoefs[t], pixels[...])
        return block

    def front_step(d, _):
        @pl.when(d > 0)
        def _():
            pltpu.make_async_remote_copy(
                src_ref=msg_ref, dst_ref=msgs.at[tx], send_sem=tx_s.at[0, d - 1],
                recv_sem=tx_r.at[0, d - 1], device_id=beside, device_id_type=MESH,
            ).wait()

        t = lax.rem(tx + 8 - d, 8)
        block = take_block(t)
        for group in range(4):
            at = pl.ds(group * count, count)
            rate, bias = rate_and_bias(block, group)
            s = scores[at] * rate + bias
            top = jnp.max(s, axis=1, keepdims=True)
            e = jnp.exp2(s - top)
            tops[t, at] = top
            totals[t, at] = jnp.sum(e, axis=1, keepdims=True)
            weights[at] = (e * rate).astype(BFLOAT)
        sums[t] = dot_nt(weights[...], pixels[0:GROUP])
        return 0

    lax.fori_loop(0, 8, front_step, 0)
    top = tops[0]
    for t in range(1, 8):
        top = jnp.maximum(top, tops[t])
    top = jnp.maximum(top[: 2 * count], top[2 * count :])
    both = jnp.concatenate([top, top], axis=0)
    scales = [jnp.exp2(tops[t] - both) for t in range(8)]
    total = sum(totals[t] * scales[t] for t in range(8))
    total = total[: 2 * count] + total[2 * count :]
    feats = features_of(sums, scales, thigh_ref, tlow_ref)
    lane = lax.broadcasted_iota(jnp.int32, feats.shape, 1)
    part_out[...] = jnp.where(
        lane < FEAT, feats, jnp.where(lane == FEAT, total, top)
    ).reshape(part_out.shape)

    copies = on_ty.start(0, lambda d: part_out.at[ty_at(d)], lambda d: part_in.at[d])
    latent = lat_ref[ty].astype(FLOAT)
    parts = [part_out[ty]]
    finish(copies)
    parts += [part_in[d] for d in range(3)]
    tops_in = [p[:, FEAT + 1 : FEAT + 2] for p in parts]
    top = jnp.maximum(
        jnp.maximum(tops_in[0], tops_in[1]), jnp.maximum(tops_in[2], tops_in[3])
    )
    joined = sum(p * jnp.exp2(t - top) for p, t in zip(parts, tops_in))
    total = joined[:, FEAT : FEAT + 1]
    raw_mix = joined / total
    shift = top + jnp.log2(total)
    mix = (raw_mix * fgain).astype(BFLOAT)
    mix_all[ty] = mix
    later = to_ty(1, mix_all.at[ty], mix_all.at[ty])
    attended = dot_nn(mix, vproj_ref[...])
    finish(loads[1:])
    one = latent + times(attended.astype(BFLOAT), cross)
    h_unit, h_rate = norm_rows(one)
    hidden = (h_unit * hgain_ref[...]).astype(BFLOAT)
    act, act_slope = gelu_pair(times(hidden, up))
    act = act.astype(BFLOAT)
    two = one + times(act, down)
    t_unit, t_rate = norm_rows(two)
    trows = (t_unit * tgain_ref[...]).astype(BFLOAT)
    for s, i in enumerate((tk, tv)):
        value = times(trows, i).astype(BFLOAT)
        for h in range(8):
            kv_out[h, 32 * s : 32 * s + 32] = value[:, 128 * h : 128 * h + 128]
    kv_copies = spread(1, kv_out, kv_in)
    value = times(trows, tq).astype(BFLOAT)
    for h in range(8):
        q_out[h] = value[:, 128 * h : 128 * h + 128]
    q_copies = spread(2, q_out, q_in)
    give_x(5, hidden)
    give_x(4, act)
    give_x(3, trows)
    back_four = times_back(cot, fdown)
    finish(kv_copies)
    copies = on_mate.start(0, lambda d: kv_in, lambda d: kv_more)
    finish(q_copies)
    q = q_in[...].reshape(8 * share, 128)
    k1 = kv_in[:, 0:32].reshape(8 * share, 128)
    v1 = kv_in[:, 32:64].reshape(8 * share, 128)
    scale = 1.0 / math.sqrt(128)
    s1 = dot_nt(q, k1) * scale
    finish(copies)
    k2 = kv_more[:, 0:32].reshape(8 * share, 128)
    v2 = kv_more[:, 32:64].reshape(8 * share, 128)
    s2 = dot_nt(q, k2) * scale
    stop = jnp.maximum(jnp.max(s1, axis=1, keepdims=True), jnp.max(s2, axis=1, keepdims=True))
    e1, e2 = jnp.exp(s1 - stop), jnp.exp(s2 - stop)
    rate = 1.0 / (jnp.sum(e1, axis=1, keepdims=True) + jnp.sum(e2, axis=1, keepdims=True))
    p1, p2 = e1 * rate, e2 * rate
    probs[0] = p1
    probs[1] = p2
    mixed_out[...] = (
        (dot_nn(p1.astype(BFLOAT), v1) + dot_nn(p2.astype(BFLOAT), v2))
        .astype(BFLOAT)
        .reshape(8, share, 128)
    )
    copies = spread(3, mixed_out, mixed_in)
    pass_g(0)
    pass_x(5)
    pass_x(4)
    pass_x(3)
    finish(copies)
    mixed = jnp.concatenate([mixed_in[h] for h in range(8)], axis=1)
    give_x(2, mixed)
    three = two + times(mixed, tproj)
    o_unit, o_rate = norm_rows(three)
    ogain = ogain_ref[...]
    frows = (o_unit * ogain).astype(BFLOAT)
    give_x(1, frows)
    fact, fact_slope = gelu_pair(times(frows, fup))
    fact = fact.astype(BFLOAT)
    give_x(0, fact)

    def put_gain(row, grad):
        for h in range(4):
            gains_out[0, h, row : row + 1] = grad[:, 256 * h : 256 * h + 256]

    g_lift = (back_four * fact_slope).astype(BFLOAT)
    give_g(1, g_lift)
    g_three, o_grad = norm_rows_back(times_back(g_lift, fup), ogain, o_unit, o_rate)
    put_gain(2, o_grad)
    g_three = cot.astype(FLOAT) + g_three
    g_tower = g_three.astype(BFLOAT)
    g_mixed = times_back(g_tower, tproj).astype(BFLOAT)
    for h in range(8):
        gm_out[h] = g_mixed[:, 128 * h : 128 * h + 128]
    copies = spread(4, gm_out, gm_in)
    give_g(2, g_tower)
    result_ref[ty] = (three + times(fact, fdown)).astype(BFLOAT)
    later += to_ty(2, result_ref.at[ty], result_ref.at[ty])
    pass_x(2)
    pass_x(1)
    pass_x(0)
    pass_g(1)
    finish(copies)
    gm = gm_in[...].reshape(8 * share, 128)
    q = q_in[...].reshape(8 * share, 128)
    k1 = kv_in[:, 0:32].reshape(8 * share, 128)
    v1 = kv_in[:, 32:64].reshape(8 * share, 128)
    k2 = kv_more[:, 0:32].reshape(8 * share, 128)
    v2 = kv_more[:, 32:64].reshape(8 * share, 128)
    p1, p2 = probs[0], probs[1]
    gp1, gp2 = dot_nt(gm, v1), dot_nt(gm, v2)
    away = jnp.sum(p1 * gp1, axis=1, keepdims=True) + jnp.sum(p2 * gp2, axis=1, keepdims=True)
    gs1 = (p1 * (gp1 - away)).astype(BFLOAT)
    gs2 = (p2 * (gp2 - away)).astype(BFLOAT)
    kvx_out[0] = (outer(gs2, q) * scale).astype(BFLOAT)
    kvx_out[1] = outer(p2.astype(BFLOAT), gm).astype(BFLOAT)
    copies = on_mate.start(1, lambda d: kvx_out, lambda d: kvx_in)
    gq = (dot_nn(gs1, k1) + dot_nn(gs2, k2)) * scale
    q_out[...] = gq.astype(BFLOAT).reshape(8, share, 128)
    q_copies = spread(5, q_out, gq_in)
    gk = outer(gs1, q) * scale
    gv = outer(p1.astype(BFLOAT), gm)
    finish(copies)
    kv_out[:, 0:32] = (gk + kvx_in[0].astype(FLOAT)).astype(BFLOAT).reshape(8, share, 128)
    kv_out[:, 32:64] = (gv + kvx_in[1].astype(FLOAT)).astype(BFLOAT).reshape(8, share, 128)
    kv_copies = spread(12, kv_out, gkv_in)
    pass_g(2)
    stage_one(0)
    finish(q_copies)
    value = jnp.concatenate([gq_in[h] for h in range(8)], axis=1)
    give_g(3, value)
    g_trows = times_back(value, tq)
    finish(kv_copies)
    for s, i in enumerate((tk, tv)):
        value = jnp.concatenate([gkv_in[h, 32 * s : 32 * s + 32] for h in range(8)], axis=1)
        give_g(4 + s, value)
        g_trows = g_trows + times_back(value, i)
    g_two, t_grad = norm_rows_back(g_trows, tgain_ref[...], t_unit, t_rate)
    put_gain(1, t_grad)
    g_two = g_three + g_two
    g_hidden = g_two.astype(BFLOAT)
    give_g(6, g_hidden)
    pass_g(3)
    stage_one(1)
    g_hlift = (times_back(g_hidden, down) * act_slope).astype(BFLOAT)
    give_g(7, g_hlift)
    pass_g(4)
    pass_g(5)
    stage_one(2)
    g_one, h_grad = norm_rows_back(times_back(g_hlift, up), hgain_ref[...], h_unit, h_rate)
    put_gain(0, h_grad)
    gain_copies = over_ty(3, gains_out.at[0], gains_all.at[0])
    g_one = g_two + g_one
    g_cross = g_one.astype(BFLOAT)
    for h in range(4):
        gcross_out[h] = g_cross[:, 256 * h : 256 * h + 256]
    gcross_copies = over_ty(4, gcross_out, gcross_all)
    g_att = times_back(g_cross, cross).astype(BFLOAT)
    raw_up = dot_nt(g_att, vproj_ref[...])
    feat_part = jnp.sum(raw_mix * raw_up, axis=0, keepdims=True)
    delta = jnp.sum(g_att.astype(FLOAT) * attended, axis=1, keepdims=True)
    lane = lax.broadcasted_iota(jnp.int32, raw_up.shape, 1)
    up_ref[ty] = jnp.where(
        lane < FEAT, raw_up * fgain, jnp.where(lane == FEAT, delta, shift)
    )
    copies = to_ty(5, up_ref.at[ty], up_ref.at[ty])
    pass_g(6)
    stage_one(3)
    finish(later, gain_copies, gcross_copies)
    gain_rows = gains_all[0, 0] + gains_all[0, 1] + gains_all[0, 2] + gains_all[0, 3]
    ncopies = product_start(
        0, mix_all[...].reshape(4 * share, LANES), gcross_all[...].reshape(4 * share, 256), gain_rows
    )
    finish(copies)
    pass_g(7)
    for i in (3, 4, 5):
        finish(xg.pop(("px", i), ()))

    coefs_by_pixel(up_ref[...].reshape(4 * share, LANES), thigh_ref, tlow_ref, upcoefs)

    def back_step(t):
        block = take_block(t)
        ups[...] = dot_nn(upcoefs[t], pixels[...])
        for group in range(4):
            at = pl.ds(group * count, count)
            rate, bias = rate_and_bias(block, group)
            b = group % 2
            mine = up_ref[2 * b : 2 * b + 2].reshape(count, LANES)
            p = jnp.exp2(scores[at] * rate + (bias - mine[:, FEAT + 1 : FEAT + 2]))
            g = p * (ups[at] * rate - mine[:, FEAT : FEAT + 1])
            weights[at] = (g * rate).astype(BFLOAT)
        sums[t] = dot_nt(weights[...], pixels[0:GROUP])

    def first_steps(t, _):
        back_step(t)
        stage_one(4 + t)
        return 0

    def second_steps(t, _):
        back_step(t)
        stage_three(t - 4)
        return 0

    lax.fori_loop(0, 3, first_steps, 0)
    ncopies = product_join(0, ncopies, value_ref)
    lax.fori_loop(3, 4, first_steps, 0)
    lax.fori_loop(4, 8, second_steps, 0)
    part_out[...] = features_of(sums, None, thigh_ref, tlow_ref).reshape(part_out.shape)
    copies = on_ty.start(9, lambda d: part_out.at[ty_at(d)], lambda d: part_in.at[d])
    ncopies = product_end(0, ncopies, value_ref)
    unit, rate = norm_rows(lat_ref[ty].astype(FLOAT))
    raw_mix = part_out[ty]
    finish(copies)
    for d in range(3):
        raw_mix = raw_mix + part_in[d]
    mix = (raw_mix * fgain).astype(BFLOAT)
    gmix[ty] = mix
    mcopies = to_ty(6, gmix.at[ty], gmix.at[ty])
    grad_q = (dot_nn(mix, kproj_ref[...]) * cross_scale).astype(BFLOAT)
    grad, qgain_grad = norm_rows_back(times_back(grad_q, 0), qgain_ref[...], unit, rate)
    features = feat_part + jnp.sum(raw_mix * raw_all[ty], axis=0, keepdims=True)
    for h in range(4):
        gains_out[1, h, 0:1] = qgain_grad[:, 256 * h : 256 * h + 256]
    gains_out[1, 0, 1:2] = features[:, 0:256]
    gains_out[1, 1, 1:2, 0:128] = features[:, 256:384]
    mcopies += over_ty(10, gains_out.at[1], gains_all.at[1])
    grad_ref[ty] = (g_one + grad).astype(BFLOAT)
    ncopies += to_ty(11, grad_ref.at[ty], grad_ref.at[ty])
    finish(mcopies)
    gain_rows = gains_all[1, 0] + gains_all[1, 1] + gains_all[1, 2] + gains_all[1, 3]
    right = qrows[:, pl.ds(pl.multiple_of(ty * 256, 256), 256)]
    mcopies = product_start(1, gmix[...].reshape(4 * share, LANES), right, gain_rows)
    stage_three(4)
    stage_three(5)
    mcopies = product_join(1, mcopies, key_ref)
    stage_three(6)
    ncopies += product_end(1, mcopies, key_ref)
    stage_three(7)
    finish(ncopies)
    for w in range(8):
        finish(out_copies(w))


def main_call(msg, lat, cot, gains, key_rows, value_rows, thigh, tlow, hot, matrices):
    _, share, width = lat.shape
    rows, length = 8 * share, msg.shape[1]
    dma = pltpu.SemaphoreType.DMA
    vmem = pl.BlockSpec(memory_space=pltpu.VMEM)
    hbm = pl.BlockSpec(memory_space=pl.ANY)
    shape = jax.ShapeDtypeStruct
    half, full = (lambda *s: pltpu.VMEM(s, BFLOAT)), (lambda *s: pltpu.VMEM(s, FLOAT))
    return pl.pallas_call(
        main_kernel,
        out_shape=(
            shape((4, share, width), BFLOAT),
            shape((4, share, width), BFLOAT),
            shape((4, 272, 256), BFLOAT),
            shape((4, 272, 256), BFLOAT),
            shape((8, 4, 128, 256), BFLOAT),
        ),
        in_specs=[vmem] * 13 + [hbm] * 10,
        out_specs=(vmem, vmem, vmem, vmem, hbm),
        scratch_shapes=[
            half(10, width, width), half(8, 16, length), half(8, rows, 2 * GROUP), half(8, rows, 2 * GROUP),
            half(2 * GROUP, length), full(rows, length), full(rows, length), half(rows, length),
            full(8, rows, GROUP), full(8, rows, 1), full(8, rows, 1), full(4, share, LANES), half(4 * share, width),
            full(4, share, LANES), full(3, share, LANES),
            half(8, share, 128), half(8, share, 128), half(8, 2 * share, 128), half(8, 2 * share, 128),
            half(8, 2 * share, 128), full(2, rows, rows), half(8, share, 128), half(8, share, 128),
            half(8, share, 128), half(8, share, 128), half(2, rows, 128), half(2, rows, 128),
            half(8, share, 128), half(8, 2 * share, 128),
            full(4, share, LANES), half(4, share, LANES), half(4, share, 256), half(4, share, 256),
            full(2, 4, 8, 256), full(2, 4, 8, 256), half(4, share, LANES),
            half(6, 2, 4, share, 128), half(6, 4, 4, share, 128), half(6, 4, 2, 4, share, 128),
            half(8, 4, share, 256), half(8, 2, 4, share, 256), full(8, 128, 256),
            half(8, 3, 128, 256), half(8, 3, 128, 256), half(8, 128, 256),
            half(2, 8, 32, 256), half(2, 16, 256), half(2, 7, 32, 256), half(2, 7, 16, 256),
            dma((10,)), dma((8,)), dma((12, 3)), dma((12, 3)), dma((13, 7)), dma((13, 7)),
            dma((2, 1)), dma((2, 1)), dma((20, 3)), dma((20, 3)), dma((14, 1)), dma((14, 1)),
            dma((8, 3)), dma((8, 3)), dma((8, 3)), dma((8, 3)),
        ],
        compiler_params=pltpu.CompilerParams(
            collective_id=1, has_side_effects=True, vmem_limit_bytes=60 << 20
        ),
        name="main",
    )(msg, lat, cot, *gains, key_rows, value_rows, thigh, tlow, hot, *matrices)


def finish_kernel(
    sums_ref, cross_core_ref, query_core_ref, latent_ref, result_in_ref, cross_ref, query_ref, value_ref, key_ref,
    *outs,
):
    tx = lax.axis_index("tx")
    result_ref, latent_out, feat_out, qgain_out, query_out, key_out, value_out, cross_out = outs[:8]
    for w, out in enumerate(outs[8:16]):
        for h in range(4):
            out[:, 256 * h : 256 * h + 256] = sums_ref[w, h].astype(FLOAT)
    result_ref[...] = result_in_ref[...]
    latent_out[...] = latent_ref[...].astype(FLOAT)
    here = pl.ds(pl.multiple_of(tx * 128, 128), 128)
    quarter = tx // 2
    inside = pl.ds(pl.multiple_of(lax.rem(tx, 2) * 128, 128), 128)
    scale = 1.0 / math.sqrt(query_ref.shape[0])
    cross_core = jnp.concatenate([cross_core_ref[h] for h in range(4)], axis=1)
    query_core = jnp.concatenate([query_core_ref[h] for h in range(4)], axis=1)
    value_out[...] = dot_nt(cross_core, cross_ref[...])[:FEAT]
    key_out[...] = (dot_nn(query_core, query_ref[...]) * scale)[:FEAT]
    row = lax.broadcasted_iota(jnp.int32, (272, 1024), 0)
    core = jnp.where(row < FEAT, cross_core.astype(FLOAT), 0.0).astype(BFLOAT)
    cross_out[...] = outer(value_ref[0:272, here], core)
    row = lax.broadcasted_iota(jnp.int32, (272, 128), 0)
    mine = query_core_ref[quarter, :, inside].astype(FLOAT)
    core = jnp.where(row < FEAT, mine, 0.0).astype(BFLOAT)
    query_out[...] = outer(core, key_ref[0:272]) * scale
    qgain_out[...] = mine[264:265]
    more = jnp.concatenate([query_core_ref[h, 256:272] for h in range(2)], axis=1).astype(FLOAT)
    feat_out[...] = more[9:10, 0:FEAT]
    mine = cross_core_ref[quarter, 256:272, inside].astype(FLOAT)
    for i, out in enumerate(outs[16:19]):
        out[...] = mine[8 + i : 9 + i]


def finish_call(sums, cross_core, query_core, latent_grad, result, cross_proj, query_proj, value_rows, key_rows):
    width = cross_proj.shape[0]
    shape = lambda *s: jax.ShapeDtypeStruct(s, FLOAT)
    rows = latent_grad.shape
    block = [shape(128, width)]
    vmem = pl.BlockSpec(memory_space=pltpu.VMEM)
    return pl.pallas_call(
        finish_kernel,
        out_shape=(
            [jax.ShapeDtypeStruct(rows, BFLOAT), shape(*rows), shape(1, FEAT), shape(1, 128)]
            + block + [shape(FEAT, width)] * 2 + block + block * 8 + [shape(1, 128)] * 3
        ),
        in_specs=[vmem] * 9,
        out_specs=[vmem] * 19,
        compiler_params=pltpu.CompilerParams(vmem_limit_bytes=48 << 20),
        name="finish",
    )(sums, cross_core, query_core, latent_grad, result, cross_proj, query_proj, value_rows, key_rows)


def pixel_tables(image_sizes, row_ids, tile_width):
    high = len(row_ids) // HALVES
    all_cols = jnp.arange(8 * tile_width, dtype=jnp.int32)
    row_table, row_coord, row_sum = axis_tables(image_sizes, row_ids, 3, 5)
    col_table, col_coord, col_sum = axis_tables(image_sizes, all_cols, 4, 5 + 2 * BANDS)
    row_table = row_table - row_sum[:, :, None] * (1.0 / FEAT)
    col_table = col_table - col_sum[:, :, None] * (1.0 / FEAT)
    row_table = row_table.reshape(2, HALVES, high, FEAT)
    col_table = col_table.reshape(2, 8, tile_width, FEAT)
    colours = np.zeros((2, HALVES, 16, FEAT), np.float32)
    for b in range(2):
        for half in range(HALVES):
            for c in range(3):
                colours[b, half, half * 8 + b * 4 + c] = -1.0 / FEAT
                colours[b, half, half * 8 + b * 4 + c, c] += 1.0
    first = jnp.concatenate(
        [jnp.asarray(colours), row_table, jnp.zeros((2, HALVES, GROUP - 16 - high, FEAT), FLOAT)], axis=2
    )
    col_from = 16 + -(-high // 8) * 8
    second = jnp.pad(col_table, ((0, 0), (0, 0), (col_from, GROUP - col_from - tile_width), (0, 0)))
    table = jnp.concatenate([first, second], axis=1).reshape(2, 10 * GROUP, FEAT)
    table = jnp.pad(table, ((0, 0), (0, 0), (0, LANES - FEAT)))
    hot = np.zeros((GROUP, -(-high * tile_width // 128) * 128), np.float32)
    for i in range(high):
        for j in range(tile_width):
            hot[16 + i, i * tile_width + j] = 1.0
            hot[col_from + j, i * tile_width + j] = 1.0
    here = lax.dynamic_slice_in_dim
    at = lax.axis_index("tx") * tile_width
    return (
        split_two(table), jnp.asarray(hot, BFLOAT),
        (row_coord, row_sum), (here(col_coord, at, tile_width, 1), here(col_sum, at, tile_width, 1)),
    )


def pixel_message(pixels, live, rows, cols, length):
    (row_coord, row_sum), (col_coord, col_sum) = rows, cols
    _, _, height, width = pixels.shape
    wide = pixels.astype(FLOAT)
    mean = (jnp.sum(wide, axis=1) + row_sum[:, :, None] + col_sum[:, None, :]) * (1.0 / FEAT)
    square = (
        jnp.sum(wide * wide, axis=1)
        + (row_coord * row_coord)[:, :, None]
        + (col_coord * col_coord)[:, None, :]
        + 2.0 * BANDS
    ) * (1.0 / FEAT)
    rate = jnp.where(live, lax.rsqrt(square - mean * mean + EPSILON), 0.0)
    rows = jnp.concatenate([pixels, rate.astype(BFLOAT)[:, None]], axis=1)
    rows = rows.reshape(2, 4, HALVES, height // HALVES * width)
    rows = jnp.transpose(rows, (2, 0, 1, 3)).reshape(16, -1)
    return jnp.pad(rows, ((0, 0), (0, length - rows.shape[1])))


def on_device_fast(
    pixels,
    pixel_mask,
    image_sizes,
    latents,
    cotangent,
    feature_gain,
    query_gain,
    query_proj,
    key_proj,
    value_proj,
    cross_proj,
    hidden_gain,
    hidden_up,
    hidden_down,
    tower_gain,
    tower_query,
    tower_key,
    tower_value,
    tower_proj,
    final_gain,
    final_up,
    final_down,
):
    item_count = pixels.shape[0]
    tile_height = pixels.shape[2]
    tile_width = pixels.shape[3]
    model_width = latents.shape[2]
    rows_here = latents.shape[1]
    cross_scale = 1.0 / math.sqrt(model_width)
    row_ids = lax.axis_index("ty") * tile_height + jnp.arange(tile_height, dtype=jnp.int32)
    col_ids = lax.axis_index("tx") * tile_width + jnp.arange(tile_width, dtype=jnp.int32)
    side_sizes = image_sizes[:, None, None]
    live = (
        (pixel_mask > 0)
        & (row_ids[None, :, None] < side_sizes)
        & (col_ids[None, None, :] < side_sizes)
    )
    (thigh, tlow), hot, rows, cols = pixel_tables(image_sizes, row_ids, tile_width)
    message = pixel_message(pixels, live, rows, cols, hot.shape[1])
    share = item_count * rows_here // 4

    def in_shares(rows):
        return rows.reshape(4, share, rows.shape[-1])

    gain_lanes = jnp.pad(feature_gain, (0, LANES - FEAT))[None]
    value_rows = jnp.pad(value_proj, ((0, LANES - FEAT), (0, 0)))
    key_rows = jnp.pad(key_proj, ((0, LANES - FEAT), (0, 0)))
    result, latent_grad, cross_core, query_core, sums = main_call(
        message, in_shares(latents), in_shares(cotangent),
        (gain_lanes, query_gain[None], hidden_gain[None], tower_gain[None], final_gain[None]),
        key_rows, value_rows, thigh, tlow, hot,
        (query_proj, cross_proj, hidden_up, hidden_down, tower_query, tower_key, tower_value,
         tower_proj, final_up, final_down),
    )
    (result, latent_grad, feature_sum, query_sum, query_grad, key_grad, value_grad, cross_grad,
     final_down_grad, final_up_grad, tower_proj_grad, tower_query_grad, tower_key_grad,
     tower_value_grad, hidden_down_grad, hidden_up_grad, hidden_sum, tower_sum, final_sum) = finish_call(
        sums, cross_core, query_core, latent_grad, result, cross_proj, query_proj, value_rows, key_rows
    )
    return (
        result.reshape(latents.shape),
        latent_grad.reshape(latents.shape),
        feature_sum[0],
        query_sum[0],
        query_grad,
        key_grad,
        value_grad,
        cross_grad,
        hidden_sum[0],
        hidden_up_grad,
        hidden_down_grad,
        tower_sum[0],
        tower_query_grad,
        tower_key_grad,
        tower_value_grad,
        tower_proj_grad,
        final_sum[0],
        final_up_grad,
        final_down_grad,
    )


def on_device(
    pixels,
    pixel_mask,
    image_sizes,
    latents,
    cotangent,
    feature_gain,
    query_gain,
    query_proj,
    key_proj,
    value_proj,
    cross_proj,
    hidden_gain,
    hidden_up,
    hidden_down,
    tower_gain,
    tower_query,
    tower_key,
    tower_value,
    tower_proj,
    final_gain,
    final_up,
    final_down,
):
    item_count = pixels.shape[0]
    tile_height = pixels.shape[2]
    tile_width = pixels.shape[3]
    model_width = latents.shape[2]
    rows_here = latents.shape[1]
    head_count = HEADS
    head_size = model_width // head_count
    cross_scale = 1.0 / math.sqrt(model_width)
    tower_scale = 1.0 / math.sqrt(head_size)
    row_ids = lax.axis_index("ty") * tile_height + jnp.arange(tile_height, dtype=jnp.int32)
    col_ids = lax.axis_index("tx") * tile_width + jnp.arange(tile_width, dtype=jnp.int32)
    all_cols = jnp.arange(tile_width * lax.axis_size("tx"), dtype=jnp.int32)
    wide_pixels = lax.all_gather(pixels, "tx", axis=3, tiled=True).astype(FLOAT)
    wide_mask = lax.all_gather(pixel_mask, "tx", axis=2, tiled=True)
    side_sizes = image_sizes[:, None, None]
    live = (
        (wide_mask > 0)
        & (row_ids[None, :, None] < side_sizes)
        & (all_cols[None, None, :] < side_sizes)
    )[:, None]
    row_table, row_coord, row_sum = axis_tables(image_sizes, row_ids, 3, 5)
    col_table, col_coord, col_sum = axis_tables(image_sizes, all_cols, 4, 5 + 2 * BANDS)
    pixel_mean = (
        jnp.sum(wide_pixels, axis=1) + row_sum[:, :, None] + col_sum[:, None, :]
    ) / FEAT
    pixel_square = (
        jnp.sum(wide_pixels * wide_pixels, axis=1)
        + (row_coord * row_coord)[:, :, None]
        + (col_coord * col_coord)[:, None, :]
        + 2.0 * BANDS
    ) / FEAT
    pixel_rate = lax.rsqrt(pixel_square - pixel_mean * pixel_mean + EPSILON)
    exact = lax.Precision.HIGHEST

    def against_pixels(coefs):
        by_row = jnp.einsum("blf,bif->bli", coefs, row_table, precision=exact)
        by_col = jnp.einsum("blf,bjf->blj", coefs, col_table, precision=exact)
        total = by_row[:, :, :, None] + by_col[:, :, None, :]
        for c in range(3):
            total = total + coefs[:, :, c][:, :, None, None] * wide_pixels[:, None, c]
        total = total - jnp.sum(coefs, axis=2)[:, :, None, None] * pixel_mean[:, None]
        return total * pixel_rate[:, None]

    def over_pixels(weights):
        scaled = weights * pixel_rate[:, None]
        by_row = jnp.sum(scaled, axis=3)
        by_col = jnp.sum(scaled, axis=2)
        total = jnp.einsum("bli,bif->blf", by_row, row_table, precision=exact)
        total = total + jnp.einsum("blj,bjf->blf", by_col, col_table, precision=exact)
        colour = jnp.stack(
            [jnp.sum(scaled * wide_pixels[:, None, c], axis=(2, 3)) for c in range(3)], axis=2
        )
        total = total + jnp.pad(colour, ((0, 0), (0, 0), (0, FEAT - 3)))
        return total - jnp.sum(scaled * pixel_mean[:, None], axis=(2, 3))[:, :, None]

    latent_rows = latents.astype(FLOAT)
    query_normed, back_query_norm = jax.vjp(layer_norm, latent_rows, query_gain)
    query_input = query_normed.astype(BFLOAT)
    own_queries = linear(query_input, query_proj).astype(BFLOAT)
    raw_query = linear_back(own_queries, key_proj) * cross_scale
    scores = against_pixels(raw_query * feature_gain)
    row_top = jnp.max(jnp.where(live, scores, -1e30), axis=(2, 3))
    all_top = lax.pmax(row_top, "ty")
    row_exp = jnp.where(live, jnp.exp(scores - all_top[:, :, None, None]), 0.0)
    row_total = lax.psum(jnp.sum(row_exp, axis=(2, 3)), "ty")
    cross_exact = row_exp / row_total[:, :, None, None]
    raw_mix = lax.psum(over_pixels(cross_exact), "ty")
    mix = raw_mix * feature_gain
    attended = linear(mix.astype(BFLOAT), value_proj)
    attended_input = attended.astype(BFLOAT)
    resid_one = latent_rows + linear(attended_input, cross_proj)
    hidden_normed, back_hidden_norm = jax.vjp(layer_norm, resid_one, hidden_gain)
    hidden_input = hidden_normed.astype(BFLOAT)
    hidden_lifted, back_hidden_gelu = jax.vjp(gelu_tanh, linear(hidden_input, hidden_up))
    hidden_act = hidden_lifted.astype(BFLOAT)
    resid_two = resid_one + linear(hidden_act, hidden_down)
    tower_normed, back_tower_norm = jax.vjp(layer_norm, resid_two, tower_gain)
    tower_input = tower_normed.astype(BFLOAT)
    tower_q = linear(tower_input, tower_query).astype(BFLOAT)
    tower_k = linear(tower_input, tower_key).astype(BFLOAT)
    tower_v = linear(tower_input, tower_value).astype(BFLOAT)
    all_keys, all_values = (
        lax.all_gather(tower_k, "tx", axis=1, tiled=True),
        lax.all_gather(tower_v, "tx", axis=1, tiled=True),
    )
    split_q = tower_q.reshape(item_count, rows_here, head_count, head_size)
    split_k = all_keys.reshape(item_count, -1, head_count, head_size)
    split_v = all_values.reshape(item_count, -1, head_count, head_size)
    tower_scores = (
        jnp.einsum("bqhd,bkhd->bhqk", split_q, split_k, preferred_element_type=FLOAT) * tower_scale
    )
    tower_top = jnp.max(tower_scores, axis=3, keepdims=True)
    tower_exp = jnp.exp(tower_scores - tower_top)
    tower_total = jnp.sum(tower_exp, axis=3, keepdims=True)
    tower_exact = tower_exp / tower_total
    tower_probs = tower_exact.astype(BFLOAT)
    mixed = jnp.einsum(
        "bhqk,bkhd->bqhd", tower_probs, split_v, preferred_element_type=FLOAT
    ).reshape(item_count, rows_here, model_width)
    mixed_input = mixed.astype(BFLOAT)
    resid_three = resid_two + linear(mixed_input, tower_proj)
    final_normed, back_final_norm = jax.vjp(layer_norm, resid_three, final_gain)
    final_input = final_normed.astype(BFLOAT)
    final_lifted, back_final_gelu = jax.vjp(gelu_tanh, linear(final_input, final_up))
    final_act = final_lifted.astype(BFLOAT)
    resid_four = resid_three + linear(final_act, final_down)
    grad_four = cotangent.astype(FLOAT)
    final_down_grad = weight_grad(final_act, cotangent)
    grad_final_lift = back_final_gelu(linear_back(cotangent, final_down))[0].astype(BFLOAT)
    final_up_grad = weight_grad(final_input, grad_final_lift)
    grad_rows_three, final_gain_grad = back_final_norm(linear_back(grad_final_lift, final_up))
    grad_three = grad_four + grad_rows_three
    grad_tower_out = grad_three.astype(BFLOAT)
    tower_proj_grad = weight_grad(mixed_input, grad_tower_out)
    grad_mixed_flat = linear_back(grad_tower_out, tower_proj).astype(BFLOAT)
    grad_mixed = grad_mixed_flat.reshape(item_count, rows_here, head_count, head_size)
    grad_tower_p = jnp.einsum("bqhd,bkhd->bhqk", grad_mixed, split_v, preferred_element_type=FLOAT)
    tower_delta = jnp.sum(tower_exact * grad_tower_p, axis=3, keepdims=True)
    grad_tower_scores = (tower_exact * (grad_tower_p - tower_delta)).astype(BFLOAT)
    grad_tower_q = (
        (
            jnp.einsum("bhqk,bkhd->bqhd", grad_tower_scores, split_k, preferred_element_type=FLOAT)
            * tower_scale
        )
        .astype(BFLOAT)
        .reshape(item_count, rows_here, model_width)
    )
    value_part = jnp.einsum(
        "bhqk,bqhd->bkhd", tower_probs, grad_mixed, preferred_element_type=FLOAT
    )
    key_part = (
        jnp.einsum("bhqk,bqhd->bkhd", grad_tower_scores, split_q, preferred_element_type=FLOAT)
        * tower_scale
    )
    key_sums, value_sums = (
        lax.psum_scatter(
            key_part.reshape(item_count, -1, model_width), "tx", scatter_dimension=1, tiled=True
        ),
        lax.psum_scatter(
            value_part.reshape(item_count, -1, model_width), "tx", scatter_dimension=1, tiled=True
        ),
    )
    grad_tower_k = key_sums.astype(BFLOAT)
    grad_tower_v = value_sums.astype(BFLOAT)
    tower_query_grad = weight_grad(tower_input, grad_tower_q)
    tower_key_grad = weight_grad(tower_input, grad_tower_k)
    tower_value_grad = weight_grad(tower_input, grad_tower_v)
    grad_tower_rows = (
        linear_back(grad_tower_q, tower_query)
        + linear_back(grad_tower_k, tower_key)
        + linear_back(grad_tower_v, tower_value)
    )
    grad_rows_two, tower_gain_grad = back_tower_norm(grad_tower_rows)
    grad_two = grad_three + grad_rows_two
    grad_hidden_out = grad_two.astype(BFLOAT)
    hidden_down_grad = weight_grad(hidden_act, grad_hidden_out)
    grad_hidden_lift = back_hidden_gelu(linear_back(grad_hidden_out, hidden_down))[0].astype(BFLOAT)
    hidden_up_grad = weight_grad(hidden_input, grad_hidden_lift)
    grad_rows_one, hidden_gain_grad = back_hidden_norm(linear_back(grad_hidden_lift, hidden_up))
    grad_one = grad_two + grad_rows_one
    grad_cross_out = grad_one.astype(BFLOAT)
    cross_proj_grad = weight_grad(attended_input, grad_cross_out)
    grad_attended = linear_back(grad_cross_out, cross_proj).astype(BFLOAT)
    raw_up = linear_back(grad_attended, value_proj)
    grad_probs = against_pixels(raw_up * feature_gain)
    cross_delta = jnp.sum(grad_attended.astype(FLOAT) * attended, axis=2)
    grad_scores = cross_exact * (grad_probs - cross_delta[:, :, None, None])
    raw_grad_mix = lax.psum(over_pixels(grad_scores), "ty")
    grad_mix = (raw_grad_mix * feature_gain).astype(BFLOAT)
    grad_queries = (linear(grad_mix, key_proj) * cross_scale).astype(BFLOAT)
    key_proj_grad = weight_grad(grad_mix, own_queries) * cross_scale
    value_proj_grad = weight_grad(mix.astype(BFLOAT), grad_attended)
    feature_part = jnp.sum(raw_grad_mix * raw_query + raw_mix * raw_up, axis=(0, 1))
    pixel_sums = lax.psum((key_proj_grad, value_proj_grad, feature_part), "tx")
    query_proj_grad = weight_grad(query_input, grad_queries)
    grad_latent_rows, query_gain_grad = back_query_norm(linear_back(grad_queries, query_proj))
    latent_grad = grad_one + grad_latent_rows
    summed = (
        lax.psum_scatter(query_gain_grad, "tx", scatter_dimension=0, tiled=True),
        lax.psum_scatter(query_proj_grad, "tx", scatter_dimension=0, tiled=True),
        lax.psum_scatter(cross_proj_grad, "tx", scatter_dimension=0, tiled=True),
        lax.psum_scatter(hidden_gain_grad, "tx", scatter_dimension=0, tiled=True),
        lax.psum_scatter(hidden_up_grad, "tx", scatter_dimension=0, tiled=True),
        lax.psum_scatter(hidden_down_grad, "tx", scatter_dimension=0, tiled=True),
        lax.psum_scatter(tower_gain_grad, "tx", scatter_dimension=0, tiled=True),
        lax.psum_scatter(tower_query_grad, "tx", scatter_dimension=0, tiled=True),
        lax.psum_scatter(tower_key_grad, "tx", scatter_dimension=0, tiled=True),
        lax.psum_scatter(tower_value_grad, "tx", scatter_dimension=0, tiled=True),
        lax.psum_scatter(tower_proj_grad, "tx", scatter_dimension=0, tiled=True),
        lax.psum_scatter(final_gain_grad, "tx", scatter_dimension=0, tiled=True),
        lax.psum_scatter(final_up_grad, "tx", scatter_dimension=0, tiled=True),
        lax.psum_scatter(final_down_grad, "tx", scatter_dimension=0, tiled=True),
    )
    return (
        resid_four.astype(BFLOAT),
        latent_grad,
        pixel_sums[2],
        summed[0],
        summed[1],
        pixel_sums[0],
        pixel_sums[1],
        summed[2],
        summed[3],
        summed[4],
        summed[5],
        summed[6],
        summed[7],
        summed[8],
        summed[9],
        summed[10],
        summed[11],
        summed[12],
        summed[13],
    )


def solution(mesh):
    in_specs = (
        P(None, None, "ty", "tx"),
        P(None, "ty", "tx"),
        P(),
        P(None, "tx", None),
        P(None, "tx", None),
        P(),
        P(),
        P(),
        P(),
        P(),
        P(),
        P(),
        P(),
        P(),
        P(),
        P(),
        P(),
        P(),
        P(),
        P(),
        P(),
        P(),
    )
    out_specs = (
        P(None, "tx", None),
        P(None, "tx", None),
        P(),
        P("tx"),
        P("tx", None),
        P(),
        P(),
        P("tx", None),
        P("tx"),
        P("tx", None),
        P("tx", None),
        P("tx"),
        P("tx", None),
        P("tx", None),
        P("tx", None),
        P("tx", None),
        P("tx"),
        P("tx", None),
        P("tx", None),
    )
    fits = mesh.shape["ty"] == 4 and mesh.shape["tx"] == HEADS
    plan = on_device_fast if fits else on_device
    return jax.shard_map(
        plan, mesh=mesh, in_specs=in_specs, out_specs=out_specs, check_vma=False
    )
```

```python
import math

import jax
import jax.numpy as jnp
import numpy as np
from jax import lax
from jax.experimental import pallas as pl
from jax.experimental.pallas import tpu as pltpu
from jax.sharding import PartitionSpec as P

BANDS = 64
FEAT = 261
HEADS = 8


EPSILON = 1e-05
FLOAT = jnp.float32
BFLOAT = jnp.bfloat16


def layer_norm(values, scales):
    centre = jnp.mean(values, axis=-1, keepdims=True)
    shifted = values - centre
    spread = jnp.mean(shifted * shifted, axis=-1, keepdims=True)
    return shifted * lax.rsqrt(spread + EPSILON) * scales


def gelu_tanh(values):
    cubic = values + 0.044715 * values * values * values
    return 0.5 * values * (1.0 + jnp.tanh(0.7978845608028654 * cubic))


def linear(inputs, weight):
    return lax.dot_general(
        inputs, weight, (((inputs.ndim - 1,), (0,)), ((), ())), preferred_element_type=FLOAT
    )


def linear_back(upstream, weight):
    return lax.dot_general(
        upstream, weight, (((upstream.ndim - 1,), (1,)), ((), ())), preferred_element_type=FLOAT
    )


def weight_grad(inputs, upstream):
    flat_inputs = inputs.reshape(-1, inputs.shape[-1])
    flat_upstream = upstream.reshape(-1, upstream.shape[-1])
    return lax.dot_general(
        flat_inputs, flat_upstream, (((0,), (0,)), ((), ())), preferred_element_type=FLOAT
    )


def axis_tables(image_sizes, ids, coord_lane, first_lane):
    side = image_sizes.astype(FLOAT)[:, None]
    coord = -1.0 + 2.0 * ids.astype(FLOAT)[None, :] / (side - 1.0)
    band = jnp.arange(BANDS, dtype=jnp.int32).astype(FLOAT)
    frequency = 1.0 + band[None, :] * (side * 0.5 - 1.0) / (BANDS - 1)
    angle = math.pi * coord[:, :, None] * frequency[:, None, :]
    waves = jnp.concatenate([jnp.sin(angle), jnp.cos(angle)], axis=2)
    count, length = coord.shape
    lead = jnp.zeros((count, length, coord_lane), FLOAT)
    gap = jnp.zeros((count, length, first_lane - coord_lane - 1), FLOAT)
    tail = jnp.zeros((count, length, FEAT - first_lane - 2 * BANDS), FLOAT)
    table = jnp.concatenate([lead, coord[:, :, None], gap, waves, tail], axis=2)
    return table, coord, jnp.sum(waves, axis=2) + coord


MESH = pl.DeviceIdType.MESH


def send(src, dst, send_sem, recv_sem, where):
    copy = pltpu.make_async_remote_copy(
        src_ref=src, dst_ref=dst, send_sem=send_sem, recv_sem=recv_sem,
        device_id=where, device_id_type=MESH,
    )
    copy.start()
    return copy


def greet(places):
    barrier = pltpu.get_barrier_semaphore()
    for place in places:
        pl.semaphore_signal(barrier, inc=1, device_id=place, device_id_type=MESH)
    pl.semaphore_wait(barrier, len(places))


def outer(left, right):
    return lax.dot_general(left, right, (((0,), (0,)), ((), ())), preferred_element_type=FLOAT)


LANES = 384
CUBE = 0.044715
SLOPE = 0.7978845608028654


def norm_rows(rows):
    shifted = rows - jnp.mean(rows, axis=-1, keepdims=True)
    rate = lax.rsqrt(jnp.mean(shifted * shifted, axis=-1, keepdims=True) + EPSILON)
    return shifted * rate, rate


def norm_rows_back(upstream, gain, unit, rate):
    scaled = upstream * gain
    along = jnp.mean(scaled * unit, axis=-1, keepdims=True)
    grad = rate * (scaled - jnp.mean(scaled, axis=-1, keepdims=True) - unit * along)
    return grad, jnp.sum(upstream * unit, axis=0, keepdims=True)


def gelu_pair(values):
    square = values * values
    bend = jnp.tanh(SLOPE * (values + CUBE * values * square))
    half = 0.5 * (1.0 + bend)
    slope = half + 0.5 * values * (1.0 - bend * bend) * (SLOPE * (1.0 + 3.0 * CUBE * square))
    return values * half, slope


def dot_nt(left, right):
    return lax.dot_general(left, right, (((1,), (1,)), ((), ())), preferred_element_type=FLOAT)


def dot_nn(left, right):
    return lax.dot_general(left, right, (((1,), (0,)), ((), ())), preferred_element_type=FLOAT)


HALVES = 2
GROUP = 128
LOG2E = 1.0 / math.log(2.0)


def split_two(values):
    high = values.astype(BFLOAT)
    return high, (values - high.astype(FLOAT)).astype(BFLOAT)


def dot_wide(dot, values, high, low):
    first, second = split_two(values)
    return dot(first, high) + (dot(first, low) + dot(second, high))


def coefs_by_pixel(coefs, thigh_ref, tlow_ref, into):
    count = coefs.shape[0] // 2
    for b in range(2):
        wide = dot_wide(dot_nt, coefs[b * count : (b + 1) * count], thigh_ref[b], tlow_ref[b])
        for half in range(HALVES):
            at = pl.ds((half * 2 + b) * count, count)
            rows = wide[:, half * GROUP : (half + 1) * GROUP]
            for t in range(8):
                high, low = split_two(rows + wide[:, (2 + t) * GROUP : (3 + t) * GROUP])
                into[t, at, 0:GROUP] = high
                into[t, at, GROUP : 2 * GROUP] = low


def features_of(sums, scales, thigh_ref, tlow_ref):
    count = sums.shape[1] // 4
    blocks = [sums[t] if scales is None else sums[t] * scales[t] for t in range(8)]
    joined = blocks[0]
    for block in blocks[1:]:
        joined = joined + block
    outs = []
    for b in range(2):
        first, second = pl.ds(b * count, count), (2 + b) * count
        lo, hi = slice(b * count, (b + 1) * count), slice((2 + b) * count, (3 + b) * count)
        wide = jnp.concatenate(
            [joined[lo], joined[hi]] + [block[lo] + block[hi] for block in blocks], axis=1
        )
        outs.append(dot_wide(dot_nn, wide, thigh_ref[b], tlow_ref[b]))
    return jnp.concatenate(outs, axis=0)


def rate_and_bias(block, group):
    rate = block[group % 2 * 4 + group // 2 * 8 + 3 :][:1].astype(FLOAT)
    return rate, jnp.where(rate == 0.0, -1e30, 0.0)


class Ring:
    def __init__(self, places, send_sems, recv_sems):
        self.places, self.sems = places, (send_sems, recv_sems)

    def copy(self, i, d, src, dst):
        return pltpu.make_async_remote_copy(
            src_ref=src, dst_ref=dst, send_sem=self.sems[0].at[i, d], recv_sem=self.sems[1].at[i, d],
            device_id=self.places[d], device_id_type=MESH,
        )

    def start(self, i, sources, into):
        copies = [self.copy(i, d, sources(d), into(d)) for d in range(len(self.places))]
        for copy in copies:
            copy.start()
        return copies


def finish(*groups):
    for copies in groups:
        for copy in copies:
            copy.wait()


def sin_half_turns(turns):
    whole = jnp.floor(turns + 0.5)
    part = turns - whole
    odd = whole - 2.0 * jnp.floor(whole * 0.5)
    square = part * part
    total = jnp.full_like(square, SINE[-1])
    for term in SINE[-2::-1]:
        total = total * square + term
    return part * total * (1.0 - 2.0 * odd)


def axis_rows(axis, side, first, lanes):
    place = (lax.broadcasted_iota(jnp.int32, (48, 1), 0) + first).astype(FLOAT)
    coord = -1.0 + 2.0 * place / (side - 1.0)
    here = lanes[:, 128 * axis : 128 * axis + 256]
    rate = 1.0 + here[0:1] * (side * 0.5 - 1.0) * (1.0 / (BANDS - 1))
    waves = sin_half_turns(coord * rate + here[1:2]) * here[2 + axis : 3 + axis]
    empty = jnp.zeros((48, LANES - 256), FLOAT)
    table = jnp.concatenate([empty, waves] if axis else [waves, empty], axis=1)
    total = jnp.sum(waves, axis=1, keepdims=True) + coord
    table = table + coord * lanes[4 + axis : 5 + axis] - (total * (1.0 / FEAT)) * lanes[6:7]
    return table, coord, total


def main_kernel(
    sizes_ref, *refs
):
    names = IN_NAMES + OUT_NAMES + SCRATCH_NAMES
    r = dict(zip(names, refs))
    matrices = [r["w%d" % i] for i in range(10)]
    result_ref, grad_ref, value_ref, key_ref, sums_ref = [r[n] for n in OUT_NAMES]
    (ws, msgs, pixcoefs, upcoefs, pixels, scores, ups, weights, sums, tops, totals, raw_all, qrows,
     part_out, part_in, q_out, q_in, kv_out, kv_in, kv_more, probs, mixed_out, mixed_in, gm_out, gm_in,
     kvx_out, kvx_in, gq_in, gkv_in, up_ref, mix_all, gcross_out, gcross_all, gains_out, gains_all, gmix,
     x_out, x_pass, x_all, g_out, g_all, own, held, relay_in, zsend, zrecv, last, nsend, nextra, nrecv, nmore,
     msg_rows, msg_ref, thigh_ref, tlow_ref, kproj_ref, vproj_ref, fgain_ref, result_v, grad_v, value_v, key_v,
     w_sem, l_sem, ty_s, ty_r, tx_s, tx_r, mate_s, mate_r, xg_s, xg_r, y_s, y_r, z_s, z_r, ac_s, ac_r, re_s, re_r,
     in_sem, out_sem,
     pix_v, mask_v, lat_ref, cot_ref, fgain_v, qgain_ref, hgain_ref, tgain_ref, ogain_ref,
     kraw_v, vraw_v, hot_ref, hotcol_ref, ids_ref, lanes_ref) = [r[n] for n in SCRATCH_NAMES]
    ty, tx = lax.axis_index("ty"), lax.axis_index("tx")
    z, y = tx // 2, lax.rem(tx, 2)
    tys = [{"ty": lax.rem(ty + d, 4), "tx": tx} for d in (1, 2, 3)]
    txs = [{"ty": ty, "tx": lax.rem(tx + d, 8)} for d in range(1, 8)]
    mate = {"ty": 2 * (ty // 2) + 1 - lax.rem(ty, 2), "tx": tx}
    beside = {"ty": ty, "tx": 2 * z + 1 - y}
    on_ty, on_tx = Ring(tys, ty_s, ty_r), Ring(txs, tx_s, tx_r)
    on_mate, across = Ring([mate], mate_s, mate_r), Ring([tys[1]], ac_s, ac_r)
    handing, passing = Ring(tys, xg_s, xg_r), Ring([beside], y_s, y_r)
    loads = []
    small = []
    for i, (name, into) in enumerate(zip(IN_NAMES, COPIED_NAMES)):
        small.append(pltpu.make_async_copy(r[name], r[into], in_sem.at[i]))
        small[i].start()
    for i, w in enumerate(matrices):
        loads.append(pltpu.make_async_copy(w, ws.at[i], w_sem.at[i]))
        loads[i].start()
    cross, up, down, tq, tk, tv, tproj, fup, fdown = range(1, 10)
    partners = tys + txs
    barrier = pltpu.get_barrier_semaphore()
    for place in partners:
        pl.semaphore_signal(barrier, inc=1, device_id=place, device_id_type=MESH)
    ty_at = lambda d: lax.rem(ty + d + 1, 4)
    tx_at = lambda d: lax.rem(tx + d + 1, 8)

    def times(rows, i):
        return dot_nn(rows, ws[i])

    def times_back(rows, i):
        return dot_nt(rows, ws[i])

    def to_ty(i, src, into):
        return on_ty.start(i, lambda d: src, lambda d: into)

    def spread(i, out, into):
        copies = on_tx.start(i, lambda d: out.at[tx_at(d)], lambda d: into.at[tx])
        into[tx] = out[tx]
        return copies

    def over_ty(i, out, into):
        copies = on_ty.start(i, lambda d: out.at[ty_at(d)], lambda d: into.at[ty])
        into[ty] = out[ty]
        return copies

    xg = {}

    def give_x(i, rows):
        for c in range(8):
            x_out[i, c % 2, c // 2] = rows[:, 128 * c : 128 * c + 128]
        x_all[i, :, 0, ty] = x_out[i, y]
        x_pass[i, :, ty] = x_out[i, 1 - y]
        xg["x", i] = handing.start(
            i, lambda d: x_out.at[i, y], lambda d: x_all.at[i, :, 0, ty]
        ) + handing.start(14 + i, lambda d: x_out.at[i, 1 - y], lambda d: x_pass.at[i, :, ty])

    def give_g(w, rows):
        for h in range(4):
            g_out[w, h] = rows[:, 256 * h : 256 * h + 256]
        g_all[w, 0, ty] = g_out[w, ty]
        xg["g", w] = handing.start(6 + w, lambda d: g_out.at[w, ty_at(d)], lambda d: g_all.at[w, 0, ty])

    def pass_x(i):
        finish(xg.pop(("x", i)))
        xg["px", i] = passing.start(i, lambda d: x_pass.at[i], lambda d: x_all.at[i, :, 1])

    def pass_g(w):
        finish(xg.pop(("g", w)))
        xg["pg", w] = passing.start(6 + w, lambda d: g_all.at[w, 0], lambda d: g_all.at[w, 1])

    def slot_x(w):
        return min(w, 3) + max(w - 5, 0) if isinstance(w, int) else jnp.minimum(w, 3) + jnp.maximum(w - 5, 0)

    def zcopy(w, c):
        return pltpu.make_async_remote_copy(
            src_ref=zsend.at[w, c], dst_ref=zrecv.at[w, c], send_sem=z_s.at[w, c],
            recv_sem=z_r.at[w, c], device_id={"ty": ty, "tx": 2 * lax.rem(z + c + 1, 4) + y},
            device_id_type=MESH,
        )

    at_end = (z == 0) | (z == 3)

    def relay(w):
        return pltpu.make_async_remote_copy(
            src_ref=zsend.at[w, 1], dst_ref=relay_in.at[w], send_sem=re_s.at[w], recv_sem=re_r.at[w],
            device_id={"ty": ty, "tx": 2 * (1 + z // 2) + y}, device_id_type=MESH,
        )

    def stage_one(w):
        i = slot_x(w)
        if isinstance(w, int):
            finish(xg.pop(("px", i), ()), xg.pop(("pg", w)))
        else:
            finish([passing.copy(6 + w, 0, g_all.at[w, 0], g_all.at[w, 1])])
        right = g_all[w].reshape(256, 256)

        def part(c):
            return outer(x_all[i, lax.rem(z + c + 1, 4)].reshape(256, 128), right)

        zsend[w, 1] = part(1).astype(BFLOAT)

        @pl.when(at_end)
        def _():
            relay(w).start()

        @pl.when(jnp.logical_not(at_end))
        def _():
            zcopy(w, 1).start()

        for c, middle in ((0, 1), (2, 2)):
            total = part(c)

            @pl.when(z == middle)
            def _():
                held[w] = total

            @pl.when(z != middle)
            def _():
                zsend[w, c] = total.astype(BFLOAT)
                zcopy(w, c).start()

        own[w] = part(3)

    def stage_two(w):
        for c, middle in ((0, 1), (2, 2)):
            @pl.when(z == middle)
            def _():
                relay(w).wait_recv()
                zsend[w, c] = (held[w] + relay_in[w].astype(FLOAT)).astype(BFLOAT)
                zcopy(w, c).start()

    def out_copies(w):
        return [
            on_mate.copy(2 + w, 0, last.at[w], sums_ref.at[w, ty]),
            across.copy(w, 0, last.at[w], sums_ref.at[w, ty]),
            pltpu.make_async_copy(last.at[w], sums_ref.at[w, ty], l_sem.at[w]),
        ]

    def stage_three(w):
        total = own[w]
        for c in (0, 2):
            zcopy(w, c).wait()
            total = total + zrecv[w, c].astype(FLOAT)
        own[w] = total

        @pl.when(at_end)
        def _():
            relay(w).wait_send()
            zcopy(w, 1).wait_recv()
            own[w] = own[w] + zrecv[w, 1].astype(FLOAT)

        @pl.when(jnp.logical_not(at_end))
        def _():
            zcopy(w, 1).wait_send()

        last[w] = own[w].astype(BFLOAT)
        for copy in out_copies(w):
            copy.start()

    def stage_four(w):
        across.copy(w, 0, last.at[w], sums_ref.at[w, ty]).wait()
        there = sums_ref.at[w, lax.rem(ty + 2, 4)]
        on_mate.copy(10 + w, 0, there, there).start()

    def stage_end(w):
        there = sums_ref.at[w, lax.rem(ty + 2, 4)]
        on_mate.copy(10 + w, 0, there, there).wait()
        mine = out_copies(w)
        finish(mine[:1], mine[2:])

    def product_start(i, left, right, gains):
        product = outer(left, right)
        nsend[i] = product[0:256].astype(BFLOAT).reshape(8, 32, 256)
        row = lax.broadcasted_iota(jnp.int32, (16, 256), 0)
        more = product[256:272] + jnp.where(row < 8, 0.0, jnp.concatenate([gains, gains], axis=0))
        nextra[i] = more.astype(BFLOAT)
        return on_tx.start(
            6 + 3 * i, lambda d: nsend.at[i, tx_at(d)], lambda d: nrecv.at[i, d]
        ) + on_tx.start(7 + 3 * i, lambda d: nextra.at[i], lambda d: nmore.at[i, d])

    def product_join(i, copies, into):
        finish(copies)
        main = nsend[i, tx].astype(FLOAT)
        more = nextra[i].astype(FLOAT)
        for d in range(7):
            main = main + nrecv[i, d].astype(FLOAT)
            more = more + nmore[i, d].astype(FLOAT)
        mine = pl.ds(pl.multiple_of(tx * 32, 32), 32)
        into[ty, mine] = main.astype(BFLOAT)
        into[ty, 256:272] = more.astype(BFLOAT)
        return on_tx.start(8 + 3 * i, lambda d: into.at[ty, mine], lambda d: into.at[ty, mine])

    def hand_out(k, source, out):
        mine = pltpu.make_async_copy(source, out.at[ty], out_sem.at[k])
        mine.start()
        return on_mate.start(18 + k, lambda d: source, lambda d: out.at[ty]) + [mine], across.start(
            8 + k, lambda d: source, lambda d: out.at[ty]
        )

    def hand_on(k, copies, out):
        near, far = copies
        finish(far)
        there = out.at[lax.rem(ty + 2, 4)]
        return near + on_mate.start(22 + k, lambda d: there, lambda d: there)

    def product_end(i, copies, into, out):
        finish(copies)
        return hand_out(i, into.at[ty], out)

    def message(d):
        return on_tx.copy(0, d, msg_ref, msgs.at[tx])

    share, width = lat_ref.shape[1], lat_ref.shape[2]
    count = 2 * share
    high, wide = pix_v.shape[2] // HALVES, pix_v.shape[3]
    for copy in small:
        copy.wait()
    lanes = lanes_ref[...]
    ids = ids_ref[...]
    sides = [jnp.zeros((1, 1), FLOAT) + sizes_ref[b].astype(FLOAT) for b in range(2)]
    live_planes = jnp.where(mask_v[...] > 0, 1.0, 0.0).reshape(4 * high, wide)
    planes = jnp.concatenate(
        [pix_v[...].astype(FLOAT).reshape(12 * high, wide), live_planes], axis=0
    ).astype(BFLOAT)
    flat = dot_nn(planes, hotcol_ref[...])
    row_of = lax.broadcasted_iota(jnp.int32, (2 * high, 1), 0).astype(FLOAT)
    picks = [ids[0:1] + half * high == row_of for half in range(HALVES)]

    def flatten(plane, half):
        rows = flat[plane * 2 * high : (plane + 1) * 2 * high]
        return jnp.sum(jnp.where(picks[half], rows, 0.0), axis=0, keepdims=True)

    def put_table(b, at, rows):
        high_part, low_part = split_two(rows)
        thigh_ref[b, at : at + rows.shape[0]] = high_part
        tlow_ref[b, at : at + rows.shape[0]] = low_part

    def by_pixel(total, coord, rows):
        square = coord * coord
        total_high, total_low = split_two(total)
        square_high, square_low = split_two(square)
        left = jnp.concatenate([total_high, total_low, square_high, square_low], axis=1)
        spread_out = outer(left, rows)
        return spread_out[0:1] + spread_out[1:2], spread_out[2:3] + spread_out[3:4]

    zeros = jnp.zeros((GROUP, LANES), BFLOAT)
    lane_at = lax.broadcasted_iota(jnp.int32, (16, LANES), 1)
    row_at = lax.broadcasted_iota(jnp.int32, (16, LANES), 0)
    for b in range(2):
        _, col_coord, col_total = axis_rows(1, sides[b], tx * wide, lanes)
        col_sum, col_square = by_pixel(col_total, col_coord, hot_ref[64:112])
        for half in range(HALVES):
            first = ty * (2 * high) + half * high
            table, coord, total = axis_rows(0, sides[b], first, lanes)
            row_sum, row_square = by_pixel(total, coord, hot_ref[16:64])
            put_table(b, half * GROUP + 16, table)
            thigh_ref[b, half * GROUP + 64 : half * GROUP + GROUP] = zeros[64:]
            tlow_ref[b, half * GROUP + 64 : half * GROUP + GROUP] = zeros[64:]
            channel = row_at - (half * 8 + b * 4)
            colour = (channel >= 0) & (channel < 3)
            value = jnp.where(channel == lane_at, 1.0, 0.0) - (1.0 / FEAT) * lanes[6:7]
            put_table(b, half * GROUP, jnp.where(colour, value, 0.0))
            colours = [flatten(b * 3 + c, half) for c in range(3)]
            mean = (colours[0] + colours[1] + colours[2] + row_sum + col_sum) * (1.0 / FEAT)
            square = sum(c * c for c in colours) + row_square + col_square + 2.0 * BANDS
            rate = lax.rsqrt(square * (1.0 / FEAT) - mean * mean + EPSILON)
            side = sides[b]
            first_row = jnp.zeros((1, 1), FLOAT) + first.astype(FLOAT)
            first_col = jnp.zeros((1, 1), FLOAT) + (tx * wide).astype(FLOAT)
            live = (
                (flatten(6 + b, half) > 0.5)
                & (ids[0:1] + first_row < side)
                & (ids[1:2] + first_col < side)
            )
            for c, row in enumerate(colours + [jnp.where(live, rate, 0.0)]):
                at = half * 8 + b * 4 + c
                msg_rows[at : at + 1] = row
    msg_ref[...] = msg_rows[...].astype(BFLOAT)
    pl.semaphore_wait(barrier, len(partners))
    for d in range(7):
        message(d).start()
    msgs[tx] = msg_ref[...]
    for b in range(2):
        for t in range(8):
            table, _, _ = axis_rows(1, sides[b], t * wide, lanes)
            at = (2 + t) * GROUP
            thigh_ref[b, at : at + 64] = zeros[:64]
            tlow_ref[b, at : at + 64] = zeros[:64]
            put_table(b, at + 64, table)
            thigh_ref[b, at + 112 : at + GROUP] = zeros[:16]
            tlow_ref[b, at + 112 : at + GROUP] = zeros[:16]
    for raw_ref, padded in ((kraw_v, kproj_ref), (vraw_v, vproj_ref)):
        padded[0:256] = raw_ref[0:256]
        padded[256:272] = jnp.concatenate(
            [raw_ref[256:FEAT].astype(FLOAT), jnp.zeros((272 - FEAT, width), FLOAT)], axis=0
        ).astype(BFLOAT)
        padded[272:LANES] = jnp.zeros((LANES - 272, width), BFLOAT)
    fgain_ref[...] = jnp.zeros_like(fgain_ref)
    fgain_ref[:, 0:FEAT] = fgain_v[...]
    pixels[0:GROUP] = hot_ref[...]
    pixels[GROUP : 2 * GROUP] = hot_ref[...]
    gains_out[...] = jnp.zeros_like(gains_out)
    cot = cot_ref[ty]
    give_g(0, cot)
    fgain = fgain_ref[...]
    unit, _ = norm_rows(lat_ref[...].reshape(4 * share, width).astype(FLOAT))
    rows = (unit * qgain_ref[...]).astype(BFLOAT)
    qrows[...] = rows
    finish(loads[:1])
    queries = times(rows, 0).astype(BFLOAT)
    cross_scale = 1.0 / math.sqrt(width)
    raw = dot_nt(queries, kproj_ref[...]) * cross_scale
    raw_all[...] = raw.reshape(raw_all.shape)
    coefs_by_pixel(raw * (fgain * LOG2E), thigh_ref, tlow_ref, pixcoefs)

    def take_block(t):
        block = msgs[t]
        pixels[0:16] = block
        pixels[GROUP : GROUP + 16] = block
        scores[...] = dot_nn(pixcoefs[t], pixels[...])
        return block

    def front_step(d, _):
        @pl.when(d > 0)
        def _():
            pltpu.make_async_remote_copy(
                src_ref=msg_ref, dst_ref=msgs.at[tx], send_sem=tx_s.at[0, d - 1],
                recv_sem=tx_r.at[0, d - 1], device_id=beside, device_id_type=MESH,
            ).wait()

        t = lax.rem(tx + 8 - d, 8)
        block = take_block(t)
        for group in range(4):
            at = pl.ds(group * count, count)
            rate, bias = rate_and_bias(block, group)
            s = scores[at] * rate + bias
            top = jnp.max(s, axis=1, keepdims=True)
            e = jnp.exp2(s - top)
            tops[t, at] = top
            totals[t, at] = jnp.sum(e, axis=1, keepdims=True)
            weights[at] = (e * rate).astype(BFLOAT)
        sums[t] = dot_nt(weights[...], pixels[0:GROUP])
        return 0

    lax.fori_loop(0, 8, front_step, 0)
    top = tops[0]
    for t in range(1, 8):
        top = jnp.maximum(top, tops[t])
    top = jnp.maximum(top[: 2 * count], top[2 * count :])
    both = jnp.concatenate([top, top], axis=0)
    scales = [jnp.exp2(tops[t] - both) for t in range(8)]
    total = sum(totals[t] * scales[t] for t in range(8))
    total = total[: 2 * count] + total[2 * count :]
    feats = features_of(sums, scales, thigh_ref, tlow_ref)
    lane = lax.broadcasted_iota(jnp.int32, feats.shape, 1)
    part_out[...] = jnp.where(
        lane < FEAT, feats, jnp.where(lane == FEAT, total, top)
    ).reshape(part_out.shape)

    copies = on_ty.start(0, lambda d: part_out.at[ty_at(d)], lambda d: part_in.at[d])
    latent = lat_ref[ty].astype(FLOAT)
    parts = [part_out[ty]]
    finish(copies)
    parts += [part_in[d] for d in range(3)]
    tops_in = [p[:, FEAT + 1 : FEAT + 2] for p in parts]
    top = jnp.maximum(
        jnp.maximum(tops_in[0], tops_in[1]), jnp.maximum(tops_in[2], tops_in[3])
    )
    joined = sum(p * jnp.exp2(t - top) for p, t in zip(parts, tops_in))
    total = joined[:, FEAT : FEAT + 1]
    raw_mix = joined / total
    shift = top + jnp.log2(total)
    mix = (raw_mix * fgain).astype(BFLOAT)
    mix_all[ty] = mix
    later = to_ty(1, mix_all.at[ty], mix_all.at[ty])
    attended = dot_nn(mix, vproj_ref[...])
    finish(loads[1:])
    one = latent + times(attended.astype(BFLOAT), cross)
    h_unit, h_rate = norm_rows(one)
    hidden = (h_unit * hgain_ref[...]).astype(BFLOAT)
    act, act_slope = gelu_pair(times(hidden, up))
    act = act.astype(BFLOAT)
    two = one + times(act, down)
    t_unit, t_rate = norm_rows(two)
    trows = (t_unit * tgain_ref[...]).astype(BFLOAT)
    for s, i in enumerate((tk, tv)):
        value = times(trows, i).astype(BFLOAT)
        for h in range(8):
            kv_out[h, 32 * s : 32 * s + 32] = value[:, 128 * h : 128 * h + 128]
    kv_copies = spread(1, kv_out, kv_in)
    value = times(trows, tq).astype(BFLOAT)
    for h in range(8):
        q_out[h] = value[:, 128 * h : 128 * h + 128]
    q_copies = spread(2, q_out, q_in)
    give_x(5, hidden)
    give_x(4, act)
    give_x(3, trows)
    back_four = times_back(cot, fdown)
    finish(kv_copies)
    copies = on_mate.start(0, lambda d: kv_in, lambda d: kv_more)
    finish(q_copies)
    q = q_in[...].reshape(8 * share, 128)
    k1 = kv_in[:, 0:32].reshape(8 * share, 128)
    v1 = kv_in[:, 32:64].reshape(8 * share, 128)
    scale = 1.0 / math.sqrt(128)
    s1 = dot_nt(q, k1) * scale
    finish(copies)
    k2 = kv_more[:, 0:32].reshape(8 * share, 128)
    v2 = kv_more[:, 32:64].reshape(8 * share, 128)
    s2 = dot_nt(q, k2) * scale
    stop = jnp.maximum(jnp.max(s1, axis=1, keepdims=True), jnp.max(s2, axis=1, keepdims=True))
    e1, e2 = jnp.exp(s1 - stop), jnp.exp(s2 - stop)
    rate = 1.0 / (jnp.sum(e1, axis=1, keepdims=True) + jnp.sum(e2, axis=1, keepdims=True))
    p1, p2 = e1 * rate, e2 * rate
    probs[0] = p1
    probs[1] = p2
    mixed_out[...] = (
        (dot_nn(p1.astype(BFLOAT), v1) + dot_nn(p2.astype(BFLOAT), v2))
        .astype(BFLOAT)
        .reshape(8, share, 128)
    )
    copies = spread(3, mixed_out, mixed_in)
    pass_g(0)
    pass_x(5)
    pass_x(4)
    pass_x(3)
    finish(copies)
    mixed = jnp.concatenate([mixed_in[h] for h in range(8)], axis=1)
    give_x(2, mixed)
    three = two + times(mixed, tproj)
    o_unit, o_rate = norm_rows(three)
    ogain = ogain_ref[...]
    frows = (o_unit * ogain).astype(BFLOAT)
    give_x(1, frows)
    fact, fact_slope = gelu_pair(times(frows, fup))
    fact = fact.astype(BFLOAT)
    give_x(0, fact)

    def put_gain(row, grad):
        for h in range(4):
            gains_out[0, h, row : row + 1] = grad[:, 256 * h : 256 * h + 256]

    g_lift = (back_four * fact_slope).astype(BFLOAT)
    give_g(1, g_lift)
    g_three, o_grad = norm_rows_back(times_back(g_lift, fup), ogain, o_unit, o_rate)
    put_gain(2, o_grad)
    g_three = cot.astype(FLOAT) + g_three
    g_tower = g_three.astype(BFLOAT)
    g_mixed = times_back(g_tower, tproj).astype(BFLOAT)
    for h in range(8):
        gm_out[h] = g_mixed[:, 128 * h : 128 * h + 128]
    copies = spread(4, gm_out, gm_in)
    give_g(2, g_tower)
    result_v[...] = (three + times(fact, fdown)).astype(BFLOAT)
    result_copies = hand_out(2, result_v, result_ref)
    pass_x(2)
    pass_x(1)
    pass_x(0)
    pass_g(1)
    finish(copies)
    gm = gm_in[...].reshape(8 * share, 128)
    q = q_in[...].reshape(8 * share, 128)
    k1 = kv_in[:, 0:32].reshape(8 * share, 128)
    v1 = kv_in[:, 32:64].reshape(8 * share, 128)
    k2 = kv_more[:, 0:32].reshape(8 * share, 128)
    v2 = kv_more[:, 32:64].reshape(8 * share, 128)
    p1, p2 = probs[0], probs[1]
    gp1, gp2 = dot_nt(gm, v1), dot_nt(gm, v2)
    away = jnp.sum(p1 * gp1, axis=1, keepdims=True) + jnp.sum(p2 * gp2, axis=1, keepdims=True)
    gs1 = (p1 * (gp1 - away)).astype(BFLOAT)
    gs2 = (p2 * (gp2 - away)).astype(BFLOAT)
    kvx_out[0] = (outer(gs2, q) * scale).astype(BFLOAT)
    kvx_out[1] = outer(p2.astype(BFLOAT), gm).astype(BFLOAT)
    copies = on_mate.start(1, lambda d: kvx_out, lambda d: kvx_in)
    gq = (dot_nn(gs1, k1) + dot_nn(gs2, k2)) * scale
    q_out[...] = gq.astype(BFLOAT).reshape(8, share, 128)
    q_copies = spread(5, q_out, gq_in)
    gk = outer(gs1, q) * scale
    gv = outer(p1.astype(BFLOAT), gm)
    finish(copies)
    kv_out[:, 0:32] = (gk + kvx_in[0].astype(FLOAT)).astype(BFLOAT).reshape(8, share, 128)
    kv_out[:, 32:64] = (gv + kvx_in[1].astype(FLOAT)).astype(BFLOAT).reshape(8, share, 128)
    kv_copies = spread(12, kv_out, gkv_in)
    pass_g(2)
    stage_one(0)
    finish(q_copies)
    value = jnp.concatenate([gq_in[h] for h in range(8)], axis=1)
    give_g(3, value)
    g_trows = times_back(value, tq)
    finish(kv_copies)
    for s, i in enumerate((tk, tv)):
        value = jnp.concatenate([gkv_in[h, 32 * s : 32 * s + 32] for h in range(8)], axis=1)
        give_g(4 + s, value)
        g_trows = g_trows + times_back(value, i)
    g_two, t_grad = norm_rows_back(g_trows, tgain_ref[...], t_unit, t_rate)
    put_gain(1, t_grad)
    g_two = g_three + g_two
    g_hidden = g_two.astype(BFLOAT)
    give_g(6, g_hidden)
    pass_g(3)
    stage_two(0)
    stage_one(1)
    g_hlift = (times_back(g_hidden, down) * act_slope).astype(BFLOAT)
    give_g(7, g_hlift)
    pass_g(4)
    pass_g(5)
    stage_two(1)
    stage_one(2)
    g_one, h_grad = norm_rows_back(times_back(g_hlift, up), hgain_ref[...], h_unit, h_rate)
    put_gain(0, h_grad)
    gain_copies = over_ty(3, gains_out.at[0], gains_all.at[0])
    g_one = g_two + g_one
    g_cross = g_one.astype(BFLOAT)
    for h in range(4):
        gcross_out[h] = g_cross[:, 256 * h : 256 * h + 256]
    gcross_copies = over_ty(4, gcross_out, gcross_all)
    g_att = times_back(g_cross, cross).astype(BFLOAT)
    raw_up = dot_nt(g_att, vproj_ref[...])
    feat_part = jnp.sum(raw_mix * raw_up, axis=0, keepdims=True)
    delta = jnp.sum(g_att.astype(FLOAT) * attended, axis=1, keepdims=True)
    lane = lax.broadcasted_iota(jnp.int32, raw_up.shape, 1)
    up_ref[ty] = jnp.where(
        lane < FEAT, raw_up * fgain, jnp.where(lane == FEAT, delta, shift)
    )
    copies = to_ty(5, up_ref.at[ty], up_ref.at[ty])
    pass_g(6)
    stage_two(2)
    stage_one(3)
    finish(later, gain_copies, gcross_copies)
    result_copies = hand_on(2, result_copies, result_ref)
    gain_rows = gains_all[0, 0] + gains_all[0, 1] + gains_all[0, 2] + gains_all[0, 3]
    ncopies = product_start(
        0, mix_all[...].reshape(4 * share, LANES), gcross_all[...].reshape(4 * share, 256), gain_rows
    )
    finish(copies)
    pass_g(7)
    for i in (3, 4, 5):
        finish(xg.pop(("px", i), ()))

    coefs_by_pixel(up_ref[...].reshape(4 * share, LANES), thigh_ref, tlow_ref, upcoefs)

    def back_step(t):
        block = take_block(t)
        ups[...] = dot_nn(upcoefs[t], pixels[...])
        for group in range(4):
            at = pl.ds(group * count, count)
            rate, bias = rate_and_bias(block, group)
            b = group % 2
            mine = up_ref[2 * b : 2 * b + 2].reshape(count, LANES)
            p = jnp.exp2(scores[at] * rate + (bias - mine[:, FEAT + 1 : FEAT + 2]))
            g = p * (ups[at] * rate - mine[:, FEAT : FEAT + 1])
            weights[at] = (g * rate).astype(BFLOAT)
        sums[t] = dot_nt(weights[...], pixels[0:GROUP])

    def first_steps(t, _):
        back_step(t)
        stage_two(3 + t)
        stage_one(4 + t)
        return 0

    def second_steps(t, _):
        back_step(t)
        stage_three(t - 4)
        return 0

    lax.fori_loop(0, 3, first_steps, 0)
    ncopies = product_join(0, ncopies, value_v)
    lax.fori_loop(3, 4, first_steps, 0)
    lax.fori_loop(4, 6, second_steps, 0)
    stage_two(7)
    lax.fori_loop(6, 8, second_steps, 0)
    part_out[...] = features_of(sums, None, thigh_ref, tlow_ref).reshape(part_out.shape)
    copies = on_ty.start(9, lambda d: part_out.at[ty_at(d)], lambda d: part_in.at[d])
    value_copies = product_end(0, ncopies, value_v, value_ref)
    unit, rate = norm_rows(lat_ref[ty].astype(FLOAT))
    raw_mix = part_out[ty]
    finish(copies)
    for d in range(3):
        raw_mix = raw_mix + part_in[d]
    mix = (raw_mix * fgain).astype(BFLOAT)
    gmix[ty] = mix
    mcopies = to_ty(6, gmix.at[ty], gmix.at[ty])
    grad_q = (dot_nn(mix, kproj_ref[...]) * cross_scale).astype(BFLOAT)
    grad, qgain_grad = norm_rows_back(times_back(grad_q, 0), qgain_ref[...], unit, rate)
    features = feat_part + jnp.sum(raw_mix * raw_all[ty], axis=0, keepdims=True)
    for h in range(4):
        gains_out[1, h, 0:1] = qgain_grad[:, 256 * h : 256 * h + 256]
    gains_out[1, 0, 1:2] = features[:, 0:256]
    gains_out[1, 1, 1:2, 0:128] = features[:, 256:384]
    mcopies += over_ty(10, gains_out.at[1], gains_all.at[1])
    grad_v[...] = (g_one + grad).astype(BFLOAT)
    grad_copies = hand_out(3, grad_v, grad_ref)
    for w in range(4):
        stage_four(w)
    finish(mcopies)
    gain_rows = gains_all[1, 0] + gains_all[1, 1] + gains_all[1, 2] + gains_all[1, 3]
    right = qrows[:, pl.ds(pl.multiple_of(ty * 256, 256), 256)]
    mcopies = product_start(1, gmix[...].reshape(4 * share, LANES), right, gain_rows)
    stage_three(4)
    stage_three(5)
    mcopies = product_join(1, mcopies, key_v)
    value_copies = hand_on(0, value_copies, value_ref)
    grad_copies = hand_on(3, grad_copies, grad_ref)
    stage_three(6)
    stage_three(7)
    key_copies = product_end(1, mcopies, key_v, key_ref)
    for w in range(4, 8):
        stage_four(w)
    key_copies = hand_on(1, key_copies, key_ref)
    finish(result_copies, value_copies, grad_copies, key_copies)
    for w in range(8):
        stage_end(w)


IN_NAMES = (
    "pixels", "pixel_mask", "latents", "cotangent", "feature_gain", "query_gain", "hidden_gain", "tower_gain",
    "final_gain", "key_proj", "value_proj", "hot", "hotcol", "ids", "lanes",
) + tuple("w%d" % i for i in range(10))
COPIED_NAMES = (
    "pix_v", "mask_v", "lat_v", "cot_v", "fgain_v", "qgain_v", "hgain_v", "tgain_v", "ogain_v", "kraw_v", "vraw_v",
    "hot_v", "hotcol_v", "ids_v", "lanes_v",
)
OUT_NAMES = ("result_ref", "grad_ref", "value_ref", "key_ref", "sums_ref")
SCRATCH_NAMES = (
    "ws", "msgs", "pixcoefs", "upcoefs", "pixels_v", "scores", "ups", "weights", "sums", "tops", "totals",
    "raw_all", "qrows", "part_out", "part_in", "q_out", "q_in", "kv_out", "kv_in", "kv_more", "probs",
    "mixed_out", "mixed_in", "gm_out", "gm_in", "kvx_out", "kvx_in", "gq_in", "gkv_in", "up_ref", "mix_all",
    "gcross_out", "gcross_all", "gains_out", "gains_all", "gmix", "x_out", "x_pass", "x_all", "g_out", "g_all",
    "own", "held", "relay_in", "zsend", "zrecv", "last", "nsend", "nextra", "nrecv", "nmore", "msg_rows", "msg", "thigh", "tlow",
    "kproj", "vproj", "fgain", "result_v", "grad_v", "value_v", "key_v",
    "w_sem", "l_sem", "ty_s", "ty_r", "tx_s", "tx_r", "mate_s", "mate_r", "xg_s", "xg_r", "y_s", "y_r",
    "z_s", "z_r", "ac_s", "ac_r", "re_s", "re_r", "in_sem", "out_sem",
) + COPIED_NAMES
SINE = tuple((-1) ** n * math.pi ** (2 * n + 1) / math.factorial(2 * n + 1) for n in range(7))


def pixel_constants(high, wide):
    length = -(-high * wide // 128) * 128
    hot = np.zeros((GROUP, length), np.float32)
    ids = np.full((8, length), 1e6, np.float32)
    for i in range(high):
        for j in range(wide):
            hot[16 + i, i * wide + j] = 1.0
            hot[64 + j, i * wide + j] = 1.0
            ids[0, i * wide + j], ids[1, i * wide + j] = i, j
    lanes = np.zeros((8, LANES), np.float32)
    for axis in range(2):
        first = 5 + 2 * BANDS * axis
        lanes[0, first : first + 2 * BANDS] = np.tile(np.arange(BANDS), 2)
        lanes[1, first + BANDS : first + 2 * BANDS] = 0.5
        lanes[2 + axis, first : first + 2 * BANDS] = 1.0
        lanes[4 + axis, 3 + axis] = 1.0
    lanes[6, :FEAT] = 1.0
    return jnp.asarray(hot, BFLOAT), jnp.asarray(hot[64 : 64 + wide], BFLOAT), jnp.asarray(ids), jnp.asarray(lanes)


def main_call(sizes, inputs, matrices):
    pixels, mask, lat, cot = inputs[:4]
    _, share, width = lat.shape
    inputs = inputs + pixel_constants(pixels.shape[2] // HALVES, pixels.shape[3])
    rows, length = 8 * share, inputs[11].shape[1]
    dma = pltpu.SemaphoreType.DMA
    hbm = pl.BlockSpec(memory_space=pl.ANY)
    shape = jax.ShapeDtypeStruct
    half, full = (lambda *s: pltpu.VMEM(s, BFLOAT)), (lambda *s: pltpu.VMEM(s, FLOAT))
    return pl.pallas_call(
        main_kernel,
        out_shape=(
            shape((4, share, width), BFLOAT),
            shape((4, share, width), BFLOAT),
            shape((4, 272, 256), BFLOAT),
            shape((4, 272, 256), BFLOAT),
            shape((8, 4, 128, 256), BFLOAT),
        ),
        in_specs=[pl.BlockSpec(memory_space=pltpu.SMEM)] + [hbm] * 25,
        out_specs=(hbm,) * 5,
        scratch_shapes=[
            half(10, width, width), half(8, 16, length), half(8, rows, 2 * GROUP), half(8, rows, 2 * GROUP),
            half(2 * GROUP, length), full(rows, length), full(rows, length), half(rows, length),
            full(8, rows, GROUP), full(8, rows, 1), full(8, rows, 1), full(4, share, LANES), half(4 * share, width),
            full(4, share, LANES), full(3, share, LANES),
            half(8, share, 128), half(8, share, 128), half(8, 2 * share, 128), half(8, 2 * share, 128),
            half(8, 2 * share, 128), full(2, rows, rows), half(8, share, 128), half(8, share, 128),
            half(8, share, 128), half(8, share, 128), half(2, rows, 128), half(2, rows, 128),
            half(8, share, 128), half(8, 2 * share, 128),
            full(4, share, LANES), half(4, share, LANES), half(4, share, 256), half(4, share, 256),
            full(2, 4, 8, 256), full(2, 4, 8, 256), half(4, share, LANES),
            half(6, 2, 4, share, 128), half(6, 4, 4, share, 128), half(6, 4, 2, 4, share, 128),
            half(8, 4, share, 256), half(8, 2, 4, share, 256), full(8, 128, 256), full(8, 128, 256), half(8, 128, 256),
            half(8, 3, 128, 256), half(8, 3, 128, 256), half(8, 128, 256),
            half(2, 8, 32, 256), half(2, 16, 256), half(2, 7, 32, 256), half(2, 7, 16, 256),
            full(16, length), half(16, length), half(2, 10 * GROUP, LANES), half(2, 10 * GROUP, LANES),
            half(LANES, width), half(LANES, width), full(1, LANES),
            half(share, width), half(share, width), half(4, 272, 256), half(4, 272, 256),
            dma((10,)), dma((8,)), dma((12, 3)), dma((12, 3)), dma((13, 7)), dma((13, 7)),
            dma((26, 1)), dma((26, 1)), dma((20, 3)), dma((20, 3)), dma((14, 1)), dma((14, 1)),
            dma((8, 3)), dma((8, 3)), dma((12, 1)), dma((12, 1)), dma((8,)), dma((8,)), dma((15,)), dma((4,)),
        ] + [pltpu.VMEM(v.shape, v.dtype) for v in inputs],
        compiler_params=pltpu.CompilerParams(
            collective_id=1, has_side_effects=True, vmem_limit_bytes=62 << 20
        ),
        name="main",
    )(sizes, *inputs, *matrices)


def finish_kernel(*refs):
    ins, outs, stage, held = refs[:9], refs[9:28], refs[28:37], refs[37:56]
    in_sem, out_sem = refs[56:]
    copies = [pltpu.make_async_copy(a, v, in_sem.at[i]) for i, (a, v) in enumerate(zip(ins, stage))]
    for copy in copies:
        copy.start()
    tx = lax.axis_index("tx")
    sums_ref, cross_core_ref, query_core_ref, latent_ref, result_in_ref, cross_ref, query_ref, value_ref, key_ref = stage
    result_ref, latent_out, feat_out, qgain_out, query_out, key_out, value_out, cross_out = held[:8]
    written = []

    def write(*places):
        for i in places:
            written.append(pltpu.make_async_copy(held[i], outs[i], out_sem.at[i]))
            written[-1].start()

    copies[0].wait()
    for w in range(8):
        for h in range(4):
            held[8 + w][:, 256 * h : 256 * h + 256] = sums_ref[w, h].astype(FLOAT)
        write(8 + w)
    for copy in copies[1:]:
        copy.wait()
    result_ref[...] = result_in_ref[...]
    latent_out[...] = latent_ref[...].astype(FLOAT)
    write(0, 1)
    here = pl.ds(pl.multiple_of(tx * 128, 128), 128)
    quarter = tx // 2
    inside = pl.ds(pl.multiple_of(lax.rem(tx, 2) * 128, 128), 128)
    scale = 1.0 / math.sqrt(query_ref.shape[0])
    cross_core = jnp.concatenate([cross_core_ref[h] for h in range(4)], axis=1)
    query_core = jnp.concatenate([query_core_ref[h] for h in range(4)], axis=1)
    value_out[...] = dot_nt(cross_core, cross_ref[...])[:FEAT]
    write(6)
    key_out[...] = (dot_nn(query_core, query_ref[...]) * scale)[:FEAT]
    write(5)
    cross_out[...] = outer(value_ref[:, here], cross_core[:FEAT])
    mine = query_core_ref[quarter, :, inside].astype(FLOAT)
    query_out[...] = outer(mine[:FEAT].astype(BFLOAT), key_ref[...]) * scale
    write(4, 7)
    qgain_out[...] = mine[264:265]
    more = jnp.concatenate([query_core_ref[h, 256:272] for h in range(2)], axis=1).astype(FLOAT)
    feat_out[...] = more[9:10, 0:FEAT]
    mine = cross_core_ref[quarter, 256:272, inside].astype(FLOAT)
    for i in range(3):
        held[16 + i][...] = mine[8 + i : 9 + i]
    write(2, 3, 16, 17, 18)
    for copy in written:
        copy.wait()


def finish_call(*inputs):
    width = inputs[5].shape[0]
    shape = lambda *s: jax.ShapeDtypeStruct(s, FLOAT)
    rows = inputs[3].shape
    block = [shape(128, width)]
    hbm = pl.BlockSpec(memory_space=pl.ANY)
    outs = (
        [jax.ShapeDtypeStruct(rows, BFLOAT), shape(*rows), shape(1, FEAT), shape(1, 128)]
        + block + [shape(FEAT, width)] * 2 + block + block * 8 + [shape(1, 128)] * 3
    )
    return pl.pallas_call(
        finish_kernel,
        out_shape=outs,
        in_specs=[hbm] * 9,
        out_specs=[hbm] * 19,
        scratch_shapes=[pltpu.VMEM(v.shape, v.dtype) for v in list(inputs) + outs]
        + [pltpu.SemaphoreType.DMA((9,)), pltpu.SemaphoreType.DMA((19,))],
        compiler_params=pltpu.CompilerParams(vmem_limit_bytes=62 << 20),
        name="finish",
    )(*inputs)


def on_device_fast(
    pixels,
    pixel_mask,
    image_sizes,
    latents,
    cotangent,
    feature_gain,
    query_gain,
    query_proj,
    key_proj,
    value_proj,
    cross_proj,
    hidden_gain,
    hidden_up,
    hidden_down,
    tower_gain,
    tower_query,
    tower_key,
    tower_value,
    tower_proj,
    final_gain,
    final_up,
    final_down,
):
    item_count = pixels.shape[0]
    tile_height = pixels.shape[2]
    tile_width = pixels.shape[3]
    model_width = latents.shape[2]
    rows_here = latents.shape[1]
    share = item_count * rows_here // 4

    def in_shares(rows):
        return rows.reshape(4, share, rows.shape[-1])

    result, latent_grad, cross_core, query_core, sums = main_call(
        image_sizes,
        (pixels, pixel_mask, in_shares(latents), in_shares(cotangent), feature_gain[None], query_gain[None],
         hidden_gain[None], tower_gain[None], final_gain[None], key_proj, value_proj),
        (query_proj, cross_proj, hidden_up, hidden_down, tower_query, tower_key, tower_value,
         tower_proj, final_up, final_down),
    )
    (result, latent_grad, feature_sum, query_sum, query_grad, key_grad, value_grad, cross_grad,
     final_down_grad, final_up_grad, tower_proj_grad, tower_query_grad, tower_key_grad,
     tower_value_grad, hidden_down_grad, hidden_up_grad, hidden_sum, tower_sum, final_sum) = finish_call(
        sums, cross_core, query_core, latent_grad, result, cross_proj, query_proj, value_proj, key_proj
    )
    return (
        result.reshape(latents.shape),
        latent_grad.reshape(latents.shape),
        feature_sum[0],
        query_sum[0],
        query_grad,
        key_grad,
        value_grad,
        cross_grad,
        hidden_sum[0],
        hidden_up_grad,
        hidden_down_grad,
        tower_sum[0],
        tower_query_grad,
        tower_key_grad,
        tower_value_grad,
        tower_proj_grad,
        final_sum[0],
        final_up_grad,
        final_down_grad,
    )


def on_device(
    pixels,
    pixel_mask,
    image_sizes,
    latents,
    cotangent,
    feature_gain,
    query_gain,
    query_proj,
    key_proj,
    value_proj,
    cross_proj,
    hidden_gain,
    hidden_up,
    hidden_down,
    tower_gain,
    tower_query,
    tower_key,
    tower_value,
    tower_proj,
    final_gain,
    final_up,
    final_down,
):
    item_count = pixels.shape[0]
    tile_height = pixels.shape[2]
    tile_width = pixels.shape[3]
    model_width = latents.shape[2]
    rows_here = latents.shape[1]
    head_count = HEADS
    head_size = model_width // head_count
    cross_scale = 1.0 / math.sqrt(model_width)
    tower_scale = 1.0 / math.sqrt(head_size)
    row_ids = lax.axis_index("ty") * tile_height + jnp.arange(tile_height, dtype=jnp.int32)
    col_ids = lax.axis_index("tx") * tile_width + jnp.arange(tile_width, dtype=jnp.int32)
    all_cols = jnp.arange(tile_width * lax.axis_size("tx"), dtype=jnp.int32)
    wide_pixels = lax.all_gather(pixels, "tx", axis=3, tiled=True).astype(FLOAT)
    wide_mask = lax.all_gather(pixel_mask, "tx", axis=2, tiled=True)
    side_sizes = image_sizes[:, None, None]
    live = (
        (wide_mask > 0)
        & (row_ids[None, :, None] < side_sizes)
        & (all_cols[None, None, :] < side_sizes)
    )[:, None]
    row_table, row_coord, row_sum = axis_tables(image_sizes, row_ids, 3, 5)
    col_table, col_coord, col_sum = axis_tables(image_sizes, all_cols, 4, 5 + 2 * BANDS)
    pixel_mean = (
        jnp.sum(wide_pixels, axis=1) + row_sum[:, :, None] + col_sum[:, None, :]
    ) / FEAT
    pixel_square = (
        jnp.sum(wide_pixels * wide_pixels, axis=1)
        + (row_coord * row_coord)[:, :, None]
        + (col_coord * col_coord)[:, None, :]
        + 2.0 * BANDS
    ) / FEAT
    pixel_rate = lax.rsqrt(pixel_square - pixel_mean * pixel_mean + EPSILON)
    exact = lax.Precision.HIGHEST

    def against_pixels(coefs):
        by_row = jnp.einsum("blf,bif->bli", coefs, row_table, precision=exact)
        by_col = jnp.einsum("blf,bjf->blj", coefs, col_table, precision=exact)
        total = by_row[:, :, :, None] + by_col[:, :, None, :]
        for c in range(3):
            total = total + coefs[:, :, c][:, :, None, None] * wide_pixels[:, None, c]
        total = total - jnp.sum(coefs, axis=2)[:, :, None, None] * pixel_mean[:, None]
        return total * pixel_rate[:, None]

    def over_pixels(weights):
        scaled = weights * pixel_rate[:, None]
        by_row = jnp.sum(scaled, axis=3)
        by_col = jnp.sum(scaled, axis=2)
        total = jnp.einsum("bli,bif->blf", by_row, row_table, precision=exact)
        total = total + jnp.einsum("blj,bjf->blf", by_col, col_table, precision=exact)
        colour = jnp.stack(
            [jnp.sum(scaled * wide_pixels[:, None, c], axis=(2, 3)) for c in range(3)], axis=2
        )
        total = total + jnp.pad(colour, ((0, 0), (0, 0), (0, FEAT - 3)))
        return total - jnp.sum(scaled * pixel_mean[:, None], axis=(2, 3))[:, :, None]

    latent_rows = latents.astype(FLOAT)
    query_normed, back_query_norm = jax.vjp(layer_norm, latent_rows, query_gain)
    query_input = query_normed.astype(BFLOAT)
    own_queries = linear(query_input, query_proj).astype(BFLOAT)
    raw_query = linear_back(own_queries, key_proj) * cross_scale
    scores = against_pixels(raw_query * feature_gain)
    row_top = jnp.max(jnp.where(live, scores, -1e30), axis=(2, 3))
    all_top = lax.pmax(row_top, "ty")
    row_exp = jnp.where(live, jnp.exp(scores - all_top[:, :, None, None]), 0.0)
    row_total = lax.psum(jnp.sum(row_exp, axis=(2, 3)), "ty")
    cross_exact = row_exp / row_total[:, :, None, None]
    raw_mix = lax.psum(over_pixels(cross_exact), "ty")
    mix = raw_mix * feature_gain
    attended = linear(mix.astype(BFLOAT), value_proj)
    attended_input = attended.astype(BFLOAT)
    resid_one = latent_rows + linear(attended_input, cross_proj)
    hidden_normed, back_hidden_norm = jax.vjp(layer_norm, resid_one, hidden_gain)
    hidden_input = hidden_normed.astype(BFLOAT)
    hidden_lifted, back_hidden_gelu = jax.vjp(gelu_tanh, linear(hidden_input, hidden_up))
    hidden_act = hidden_lifted.astype(BFLOAT)
    resid_two = resid_one + linear(hidden_act, hidden_down)
    tower_normed, back_tower_norm = jax.vjp(layer_norm, resid_two, tower_gain)
    tower_input = tower_normed.astype(BFLOAT)
    tower_q = linear(tower_input, tower_query).astype(BFLOAT)
    tower_k = linear(tower_input, tower_key).astype(BFLOAT)
    tower_v = linear(tower_input, tower_value).astype(BFLOAT)
    all_keys, all_values = (
        lax.all_gather(tower_k, "tx", axis=1, tiled=True),
        lax.all_gather(tower_v, "tx", axis=1, tiled=True),
    )
    split_q = tower_q.reshape(item_count, rows_here, head_count, head_size)
    split_k = all_keys.reshape(item_count, -1, head_count, head_size)
    split_v = all_values.reshape(item_count, -1, head_count, head_size)
    tower_scores = (
        jnp.einsum("bqhd,bkhd->bhqk", split_q, split_k, preferred_element_type=FLOAT) * tower_scale
    )
    tower_top = jnp.max(tower_scores, axis=3, keepdims=True)
    tower_exp = jnp.exp(tower_scores - tower_top)
    tower_total = jnp.sum(tower_exp, axis=3, keepdims=True)
    tower_exact = tower_exp / tower_total
    tower_probs = tower_exact.astype(BFLOAT)
    mixed = jnp.einsum(
        "bhqk,bkhd->bqhd", tower_probs, split_v, preferred_element_type=FLOAT
    ).reshape(item_count, rows_here, model_width)
    mixed_input = mixed.astype(BFLOAT)
    resid_three = resid_two + linear(mixed_input, tower_proj)
    final_normed, back_final_norm = jax.vjp(layer_norm, resid_three, final_gain)
    final_input = final_normed.astype(BFLOAT)
    final_lifted, back_final_gelu = jax.vjp(gelu_tanh, linear(final_input, final_up))
    final_act = final_lifted.astype(BFLOAT)
    resid_four = resid_three + linear(final_act, final_down)
    grad_four = cotangent.astype(FLOAT)
    final_down_grad = weight_grad(final_act, cotangent)
    grad_final_lift = back_final_gelu(linear_back(cotangent, final_down))[0].astype(BFLOAT)
    final_up_grad = weight_grad(final_input, grad_final_lift)
    grad_rows_three, final_gain_grad = back_final_norm(linear_back(grad_final_lift, final_up))
    grad_three = grad_four + grad_rows_three
    grad_tower_out = grad_three.astype(BFLOAT)
    tower_proj_grad = weight_grad(mixed_input, grad_tower_out)
    grad_mixed_flat = linear_back(grad_tower_out, tower_proj).astype(BFLOAT)
    grad_mixed = grad_mixed_flat.reshape(item_count, rows_here, head_count, head_size)
    grad_tower_p = jnp.einsum("bqhd,bkhd->bhqk", grad_mixed, split_v, preferred_element_type=FLOAT)
    tower_delta = jnp.sum(tower_exact * grad_tower_p, axis=3, keepdims=True)
    grad_tower_scores = (tower_exact * (grad_tower_p - tower_delta)).astype(BFLOAT)
    grad_tower_q = (
        (
            jnp.einsum("bhqk,bkhd->bqhd", grad_tower_scores, split_k, preferred_element_type=FLOAT)
            * tower_scale
        )
        .astype(BFLOAT)
        .reshape(item_count, rows_here, model_width)
    )
    value_part = jnp.einsum(
        "bhqk,bqhd->bkhd", tower_probs, grad_mixed, preferred_element_type=FLOAT
    )
    key_part = (
        jnp.einsum("bhqk,bqhd->bkhd", grad_tower_scores, split_q, preferred_element_type=FLOAT)
        * tower_scale
    )
    key_sums, value_sums = (
        lax.psum_scatter(
            key_part.reshape(item_count, -1, model_width), "tx", scatter_dimension=1, tiled=True
        ),
        lax.psum_scatter(
            value_part.reshape(item_count, -1, model_width), "tx", scatter_dimension=1, tiled=True
        ),
    )
    grad_tower_k = key_sums.astype(BFLOAT)
    grad_tower_v = value_sums.astype(BFLOAT)
    tower_query_grad = weight_grad(tower_input, grad_tower_q)
    tower_key_grad = weight_grad(tower_input, grad_tower_k)
    tower_value_grad = weight_grad(tower_input, grad_tower_v)
    grad_tower_rows = (
        linear_back(grad_tower_q, tower_query)
        + linear_back(grad_tower_k, tower_key)
        + linear_back(grad_tower_v, tower_value)
    )
    grad_rows_two, tower_gain_grad = back_tower_norm(grad_tower_rows)
    grad_two = grad_three + grad_rows_two
    grad_hidden_out = grad_two.astype(BFLOAT)
    hidden_down_grad = weight_grad(hidden_act, grad_hidden_out)
    grad_hidden_lift = back_hidden_gelu(linear_back(grad_hidden_out, hidden_down))[0].astype(BFLOAT)
    hidden_up_grad = weight_grad(hidden_input, grad_hidden_lift)
    grad_rows_one, hidden_gain_grad = back_hidden_norm(linear_back(grad_hidden_lift, hidden_up))
    grad_one = grad_two + grad_rows_one
    grad_cross_out = grad_one.astype(BFLOAT)
    cross_proj_grad = weight_grad(attended_input, grad_cross_out)
    grad_attended = linear_back(grad_cross_out, cross_proj).astype(BFLOAT)
    raw_up = linear_back(grad_attended, value_proj)
    grad_probs = against_pixels(raw_up * feature_gain)
    cross_delta = jnp.sum(grad_attended.astype(FLOAT) * attended, axis=2)
    grad_scores = cross_exact * (grad_probs - cross_delta[:, :, None, None])
    raw_grad_mix = lax.psum(over_pixels(grad_scores), "ty")
    grad_mix = (raw_grad_mix * feature_gain).astype(BFLOAT)
    grad_queries = (linear(grad_mix, key_proj) * cross_scale).astype(BFLOAT)
    key_proj_grad = weight_grad(grad_mix, own_queries) * cross_scale
    value_proj_grad = weight_grad(mix.astype(BFLOAT), grad_attended)
    feature_part = jnp.sum(raw_grad_mix * raw_query + raw_mix * raw_up, axis=(0, 1))
    pixel_sums = lax.psum((key_proj_grad, value_proj_grad, feature_part), "tx")
    query_proj_grad = weight_grad(query_input, grad_queries)
    grad_latent_rows, query_gain_grad = back_query_norm(linear_back(grad_queries, query_proj))
    latent_grad = grad_one + grad_latent_rows
    summed = (
        lax.psum_scatter(query_gain_grad, "tx", scatter_dimension=0, tiled=True),
        lax.psum_scatter(query_proj_grad, "tx", scatter_dimension=0, tiled=True),
        lax.psum_scatter(cross_proj_grad, "tx", scatter_dimension=0, tiled=True),
        lax.psum_scatter(hidden_gain_grad, "tx", scatter_dimension=0, tiled=True),
        lax.psum_scatter(hidden_up_grad, "tx", scatter_dimension=0, tiled=True),
        lax.psum_scatter(hidden_down_grad, "tx", scatter_dimension=0, tiled=True),
        lax.psum_scatter(tower_gain_grad, "tx", scatter_dimension=0, tiled=True),
        lax.psum_scatter(tower_query_grad, "tx", scatter_dimension=0, tiled=True),
        lax.psum_scatter(tower_key_grad, "tx", scatter_dimension=0, tiled=True),
        lax.psum_scatter(tower_value_grad, "tx", scatter_dimension=0, tiled=True),
        lax.psum_scatter(tower_proj_grad, "tx", scatter_dimension=0, tiled=True),
        lax.psum_scatter(final_gain_grad, "tx", scatter_dimension=0, tiled=True),
        lax.psum_scatter(final_up_grad, "tx", scatter_dimension=0, tiled=True),
        lax.psum_scatter(final_down_grad, "tx", scatter_dimension=0, tiled=True),
    )
    return (
        resid_four.astype(BFLOAT),
        latent_grad,
        pixel_sums[2],
        summed[0],
        summed[1],
        pixel_sums[0],
        pixel_sums[1],
        summed[2],
        summed[3],
        summed[4],
        summed[5],
        summed[6],
        summed[7],
        summed[8],
        summed[9],
        summed[10],
        summed[11],
        summed[12],
        summed[13],
    )


def solution(mesh):
    in_specs = (
        P(None, None, "ty", "tx"),
        P(None, "ty", "tx"),
        P(),
        P(None, "tx", None),
        P(None, "tx", None),
        P(),
        P(),
        P(),
        P(),
        P(),
        P(),
        P(),
        P(),
        P(),
        P(),
        P(),
        P(),
        P(),
        P(),
        P(),
        P(),
        P(),
    )
    out_specs = (
        P(None, "tx", None),
        P(None, "tx", None),
        P(),
        P("tx"),
        P("tx", None),
        P(),
        P(),
        P("tx", None),
        P("tx"),
        P("tx", None),
        P("tx", None),
        P("tx"),
        P("tx", None),
        P("tx", None),
        P("tx", None),
        P("tx", None),
        P("tx"),
        P("tx", None),
        P("tx", None),
    )
    fits = mesh.shape["ty"] == 4 and mesh.shape["tx"] == HEADS
    plan = on_device_fast if fits else on_device
    return jax.shard_map(
        plan, mesh=mesh, in_specs=in_specs, out_specs=out_specs, check_vma=False
    )
```

```python
import math

import jax
import jax.numpy as jnp
import numpy as np
from jax import lax
from jax.experimental import pallas as pl
from jax.experimental.pallas import tpu as pltpu
from jax.sharding import PartitionSpec as P

BANDS = 64
FEAT = 261
HEADS = 8


EPSILON = 1e-05
FLOAT = jnp.float32
BFLOAT = jnp.bfloat16


def layer_norm(values, scales):
    centre = jnp.mean(values, axis=-1, keepdims=True)
    shifted = values - centre
    spread = jnp.mean(shifted * shifted, axis=-1, keepdims=True)
    return shifted * lax.rsqrt(spread + EPSILON) * scales


def gelu_tanh(values):
    cubic = values + 0.044715 * values * values * values
    return 0.5 * values * (1.0 + jnp.tanh(0.7978845608028654 * cubic))


def linear(inputs, weight):
    return lax.dot_general(
        inputs, weight, (((inputs.ndim - 1,), (0,)), ((), ())), preferred_element_type=FLOAT
    )


def linear_back(upstream, weight):
    return lax.dot_general(
        upstream, weight, (((upstream.ndim - 1,), (1,)), ((), ())), preferred_element_type=FLOAT
    )


def weight_grad(inputs, upstream):
    flat_inputs = inputs.reshape(-1, inputs.shape[-1])
    flat_upstream = upstream.reshape(-1, upstream.shape[-1])
    return lax.dot_general(
        flat_inputs, flat_upstream, (((0,), (0,)), ((), ())), preferred_element_type=FLOAT
    )


def axis_tables(image_sizes, ids, coord_lane, first_lane):
    side = image_sizes.astype(FLOAT)[:, None]
    coord = -1.0 + 2.0 * ids.astype(FLOAT)[None, :] / (side - 1.0)
    band = jnp.arange(BANDS, dtype=jnp.int32).astype(FLOAT)
    frequency = 1.0 + band[None, :] * (side * 0.5 - 1.0) / (BANDS - 1)
    angle = math.pi * coord[:, :, None] * frequency[:, None, :]
    waves = jnp.concatenate([jnp.sin(angle), jnp.cos(angle)], axis=2)
    count, length = coord.shape
    lead = jnp.zeros((count, length, coord_lane), FLOAT)
    gap = jnp.zeros((count, length, first_lane - coord_lane - 1), FLOAT)
    tail = jnp.zeros((count, length, FEAT - first_lane - 2 * BANDS), FLOAT)
    table = jnp.concatenate([lead, coord[:, :, None], gap, waves, tail], axis=2)
    return table, coord, jnp.sum(waves, axis=2) + coord


MESH = pl.DeviceIdType.MESH


def send(src, dst, send_sem, recv_sem, where):
    copy = pltpu.make_async_remote_copy(
        src_ref=src, dst_ref=dst, send_sem=send_sem, recv_sem=recv_sem,
        device_id=where, device_id_type=MESH,
    )
    copy.start()
    return copy


def greet(places):
    barrier = pltpu.get_barrier_semaphore()
    for place in places:
        pl.semaphore_signal(barrier, inc=1, device_id=place, device_id_type=MESH)
    pl.semaphore_wait(barrier, len(places))


def outer(left, right):
    return lax.dot_general(left, right, (((0,), (0,)), ((), ())), preferred_element_type=FLOAT)


LANES = 384
CUBE = 0.044715
SLOPE = 0.7978845608028654


def norm_rows(rows):
    shifted = rows - jnp.mean(rows, axis=-1, keepdims=True)
    rate = lax.rsqrt(jnp.mean(shifted * shifted, axis=-1, keepdims=True) + EPSILON)
    return shifted * rate, rate


def norm_rows_back(upstream, gain, unit, rate):
    scaled = upstream * gain
    along = jnp.mean(scaled * unit, axis=-1, keepdims=True)
    grad = rate * (scaled - jnp.mean(scaled, axis=-1, keepdims=True) - unit * along)
    return grad, jnp.sum(upstream * unit, axis=0, keepdims=True)


def gelu_pair(values):
    square = values * values
    bend = jnp.tanh(SLOPE * (values + CUBE * values * square))
    half = 0.5 * (1.0 + bend)
    slope = half + 0.5 * values * (1.0 - bend * bend) * (SLOPE * (1.0 + 3.0 * CUBE * square))
    return values * half, slope


def dot_nt(left, right):
    return lax.dot_general(left, right, (((1,), (1,)), ((), ())), preferred_element_type=FLOAT)


def dot_nn(left, right):
    return lax.dot_general(left, right, (((1,), (0,)), ((), ())), preferred_element_type=FLOAT)


HALVES = 2
GROUP = 128
LOG2E = 1.0 / math.log(2.0)


def split_two(values):
    high = values.astype(BFLOAT)
    return high, (values - high.astype(FLOAT)).astype(BFLOAT)


def dot_wide(dot, values, high, low):
    first, second = split_two(values)
    return dot(first, high) + (dot(first, low) + dot(second, high))


def coefs_by_pixel(coefs, thigh_ref, tlow_ref, into):
    count = coefs.shape[0] // 2
    for b in range(2):
        wide = dot_wide(dot_nt, coefs[b * count : (b + 1) * count], thigh_ref[b], tlow_ref[b])
        for half in range(HALVES):
            at = pl.ds((half * 2 + b) * count, count)
            rows = wide[:, half * GROUP : (half + 1) * GROUP]
            for t in range(8):
                high, low = split_two(rows + wide[:, (2 + t) * GROUP : (3 + t) * GROUP])
                into[t, at, 0:GROUP] = high
                into[t, at, GROUP : 2 * GROUP] = low


def features_of(sums, scales, thigh_ref, tlow_ref):
    count = sums.shape[1] // 4
    blocks = [sums[t] if scales is None else sums[t] * scales[t] for t in range(8)]
    joined = blocks[0]
    for block in blocks[1:]:
        joined = joined + block
    outs = []
    for b in range(2):
        first, second = pl.ds(b * count, count), (2 + b) * count
        lo, hi = slice(b * count, (b + 1) * count), slice((2 + b) * count, (3 + b) * count)
        wide = jnp.concatenate(
            [joined[lo], joined[hi]] + [block[lo] + block[hi] for block in blocks], axis=1
        )
        outs.append(dot_wide(dot_nn, wide, thigh_ref[b], tlow_ref[b]))
    return jnp.concatenate(outs, axis=0)


def rate_and_bias(block, group):
    rate = block[group % 2 * 4 + group // 2 * 8 + 3 :][:1].astype(FLOAT)
    return rate, jnp.where(rate == 0.0, -1e30, 0.0)


class Ring:
    def __init__(self, places, send_sems, recv_sems):
        self.places, self.sems = places, (send_sems, recv_sems)

    def copy(self, i, d, src, dst):
        return pltpu.make_async_remote_copy(
            src_ref=src, dst_ref=dst, send_sem=self.sems[0].at[i, d], recv_sem=self.sems[1].at[i, d],
            device_id=self.places[d], device_id_type=MESH,
        )

    def start(self, i, sources, into):
        copies = [self.copy(i, d, sources(d), into(d)) for d in range(len(self.places))]
        for copy in copies:
            copy.start()
        return copies


def finish(*groups):
    for copies in groups:
        for copy in copies:
            copy.wait()


def sin_half_turns(turns):
    whole = jnp.floor(turns + 0.5)
    part = turns - whole
    odd = whole - 2.0 * jnp.floor(whole * 0.5)
    square = part * part
    total = jnp.full_like(square, SINE[-1])
    for term in SINE[-2::-1]:
        total = total * square + term
    return part * total * (1.0 - 2.0 * odd)


def axis_rows(axis, side, first, lanes):
    place = (lax.broadcasted_iota(jnp.int32, (48, 1), 0) + first).astype(FLOAT)
    coord = -1.0 + 2.0 * place / (side - 1.0)
    here = lanes[:, 128 * axis : 128 * axis + 256]
    rate = 1.0 + here[0:1] * (side * 0.5 - 1.0) * (1.0 / (BANDS - 1))
    waves = sin_half_turns(coord * rate + here[1:2]) * here[2 + axis : 3 + axis]
    empty = jnp.zeros((48, LANES - 256), FLOAT)
    table = jnp.concatenate([empty, waves] if axis else [waves, empty], axis=1)
    total = jnp.sum(waves, axis=1, keepdims=True) + coord
    table = table + coord * lanes[4 + axis : 5 + axis] - (total * (1.0 / FEAT)) * lanes[6:7]
    return table, coord, total


def main_kernel(
    sizes_ref, *refs
):
    names = IN_NAMES + OUT_NAMES + SCRATCH_NAMES
    r = dict(zip(names, refs))
    matrices = [r["w%d" % i] for i in range(10)]
    result_ref, grad_ref, value_ref, key_ref, sums_ref = [r[n] for n in OUT_NAMES]
    (ws, msgs, pixcoefs, upcoefs, pixels, scores, ups, weights, sums, tops, totals, raw_all, qrows,
     part_out, part_in, half_out, half_in, up_sent, q_out, q_in, kv_out, kv_in, kv_more, probs, mixed_out, mixed_in, gm_out, gm_in,
     kvx_out, kvx_in, gq_in, gkv_in, up_ref, mix_all, gcross_out, gcross_all, gains_out, gains_all, gmix,
     x_out, x_all, g_out, g_all, own, held, relay_in, zsend, zrecv, last, nsend, nextra, nrecv, nmore,
     msg_rows, msg_ref, thigh_ref, tlow_ref, kproj_ref, vproj_ref, fgain_ref, result_v, grad_v, value_v, key_v,
     w_sem, l_sem, ty_s, ty_r, tx_s, tx_r, mate_s, mate_r, xg_s, xg_r, z_s, z_r, ac_s, ac_r, re_s, re_r, g_s, g_r,
     in_sem, out_sem,
     pix_v, mask_v, lat_ref, cot_ref, fgain_v, qgain_ref, hgain_ref, tgain_ref, ogain_ref,
     kraw_v, vraw_v, hot_ref, hotrow_ref, ids_ref, lanes_ref) = [r[n] for n in SCRATCH_NAMES]
    ty, tx = lax.axis_index("ty"), lax.axis_index("tx")
    z, y = tx // 2, lax.rem(tx, 2)
    tys = [{"ty": lax.rem(ty + d, 4), "tx": tx} for d in (1, 2, 3)]
    txs = [{"ty": ty, "tx": lax.rem(tx + d, 8)} for d in range(1, 8)]
    mate = {"ty": 2 * (ty // 2) + 1 - lax.rem(ty, 2), "tx": tx}
    beside = {"ty": ty, "tx": 2 * z + 1 - y}
    on_ty, on_tx = Ring(tys, ty_s, ty_r), Ring(txs, tx_s, tx_r)
    on_mate, across = Ring([mate], mate_s, mate_r), Ring([tys[1]], ac_s, ac_r)
    over = [{"ty": lax.rem(ty + d, 4), "tx": 2 * z + 1 - y} for d in range(4)]
    handing = Ring(tys + over, xg_s, xg_r)
    loads = []
    small = []
    for i, (name, into) in enumerate(zip(IN_NAMES, COPIED_NAMES)):
        small.append(pltpu.make_async_copy(r[name], r[into], in_sem.at[i]))
        small[i].start()
    for i, w in enumerate(matrices):
        loads.append(pltpu.make_async_copy(w, ws.at[i], w_sem.at[i]))
    loads[0].start()
    cross, up, down, tq, tk, tv, tproj, fup, fdown = range(1, 10)
    partners = tys + txs + over[1:]
    barrier = pltpu.get_barrier_semaphore()
    for place in partners:
        pl.semaphore_signal(barrier, inc=1, device_id=place, device_id_type=MESH)
    ty_at = lambda d: lax.rem(ty + d + 1, 4)
    tx_at = lambda d: lax.rem(tx + d + 1, 8)

    def times(rows, i):
        return dot_nn(rows, ws[i])

    def times_back(rows, i):
        return dot_nt(rows, ws[i])

    def to_ty(i, src, into):
        return on_ty.start(i, lambda d: src, lambda d: into)

    def spread(i, out, into):
        copies = on_tx.start(i, lambda d: out.at[tx_at(d)], lambda d: into.at[tx])
        into[tx] = out[tx]
        return copies

    def over_ty(i, out, into):
        copies = on_ty.start(i, lambda d: out.at[ty_at(d)], lambda d: into.at[ty])
        into[ty] = out[ty]
        return copies

    xg = {}

    def handed(i, source, into):
        return [
            handing.copy(i, k, source(k), into(0 if k < 3 else 1)) for k in range(7)
        ]

    def give_x(i, rows):
        for c in range(8):
            x_out[i, c % 2, c // 2] = rows[:, 128 * c : 128 * c + 128]
        x_all[i, :, 0, ty] = x_out[i, y]
        xg["x", i] = handed(
            i, lambda k: x_out.at[i, y if k < 3 else 1 - y], lambda slot: x_all.at[i, :, slot, ty]
        )
        for copy in xg["x", i]:
            copy.start()

    def g_copies(w):
        return handed(
            6 + w, lambda k: g_out.at[w, lax.rem(ty + k + 1, 4)], lambda slot: g_all.at[w, slot, ty]
        )

    def give_g(w, rows):
        for h in range(4):
            g_out[w, h] = rows[:, 256 * h : 256 * h + 256]
        g_all[w, 0, ty] = g_out[w, ty]
        for copy in g_copies(w):
            copy.start()

    def slot_x(w):
        return min(w, 3) + max(w - 5, 0) if isinstance(w, int) else jnp.minimum(w, 3) + jnp.maximum(w - 5, 0)

    def zcopy(w, c):
        return pltpu.make_async_remote_copy(
            src_ref=zsend.at[w, c], dst_ref=zrecv.at[w, c], send_sem=z_s.at[w, c],
            recv_sem=z_r.at[w, c], device_id={"ty": ty, "tx": 2 * lax.rem(z + c + 1, 4) + y},
            device_id_type=MESH,
        )

    at_end = (z == 0) | (z == 3)

    def relay(w):
        return pltpu.make_async_remote_copy(
            src_ref=zsend.at[w, 1], dst_ref=relay_in.at[w], send_sem=re_s.at[w], recv_sem=re_r.at[w],
            device_id={"ty": ty, "tx": 2 * (1 + z // 2) + y}, device_id_type=MESH,
        )

    def stage_one(w):
        i = slot_x(w)
        if isinstance(w, int):
            finish(xg.pop(("x", i), ()))
        finish(g_copies(w))
        right = g_all[w].reshape(256, 256)

        def part(c):
            return outer(x_all[i, lax.rem(z + c + 1, 4)].reshape(256, 128), right)

        zsend[w, 1] = part(1).astype(BFLOAT)

        @pl.when(at_end)
        def _():
            relay(w).start()

        @pl.when(jnp.logical_not(at_end))
        def _():
            zcopy(w, 1).start()

        for c, middle in ((0, 1), (2, 2)):
            total = part(c)

            @pl.when(z == middle)
            def _():
                held[w] = total

            @pl.when(z != middle)
            def _():
                zsend[w, c] = total.astype(BFLOAT)
                zcopy(w, c).start()

        own[w] = part(3)

    def stage_two(w):
        for c, middle in ((0, 1), (2, 2)):
            @pl.when(z == middle)
            def _():
                relay(w).wait_recv()
                zsend[w, c] = (held[w] + relay_in[w].astype(FLOAT)).astype(BFLOAT)
                zcopy(w, c).start()

    def out_copies(w):
        return [
            on_mate.copy(2 + w, 0, last.at[w], sums_ref.at[w, ty]),
            across.copy(w, 0, last.at[w], sums_ref.at[w, ty]),
            pltpu.make_async_copy(last.at[w], sums_ref.at[w, ty], l_sem.at[w]),
        ]

    def stage_three(w):
        total = own[w]
        for c in (0, 2):
            zcopy(w, c).wait()
            total = total + zrecv[w, c].astype(FLOAT)
        own[w] = total

        @pl.when(at_end)
        def _():
            relay(w).wait_send()
            zcopy(w, 1).wait_recv()
            own[w] = own[w] + zrecv[w, 1].astype(FLOAT)

        @pl.when(jnp.logical_not(at_end))
        def _():
            zcopy(w, 1).wait_send()

        last[w] = own[w].astype(BFLOAT)
        for copy in out_copies(w):
            copy.start()

    def stage_four(w):
        across.copy(w, 0, last.at[w], sums_ref.at[w, ty]).wait()
        there = sums_ref.at[w, lax.rem(ty + 2, 4)]
        on_mate.copy(10 + w, 0, there, there).start()

    def stage_end(w):
        there = sums_ref.at[w, lax.rem(ty + 2, 4)]
        on_mate.copy(10 + w, 0, there, there).wait()
        on_mate.copy(2 + w, 0, last.at[w], sums_ref.at[w, ty]).wait()
        pltpu.make_async_copy(last.at[w], sums_ref.at[w, ty], l_sem.at[w]).wait()

    def product_start(i, left, right, gains):
        product = outer(left, right)
        nsend[i] = product[0:256].astype(BFLOAT).reshape(8, 32, 256)
        row = lax.broadcasted_iota(jnp.int32, (16, 256), 0)
        more = product[256:272] + jnp.where(row < 8, 0.0, jnp.concatenate([gains, gains], axis=0))
        nextra[i] = more.astype(BFLOAT)
        return on_tx.start(
            6 + 3 * i, lambda d: nsend.at[i, tx_at(d)], lambda d: nrecv.at[i, d]
        ) + on_tx.start(7 + 3 * i, lambda d: nextra.at[i], lambda d: nmore.at[i, d])

    def product_join(i, copies, into):
        finish(copies)
        main = nsend[i, tx].astype(FLOAT)
        more = nextra[i].astype(FLOAT)
        for d in range(7):
            main = main + nrecv[i, d].astype(FLOAT)
            more = more + nmore[i, d].astype(FLOAT)
        mine = pl.ds(pl.multiple_of(tx * 32, 32), 32)
        into[ty, mine] = main.astype(BFLOAT)
        into[ty, 256:272] = more.astype(BFLOAT)
        return on_tx.start(8 + 3 * i, lambda d: into.at[ty, mine], lambda d: into.at[ty, mine])

    def hand_out(k, source, out):
        mine = pltpu.make_async_copy(source, out.at[ty], out_sem.at[k])
        mine.start()
        return on_mate.start(18 + k, lambda d: source, lambda d: out.at[ty]) + [mine], across.start(
            8 + k, lambda d: source, lambda d: out.at[ty]
        )

    def hand_on(k, copies, out):
        near, far = copies
        finish(far)
        there = out.at[lax.rem(ty + 2, 4)]
        return near + on_mate.start(22 + k, lambda d: there, lambda d: there)

    def product_end(i, copies, into, out):
        finish(copies)
        return hand_out(i, into.at[ty], out)

    def message(k, src, at, where):
        return pltpu.make_async_remote_copy(
            src_ref=src, dst_ref=msgs.at[at], send_sem=g_s.at[k], recv_sem=g_r.at[k],
            device_id=where, device_id_type=MESH,
        )

    def message_from(k):
        far = lax.rem(z + 8 - jnp.where(k < 5, k - 1, k - 4), 4)
        return jnp.where(
            k == 0, tx, jnp.where(k == 1, 2 * z + 1 - y, 2 * far + jnp.where(k < 5, y, 1 - y))
        )

    share, width = lat_ref.shape[1], lat_ref.shape[2]
    count = 2 * share
    high, wide = pix_v.shape[3] // HALVES, pix_v.shape[1]
    for copy in small:
        copy.wait()
    lanes = lanes_ref[...]
    ids = ids_ref[...]
    sides = [jnp.zeros((1, 1), FLOAT) + sizes_ref[b].astype(FLOAT) for b in range(2)]
    colours_in, live_in = pix_v[...].astype(FLOAT), jnp.where(mask_v[...] > 0, 1.0, 0.0)
    plane_rows = -(-wide // 8) * 8
    filler = [jnp.zeros((plane_rows - wide, HALVES * high), FLOAT)] if plane_rows > wide else []
    planes = []
    for b in range(2):
        for plane in [colours_in[c, :, b, :] for c in range(3)] + [live_in[:, b, :]]:
            planes += [plane] + filler
    planes = jnp.concatenate(planes, axis=0).astype(BFLOAT)
    flat = [dot_nn(planes, hotrow_ref[half]) for half in range(HALVES)]
    row_of = lax.broadcasted_iota(jnp.int32, (plane_rows, 1), 0).astype(FLOAT)
    pick = ids[1:2] == row_of

    def flatten(plane, half):
        rows = flat[half][plane * plane_rows : (plane + 1) * plane_rows]
        return jnp.sum(jnp.where(pick, rows, 0.0), axis=0, keepdims=True)

    def put_table(b, at, rows):
        high_part, low_part = split_two(rows)
        thigh_ref[b, at : at + rows.shape[0]] = high_part
        tlow_ref[b, at : at + rows.shape[0]] = low_part

    def by_pixel(total, coord, rows):
        square = coord * coord
        total_high, total_low = split_two(total)
        square_high, square_low = split_two(square)
        left = jnp.concatenate([total_high, total_low, square_high, square_low], axis=1)
        spread_out = outer(left, rows)
        return spread_out[0:1] + spread_out[1:2], spread_out[2:3] + spread_out[3:4]

    zeros = jnp.zeros((GROUP, LANES), BFLOAT)
    lane_at = lax.broadcasted_iota(jnp.int32, (16, LANES), 1)
    row_at = lax.broadcasted_iota(jnp.int32, (16, LANES), 0)
    for b in range(2):
        _, col_coord, col_total = axis_rows(1, sides[b], tx * wide, lanes)
        col_sum, col_square = by_pixel(col_total, col_coord, hot_ref[64:112])
        for half in range(HALVES):
            first = ty * (2 * high) + half * high
            table, coord, total = axis_rows(0, sides[b], first, lanes)
            row_sum, row_square = by_pixel(total, coord, hot_ref[16:64])
            put_table(b, half * GROUP + 16, table)
            thigh_ref[b, half * GROUP + 64 : half * GROUP + GROUP] = zeros[64:]
            tlow_ref[b, half * GROUP + 64 : half * GROUP + GROUP] = zeros[64:]
            channel = row_at - (half * 8 + b * 4)
            colour = (channel >= 0) & (channel < 3)
            value = jnp.where(channel == lane_at, 1.0, 0.0) - (1.0 / FEAT) * lanes[6:7]
            put_table(b, half * GROUP, jnp.where(colour, value, 0.0))
            colours = [flatten(b * 4 + c, half) for c in range(3)]
            mean = (colours[0] + colours[1] + colours[2] + row_sum + col_sum) * (1.0 / FEAT)
            square = sum(c * c for c in colours) + row_square + col_square + 2.0 * BANDS
            rate = lax.rsqrt(square * (1.0 / FEAT) - mean * mean + EPSILON)
            side = sides[b]
            first_row = jnp.zeros((1, 1), FLOAT) + first.astype(FLOAT)
            first_col = jnp.zeros((1, 1), FLOAT) + (tx * wide).astype(FLOAT)
            live = (
                (flatten(4 * b + 3, half) > 0.5)
                & (ids[0:1] + first_row < side)
                & (ids[1:2] + first_col < side)
            )
            for c, row in enumerate(colours + [jnp.where(live, rate, 0.0)]):
                at = half * 8 + b * 4 + c
                msg_rows[at : at + 1] = row
    msg_ref[...] = msg_rows[...].astype(BFLOAT)
    pl.semaphore_wait(barrier, len(partners))
    message(0, msg_ref, tx, beside).start()
    for d in range(3):
        message(1 + d, msg_ref, tx, {"ty": ty, "tx": 2 * lax.rem(z + 1 + d, 4) + y}).start()
    msgs[tx] = msg_ref[...]
    for load in loads[1:]:
        load.start()
    for b in range(2):
        for t in range(8):
            table, _, _ = axis_rows(1, sides[b], t * wide, lanes)
            at = (2 + t) * GROUP
            thigh_ref[b, at : at + 64] = zeros[:64]
            tlow_ref[b, at : at + 64] = zeros[:64]
            put_table(b, at + 64, table)
            thigh_ref[b, at + 112 : at + GROUP] = zeros[:16]
            tlow_ref[b, at + 112 : at + GROUP] = zeros[:16]
    for raw_ref, padded in ((kraw_v, kproj_ref), (vraw_v, vproj_ref)):
        padded[0:256] = raw_ref[0:256]
        padded[256:272] = jnp.concatenate(
            [raw_ref[256:FEAT].astype(FLOAT), jnp.zeros((272 - FEAT, width), FLOAT)], axis=0
        ).astype(BFLOAT)
        padded[272:LANES] = jnp.zeros((LANES - 272, width), BFLOAT)
    fgain_ref[...] = jnp.zeros_like(fgain_ref)
    fgain_ref[:, 0:FEAT] = fgain_v[...].reshape(1, FEAT)
    pixels[0:GROUP] = hot_ref[...]
    pixels[GROUP : 2 * GROUP] = hot_ref[...]
    gains_out[...] = jnp.zeros_like(gains_out)
    cot = cot_ref[ty]
    give_g(0, cot)
    fgain = fgain_ref[...]
    unit, _ = norm_rows(lat_ref[...].reshape(4 * share, width).astype(FLOAT))
    rows = (unit * qgain_ref[...]).astype(BFLOAT)
    qrows[...] = rows
    finish(loads[:1])
    queries = times(rows, 0).astype(BFLOAT)
    cross_scale = 1.0 / math.sqrt(width)
    raw = dot_nt(queries, kproj_ref[...]) * cross_scale
    raw_all[...] = raw.reshape(raw_all.shape)
    coefs_by_pixel(raw * (fgain * LOG2E), thigh_ref, tlow_ref, pixcoefs)

    def take_block(t):
        block = msgs[t]
        pixels[0:16] = block
        pixels[GROUP : GROUP + 16] = block
        scores[...] = dot_nn(pixcoefs[t], pixels[...])
        return block

    def front_step(k, _):
        t = message_from(k)

        @pl.when(k > 0)
        def _():
            message(k - 1, msg_ref, tx, beside).wait()

        @pl.when((k > 1) & (k < 5))
        def _():
            message(k + 2, msgs.at[t], t, beside).start()

        block = take_block(t)
        for group in range(4):
            at = pl.ds(group * count, count)
            rate, bias = rate_and_bias(block, group)
            s = scores[at] * rate + bias
            top = jnp.max(s, axis=1, keepdims=True)
            e = jnp.exp2(s - top)
            tops[t, at] = top
            totals[t, at] = jnp.sum(e, axis=1, keepdims=True)
            weights[at] = (e * rate).astype(BFLOAT)
        sums[t] = dot_nt(weights[...], pixels[0:GROUP])
        return 0

    lax.fori_loop(0, 8, front_step, 0)
    top = tops[0]
    for t in range(1, 8):
        top = jnp.maximum(top, tops[t])
    top = jnp.maximum(top[: 2 * count], top[2 * count :])
    both = jnp.concatenate([top, top], axis=0)
    scales = [jnp.exp2(tops[t] - both) for t in range(8)]
    total = sum(totals[t] * scales[t] for t in range(8))
    total = total[: 2 * count] + total[2 * count :]
    feats = features_of(sums, scales, thigh_ref, tlow_ref)
    lane = lax.broadcasted_iota(jnp.int32, feats.shape, 1)
    part_out[...] = jnp.where(
        lane < FEAT, feats, jnp.where(lane == FEAT, total, top)
    ).reshape(part_out.shape)

    copies = on_ty.start(0, lambda d: part_out.at[ty_at(d)], lambda d: part_in.at[d])
    latent = lat_ref[ty].astype(FLOAT)
    parts = [part_out[ty]]
    finish(copies)
    parts += [part_in[d] for d in range(3)]
    tops_in = [p[:, FEAT + 1 : FEAT + 2] for p in parts]
    top = jnp.maximum(
        jnp.maximum(tops_in[0], tops_in[1]), jnp.maximum(tops_in[2], tops_in[3])
    )
    joined = sum(p * jnp.exp2(t - top) for p, t in zip(parts, tops_in))
    total = joined[:, FEAT : FEAT + 1]
    raw_mix = joined / total
    shift = top + jnp.log2(total)
    mix = (raw_mix * fgain).astype(BFLOAT)
    mix_all[ty] = mix
    later = to_ty(1, mix_all.at[ty], mix_all.at[ty])
    attended = dot_nn(mix, vproj_ref[...])
    finish(loads[1:])
    one = latent + times(attended.astype(BFLOAT), cross)
    h_unit, h_rate = norm_rows(one)
    hidden = (h_unit * hgain_ref[...]).astype(BFLOAT)
    act, act_slope = gelu_pair(times(hidden, up))
    act = act.astype(BFLOAT)
    two = one + times(act, down)
    t_unit, t_rate = norm_rows(two)
    trows = (t_unit * tgain_ref[...]).astype(BFLOAT)
    for s, i in enumerate((tk, tv)):
        value = times(trows, i).astype(BFLOAT)
        for h in range(8):
            kv_out[h, 32 * s : 32 * s + 32] = value[:, 128 * h : 128 * h + 128]
    kv_copies = spread(1, kv_out, kv_in)
    value = times(trows, tq).astype(BFLOAT)
    for h in range(8):
        q_out[h] = value[:, 128 * h : 128 * h + 128]
    q_copies = spread(2, q_out, q_in)
    give_x(3, trows)
    back_four = times_back(cot, fdown)
    finish(kv_copies)
    copies = on_mate.start(0, lambda d: kv_in, lambda d: kv_more)
    finish(q_copies)
    q = q_in[...].reshape(8 * share, 128)
    k1 = kv_in[:, 0:32].reshape(8 * share, 128)
    v1 = kv_in[:, 32:64].reshape(8 * share, 128)
    scale = 1.0 / math.sqrt(128)
    s1 = dot_nt(q, k1) * scale
    finish(copies)
    k2 = kv_more[:, 0:32].reshape(8 * share, 128)
    v2 = kv_more[:, 32:64].reshape(8 * share, 128)
    s2 = dot_nt(q, k2) * scale
    stop = jnp.maximum(jnp.max(s1, axis=1, keepdims=True), jnp.max(s2, axis=1, keepdims=True))
    e1, e2 = jnp.exp(s1 - stop), jnp.exp(s2 - stop)
    rate = 1.0 / (jnp.sum(e1, axis=1, keepdims=True) + jnp.sum(e2, axis=1, keepdims=True))
    p1, p2 = e1 * rate, e2 * rate
    probs[0] = p1
    probs[1] = p2
    mixed_out[...] = (
        (dot_nn(p1.astype(BFLOAT), v1) + dot_nn(p2.astype(BFLOAT), v2))
        .astype(BFLOAT)
        .reshape(8, share, 128)
    )
    copies = spread(3, mixed_out, mixed_in)
    finish(copies)
    mixed = jnp.concatenate([mixed_in[h] for h in range(8)], axis=1)
    give_x(2, mixed)
    three = two + times(mixed, tproj)
    o_unit, o_rate = norm_rows(three)
    ogain = ogain_ref[...]
    frows = (o_unit * ogain).astype(BFLOAT)
    give_x(1, frows)
    fact, fact_slope = gelu_pair(times(frows, fup))
    fact = fact.astype(BFLOAT)

    def put_gain(row, grad):
        for h in range(4):
            gains_out[0, h, row : row + 1] = grad[:, 256 * h : 256 * h + 256]

    g_lift = (back_four * fact_slope).astype(BFLOAT)
    give_g(1, g_lift)
    g_three, o_grad = norm_rows_back(times_back(g_lift, fup), ogain, o_unit, o_rate)
    put_gain(2, o_grad)
    g_three = cot.astype(FLOAT) + g_three
    g_tower = g_three.astype(BFLOAT)
    g_mixed = times_back(g_tower, tproj).astype(BFLOAT)
    for h in range(8):
        gm_out[h] = g_mixed[:, 128 * h : 128 * h + 128]
    copies = spread(4, gm_out, gm_in)
    give_g(2, g_tower)
    result_v[...] = (three + times(fact, fdown)).astype(BFLOAT)
    result_copies = hand_out(2, result_v, result_ref)
    finish(copies)
    give_x(0, fact)
    gm = gm_in[...].reshape(8 * share, 128)
    q = q_in[...].reshape(8 * share, 128)
    k1 = kv_in[:, 0:32].reshape(8 * share, 128)
    v1 = kv_in[:, 32:64].reshape(8 * share, 128)
    k2 = kv_more[:, 0:32].reshape(8 * share, 128)
    v2 = kv_more[:, 32:64].reshape(8 * share, 128)
    p1, p2 = probs[0], probs[1]
    gp1, gp2 = dot_nt(gm, v1), dot_nt(gm, v2)
    away = jnp.sum(p1 * gp1, axis=1, keepdims=True) + jnp.sum(p2 * gp2, axis=1, keepdims=True)
    gs1 = (p1 * (gp1 - away)).astype(BFLOAT)
    gs2 = (p2 * (gp2 - away)).astype(BFLOAT)
    kvx_out[0] = (outer(gs2, q) * scale).astype(BFLOAT)
    kvx_out[1] = outer(p2.astype(BFLOAT), gm).astype(BFLOAT)
    copies = on_mate.start(1, lambda d: kvx_out, lambda d: kvx_in)
    gq = (dot_nn(gs1, k1) + dot_nn(gs2, k2)) * scale
    q_out[...] = gq.astype(BFLOAT).reshape(8, share, 128)
    q_copies = spread(5, q_out, gq_in)
    gk = outer(gs1, q) * scale
    gv = outer(p1.astype(BFLOAT), gm)
    finish(copies)
    kv_out[:, 0:32] = (gk + kvx_in[0].astype(FLOAT)).astype(BFLOAT).reshape(8, share, 128)
    kv_out[:, 32:64] = (gv + kvx_in[1].astype(FLOAT)).astype(BFLOAT).reshape(8, share, 128)
    kv_copies = spread(12, kv_out, gkv_in)
    stage_one(0)
    finish(q_copies)
    value = jnp.concatenate([gq_in[h] for h in range(8)], axis=1)
    give_g(3, value)
    g_trows = times_back(value, tq)
    finish(kv_copies)
    for s, i in enumerate((tk, tv)):
        value = jnp.concatenate([gkv_in[h, 32 * s : 32 * s + 32] for h in range(8)], axis=1)
        give_g(4 + s, value)
        g_trows = g_trows + times_back(value, i)
    g_two, t_grad = norm_rows_back(g_trows, tgain_ref[...], t_unit, t_rate)
    put_gain(1, t_grad)
    g_two = g_three + g_two
    g_hidden = g_two.astype(BFLOAT)
    stage_two(0)
    stage_one(1)
    g_hlift = (times_back(g_hidden, down) * act_slope).astype(BFLOAT)
    stage_two(1)
    stage_one(2)
    g_one, h_grad = norm_rows_back(times_back(g_hlift, up), hgain_ref[...], h_unit, h_rate)
    put_gain(0, h_grad)
    gain_copies = over_ty(3, gains_out.at[0], gains_all.at[0])
    g_one = g_two + g_one
    g_cross = g_one.astype(BFLOAT)
    for h in range(4):
        gcross_out[h] = g_cross[:, 256 * h : 256 * h + 256]
    gcross_copies = over_ty(4, gcross_out, gcross_all)
    g_att = times_back(g_cross, cross).astype(BFLOAT)
    raw_up = dot_nt(g_att, vproj_ref[...])
    feat_part = jnp.sum(raw_mix * raw_up, axis=0, keepdims=True)
    delta = jnp.sum(g_att.astype(FLOAT) * attended, axis=1, keepdims=True)
    lane = lax.broadcasted_iota(jnp.int32, raw_up.shape, 1)
    sent = raw_up * fgain
    for at, number in ((FEAT, delta), (FEAT + 3, shift)):
        for k in range(3):
            piece = number.astype(BFLOAT).astype(FLOAT)
            sent = jnp.where(lane == at + k, piece, sent)
            number = number - piece
    up_sent[ty] = sent.astype(BFLOAT)
    copies = to_ty(5, up_sent.at[ty], up_sent.at[ty])
    give_x(4, act)
    give_g(6, g_hidden)
    give_x(5, hidden)
    give_g(7, g_hlift)
    stage_two(2)
    stage_one(3)
    finish(later, gain_copies, gcross_copies)
    result_copies = hand_on(2, result_copies, result_ref)
    gain_rows = gains_all[0, 0] + gains_all[0, 1] + gains_all[0, 2] + gains_all[0, 3]
    ncopies = product_start(
        0, mix_all[...].reshape(4 * share, LANES), gcross_all[...].reshape(4 * share, 256), gain_rows
    )
    finish(copies)
    finish(xg.pop(("x", 3), ()))

    sent = up_sent[...].astype(FLOAT).reshape(4 * share, LANES)
    lane = lax.broadcasted_iota(jnp.int32, sent.shape, 1)
    delta, shift = [
        sent[:, at : at + 1] + sent[:, at + 1 : at + 2] + sent[:, at + 2 : at + 3]
        for at in (FEAT, FEAT + 3)
    ]
    up_ref[...] = jnp.where(
        lane < FEAT, sent, jnp.where(lane == FEAT, delta, shift)
    ).reshape(up_ref.shape)
    coefs_by_pixel(up_ref[...].reshape(4 * share, LANES), thigh_ref, tlow_ref, upcoefs)

    def back_step(t):
        block = take_block(t)
        ups[...] = dot_nn(upcoefs[t], pixels[...])
        for group in range(4):
            at = pl.ds(group * count, count)
            rate, bias = rate_and_bias(block, group)
            b = group % 2
            mine = up_ref[2 * b : 2 * b + 2].reshape(count, LANES)
            p = jnp.exp2(scores[at] * rate + (bias - mine[:, FEAT + 1 : FEAT + 2]))
            g = p * (ups[at] * rate - mine[:, FEAT : FEAT + 1])
            weights[at] = (g * rate).astype(BFLOAT)
        sums[t] = dot_nt(weights[...], pixels[0:GROUP])

    def first_steps(t, _):
        back_step(t)
        stage_two(3 + t)
        stage_one(4 + t)
        return 0

    def second_steps(t, _):
        back_step(t)
        stage_three(t - 4)
        return 0

    lax.fori_loop(0, 2, first_steps, 0)
    finish(xg.pop(("x", 4)), xg.pop(("x", 5)))
    lax.fori_loop(2, 3, first_steps, 0)
    ncopies = product_join(0, ncopies, value_v)
    lax.fori_loop(3, 4, first_steps, 0)
    lax.fori_loop(4, 6, second_steps, 0)
    stage_two(7)
    lax.fori_loop(6, 8, second_steps, 0)
    part_out[...] = features_of(sums, None, thigh_ref, tlow_ref).reshape(part_out.shape)
    half_out[...] = part_out[...].astype(BFLOAT)
    copies = on_ty.start(9, lambda d: half_out.at[ty_at(d)], lambda d: half_in.at[d])
    value_copies = product_end(0, ncopies, value_v, value_ref)
    unit, rate = norm_rows(lat_ref[ty].astype(FLOAT))
    raw_mix = part_out[ty]
    finish(copies)
    for d in range(3):
        raw_mix = raw_mix + half_in[d].astype(FLOAT)
    mix = (raw_mix * fgain).astype(BFLOAT)
    gmix[ty] = mix
    mcopies = to_ty(6, gmix.at[ty], gmix.at[ty])
    grad_q = (dot_nn(mix, kproj_ref[...]) * cross_scale).astype(BFLOAT)
    grad, qgain_grad = norm_rows_back(times_back(grad_q, 0), qgain_ref[...], unit, rate)
    features = feat_part + jnp.sum(raw_mix * raw_all[ty], axis=0, keepdims=True)
    for h in range(4):
        gains_out[1, h, 0:1] = qgain_grad[:, 256 * h : 256 * h + 256]
    gains_out[1, 0, 1:2] = features[:, 0:256]
    gains_out[1, 1, 1:2, 0:128] = features[:, 256:384]
    mcopies += over_ty(10, gains_out.at[1], gains_all.at[1])
    grad_v[...] = (g_one + grad).astype(BFLOAT)
    grad_copies = hand_out(3, grad_v, grad_ref)
    for w in range(4):
        stage_four(w)
    finish(mcopies)
    gain_rows = gains_all[1, 0] + gains_all[1, 1] + gains_all[1, 2] + gains_all[1, 3]
    right = qrows[:, pl.ds(pl.multiple_of(ty * 256, 256), 256)]
    mcopies = product_start(1, gmix[...].reshape(4 * share, LANES), right, gain_rows)
    stage_three(4)
    stage_three(5)
    mcopies = product_join(1, mcopies, key_v)
    value_copies = hand_on(0, value_copies, value_ref)
    grad_copies = hand_on(3, grad_copies, grad_ref)
    stage_three(6)
    stage_three(7)
    key_copies = product_end(1, mcopies, key_v, key_ref)
    for w in range(4, 8):
        stage_four(w)
    key_copies = hand_on(1, key_copies, key_ref)
    finish(result_copies, value_copies, grad_copies, key_copies)
    for w in range(8):
        stage_end(w)


IN_NAMES = (
    "pixels", "pixel_mask", "latents", "cotangent", "feature_gain", "query_gain", "hidden_gain", "tower_gain",
    "final_gain", "key_proj", "value_proj", "hot", "hotrow", "ids", "lanes",
) + tuple("w%d" % i for i in range(10))
COPIED_NAMES = (
    "pix_v", "mask_v", "lat_v", "cot_v", "fgain_v", "qgain_v", "hgain_v", "tgain_v", "ogain_v", "kraw_v", "vraw_v",
    "hot_v", "hotrow_v", "ids_v", "lanes_v",
)
OUT_NAMES = ("result_ref", "grad_ref", "value_ref", "key_ref", "sums_ref")
SCRATCH_NAMES = (
    "ws", "msgs", "pixcoefs", "upcoefs", "pixels_v", "scores", "ups", "weights", "sums", "tops", "totals",
    "raw_all", "qrows", "part_out", "part_in", "half_out", "half_in", "up_sent", "q_out", "q_in", "kv_out", "kv_in", "kv_more", "probs",
    "mixed_out", "mixed_in", "gm_out", "gm_in", "kvx_out", "kvx_in", "gq_in", "gkv_in", "up_ref", "mix_all",
    "gcross_out", "gcross_all", "gains_out", "gains_all", "gmix", "x_out", "x_all", "g_out", "g_all",
    "own", "held", "relay_in", "zsend", "zrecv", "last", "nsend", "nextra", "nrecv", "nmore", "msg_rows", "msg", "thigh", "tlow",
    "kproj", "vproj", "fgain", "result_v", "grad_v", "value_v", "key_v",
    "w_sem", "l_sem", "ty_s", "ty_r", "tx_s", "tx_r", "mate_s", "mate_r", "xg_s", "xg_r",
    "z_s", "z_r", "ac_s", "ac_r", "re_s", "re_r", "g_s", "g_r", "in_sem", "out_sem",
) + COPIED_NAMES
SINE = tuple((-1) ** n * math.pi ** (2 * n + 1) / math.factorial(2 * n + 1) for n in range(7))


def pixel_constants(high, wide):
    length = -(-high * wide // 128) * 128
    hot = np.zeros((GROUP, length), np.float32)
    ids = np.full((8, length), 1e6, np.float32)
    for i in range(high):
        for j in range(wide):
            hot[16 + i, i * wide + j] = 1.0
            hot[64 + j, i * wide + j] = 1.0
            ids[0, i * wide + j], ids[1, i * wide + j] = i, j
    lanes = np.zeros((8, LANES), np.float32)
    for axis in range(2):
        first = 5 + 2 * BANDS * axis
        lanes[0, first : first + 2 * BANDS] = np.tile(np.arange(BANDS), 2)
        lanes[1, first + BANDS : first + 2 * BANDS] = 0.5
        lanes[2 + axis, first : first + 2 * BANDS] = 1.0
        lanes[4 + axis, 3 + axis] = 1.0
    lanes[6, :FEAT] = 1.0
    rows = np.zeros((HALVES, HALVES * high, length), np.float32)
    for half in range(HALVES):
        rows[half, half * high : (half + 1) * high] = hot[16 : 16 + high]
    return jnp.asarray(hot, BFLOAT), jnp.asarray(rows, BFLOAT), jnp.asarray(ids), jnp.asarray(lanes)


def main_call(sizes, inputs, matrices):
    pixels, mask, lat, cot = inputs[:4]
    _, share, width = lat.shape
    inputs = inputs + pixel_constants(pixels.shape[3] // HALVES, pixels.shape[1])
    rows, length = 8 * share, inputs[11].shape[1]
    dma = pltpu.SemaphoreType.DMA
    hbm = pl.BlockSpec(memory_space=pl.ANY)
    shape = jax.ShapeDtypeStruct
    half, full = (lambda *s: pltpu.VMEM(s, BFLOAT)), (lambda *s: pltpu.VMEM(s, FLOAT))
    return pl.pallas_call(
        main_kernel,
        out_shape=(
            shape((4, share, width), BFLOAT),
            shape((4, share, width), BFLOAT),
            shape((4, 272, 256), BFLOAT),
            shape((4, 272, 256), BFLOAT),
            shape((8, 4, 128, 256), BFLOAT),
        ),
        in_specs=[pl.BlockSpec(memory_space=pltpu.SMEM)] + [hbm] * 25,
        out_specs=(hbm,) * 5,
        scratch_shapes=[
            half(10, width, width), half(8, 16, length), half(8, rows, 2 * GROUP), half(8, rows, 2 * GROUP),
            half(2 * GROUP, length), full(rows, length), full(rows, length), half(rows, length),
            full(8, rows, GROUP), full(8, rows, 1), full(8, rows, 1), full(4, share, LANES), half(4 * share, width),
            full(4, share, LANES), full(3, share, LANES),
            half(4, share, LANES), half(3, share, LANES), half(4, share, LANES),
            half(8, share, 128), half(8, share, 128), half(8, 2 * share, 128), half(8, 2 * share, 128),
            half(8, 2 * share, 128), full(2, rows, rows), half(8, share, 128), half(8, share, 128),
            half(8, share, 128), half(8, share, 128), half(2, rows, 128), half(2, rows, 128),
            half(8, share, 128), half(8, 2 * share, 128),
            full(4, share, LANES), half(4, share, LANES), half(4, share, 256), half(4, share, 256),
            full(2, 4, 8, 256), full(2, 4, 8, 256), half(4, share, LANES),
            half(6, 2, 4, share, 128), half(6, 4, 2, 4, share, 128),
            half(8, 4, share, 256), half(8, 2, 4, share, 256), full(8, 128, 256), full(8, 128, 256), half(8, 128, 256),
            half(8, 3, 128, 256), half(8, 3, 128, 256), half(8, 128, 256),
            half(2, 8, 32, 256), half(2, 16, 256), half(2, 7, 32, 256), half(2, 7, 16, 256),
            full(16, length), half(16, length), half(2, 10 * GROUP, LANES), half(2, 10 * GROUP, LANES),
            half(LANES, width), half(LANES, width), full(1, LANES),
            half(share, width), half(share, width), half(4, 272, 256), half(4, 272, 256),
            dma((10,)), dma((8,)), dma((12, 3)), dma((12, 3)), dma((13, 7)), dma((13, 7)),
            dma((26, 1)), dma((26, 1)), dma((14, 7)), dma((14, 7)),
            dma((8, 3)), dma((8, 3)), dma((12, 1)), dma((12, 1)), dma((8,)), dma((8,)), dma((7,)), dma((7,)), dma((15,)), dma((4,)),
        ] + [pltpu.VMEM(v.shape, v.dtype) for v in inputs],
        compiler_params=pltpu.CompilerParams(
            collective_id=1, has_side_effects=True, vmem_limit_bytes=62 << 20
        ),
        name="main",
    )(sizes, *inputs, *matrices)


def finish_kernel(*refs):
    ins, outs, stage, held = refs[:9], refs[9:28], refs[28:37], refs[37:56]
    in_sem, out_sem = refs[56:]
    copies = [pltpu.make_async_copy(a, v, in_sem.at[i]) for i, (a, v) in enumerate(zip(ins, stage))]
    for copy in copies:
        copy.start()
    tx = lax.axis_index("tx")
    sums_ref, cross_core_ref, query_core_ref, latent_ref, result_in_ref, cross_ref, query_ref, value_ref, key_ref = stage
    result_ref, latent_out, feat_out, qgain_out, query_out, key_out, value_out, cross_out = held[:8]
    written = []

    def write(*places):
        for i in places:
            written.append(pltpu.make_async_copy(held[i], outs[i], out_sem.at[i]))
            written[-1].start()

    copies[0].wait()
    for w in range(8):
        for h in range(4):
            held[8 + w][:, 256 * h : 256 * h + 256] = sums_ref[w, h].astype(FLOAT)
        write(8 + w)
    for copy in copies[1:]:
        copy.wait()
    result_ref[...] = result_in_ref[...]
    latent_out[...] = latent_ref[...].astype(FLOAT)
    write(0, 1)
    here = pl.ds(pl.multiple_of(tx * 128, 128), 128)
    quarter = tx // 2
    inside = pl.ds(pl.multiple_of(lax.rem(tx, 2) * 128, 128), 128)
    scale = 1.0 / math.sqrt(query_ref.shape[0])
    cross_core = jnp.concatenate([cross_core_ref[h] for h in range(4)], axis=1)
    query_core = jnp.concatenate([query_core_ref[h] for h in range(4)], axis=1)
    value_out[...] = dot_nt(cross_core, cross_ref[...])[:FEAT]
    write(6)
    key_out[...] = (dot_nn(query_core, query_ref[...]) * scale)[:FEAT]
    write(5)
    cross_out[...] = outer(value_ref[:, here], cross_core[:FEAT])
    mine = query_core_ref[quarter, :, inside].astype(FLOAT)
    query_out[...] = outer(mine[:FEAT].astype(BFLOAT), key_ref[...]) * scale
    write(4, 7)
    qgain_out[...] = mine[264:265]
    more = jnp.concatenate([query_core_ref[h, 256:272] for h in range(2)], axis=1).astype(FLOAT)
    feat_out[...] = more[9:10, 0:FEAT].reshape(FEAT)
    mine = cross_core_ref[quarter, 256:272, inside].astype(FLOAT)
    for i in range(3):
        held[16 + i][...] = mine[8 + i : 9 + i]
    write(2, 3, 16, 17, 18)
    for copy in written:
        copy.wait()


def finish_call(*inputs):
    width = inputs[5].shape[0]
    shape = lambda *s: jax.ShapeDtypeStruct(s, FLOAT)
    rows = inputs[3].shape
    block = [shape(128, width)]
    hbm = pl.BlockSpec(memory_space=pl.ANY)
    outs = (
        [jax.ShapeDtypeStruct(rows, BFLOAT), shape(*rows), shape(FEAT), shape(1, 128)]
        + block + [shape(FEAT, width)] * 2 + block + block * 8 + [shape(1, 128)] * 3
    )
    return pl.pallas_call(
        finish_kernel,
        out_shape=outs,
        in_specs=[hbm] * 9,
        out_specs=[hbm] * 19,
        scratch_shapes=[pltpu.VMEM(v.shape, v.dtype) for v in list(inputs) + outs]
        + [pltpu.SemaphoreType.DMA((9,)), pltpu.SemaphoreType.DMA((19,))],
        compiler_params=pltpu.CompilerParams(vmem_limit_bytes=62 << 20),
        name="finish",
    )(*inputs)


def on_device_fast(
    pixels,
    pixel_mask,
    image_sizes,
    latents,
    cotangent,
    feature_gain,
    query_gain,
    query_proj,
    key_proj,
    value_proj,
    cross_proj,
    hidden_gain,
    hidden_up,
    hidden_down,
    tower_gain,
    tower_query,
    tower_key,
    tower_value,
    tower_proj,
    final_gain,
    final_up,
    final_down,
):
    item_count = pixels.shape[0]
    tile_height = pixels.shape[2]
    tile_width = pixels.shape[3]
    model_width = latents.shape[2]
    rows_here = latents.shape[1]
    share = item_count * rows_here // 4

    def in_shares(rows):
        return rows.reshape(4, share, rows.shape[-1])

    result, latent_grad, cross_core, query_core, sums = main_call(
        image_sizes,
        (jnp.transpose(pixels, (1, 3, 0, 2)), jnp.transpose(pixel_mask, (2, 0, 1)), in_shares(latents),
         in_shares(cotangent), feature_gain, query_gain[None],
         hidden_gain[None], tower_gain[None], final_gain[None], key_proj, value_proj),
        (query_proj, cross_proj, hidden_up, hidden_down, tower_query, tower_key, tower_value,
         tower_proj, final_up, final_down),
    )
    (result, latent_grad, feature_sum, query_sum, query_grad, key_grad, value_grad, cross_grad,
     final_down_grad, final_up_grad, tower_proj_grad, tower_query_grad, tower_key_grad,
     tower_value_grad, hidden_down_grad, hidden_up_grad, hidden_sum, tower_sum, final_sum) = finish_call(
        sums, cross_core, query_core, latent_grad, result, cross_proj, query_proj, value_proj, key_proj
    )
    return (
        result.reshape(latents.shape),
        latent_grad.reshape(latents.shape),
        feature_sum,
        query_sum[0],
        query_grad,
        key_grad,
        value_grad,
        cross_grad,
        hidden_sum[0],
        hidden_up_grad,
        hidden_down_grad,
        tower_sum[0],
        tower_query_grad,
        tower_key_grad,
        tower_value_grad,
        tower_proj_grad,
        final_sum[0],
        final_up_grad,
        final_down_grad,
    )


def on_device(
    pixels,
    pixel_mask,
    image_sizes,
    latents,
    cotangent,
    feature_gain,
    query_gain,
    query_proj,
    key_proj,
    value_proj,
    cross_proj,
    hidden_gain,
    hidden_up,
    hidden_down,
    tower_gain,
    tower_query,
    tower_key,
    tower_value,
    tower_proj,
    final_gain,
    final_up,
    final_down,
):
    item_count = pixels.shape[0]
    tile_height = pixels.shape[2]
    tile_width = pixels.shape[3]
    model_width = latents.shape[2]
    rows_here = latents.shape[1]
    head_count = HEADS
    head_size = model_width // head_count
    cross_scale = 1.0 / math.sqrt(model_width)
    tower_scale = 1.0 / math.sqrt(head_size)
    row_ids = lax.axis_index("ty") * tile_height + jnp.arange(tile_height, dtype=jnp.int32)
    col_ids = lax.axis_index("tx") * tile_width + jnp.arange(tile_width, dtype=jnp.int32)
    all_cols = jnp.arange(tile_width * lax.axis_size("tx"), dtype=jnp.int32)
    wide_pixels = lax.all_gather(pixels, "tx", axis=3, tiled=True).astype(FLOAT)
    wide_mask = lax.all_gather(pixel_mask, "tx", axis=2, tiled=True)
    side_sizes = image_sizes[:, None, None]
    live = (
        (wide_mask > 0)
        & (row_ids[None, :, None] < side_sizes)
        & (all_cols[None, None, :] < side_sizes)
    )[:, None]
    row_table, row_coord, row_sum = axis_tables(image_sizes, row_ids, 3, 5)
    col_table, col_coord, col_sum = axis_tables(image_sizes, all_cols, 4, 5 + 2 * BANDS)
    pixel_mean = (
        jnp.sum(wide_pixels, axis=1) + row_sum[:, :, None] + col_sum[:, None, :]
    ) / FEAT
    pixel_square = (
        jnp.sum(wide_pixels * wide_pixels, axis=1)
        + (row_coord * row_coord)[:, :, None]
        + (col_coord * col_coord)[:, None, :]
        + 2.0 * BANDS
    ) / FEAT
    pixel_rate = lax.rsqrt(pixel_square - pixel_mean * pixel_mean + EPSILON)
    exact = lax.Precision.HIGHEST

    def against_pixels(coefs):
        by_row = jnp.einsum("blf,bif->bli", coefs, row_table, precision=exact)
        by_col = jnp.einsum("blf,bjf->blj", coefs, col_table, precision=exact)
        total = by_row[:, :, :, None] + by_col[:, :, None, :]
        for c in range(3):
            total = total + coefs[:, :, c][:, :, None, None] * wide_pixels[:, None, c]
        total = total - jnp.sum(coefs, axis=2)[:, :, None, None] * pixel_mean[:, None]
        return total * pixel_rate[:, None]

    def over_pixels(weights):
        scaled = weights * pixel_rate[:, None]
        by_row = jnp.sum(scaled, axis=3)
        by_col = jnp.sum(scaled, axis=2)
        total = jnp.einsum("bli,bif->blf", by_row, row_table, precision=exact)
        total = total + jnp.einsum("blj,bjf->blf", by_col, col_table, precision=exact)
        colour = jnp.stack(
            [jnp.sum(scaled * wide_pixels[:, None, c], axis=(2, 3)) for c in range(3)], axis=2
        )
        total = total + jnp.pad(colour, ((0, 0), (0, 0), (0, FEAT - 3)))
        return total - jnp.sum(scaled * pixel_mean[:, None], axis=(2, 3))[:, :, None]

    latent_rows = latents.astype(FLOAT)
    query_normed, back_query_norm = jax.vjp(layer_norm, latent_rows, query_gain)
    query_input = query_normed.astype(BFLOAT)
    own_queries = linear(query_input, query_proj).astype(BFLOAT)
    raw_query = linear_back(own_queries, key_proj) * cross_scale
    scores = against_pixels(raw_query * feature_gain)
    row_top = jnp.max(jnp.where(live, scores, -1e30), axis=(2, 3))
    all_top = lax.pmax(row_top, "ty")
    row_exp = jnp.where(live, jnp.exp(scores - all_top[:, :, None, None]), 0.0)
    row_total = lax.psum(jnp.sum(row_exp, axis=(2, 3)), "ty")
    cross_exact = row_exp / row_total[:, :, None, None]
    raw_mix = lax.psum(over_pixels(cross_exact), "ty")
    mix = raw_mix * feature_gain
    attended = linear(mix.astype(BFLOAT), value_proj)
    attended_input = attended.astype(BFLOAT)
    resid_one = latent_rows + linear(attended_input, cross_proj)
    hidden_normed, back_hidden_norm = jax.vjp(layer_norm, resid_one, hidden_gain)
    hidden_input = hidden_normed.astype(BFLOAT)
    hidden_lifted, back_hidden_gelu = jax.vjp(gelu_tanh, linear(hidden_input, hidden_up))
    hidden_act = hidden_lifted.astype(BFLOAT)
    resid_two = resid_one + linear(hidden_act, hidden_down)
    tower_normed, back_tower_norm = jax.vjp(layer_norm, resid_two, tower_gain)
    tower_input = tower_normed.astype(BFLOAT)
    tower_q = linear(tower_input, tower_query).astype(BFLOAT)
    tower_k = linear(tower_input, tower_key).astype(BFLOAT)
    tower_v = linear(tower_input, tower_value).astype(BFLOAT)
    all_keys, all_values = (
        lax.all_gather(tower_k, "tx", axis=1, tiled=True),
        lax.all_gather(tower_v, "tx", axis=1, tiled=True),
    )
    split_q = tower_q.reshape(item_count, rows_here, head_count, head_size)
    split_k = all_keys.reshape(item_count, -1, head_count, head_size)
    split_v = all_values.reshape(item_count, -1, head_count, head_size)
    tower_scores = (
        jnp.einsum("bqhd,bkhd->bhqk", split_q, split_k, preferred_element_type=FLOAT) * tower_scale
    )
    tower_top = jnp.max(tower_scores, axis=3, keepdims=True)
    tower_exp = jnp.exp(tower_scores - tower_top)
    tower_total = jnp.sum(tower_exp, axis=3, keepdims=True)
    tower_exact = tower_exp / tower_total
    tower_probs = tower_exact.astype(BFLOAT)
    mixed = jnp.einsum(
        "bhqk,bkhd->bqhd", tower_probs, split_v, preferred_element_type=FLOAT
    ).reshape(item_count, rows_here, model_width)
    mixed_input = mixed.astype(BFLOAT)
    resid_three = resid_two + linear(mixed_input, tower_proj)
    final_normed, back_final_norm = jax.vjp(layer_norm, resid_three, final_gain)
    final_input = final_normed.astype(BFLOAT)
    final_lifted, back_final_gelu = jax.vjp(gelu_tanh, linear(final_input, final_up))
    final_act = final_lifted.astype(BFLOAT)
    resid_four = resid_three + linear(final_act, final_down)
    grad_four = cotangent.astype(FLOAT)
    final_down_grad = weight_grad(final_act, cotangent)
    grad_final_lift = back_final_gelu(linear_back(cotangent, final_down))[0].astype(BFLOAT)
    final_up_grad = weight_grad(final_input, grad_final_lift)
    grad_rows_three, final_gain_grad = back_final_norm(linear_back(grad_final_lift, final_up))
    grad_three = grad_four + grad_rows_three
    grad_tower_out = grad_three.astype(BFLOAT)
    tower_proj_grad = weight_grad(mixed_input, grad_tower_out)
    grad_mixed_flat = linear_back(grad_tower_out, tower_proj).astype(BFLOAT)
    grad_mixed = grad_mixed_flat.reshape(item_count, rows_here, head_count, head_size)
    grad_tower_p = jnp.einsum("bqhd,bkhd->bhqk", grad_mixed, split_v, preferred_element_type=FLOAT)
    tower_delta = jnp.sum(tower_exact * grad_tower_p, axis=3, keepdims=True)
    grad_tower_scores = (tower_exact * (grad_tower_p - tower_delta)).astype(BFLOAT)
    grad_tower_q = (
        (
            jnp.einsum("bhqk,bkhd->bqhd", grad_tower_scores, split_k, preferred_element_type=FLOAT)
            * tower_scale
        )
        .astype(BFLOAT)
        .reshape(item_count, rows_here, model_width)
    )
    value_part = jnp.einsum(
        "bhqk,bqhd->bkhd", tower_probs, grad_mixed, preferred_element_type=FLOAT
    )
    key_part = (
        jnp.einsum("bhqk,bqhd->bkhd", grad_tower_scores, split_q, preferred_element_type=FLOAT)
        * tower_scale
    )
    key_sums, value_sums = (
        lax.psum_scatter(
            key_part.reshape(item_count, -1, model_width), "tx", scatter_dimension=1, tiled=True
        ),
        lax.psum_scatter(
            value_part.reshape(item_count, -1, model_width), "tx", scatter_dimension=1, tiled=True
        ),
    )
    grad_tower_k = key_sums.astype(BFLOAT)
    grad_tower_v = value_sums.astype(BFLOAT)
    tower_query_grad = weight_grad(tower_input, grad_tower_q)
    tower_key_grad = weight_grad(tower_input, grad_tower_k)
    tower_value_grad = weight_grad(tower_input, grad_tower_v)
    grad_tower_rows = (
        linear_back(grad_tower_q, tower_query)
        + linear_back(grad_tower_k, tower_key)
        + linear_back(grad_tower_v, tower_value)
    )
    grad_rows_two, tower_gain_grad = back_tower_norm(grad_tower_rows)
    grad_two = grad_three + grad_rows_two
    grad_hidden_out = grad_two.astype(BFLOAT)
    hidden_down_grad = weight_grad(hidden_act, grad_hidden_out)
    grad_hidden_lift = back_hidden_gelu(linear_back(grad_hidden_out, hidden_down))[0].astype(BFLOAT)
    hidden_up_grad = weight_grad(hidden_input, grad_hidden_lift)
    grad_rows_one, hidden_gain_grad = back_hidden_norm(linear_back(grad_hidden_lift, hidden_up))
    grad_one = grad_two + grad_rows_one
    grad_cross_out = grad_one.astype(BFLOAT)
    cross_proj_grad = weight_grad(attended_input, grad_cross_out)
    grad_attended = linear_back(grad_cross_out, cross_proj).astype(BFLOAT)
    raw_up = linear_back(grad_attended, value_proj)
    grad_probs = against_pixels(raw_up * feature_gain)
    cross_delta = jnp.sum(grad_attended.astype(FLOAT) * attended, axis=2)
    grad_scores = cross_exact * (grad_probs - cross_delta[:, :, None, None])
    raw_grad_mix = lax.psum(over_pixels(grad_scores), "ty")
    grad_mix = (raw_grad_mix * feature_gain).astype(BFLOAT)
    grad_queries = (linear(grad_mix, key_proj) * cross_scale).astype(BFLOAT)
    key_proj_grad = weight_grad(grad_mix, own_queries) * cross_scale
    value_proj_grad = weight_grad(mix.astype(BFLOAT), grad_attended)
    feature_part = jnp.sum(raw_grad_mix * raw_query + raw_mix * raw_up, axis=(0, 1))
    pixel_sums = lax.psum((key_proj_grad, value_proj_grad, feature_part), "tx")
    query_proj_grad = weight_grad(query_input, grad_queries)
    grad_latent_rows, query_gain_grad = back_query_norm(linear_back(grad_queries, query_proj))
    latent_grad = grad_one + grad_latent_rows
    summed = (
        lax.psum_scatter(query_gain_grad, "tx", scatter_dimension=0, tiled=True),
        lax.psum_scatter(query_proj_grad, "tx", scatter_dimension=0, tiled=True),
        lax.psum_scatter(cross_proj_grad, "tx", scatter_dimension=0, tiled=True),
        lax.psum_scatter(hidden_gain_grad, "tx", scatter_dimension=0, tiled=True),
        lax.psum_scatter(hidden_up_grad, "tx", scatter_dimension=0, tiled=True),
        lax.psum_scatter(hidden_down_grad, "tx", scatter_dimension=0, tiled=True),
        lax.psum_scatter(tower_gain_grad, "tx", scatter_dimension=0, tiled=True),
        lax.psum_scatter(tower_query_grad, "tx", scatter_dimension=0, tiled=True),
        lax.psum_scatter(tower_key_grad, "tx", scatter_dimension=0, tiled=True),
        lax.psum_scatter(tower_value_grad, "tx", scatter_dimension=0, tiled=True),
        lax.psum_scatter(tower_proj_grad, "tx", scatter_dimension=0, tiled=True),
        lax.psum_scatter(final_gain_grad, "tx", scatter_dimension=0, tiled=True),
        lax.psum_scatter(final_up_grad, "tx", scatter_dimension=0, tiled=True),
        lax.psum_scatter(final_down_grad, "tx", scatter_dimension=0, tiled=True),
    )
    return (
        resid_four.astype(BFLOAT),
        latent_grad,
        pixel_sums[2],
        summed[0],
        summed[1],
        pixel_sums[0],
        pixel_sums[1],
        summed[2],
        summed[3],
        summed[4],
        summed[5],
        summed[6],
        summed[7],
        summed[8],
        summed[9],
        summed[10],
        summed[11],
        summed[12],
        summed[13],
    )


def solution(mesh):
    in_specs = (
        P(None, None, "ty", "tx"),
        P(None, "ty", "tx"),
        P(),
        P(None, "tx", None),
        P(None, "tx", None),
        P(),
        P(),
        P(),
        P(),
        P(),
        P(),
        P(),
        P(),
        P(),
        P(),
        P(),
        P(),
        P(),
        P(),
        P(),
        P(),
        P(),
    )
    out_specs = (
        P(None, "tx", None),
        P(None, "tx", None),
        P(),
        P("tx"),
        P("tx", None),
        P(),
        P(),
        P("tx", None),
        P("tx"),
        P("tx", None),
        P("tx", None),
        P("tx"),
        P("tx", None),
        P("tx", None),
        P("tx", None),
        P("tx", None),
        P("tx"),
        P("tx", None),
        P("tx", None),
    )
    fits = mesh.shape["ty"] == 4 and mesh.shape["tx"] == HEADS
    plan = on_device_fast if fits else on_device
    return jax.shard_map(
        plan, mesh=mesh, in_specs=in_specs, out_specs=out_specs, check_vma=False
    )
```

```python
import math

import jax
import jax.numpy as jnp
import numpy as np
from jax import lax
from jax.experimental import pallas as pl
from jax.experimental.pallas import tpu as pltpu
from jax.sharding import PartitionSpec as P

BANDS = 64
FEAT = 261
HEADS = 8


EPSILON = 1e-05
FLOAT = jnp.float32
BFLOAT = jnp.bfloat16


def layer_norm(values, scales):
    centre = jnp.mean(values, axis=-1, keepdims=True)
    shifted = values - centre
    spread = jnp.mean(shifted * shifted, axis=-1, keepdims=True)
    return shifted * lax.rsqrt(spread + EPSILON) * scales


def gelu_tanh(values):
    cubic = values + 0.044715 * values * values * values
    return 0.5 * values * (1.0 + jnp.tanh(0.7978845608028654 * cubic))


def linear(inputs, weight):
    return lax.dot_general(
        inputs, weight, (((inputs.ndim - 1,), (0,)), ((), ())), preferred_element_type=FLOAT
    )


def linear_back(upstream, weight):
    return lax.dot_general(
        upstream, weight, (((upstream.ndim - 1,), (1,)), ((), ())), preferred_element_type=FLOAT
    )


def weight_grad(inputs, upstream):
    flat_inputs = inputs.reshape(-1, inputs.shape[-1])
    flat_upstream = upstream.reshape(-1, upstream.shape[-1])
    return lax.dot_general(
        flat_inputs, flat_upstream, (((0,), (0,)), ((), ())), preferred_element_type=FLOAT
    )


def axis_tables(image_sizes, ids, coord_lane, first_lane):
    side = image_sizes.astype(FLOAT)[:, None]
    coord = -1.0 + 2.0 * ids.astype(FLOAT)[None, :] / (side - 1.0)
    band = jnp.arange(BANDS, dtype=jnp.int32).astype(FLOAT)
    frequency = 1.0 + band[None, :] * (side * 0.5 - 1.0) / (BANDS - 1)
    angle = math.pi * coord[:, :, None] * frequency[:, None, :]
    waves = jnp.concatenate([jnp.sin(angle), jnp.cos(angle)], axis=2)
    count, length = coord.shape
    lead = jnp.zeros((count, length, coord_lane), FLOAT)
    gap = jnp.zeros((count, length, first_lane - coord_lane - 1), FLOAT)
    tail = jnp.zeros((count, length, FEAT - first_lane - 2 * BANDS), FLOAT)
    table = jnp.concatenate([lead, coord[:, :, None], gap, waves, tail], axis=2)
    return table, coord, jnp.sum(waves, axis=2) + coord


MESH = pl.DeviceIdType.MESH


def send(src, dst, send_sem, recv_sem, where):
    copy = pltpu.make_async_remote_copy(
        src_ref=src, dst_ref=dst, send_sem=send_sem, recv_sem=recv_sem,
        device_id=where, device_id_type=MESH,
    )
    copy.start()
    return copy


def greet(places):
    barrier = pltpu.get_barrier_semaphore()
    for place in places:
        pl.semaphore_signal(barrier, inc=1, device_id=place, device_id_type=MESH)
    pl.semaphore_wait(barrier, len(places))


def outer(left, right):
    return lax.dot_general(left, right, (((0,), (0,)), ((), ())), preferred_element_type=FLOAT)


LANES = 384
CUBE = 0.044715
SLOPE = 0.7978845608028654


def norm_rows(rows):
    shifted = rows - jnp.mean(rows, axis=-1, keepdims=True)
    rate = lax.rsqrt(jnp.mean(shifted * shifted, axis=-1, keepdims=True) + EPSILON)
    return shifted * rate, rate


def norm_rows_back(upstream, gain, unit, rate):
    scaled = upstream * gain
    along = jnp.mean(scaled * unit, axis=-1, keepdims=True)
    grad = rate * (scaled - jnp.mean(scaled, axis=-1, keepdims=True) - unit * along)
    return grad, jnp.sum(upstream * unit, axis=0, keepdims=True)


def gelu_pair(values):
    square = values * values
    bend = jnp.tanh(SLOPE * (values + CUBE * values * square))
    half = 0.5 * (1.0 + bend)
    slope = half + 0.5 * values * (1.0 - bend * bend) * (SLOPE * (1.0 + 3.0 * CUBE * square))
    return values * half, slope


def dot_nt(left, right):
    return lax.dot_general(left, right, (((1,), (1,)), ((), ())), preferred_element_type=FLOAT)


def dot_nn(left, right):
    return lax.dot_general(left, right, (((1,), (0,)), ((), ())), preferred_element_type=FLOAT)


HALVES = 2
GROUP = 128
LOG2E = 1.0 / math.log(2.0)


def split_two(values):
    high = values.astype(BFLOAT)
    return high, (values - high.astype(FLOAT)).astype(BFLOAT)


def dot_wide(dot, values, high, low):
    first, second = split_two(values)
    return dot(first, high) + (dot(first, low) + dot(second, high))


def coefs_by_pixel(coefs, thigh_ref, tlow_ref, into):
    count = coefs.shape[0] // 2
    for b in range(2):
        wide = dot_wide(dot_nt, coefs[b * count : (b + 1) * count], thigh_ref[b], tlow_ref[b])
        for half in range(HALVES):
            at = pl.ds((half * 2 + b) * count, count)
            rows = wide[:, half * GROUP : (half + 1) * GROUP]
            for t in range(8):
                high, low = split_two(rows + wide[:, (2 + t) * GROUP : (3 + t) * GROUP])
                into[t, at, 0:GROUP] = high
                into[t, at, GROUP : 2 * GROUP] = low


def features_of(sums, scales, thigh_ref, tlow_ref):
    count = sums.shape[1] // 4
    blocks = [sums[t] if scales is None else sums[t] * scales[t] for t in range(8)]
    joined = blocks[0]
    for block in blocks[1:]:
        joined = joined + block
    outs = []
    for b in range(2):
        first, second = pl.ds(b * count, count), (2 + b) * count
        lo, hi = slice(b * count, (b + 1) * count), slice((2 + b) * count, (3 + b) * count)
        wide = jnp.concatenate(
            [joined[lo], joined[hi]] + [block[lo] + block[hi] for block in blocks], axis=1
        )
        outs.append(dot_wide(dot_nn, wide, thigh_ref[b], tlow_ref[b]))
    return jnp.concatenate(outs, axis=0)


def rate_and_bias(block, group):
    rate = block[group % 2 * 4 + group // 2 * 8 + 3 :][:1].astype(FLOAT)
    return rate, jnp.where(rate == 0.0, -1e30, 0.0)


class Ring:
    def __init__(self, places, send_sems, recv_sems):
        self.places, self.sems = places, (send_sems, recv_sems)

    def copy(self, i, d, src, dst):
        return pltpu.make_async_remote_copy(
            src_ref=src, dst_ref=dst, send_sem=self.sems[0].at[i, d], recv_sem=self.sems[1].at[i, d],
            device_id=self.places[d], device_id_type=MESH,
        )

    def start(self, i, sources, into):
        copies = [self.copy(i, d, sources(d), into(d)) for d in range(len(self.places))]
        for copy in copies:
            copy.start()
        return copies


def finish(*groups):
    for copies in groups:
        for copy in copies:
            copy.wait()


def sin_half_turns(turns):
    whole = jnp.floor(turns + 0.5)
    part = turns - whole
    odd = whole - 2.0 * jnp.floor(whole * 0.5)
    square = part * part
    total = jnp.full_like(square, SINE[-1])
    for term in SINE[-2::-1]:
        total = total * square + term
    return part * total * (1.0 - 2.0 * odd)


def axis_rows(axis, side, first, lanes):
    place = (lax.broadcasted_iota(jnp.int32, (48, 1), 0) + first).astype(FLOAT)
    coord = -1.0 + 2.0 * place / (side - 1.0)
    here = lanes[:, 128 * axis : 128 * axis + 256]
    rate = 1.0 + here[0:1] * (side * 0.5 - 1.0) * (1.0 / (BANDS - 1))
    waves = sin_half_turns(coord * rate + here[1:2]) * here[2 + axis : 3 + axis]
    empty = jnp.zeros((48, LANES - 256), FLOAT)
    table = jnp.concatenate([empty, waves] if axis else [waves, empty], axis=1)
    total = jnp.sum(waves, axis=1, keepdims=True) + coord
    table = table + coord * lanes[4 + axis : 5 + axis] - (total * (1.0 / FEAT)) * lanes[6:7]
    return table, coord, total


def main_kernel(
    sizes_ref, *refs
):
    names = IN_NAMES + OUT_NAMES + SCRATCH_NAMES
    r = dict(zip(names, refs))
    matrices = [r["w%d" % i] for i in range(10)]
    result_ref, grad_ref, value_ref, key_ref, sums_ref = [r[n] for n in OUT_NAMES]
    (ws, msgs, pixcoefs, upcoefs, pixels, scores, ups, weights, sums, tops, totals, raw_all, qrows,
     part_out, part_in, half_out, half_in, up_sent, q_out, q_in, kv_out, kv_in, kv_more, probs, mixed_out, mixed_in, gm_out, gm_in,
     kvx_out, kvx_in, gq_in, gkv_in, up_ref, mix_all, gcross_out, gcross_all, gains_out, gains_all, gmix,
     x_out, x_all, g_out, g_all, own, held, relay_in, zsend, zrecv, last, nrest, nsend, nextra, nrecv, nmore,
     msg_rows, msg_ref, thigh_ref, tlow_ref, kproj_ref, vproj_ref, fgain_ref, result_v, grad_v, value_v, key_v,
     w_sem, l_sem, ty_s, ty_r, tx_s, tx_r, mate_s, mate_r, xg_s, xg_r, z_s, z_r, ac_s, ac_r, re_s, re_r, g_s, g_r,
     in_sem, out_sem,
     pix_v, mask_v, lat_ref, cot_ref, fgain_v, qgain_ref, hgain_ref, tgain_ref, ogain_ref,
     kraw_v, vraw_v, hot_ref, hotrow_ref, ids_ref, lanes_ref) = [r[n] for n in SCRATCH_NAMES]
    ty, tx = lax.axis_index("ty"), lax.axis_index("tx")
    z, y = tx // 2, lax.rem(tx, 2)
    tys = [{"ty": lax.rem(ty + d, 4), "tx": tx} for d in (1, 2, 3)]
    txs = [{"ty": ty, "tx": lax.rem(tx + d, 8)} for d in range(1, 8)]
    mate = {"ty": 2 * (ty // 2) + 1 - lax.rem(ty, 2), "tx": tx}
    beside = {"ty": ty, "tx": 2 * z + 1 - y}
    on_ty, on_tx = Ring(tys, ty_s, ty_r), Ring(txs, tx_s, tx_r)
    on_mate, across = Ring([mate], mate_s, mate_r), Ring([tys[1]], ac_s, ac_r)
    over = [{"ty": lax.rem(ty + d, 4), "tx": 2 * z + 1 - y} for d in range(4)]
    handing = Ring(tys + over, xg_s, xg_r)
    loads = []
    small = []
    for i, (name, into) in enumerate(zip(IN_NAMES, COPIED_NAMES)):
        small.append(pltpu.make_async_copy(r[name], r[into], in_sem.at[i]))
        small[i].start()
    for i, w in enumerate(matrices):
        loads.append(pltpu.make_async_copy(w, ws.at[i], w_sem.at[i]))
    loads[0].start()
    cross, up, down, tq, tk, tv, tproj, fup, fdown = range(1, 10)
    partners = tys + txs + over[1:]
    barrier = pltpu.get_barrier_semaphore()
    for place in partners:
        pl.semaphore_signal(barrier, inc=1, device_id=place, device_id_type=MESH)
    ty_at = lambda d: lax.rem(ty + d + 1, 4)
    tx_at = lambda d: lax.rem(tx + d + 1, 8)

    def times(rows, i):
        return dot_nn(rows, ws[i])

    def times_back(rows, i):
        return dot_nt(rows, ws[i])

    def to_ty(i, src, into):
        return on_ty.start(i, lambda d: src, lambda d: into)

    def spread(i, out, into):
        copies = on_tx.start(i, lambda d: out.at[tx_at(d)], lambda d: into.at[tx])
        into[tx] = out[tx]
        return copies

    def over_ty(i, out, into):
        copies = on_ty.start(i, lambda d: out.at[ty_at(d)], lambda d: into.at[ty])
        into[ty] = out[ty]
        return copies

    xg = {}

    def handed(i, source, into):
        return [
            handing.copy(i, k, source(k), into(0 if k < 3 else 1)) for k in range(7)
        ]

    def give_x(i, rows):
        for c in range(8):
            x_out[i, c % 2, c // 2] = rows[:, 128 * c : 128 * c + 128]
        x_all[i, :, 0, ty] = x_out[i, y]
        xg["x", i] = handed(
            i, lambda k: x_out.at[i, y if k < 3 else 1 - y], lambda slot: x_all.at[i, :, slot, ty]
        )
        for copy in xg["x", i]:
            copy.start()

    def g_copies(w):
        return handed(
            6 + w, lambda k: g_out.at[w, lax.rem(ty + k + 1, 4)], lambda slot: g_all.at[w, slot, ty]
        )

    def give_g(w, rows):
        for h in range(4):
            g_out[w, h] = rows[:, 256 * h : 256 * h + 256]
        g_all[w, 0, ty] = g_out[w, ty]
        for copy in g_copies(w):
            copy.start()

    def slot_x(w):
        return min(w, 3) + max(w - 5, 0) if isinstance(w, int) else jnp.minimum(w, 3) + jnp.maximum(w - 5, 0)

    def zcopy(w, c):
        return pltpu.make_async_remote_copy(
            src_ref=zsend.at[w, c], dst_ref=zrecv.at[w, c], send_sem=z_s.at[w, c],
            recv_sem=z_r.at[w, c], device_id={"ty": ty, "tx": 2 * lax.rem(z + c + 1, 4) + y},
            device_id_type=MESH,
        )

    at_end = (z == 0) | (z == 3)

    def relay(w):
        return pltpu.make_async_remote_copy(
            src_ref=zsend.at[w, 1], dst_ref=relay_in.at[w], send_sem=re_s.at[w], recv_sem=re_r.at[w],
            device_id={"ty": ty, "tx": 2 * (1 + z // 2) + y}, device_id_type=MESH,
        )

    def stage_one(w):
        i = slot_x(w)
        if isinstance(w, int):
            finish(xg.pop(("x", i), ()))
        finish(g_copies(w))
        right = g_all[w].reshape(256, 256)

        def part(c):
            return outer(x_all[i, lax.rem(z + c + 1, 4)].reshape(256, 128), right)

        zsend[w, 1] = part(1).astype(BFLOAT)

        @pl.when(at_end)
        def _():
            relay(w).start()

        @pl.when(jnp.logical_not(at_end))
        def _():
            zcopy(w, 1).start()

        for c, middle in ((0, 1), (2, 2)):
            total = part(c)

            @pl.when(z == middle)
            def _():
                held[w] = total

            @pl.when(z != middle)
            def _():
                zsend[w, c] = total.astype(BFLOAT)
                zcopy(w, c).start()

        own[w] = part(3)

    def stage_two(w):
        for c, middle in ((0, 1), (2, 2)):
            @pl.when(z == middle)
            def _():
                relay(w).wait_recv()
                zsend[w, c] = (held[w] + relay_in[w].astype(FLOAT)).astype(BFLOAT)
                zcopy(w, c).start()

    def out_copies(w):
        return [
            on_mate.copy(2 + w, 0, last.at[w], sums_ref.at[w, ty]),
            across.copy(w, 0, last.at[w], sums_ref.at[w, ty]),
            pltpu.make_async_copy(last.at[w], sums_ref.at[w, ty], l_sem.at[w]),
        ]

    def stage_three(w):
        total = own[w]
        for c in (0, 2):
            zcopy(w, c).wait()
            total = total + zrecv[w, c].astype(FLOAT)
        own[w] = total

        @pl.when(at_end)
        def _():
            relay(w).wait_send()
            zcopy(w, 1).wait_recv()
            own[w] = own[w] + zrecv[w, 1].astype(FLOAT)

        @pl.when(jnp.logical_not(at_end))
        def _():
            zcopy(w, 1).wait_send()

        last[w] = own[w].astype(BFLOAT)
        for copy in out_copies(w):
            copy.start()

    def stage_four(w):
        across.copy(w, 0, last.at[w], sums_ref.at[w, ty]).wait()
        there = sums_ref.at[w, lax.rem(ty + 2, 4)]
        on_mate.copy(10 + w, 0, there, there).start()

    def stage_end(w):
        there = sums_ref.at[w, lax.rem(ty + 2, 4)]
        on_mate.copy(10 + w, 0, there, there).wait()
        on_mate.copy(2 + w, 0, last.at[w], sums_ref.at[w, ty]).wait()
        pltpu.make_async_copy(last.at[w], sums_ref.at[w, ty], l_sem.at[w]).wait()

    def product_main(i, left, right):
        product = outer(left, right)
        nsend[i] = product[0:256].astype(BFLOAT).reshape(8, 32, 256)
        nrest[i] = product[256:272]
        return on_tx.start(6 + 3 * i, lambda d: nsend.at[i, tx_at(d)], lambda d: nrecv.at[i, d])

    def product_rest(i, gains):
        row = lax.broadcasted_iota(jnp.int32, (16, 256), 0)
        more = nrest[i] + jnp.where(row < 8, 0.0, jnp.concatenate([gains, gains], axis=0))
        nextra[i] = more.astype(BFLOAT)
        return on_tx.start(7 + 3 * i, lambda d: nextra.at[i], lambda d: nmore.at[i, d])

    def product_join(i, copies, into):
        finish(copies)
        main = nsend[i, tx].astype(FLOAT)
        more = nextra[i].astype(FLOAT)
        for d in range(7):
            main = main + nrecv[i, d].astype(FLOAT)
            more = more + nmore[i, d].astype(FLOAT)
        mine = pl.ds(pl.multiple_of(tx * 32, 32), 32)
        into[ty, mine] = main.astype(BFLOAT)
        into[ty, 256:272] = more.astype(BFLOAT)
        return on_tx.start(8 + 3 * i, lambda d: into.at[ty, mine], lambda d: into.at[ty, mine])

    def hand_out(k, source, out):
        mine = pltpu.make_async_copy(source, out.at[ty], out_sem.at[k])
        mine.start()
        return on_mate.start(18 + k, lambda d: source, lambda d: out.at[ty]) + [mine], across.start(
            8 + k, lambda d: source, lambda d: out.at[ty]
        )

    def hand_on(k, copies, out):
        near, far = copies
        finish(far)
        there = out.at[lax.rem(ty + 2, 4)]
        return near + on_mate.start(22 + k, lambda d: there, lambda d: there)

    def block_end(copies, into, out):
        near, far, places = [], [], []
        for k in range(8):
            if k:
                copies[k - 1].wait()
            rows = pl.ds(pl.multiple_of(lax.rem(tx + 8 - k, 8) * 32, 32), 32)
            block = into.at[ty, rows]
            near += on_mate.start(26 + k, lambda d: block, lambda d: out.at[ty, rows])
            far += across.start(12 + k, lambda d: block, lambda d: out.at[ty, rows])
            mine = pltpu.make_async_copy(block, out.at[ty, rows], out_sem.at[4 + k])
            mine.start()
            near.append(mine)
            places.append(rows)
        rows = pl.ds(256, 16)
        block = into.at[ty, rows]
        near += on_mate.start(34, lambda d: block, lambda d: out.at[ty, rows])
        far += across.start(20, lambda d: block, lambda d: out.at[ty, rows])
        mine = pltpu.make_async_copy(block, out.at[ty, rows], out_sem.at[12])
        mine.start()
        return near + [mine], far, places + [rows]

    def block_on(state, out):
        near, far, places = state
        for k in range(9):
            far[k].wait()
            there = out.at[lax.rem(ty + 2, 4), places[k]]
            near += on_mate.start(35 + k, lambda d: there, lambda d: there)
        return near

    def product_end(i, copies, into, out):
        finish(copies)
        return hand_out(i, into.at[ty], out)

    def message(k, src, at, where):
        return pltpu.make_async_remote_copy(
            src_ref=src, dst_ref=msgs.at[at], send_sem=g_s.at[k], recv_sem=g_r.at[k],
            device_id=where, device_id_type=MESH,
        )

    def message_from(k):
        far = lax.rem(z + 8 - jnp.where(k < 5, k - 1, k - 4), 4)
        return jnp.where(
            k == 0, tx, jnp.where(k == 1, 2 * z + 1 - y, 2 * far + jnp.where(k < 5, y, 1 - y))
        )

    share, width = lat_ref.shape[1], lat_ref.shape[2]
    count = 2 * share
    high, wide = pix_v.shape[3] // HALVES, pix_v.shape[1]
    for copy in small:
        copy.wait()
    lanes = lanes_ref[...]
    ids = ids_ref[...]
    sides = [jnp.zeros((1, 1), FLOAT) + sizes_ref[b].astype(FLOAT) for b in range(2)]
    colours_in, live_in = pix_v[...].astype(FLOAT), jnp.where(mask_v[...] > 0, 1.0, 0.0)
    plane_rows = -(-wide // 8) * 8
    filler = [jnp.zeros((plane_rows - wide, HALVES * high), FLOAT)] if plane_rows > wide else []
    planes = []
    for b in range(2):
        for plane in [colours_in[c, :, b, :] for c in range(3)] + [live_in[:, b, :]]:
            planes += [plane] + filler
    planes = jnp.concatenate(planes, axis=0).astype(BFLOAT)
    flat = [dot_nn(planes, hotrow_ref[half]) for half in range(HALVES)]
    row_of = lax.broadcasted_iota(jnp.int32, (plane_rows, 1), 0).astype(FLOAT)
    pick = ids[1:2] == row_of

    def flatten(plane, half):
        rows = flat[half][plane * plane_rows : (plane + 1) * plane_rows]
        return jnp.sum(jnp.where(pick, rows, 0.0), axis=0, keepdims=True)

    def put_table(b, at, rows):
        high_part, low_part = split_two(rows)
        thigh_ref[b, at : at + rows.shape[0]] = high_part
        tlow_ref[b, at : at + rows.shape[0]] = low_part

    def by_pixel(total, coord, rows):
        square = coord * coord
        total_high, total_low = split_two(total)
        square_high, square_low = split_two(square)
        left = jnp.concatenate([total_high, total_low, square_high, square_low], axis=1)
        spread_out = outer(left, rows)
        return spread_out[0:1] + spread_out[1:2], spread_out[2:3] + spread_out[3:4]

    zeros = jnp.zeros((GROUP, LANES), BFLOAT)
    lane_at = lax.broadcasted_iota(jnp.int32, (16, LANES), 1)
    row_at = lax.broadcasted_iota(jnp.int32, (16, LANES), 0)
    for b in range(2):
        _, col_coord, col_total = axis_rows(1, sides[b], tx * wide, lanes)
        col_sum, col_square = by_pixel(col_total, col_coord, hot_ref[64:112])
        for half in range(HALVES):
            first = ty * (2 * high) + half * high
            table, coord, total = axis_rows(0, sides[b], first, lanes)
            row_sum, row_square = by_pixel(total, coord, hot_ref[16:64])
            put_table(b, half * GROUP + 16, table)
            thigh_ref[b, half * GROUP + 64 : half * GROUP + GROUP] = zeros[64:]
            tlow_ref[b, half * GROUP + 64 : half * GROUP + GROUP] = zeros[64:]
            channel = row_at - (half * 8 + b * 4)
            colour = (channel >= 0) & (channel < 3)
            value = jnp.where(channel == lane_at, 1.0, 0.0) - (1.0 / FEAT) * lanes[6:7]
            put_table(b, half * GROUP, jnp.where(colour, value, 0.0))
            colours = [flatten(b * 4 + c, half) for c in range(3)]
            mean = (colours[0] + colours[1] + colours[2] + row_sum + col_sum) * (1.0 / FEAT)
            square = sum(c * c for c in colours) + row_square + col_square + 2.0 * BANDS
            rate = lax.rsqrt(square * (1.0 / FEAT) - mean * mean + EPSILON)
            side = sides[b]
            first_row = jnp.zeros((1, 1), FLOAT) + first.astype(FLOAT)
            first_col = jnp.zeros((1, 1), FLOAT) + (tx * wide).astype(FLOAT)
            live = (
                (flatten(4 * b + 3, half) > 0.5)
                & (ids[0:1] + first_row < side)
                & (ids[1:2] + first_col < side)
            )
            for c, row in enumerate(colours + [jnp.where(live, rate, 0.0)]):
                at = half * 8 + b * 4 + c
                msg_rows[at : at + 1] = row
    msg_ref[...] = msg_rows[...].astype(BFLOAT)
    pl.semaphore_wait(barrier, len(partners))
    message(0, msg_ref, tx, beside).start()
    for d in range(3):
        message(1 + d, msg_ref, tx, {"ty": ty, "tx": 2 * lax.rem(z + 1 + d, 4) + y}).start()
    msgs[tx] = msg_ref[...]
    for load in loads[1:]:
        load.start()
    for b in range(2):
        for t in range(8):
            table, _, _ = axis_rows(1, sides[b], t * wide, lanes)
            at = (2 + t) * GROUP
            thigh_ref[b, at : at + 64] = zeros[:64]
            tlow_ref[b, at : at + 64] = zeros[:64]
            put_table(b, at + 64, table)
            thigh_ref[b, at + 112 : at + GROUP] = zeros[:16]
            tlow_ref[b, at + 112 : at + GROUP] = zeros[:16]
    for raw_ref, padded in ((kraw_v, kproj_ref), (vraw_v, vproj_ref)):
        padded[0:256] = raw_ref[0:256]
        padded[256:272] = jnp.concatenate(
            [raw_ref[256:FEAT].astype(FLOAT), jnp.zeros((272 - FEAT, width), FLOAT)], axis=0
        ).astype(BFLOAT)
        padded[272:LANES] = jnp.zeros((LANES - 272, width), BFLOAT)
    fgain_ref[...] = jnp.zeros_like(fgain_ref)
    fgain_ref[:, 0:FEAT] = fgain_v[...].reshape(1, FEAT)
    pixels[0:GROUP] = hot_ref[...]
    pixels[GROUP : 2 * GROUP] = hot_ref[...]
    gains_out[...] = jnp.zeros_like(gains_out)
    cot = cot_ref[ty]
    give_g(0, cot)
    fgain = fgain_ref[...]
    unit, _ = norm_rows(lat_ref[...].reshape(4 * share, width).astype(FLOAT))
    rows = (unit * qgain_ref[...]).astype(BFLOAT)
    qrows[...] = rows
    finish(loads[:1])
    queries = times(rows, 0).astype(BFLOAT)
    cross_scale = 1.0 / math.sqrt(width)
    raw = dot_nt(queries, kproj_ref[...]) * cross_scale
    raw_all[...] = raw.reshape(raw_all.shape)
    coefs_by_pixel(raw * (fgain * LOG2E), thigh_ref, tlow_ref, pixcoefs)

    def take_block(t):
        block = msgs[t]
        pixels[0:16] = block
        pixels[GROUP : GROUP + 16] = block
        scores[...] = dot_nn(pixcoefs[t], pixels[...])
        return block

    def front_step(k, _):
        t = message_from(k)

        @pl.when(k > 0)
        def _():
            message(k - 1, msg_ref, tx, beside).wait()

        @pl.when((k > 1) & (k < 5))
        def _():
            message(k + 2, msgs.at[t], t, beside).start()

        block = take_block(t)
        for group in range(4):
            at = pl.ds(group * count, count)
            rate, bias = rate_and_bias(block, group)
            s = scores[at] * rate + bias
            top = jnp.max(s, axis=1, keepdims=True)
            e = jnp.exp2(s - top)
            tops[t, at] = top
            totals[t, at] = jnp.sum(e, axis=1, keepdims=True)
            weights[at] = (e * rate).astype(BFLOAT)
        sums[t] = dot_nt(weights[...], pixels[0:GROUP])
        return 0

    lax.fori_loop(0, 8, front_step, 0)
    top = tops[0]
    for t in range(1, 8):
        top = jnp.maximum(top, tops[t])
    top = jnp.maximum(top[: 2 * count], top[2 * count :])
    both = jnp.concatenate([top, top], axis=0)
    scales = [jnp.exp2(tops[t] - both) for t in range(8)]
    total = sum(totals[t] * scales[t] for t in range(8))
    total = total[: 2 * count] + total[2 * count :]
    feats = features_of(sums, scales, thigh_ref, tlow_ref)
    lane = lax.broadcasted_iota(jnp.int32, feats.shape, 1)
    part_out[...] = jnp.where(
        lane < FEAT, feats, jnp.where(lane == FEAT, total, top)
    ).reshape(part_out.shape)

    copies = on_ty.start(0, lambda d: part_out.at[ty_at(d)], lambda d: part_in.at[d])
    latent = lat_ref[ty].astype(FLOAT)
    parts = [part_out[ty]]
    finish(copies)
    parts += [part_in[d] for d in range(3)]
    tops_in = [p[:, FEAT + 1 : FEAT + 2] for p in parts]
    top = jnp.maximum(
        jnp.maximum(tops_in[0], tops_in[1]), jnp.maximum(tops_in[2], tops_in[3])
    )
    joined = sum(p * jnp.exp2(t - top) for p, t in zip(parts, tops_in))
    total = joined[:, FEAT : FEAT + 1]
    raw_mix = joined / total
    shift = top + jnp.log2(total)
    mix = (raw_mix * fgain).astype(BFLOAT)
    mix_all[ty] = mix
    later = to_ty(1, mix_all.at[ty], mix_all.at[ty])
    attended = dot_nn(mix, vproj_ref[...])
    finish(loads[1:])
    one = latent + times(attended.astype(BFLOAT), cross)
    h_unit, h_rate = norm_rows(one)
    hidden = (h_unit * hgain_ref[...]).astype(BFLOAT)
    act, act_slope = gelu_pair(times(hidden, up))
    act = act.astype(BFLOAT)
    two = one + times(act, down)
    t_unit, t_rate = norm_rows(two)
    trows = (t_unit * tgain_ref[...]).astype(BFLOAT)
    for s, i in enumerate((tk, tv)):
        value = times(trows, i).astype(BFLOAT)
        for h in range(8):
            kv_out[h, 32 * s : 32 * s + 32] = value[:, 128 * h : 128 * h + 128]
    kv_copies = spread(1, kv_out, kv_in)
    value = times(trows, tq).astype(BFLOAT)
    for h in range(8):
        q_out[h] = value[:, 128 * h : 128 * h + 128]
    q_copies = spread(2, q_out, q_in)
    give_x(3, trows)
    back_four = times_back(cot, fdown)
    finish(kv_copies)
    copies = on_mate.start(0, lambda d: kv_in, lambda d: kv_more)
    finish(q_copies)
    q = q_in[...].reshape(8 * share, 128)
    k1 = kv_in[:, 0:32].reshape(8 * share, 128)
    v1 = kv_in[:, 32:64].reshape(8 * share, 128)
    scale = 1.0 / math.sqrt(128)
    s1 = dot_nt(q, k1) * scale
    finish(copies)
    k2 = kv_more[:, 0:32].reshape(8 * share, 128)
    v2 = kv_more[:, 32:64].reshape(8 * share, 128)
    s2 = dot_nt(q, k2) * scale
    stop = jnp.maximum(jnp.max(s1, axis=1, keepdims=True), jnp.max(s2, axis=1, keepdims=True))
    e1, e2 = jnp.exp(s1 - stop), jnp.exp(s2 - stop)
    rate = 1.0 / (jnp.sum(e1, axis=1, keepdims=True) + jnp.sum(e2, axis=1, keepdims=True))
    p1, p2 = e1 * rate, e2 * rate
    probs[0] = p1
    probs[1] = p2
    mixed_out[...] = (
        (dot_nn(p1.astype(BFLOAT), v1) + dot_nn(p2.astype(BFLOAT), v2))
        .astype(BFLOAT)
        .reshape(8, share, 128)
    )
    copies = spread(3, mixed_out, mixed_in)
    finish(copies)
    mixed = jnp.concatenate([mixed_in[h] for h in range(8)], axis=1)
    give_x(2, mixed)
    three = two + times(mixed, tproj)
    o_unit, o_rate = norm_rows(three)
    ogain = ogain_ref[...]
    frows = (o_unit * ogain).astype(BFLOAT)
    give_x(1, frows)
    fact, fact_slope = gelu_pair(times(frows, fup))
    fact = fact.astype(BFLOAT)

    def put_gain(row, grad):
        for h in range(4):
            gains_out[0, h, row : row + 1] = grad[:, 256 * h : 256 * h + 256]

    g_lift = (back_four * fact_slope).astype(BFLOAT)
    give_g(1, g_lift)
    g_three, o_grad = norm_rows_back(times_back(g_lift, fup), ogain, o_unit, o_rate)
    put_gain(2, o_grad)
    g_three = cot.astype(FLOAT) + g_three
    g_tower = g_three.astype(BFLOAT)
    g_mixed = times_back(g_tower, tproj).astype(BFLOAT)
    for h in range(8):
        gm_out[h] = g_mixed[:, 128 * h : 128 * h + 128]
    copies = spread(4, gm_out, gm_in)
    give_g(2, g_tower)
    result_v[...] = (three + times(fact, fdown)).astype(BFLOAT)
    result_copies = hand_out(2, result_v, result_ref)
    finish(copies)
    give_x(0, fact)
    gm = gm_in[...].reshape(8 * share, 128)
    q = q_in[...].reshape(8 * share, 128)
    k1 = kv_in[:, 0:32].reshape(8 * share, 128)
    v1 = kv_in[:, 32:64].reshape(8 * share, 128)
    k2 = kv_more[:, 0:32].reshape(8 * share, 128)
    v2 = kv_more[:, 32:64].reshape(8 * share, 128)
    p1, p2 = probs[0], probs[1]
    gp1, gp2 = dot_nt(gm, v1), dot_nt(gm, v2)
    away = jnp.sum(p1 * gp1, axis=1, keepdims=True) + jnp.sum(p2 * gp2, axis=1, keepdims=True)
    gs1 = (p1 * (gp1 - away)).astype(BFLOAT)
    gs2 = (p2 * (gp2 - away)).astype(BFLOAT)
    kvx_out[0] = (outer(gs2, q) * scale).astype(BFLOAT)
    kvx_out[1] = outer(p2.astype(BFLOAT), gm).astype(BFLOAT)
    copies = on_mate.start(1, lambda d: kvx_out, lambda d: kvx_in)
    gq = (dot_nn(gs1, k1) + dot_nn(gs2, k2)) * scale
    q_out[...] = gq.astype(BFLOAT).reshape(8, share, 128)
    q_copies = spread(5, q_out, gq_in)
    gk = outer(gs1, q) * scale
    gv = outer(p1.astype(BFLOAT), gm)
    finish(copies)
    kv_out[:, 0:32] = (gk + kvx_in[0].astype(FLOAT)).astype(BFLOAT).reshape(8, share, 128)
    kv_out[:, 32:64] = (gv + kvx_in[1].astype(FLOAT)).astype(BFLOAT).reshape(8, share, 128)
    kv_copies = spread(12, kv_out, gkv_in)
    stage_one(0)
    finish(q_copies)
    value = jnp.concatenate([gq_in[h] for h in range(8)], axis=1)
    give_g(3, value)
    g_trows = times_back(value, tq)
    finish(kv_copies)
    for s, i in enumerate((tk, tv)):
        value = jnp.concatenate([gkv_in[h, 32 * s : 32 * s + 32] for h in range(8)], axis=1)
        give_g(4 + s, value)
        g_trows = g_trows + times_back(value, i)
    g_two, t_grad = norm_rows_back(g_trows, tgain_ref[...], t_unit, t_rate)
    put_gain(1, t_grad)
    g_two = g_three + g_two
    g_hidden = g_two.astype(BFLOAT)
    stage_two(0)
    stage_one(1)
    g_hlift = (times_back(g_hidden, down) * act_slope).astype(BFLOAT)
    stage_two(1)
    stage_one(2)
    g_one, h_grad = norm_rows_back(times_back(g_hlift, up), hgain_ref[...], h_unit, h_rate)
    put_gain(0, h_grad)
    gain_copies = over_ty(3, gains_out.at[0], gains_all.at[0])
    g_one = g_two + g_one
    g_cross = g_one.astype(BFLOAT)
    for h in range(4):
        gcross_out[h] = g_cross[:, 256 * h : 256 * h + 256]
    gcross_copies = over_ty(4, gcross_out, gcross_all)
    g_att = times_back(g_cross, cross).astype(BFLOAT)
    raw_up = dot_nt(g_att, vproj_ref[...])
    feat_part = jnp.sum(raw_mix * raw_up, axis=0, keepdims=True)
    delta = jnp.sum(g_att.astype(FLOAT) * attended, axis=1, keepdims=True)
    lane = lax.broadcasted_iota(jnp.int32, raw_up.shape, 1)
    sent = raw_up * fgain
    for at, number in ((FEAT, delta), (FEAT + 3, shift)):
        for k in range(3):
            piece = number.astype(BFLOAT).astype(FLOAT)
            sent = jnp.where(lane == at + k, piece, sent)
            number = number - piece
    up_sent[ty] = sent.astype(BFLOAT)
    copies = to_ty(5, up_sent.at[ty], up_sent.at[ty])
    give_x(4, act)
    give_g(6, g_hidden)
    give_x(5, hidden)
    give_g(7, g_hlift)
    stage_two(2)
    stage_one(3)
    finish(later, gain_copies, gcross_copies)
    result_copies = hand_on(2, result_copies, result_ref)
    gain_rows = gains_all[0, 0] + gains_all[0, 1] + gains_all[0, 2] + gains_all[0, 3]
    ncopies = product_main(
        0, mix_all[...].reshape(4 * share, LANES), gcross_all[...].reshape(4 * share, 256)
    ) + product_rest(0, gain_rows)
    finish(copies)
    finish(xg.pop(("x", 3), ()))

    sent = up_sent[...].astype(FLOAT).reshape(4 * share, LANES)
    lane = lax.broadcasted_iota(jnp.int32, sent.shape, 1)
    delta, shift = [
        sent[:, at : at + 1] + sent[:, at + 1 : at + 2] + sent[:, at + 2 : at + 3]
        for at in (FEAT, FEAT + 3)
    ]
    up_ref[...] = jnp.where(
        lane < FEAT, sent, jnp.where(lane == FEAT, delta, shift)
    ).reshape(up_ref.shape)
    coefs_by_pixel(up_ref[...].reshape(4 * share, LANES), thigh_ref, tlow_ref, upcoefs)

    def back_step(t):
        block = take_block(t)
        ups[...] = dot_nn(upcoefs[t], pixels[...])
        for group in range(4):
            at = pl.ds(group * count, count)
            rate, bias = rate_and_bias(block, group)
            b = group % 2
            mine = up_ref[2 * b : 2 * b + 2].reshape(count, LANES)
            p = jnp.exp2(scores[at] * rate + (bias - mine[:, FEAT + 1 : FEAT + 2]))
            g = p * (ups[at] * rate - mine[:, FEAT : FEAT + 1])
            weights[at] = (g * rate).astype(BFLOAT)
        sums[t] = dot_nt(weights[...], pixels[0:GROUP])

    def first_steps(t, _):
        back_step(t)
        stage_two(3 + t)
        stage_one(4 + t)
        return 0

    def second_steps(t, _):
        back_step(t)
        stage_three(t - 4)
        return 0

    lax.fori_loop(0, 2, first_steps, 0)
    finish(xg.pop(("x", 4)), xg.pop(("x", 5)))
    lax.fori_loop(2, 3, first_steps, 0)
    ncopies = product_join(0, ncopies, value_v)
    back_step(3)
    stage_two(6)
    lax.fori_loop(4, 8, second_steps, 0)
    part_out[...] = features_of(sums, None, thigh_ref, tlow_ref).reshape(part_out.shape)
    half_out[...] = part_out[...].astype(BFLOAT)
    copies = on_ty.start(9, lambda d: half_out.at[ty_at(d)], lambda d: half_in.at[d])
    value_copies = product_end(0, ncopies, value_v, value_ref)
    unit, rate = norm_rows(lat_ref[ty].astype(FLOAT))
    raw_mix = part_out[ty]
    finish(copies)
    for d in range(3):
        raw_mix = raw_mix + half_in[d].astype(FLOAT)
    mix = (raw_mix * fgain).astype(BFLOAT)
    gmix[ty] = mix
    mcopies = to_ty(6, gmix.at[ty], gmix.at[ty])
    grad_q = (dot_nn(mix, kproj_ref[...]) * cross_scale).astype(BFLOAT)
    finish(mcopies)
    right = qrows[:, pl.ds(pl.multiple_of(ty * 256, 256), 256)]
    mcopies = product_main(1, gmix[...].reshape(4 * share, LANES), right)
    stage_one(7)
    grad, qgain_grad = norm_rows_back(times_back(grad_q, 0), qgain_ref[...], unit, rate)
    features = feat_part + jnp.sum(raw_mix * raw_all[ty], axis=0, keepdims=True)
    for h in range(4):
        gains_out[1, h, 0:1] = qgain_grad[:, 256 * h : 256 * h + 256]
    gains_out[1, 0, 1:2] = features[:, 0:256]
    gains_out[1, 1, 1:2, 0:128] = features[:, 256:384]
    gain_copies = over_ty(10, gains_out.at[1], gains_all.at[1])
    grad_v[...] = (g_one + grad).astype(BFLOAT)
    grad_copies = hand_out(3, grad_v, grad_ref)
    for w in range(4):
        stage_four(w)
    finish(gain_copies)
    gain_rows = gains_all[1, 0] + gains_all[1, 1] + gains_all[1, 2] + gains_all[1, 3]
    mcopies += product_rest(1, gain_rows)
    stage_three(4)
    stage_three(5)
    stage_two(7)
    mcopies = product_join(1, mcopies, key_v)
    value_copies = hand_on(0, value_copies, value_ref)
    grad_copies = hand_on(3, grad_copies, grad_ref)
    stage_three(6)
    stage_three(7)
    key_copies = block_end(mcopies, key_v, key_ref)
    for w in range(4, 6):
        stage_four(w)
    key_copies = block_on(key_copies, key_ref)
    for w in range(6, 8):
        stage_four(w)
    finish(result_copies, value_copies, grad_copies, key_copies)
    for w in range(8):
        stage_end(w)


IN_NAMES = (
    "pixels", "pixel_mask", "latents", "cotangent", "feature_gain", "query_gain", "hidden_gain", "tower_gain",
    "final_gain", "key_proj", "value_proj", "hot", "hotrow", "ids", "lanes",
) + tuple("w%d" % i for i in range(10))
COPIED_NAMES = (
    "pix_v", "mask_v", "lat_v", "cot_v", "fgain_v", "qgain_v", "hgain_v", "tgain_v", "ogain_v", "kraw_v", "vraw_v",
    "hot_v", "hotrow_v", "ids_v", "lanes_v",
)
OUT_NAMES = ("result_ref", "grad_ref", "value_ref", "key_ref", "sums_ref")
SCRATCH_NAMES = (
    "ws", "msgs", "pixcoefs", "upcoefs", "pixels_v", "scores", "ups", "weights", "sums", "tops", "totals",
    "raw_all", "qrows", "part_out", "part_in", "half_out", "half_in", "up_sent", "q_out", "q_in", "kv_out", "kv_in", "kv_more", "probs",
    "mixed_out", "mixed_in", "gm_out", "gm_in", "kvx_out", "kvx_in", "gq_in", "gkv_in", "up_ref", "mix_all",
    "gcross_out", "gcross_all", "gains_out", "gains_all", "gmix", "x_out", "x_all", "g_out", "g_all",
    "own", "held", "relay_in", "zsend", "zrecv", "last", "nrest", "nsend", "nextra", "nrecv", "nmore", "msg_rows", "msg", "thigh", "tlow",
    "kproj", "vproj", "fgain", "result_v", "grad_v", "value_v", "key_v",
    "w_sem", "l_sem", "ty_s", "ty_r", "tx_s", "tx_r", "mate_s", "mate_r", "xg_s", "xg_r",
    "z_s", "z_r", "ac_s", "ac_r", "re_s", "re_r", "g_s", "g_r", "in_sem", "out_sem",
) + COPIED_NAMES
SINE = tuple((-1) ** n * math.pi ** (2 * n + 1) / math.factorial(2 * n + 1) for n in range(7))


def pixel_constants(high, wide):
    length = -(-high * wide // 128) * 128
    hot = np.zeros((GROUP, length), np.float32)
    ids = np.full((8, length), 1e6, np.float32)
    for i in range(high):
        for j in range(wide):
            hot[16 + i, i * wide + j] = 1.0
            hot[64 + j, i * wide + j] = 1.0
            ids[0, i * wide + j], ids[1, i * wide + j] = i, j
    lanes = np.zeros((8, LANES), np.float32)
    for axis in range(2):
        first = 5 + 2 * BANDS * axis
        lanes[0, first : first + 2 * BANDS] = np.tile(np.arange(BANDS), 2)
        lanes[1, first + BANDS : first + 2 * BANDS] = 0.5
        lanes[2 + axis, first : first + 2 * BANDS] = 1.0
        lanes[4 + axis, 3 + axis] = 1.0
    lanes[6, :FEAT] = 1.0
    rows = np.zeros((HALVES, HALVES * high, length), np.float32)
    for half in range(HALVES):
        rows[half, half * high : (half + 1) * high] = hot[16 : 16 + high]
    return jnp.asarray(hot, BFLOAT), jnp.asarray(rows, BFLOAT), jnp.asarray(ids), jnp.asarray(lanes)


def main_call(sizes, inputs, matrices):
    pixels, mask, lat, cot = inputs[:4]
    _, share, width = lat.shape
    inputs = inputs + pixel_constants(pixels.shape[3] // HALVES, pixels.shape[1])
    rows, length = 8 * share, inputs[11].shape[1]
    dma = pltpu.SemaphoreType.DMA
    hbm = pl.BlockSpec(memory_space=pl.ANY)
    shape = jax.ShapeDtypeStruct
    half, full = (lambda *s: pltpu.VMEM(s, BFLOAT)), (lambda *s: pltpu.VMEM(s, FLOAT))
    return pl.pallas_call(
        main_kernel,
        out_shape=(
            shape((4, share, width), BFLOAT),
            shape((4, share, width), BFLOAT),
            shape((4, 272, 256), BFLOAT),
            shape((4, 272, 256), BFLOAT),
            shape((8, 4, 128, 256), BFLOAT),
        ),
        in_specs=[pl.BlockSpec(memory_space=pltpu.SMEM)] + [hbm] * 25,
        out_specs=(hbm,) * 5,
        scratch_shapes=[
            half(10, width, width), half(8, 16, length), half(8, rows, 2 * GROUP), half(8, rows, 2 * GROUP),
            half(2 * GROUP, length), full(rows, length), full(rows, length), half(rows, length),
            full(8, rows, GROUP), full(8, rows, 1), full(8, rows, 1), full(4, share, LANES), half(4 * share, width),
            full(4, share, LANES), full(3, share, LANES),
            half(4, share, LANES), half(3, share, LANES), half(4, share, LANES),
            half(8, share, 128), half(8, share, 128), half(8, 2 * share, 128), half(8, 2 * share, 128),
            half(8, 2 * share, 128), full(2, rows, rows), half(8, share, 128), half(8, share, 128),
            half(8, share, 128), half(8, share, 128), half(2, rows, 128), half(2, rows, 128),
            half(8, share, 128), half(8, 2 * share, 128),
            full(4, share, LANES), half(4, share, LANES), half(4, share, 256), half(4, share, 256),
            full(2, 4, 8, 256), full(2, 4, 8, 256), half(4, share, LANES),
            half(6, 2, 4, share, 128), half(6, 4, 2, 4, share, 128),
            half(8, 4, share, 256), half(8, 2, 4, share, 256), full(8, 128, 256), full(8, 128, 256), half(8, 128, 256),
            half(8, 3, 128, 256), half(8, 3, 128, 256), half(8, 128, 256),
            full(2, 16, 256), half(2, 8, 32, 256), half(2, 16, 256), half(2, 7, 32, 256), half(2, 7, 16, 256),
            full(16, length), half(16, length), half(2, 10 * GROUP, LANES), half(2, 10 * GROUP, LANES),
            half(LANES, width), half(LANES, width), full(1, LANES),
            half(share, width), half(share, width), half(4, 272, 256), half(4, 272, 256),
            dma((10,)), dma((8,)), dma((12, 3)), dma((12, 3)), dma((13, 7)), dma((13, 7)),
            dma((44, 1)), dma((44, 1)), dma((14, 7)), dma((14, 7)),
            dma((8, 3)), dma((8, 3)), dma((21, 1)), dma((21, 1)), dma((8,)), dma((8,)), dma((7,)), dma((7,)), dma((15,)), dma((13,)),
        ] + [pltpu.VMEM(v.shape, v.dtype) for v in inputs],
        compiler_params=pltpu.CompilerParams(
            collective_id=1, has_side_effects=True, vmem_limit_bytes=62 << 20
        ),
        name="main",
    )(sizes, *inputs, *matrices)


def finish_kernel(*refs):
    ins, outs, stage, held = refs[:9], refs[9:28], refs[28:37], refs[37:56]
    in_sem, out_sem = refs[56:]
    copies = [pltpu.make_async_copy(a, v, in_sem.at[i]) for i, (a, v) in enumerate(zip(ins, stage))]
    for i in (1, 5, 2, 6, 7, 8, 0, 4, 3):
        copies[i].start()
    tx = lax.axis_index("tx")
    sums_ref, cross_core_ref, query_core_ref, latent_ref, result_in_ref, cross_ref, query_ref, value_ref, key_ref = stage
    result_ref, latent_out, feat_out, qgain_out, query_out, key_out, value_out, cross_out = held[:8]
    written = []

    def write(*places):
        for i in places:
            written.append(pltpu.make_async_copy(held[i], outs[i], out_sem.at[i]))
            written[-1].start()

    here = pl.ds(pl.multiple_of(tx * 128, 128), 128)
    quarter = tx // 2
    inside = pl.ds(pl.multiple_of(lax.rem(tx, 2) * 128, 128), 128)
    scale = 1.0 / math.sqrt(query_ref.shape[0])
    copies[1].wait()
    copies[5].wait()
    cross_core = jnp.concatenate([cross_core_ref[h] for h in range(4)], axis=1)
    value_out[...] = dot_nt(cross_core, cross_ref[...])[:FEAT]
    write(6)
    copies[2].wait()
    copies[6].wait()
    query_core = jnp.concatenate([query_core_ref[h] for h in range(4)], axis=1)
    key_out[...] = (dot_nn(query_core, query_ref[...]) * scale)[:FEAT]
    write(5)
    copies[7].wait()
    cross_out[...] = outer(value_ref[:, here], cross_core[:FEAT])
    write(7)
    copies[8].wait()
    mine = query_core_ref[quarter, :, inside].astype(FLOAT)
    query_out[...] = outer(mine[:FEAT].astype(BFLOAT), key_ref[...]) * scale
    qgain_out[...] = mine[264:265]
    more = jnp.concatenate([query_core_ref[h, 256:272] for h in range(2)], axis=1).astype(FLOAT)
    feat_out[...] = more[9:10, 0:FEAT].reshape(FEAT)
    mine = cross_core_ref[quarter, 256:272, inside].astype(FLOAT)
    for i in range(3):
        held[16 + i][...] = mine[8 + i : 9 + i]
    write(4, 2, 3, 16, 17, 18)
    copies[0].wait()
    for w in range(8):
        for h in range(4):
            held[8 + w][:, 256 * h : 256 * h + 256] = sums_ref[w, h].astype(FLOAT)
        write(8 + w)
    copies[4].wait()
    copies[3].wait()
    result_ref[...] = result_in_ref[...]
    latent_out[...] = latent_ref[...].astype(FLOAT)
    write(0, 1)
    for copy in written:
        copy.wait()


def finish_call(*inputs):
    width = inputs[5].shape[0]
    shape = lambda *s: jax.ShapeDtypeStruct(s, FLOAT)
    rows = inputs[3].shape
    block = [shape(128, width)]
    hbm = pl.BlockSpec(memory_space=pl.ANY)
    outs = (
        [jax.ShapeDtypeStruct(rows, BFLOAT), shape(*rows), shape(FEAT), shape(1, 128)]
        + block + [shape(FEAT, width)] * 2 + block + block * 8 + [shape(1, 128)] * 3
    )
    return pl.pallas_call(
        finish_kernel,
        out_shape=outs,
        in_specs=[hbm] * 9,
        out_specs=[hbm] * 19,
        scratch_shapes=[pltpu.VMEM(v.shape, v.dtype) for v in list(inputs) + outs]
        + [pltpu.SemaphoreType.DMA((9,)), pltpu.SemaphoreType.DMA((19,))],
        compiler_params=pltpu.CompilerParams(vmem_limit_bytes=62 << 20),
        name="finish",
    )(*inputs)


def on_device_fast(
    pixels,
    pixel_mask,
    image_sizes,
    latents,
    cotangent,
    feature_gain,
    query_gain,
    query_proj,
    key_proj,
    value_proj,
    cross_proj,
    hidden_gain,
    hidden_up,
    hidden_down,
    tower_gain,
    tower_query,
    tower_key,
    tower_value,
    tower_proj,
    final_gain,
    final_up,
    final_down,
):
    item_count = pixels.shape[0]
    tile_height = pixels.shape[2]
    tile_width = pixels.shape[3]
    model_width = latents.shape[2]
    rows_here = latents.shape[1]
    share = item_count * rows_here // 4

    def in_shares(rows):
        return rows.reshape(4, share, rows.shape[-1])

    result, latent_grad, cross_core, query_core, sums = main_call(
        image_sizes,
        (jnp.transpose(pixels, (1, 3, 0, 2)), jnp.transpose(pixel_mask, (2, 0, 1)), in_shares(latents),
         in_shares(cotangent), feature_gain, query_gain[None],
         hidden_gain[None], tower_gain[None], final_gain[None], key_proj, value_proj),
        (query_proj, cross_proj, hidden_up, hidden_down, tower_query, tower_key, tower_value,
         tower_proj, final_up, final_down),
    )
    (result, latent_grad, feature_sum, query_sum, query_grad, key_grad, value_grad, cross_grad,
     final_down_grad, final_up_grad, tower_proj_grad, tower_query_grad, tower_key_grad,
     tower_value_grad, hidden_down_grad, hidden_up_grad, hidden_sum, tower_sum, final_sum) = finish_call(
        sums, cross_core, query_core, latent_grad, result, cross_proj, query_proj, value_proj, key_proj
    )
    return (
        result.reshape(latents.shape),
        latent_grad.reshape(latents.shape),
        feature_sum,
        query_sum[0],
        query_grad,
        key_grad,
        value_grad,
        cross_grad,
        hidden_sum[0],
        hidden_up_grad,
        hidden_down_grad,
        tower_sum[0],
        tower_query_grad,
        tower_key_grad,
        tower_value_grad,
        tower_proj_grad,
        final_sum[0],
        final_up_grad,
        final_down_grad,
    )


def on_device(
    pixels,
    pixel_mask,
    image_sizes,
    latents,
    cotangent,
    feature_gain,
    query_gain,
    query_proj,
    key_proj,
    value_proj,
    cross_proj,
    hidden_gain,
    hidden_up,
    hidden_down,
    tower_gain,
    tower_query,
    tower_key,
    tower_value,
    tower_proj,
    final_gain,
    final_up,
    final_down,
):
    item_count = pixels.shape[0]
    tile_height = pixels.shape[2]
    tile_width = pixels.shape[3]
    model_width = latents.shape[2]
    rows_here = latents.shape[1]
    head_count = HEADS
    head_size = model_width // head_count
    cross_scale = 1.0 / math.sqrt(model_width)
    tower_scale = 1.0 / math.sqrt(head_size)
    row_ids = lax.axis_index("ty") * tile_height + jnp.arange(tile_height, dtype=jnp.int32)
    col_ids = lax.axis_index("tx") * tile_width + jnp.arange(tile_width, dtype=jnp.int32)
    all_cols = jnp.arange(tile_width * lax.axis_size("tx"), dtype=jnp.int32)
    wide_pixels = lax.all_gather(pixels, "tx", axis=3, tiled=True).astype(FLOAT)
    wide_mask = lax.all_gather(pixel_mask, "tx", axis=2, tiled=True)
    side_sizes = image_sizes[:, None, None]
    live = (
        (wide_mask > 0)
        & (row_ids[None, :, None] < side_sizes)
        & (all_cols[None, None, :] < side_sizes)
    )[:, None]
    row_table, row_coord, row_sum = axis_tables(image_sizes, row_ids, 3, 5)
    col_table, col_coord, col_sum = axis_tables(image_sizes, all_cols, 4, 5 + 2 * BANDS)
    pixel_mean = (
        jnp.sum(wide_pixels, axis=1) + row_sum[:, :, None] + col_sum[:, None, :]
    ) / FEAT
    pixel_square = (
        jnp.sum(wide_pixels * wide_pixels, axis=1)
        + (row_coord * row_coord)[:, :, None]
        + (col_coord * col_coord)[:, None, :]
        + 2.0 * BANDS
    ) / FEAT
    pixel_rate = lax.rsqrt(pixel_square - pixel_mean * pixel_mean + EPSILON)
    exact = lax.Precision.HIGHEST

    def against_pixels(coefs):
        by_row = jnp.einsum("blf,bif->bli", coefs, row_table, precision=exact)
        by_col = jnp.einsum("blf,bjf->blj", coefs, col_table, precision=exact)
        total = by_row[:, :, :, None] + by_col[:, :, None, :]
        for c in range(3):
            total = total + coefs[:, :, c][:, :, None, None] * wide_pixels[:, None, c]
        total = total - jnp.sum(coefs, axis=2)[:, :, None, None] * pixel_mean[:, None]
        return total * pixel_rate[:, None]

    def over_pixels(weights):
        scaled = weights * pixel_rate[:, None]
        by_row = jnp.sum(scaled, axis=3)
        by_col = jnp.sum(scaled, axis=2)
        total = jnp.einsum("bli,bif->blf", by_row, row_table, precision=exact)
        total = total + jnp.einsum("blj,bjf->blf", by_col, col_table, precision=exact)
        colour = jnp.stack(
            [jnp.sum(scaled * wide_pixels[:, None, c], axis=(2, 3)) for c in range(3)], axis=2
        )
        total = total + jnp.pad(colour, ((0, 0), (0, 0), (0, FEAT - 3)))
        return total - jnp.sum(scaled * pixel_mean[:, None], axis=(2, 3))[:, :, None]

    latent_rows = latents.astype(FLOAT)
    query_normed, back_query_norm = jax.vjp(layer_norm, latent_rows, query_gain)
    query_input = query_normed.astype(BFLOAT)
    own_queries = linear(query_input, query_proj).astype(BFLOAT)
    raw_query = linear_back(own_queries, key_proj) * cross_scale
    scores = against_pixels(raw_query * feature_gain)
    row_top = jnp.max(jnp.where(live, scores, -1e30), axis=(2, 3))
    all_top = lax.pmax(row_top, "ty")
    row_exp = jnp.where(live, jnp.exp(scores - all_top[:, :, None, None]), 0.0)
    row_total = lax.psum(jnp.sum(row_exp, axis=(2, 3)), "ty")
    cross_exact = row_exp / row_total[:, :, None, None]
    raw_mix = lax.psum(over_pixels(cross_exact), "ty")
    mix = raw_mix * feature_gain
    attended = linear(mix.astype(BFLOAT), value_proj)
    attended_input = attended.astype(BFLOAT)
    resid_one = latent_rows + linear(attended_input, cross_proj)
    hidden_normed, back_hidden_norm = jax.vjp(layer_norm, resid_one, hidden_gain)
    hidden_input = hidden_normed.astype(BFLOAT)
    hidden_lifted, back_hidden_gelu = jax.vjp(gelu_tanh, linear(hidden_input, hidden_up))
    hidden_act = hidden_lifted.astype(BFLOAT)
    resid_two = resid_one + linear(hidden_act, hidden_down)
    tower_normed, back_tower_norm = jax.vjp(layer_norm, resid_two, tower_gain)
    tower_input = tower_normed.astype(BFLOAT)
    tower_q = linear(tower_input, tower_query).astype(BFLOAT)
    tower_k = linear(tower_input, tower_key).astype(BFLOAT)
    tower_v = linear(tower_input, tower_value).astype(BFLOAT)
    all_keys, all_values = (
        lax.all_gather(tower_k, "tx", axis=1, tiled=True),
        lax.all_gather(tower_v, "tx", axis=1, tiled=True),
    )
    split_q = tower_q.reshape(item_count, rows_here, head_count, head_size)
    split_k = all_keys.reshape(item_count, -1, head_count, head_size)
    split_v = all_values.reshape(item_count, -1, head_count, head_size)
    tower_scores = (
        jnp.einsum("bqhd,bkhd->bhqk", split_q, split_k, preferred_element_type=FLOAT) * tower_scale
    )
    tower_top = jnp.max(tower_scores, axis=3, keepdims=True)
    tower_exp = jnp.exp(tower_scores - tower_top)
    tower_total = jnp.sum(tower_exp, axis=3, keepdims=True)
    tower_exact = tower_exp / tower_total
    tower_probs = tower_exact.astype(BFLOAT)
    mixed = jnp.einsum(
        "bhqk,bkhd->bqhd", tower_probs, split_v, preferred_element_type=FLOAT
    ).reshape(item_count, rows_here, model_width)
    mixed_input = mixed.astype(BFLOAT)
    resid_three = resid_two + linear(mixed_input, tower_proj)
    final_normed, back_final_norm = jax.vjp(layer_norm, resid_three, final_gain)
    final_input = final_normed.astype(BFLOAT)
    final_lifted, back_final_gelu = jax.vjp(gelu_tanh, linear(final_input, final_up))
    final_act = final_lifted.astype(BFLOAT)
    resid_four = resid_three + linear(final_act, final_down)
    grad_four = cotangent.astype(FLOAT)
    final_down_grad = weight_grad(final_act, cotangent)
    grad_final_lift = back_final_gelu(linear_back(cotangent, final_down))[0].astype(BFLOAT)
    final_up_grad = weight_grad(final_input, grad_final_lift)
    grad_rows_three, final_gain_grad = back_final_norm(linear_back(grad_final_lift, final_up))
    grad_three = grad_four + grad_rows_three
    grad_tower_out = grad_three.astype(BFLOAT)
    tower_proj_grad = weight_grad(mixed_input, grad_tower_out)
    grad_mixed_flat = linear_back(grad_tower_out, tower_proj).astype(BFLOAT)
    grad_mixed = grad_mixed_flat.reshape(item_count, rows_here, head_count, head_size)
    grad_tower_p = jnp.einsum("bqhd,bkhd->bhqk", grad_mixed, split_v, preferred_element_type=FLOAT)
    tower_delta = jnp.sum(tower_exact * grad_tower_p, axis=3, keepdims=True)
    grad_tower_scores = (tower_exact * (grad_tower_p - tower_delta)).astype(BFLOAT)
    grad_tower_q = (
        (
            jnp.einsum("bhqk,bkhd->bqhd", grad_tower_scores, split_k, preferred_element_type=FLOAT)
            * tower_scale
        )
        .astype(BFLOAT)
        .reshape(item_count, rows_here, model_width)
    )
    value_part = jnp.einsum(
        "bhqk,bqhd->bkhd", tower_probs, grad_mixed, preferred_element_type=FLOAT
    )
    key_part = (
        jnp.einsum("bhqk,bqhd->bkhd", grad_tower_scores, split_q, preferred_element_type=FLOAT)
        * tower_scale
    )
    key_sums, value_sums = (
        lax.psum_scatter(
            key_part.reshape(item_count, -1, model_width), "tx", scatter_dimension=1, tiled=True
        ),
        lax.psum_scatter(
            value_part.reshape(item_count, -1, model_width), "tx", scatter_dimension=1, tiled=True
        ),
    )
    grad_tower_k = key_sums.astype(BFLOAT)
    grad_tower_v = value_sums.astype(BFLOAT)
    tower_query_grad = weight_grad(tower_input, grad_tower_q)
    tower_key_grad = weight_grad(tower_input, grad_tower_k)
    tower_value_grad = weight_grad(tower_input, grad_tower_v)
    grad_tower_rows = (
        linear_back(grad_tower_q, tower_query)
        + linear_back(grad_tower_k, tower_key)
        + linear_back(grad_tower_v, tower_value)
    )
    grad_rows_two, tower_gain_grad = back_tower_norm(grad_tower_rows)
    grad_two = grad_three + grad_rows_two
    grad_hidden_out = grad_two.astype(BFLOAT)
    hidden_down_grad = weight_grad(hidden_act, grad_hidden_out)
    grad_hidden_lift = back_hidden_gelu(linear_back(grad_hidden_out, hidden_down))[0].astype(BFLOAT)
    hidden_up_grad = weight_grad(hidden_input, grad_hidden_lift)
    grad_rows_one, hidden_gain_grad = back_hidden_norm(linear_back(grad_hidden_lift, hidden_up))
    grad_one = grad_two + grad_rows_one
    grad_cross_out = grad_one.astype(BFLOAT)
    cross_proj_grad = weight_grad(attended_input, grad_cross_out)
    grad_attended = linear_back(grad_cross_out, cross_proj).astype(BFLOAT)
    raw_up = linear_back(grad_attended, value_proj)
    grad_probs = against_pixels(raw_up * feature_gain)
    cross_delta = jnp.sum(grad_attended.astype(FLOAT) * attended, axis=2)
    grad_scores = cross_exact * (grad_probs - cross_delta[:, :, None, None])
    raw_grad_mix = lax.psum(over_pixels(grad_scores), "ty")
    grad_mix = (raw_grad_mix * feature_gain).astype(BFLOAT)
    grad_queries = (linear(grad_mix, key_proj) * cross_scale).astype(BFLOAT)
    key_proj_grad = weight_grad(grad_mix, own_queries) * cross_scale
    value_proj_grad = weight_grad(mix.astype(BFLOAT), grad_attended)
    feature_part = jnp.sum(raw_grad_mix * raw_query + raw_mix * raw_up, axis=(0, 1))
    pixel_sums = lax.psum((key_proj_grad, value_proj_grad, feature_part), "tx")
    query_proj_grad = weight_grad(query_input, grad_queries)
    grad_latent_rows, query_gain_grad = back_query_norm(linear_back(grad_queries, query_proj))
    latent_grad = grad_one + grad_latent_rows
    summed = (
        lax.psum_scatter(query_gain_grad, "tx", scatter_dimension=0, tiled=True),
        lax.psum_scatter(query_proj_grad, "tx", scatter_dimension=0, tiled=True),
        lax.psum_scatter(cross_proj_grad, "tx", scatter_dimension=0, tiled=True),
        lax.psum_scatter(hidden_gain_grad, "tx", scatter_dimension=0, tiled=True),
        lax.psum_scatter(hidden_up_grad, "tx", scatter_dimension=0, tiled=True),
        lax.psum_scatter(hidden_down_grad, "tx", scatter_dimension=0, tiled=True),
        lax.psum_scatter(tower_gain_grad, "tx", scatter_dimension=0, tiled=True),
        lax.psum_scatter(tower_query_grad, "tx", scatter_dimension=0, tiled=True),
        lax.psum_scatter(tower_key_grad, "tx", scatter_dimension=0, tiled=True),
        lax.psum_scatter(tower_value_grad, "tx", scatter_dimension=0, tiled=True),
        lax.psum_scatter(tower_proj_grad, "tx", scatter_dimension=0, tiled=True),
        lax.psum_scatter(final_gain_grad, "tx", scatter_dimension=0, tiled=True),
        lax.psum_scatter(final_up_grad, "tx", scatter_dimension=0, tiled=True),
        lax.psum_scatter(final_down_grad, "tx", scatter_dimension=0, tiled=True),
    )
    return (
        resid_four.astype(BFLOAT),
        latent_grad,
        pixel_sums[2],
        summed[0],
        summed[1],
        pixel_sums[0],
        pixel_sums[1],
        summed[2],
        summed[3],
        summed[4],
        summed[5],
        summed[6],
        summed[7],
        summed[8],
        summed[9],
        summed[10],
        summed[11],
        summed[12],
        summed[13],
    )


def solution(mesh):
    in_specs = (
        P(None, None, "ty", "tx"),
        P(None, "ty", "tx"),
        P(),
        P(None, "tx", None),
        P(None, "tx", None),
        P(),
        P(),
        P(),
        P(),
        P(),
        P(),
        P(),
        P(),
        P(),
        P(),
        P(),
        P(),
        P(),
        P(),
        P(),
        P(),
        P(),
    )
    out_specs = (
        P(None, "tx", None),
        P(None, "tx", None),
        P(),
        P("tx"),
        P("tx", None),
        P(),
        P(),
        P("tx", None),
        P("tx"),
        P("tx", None),
        P("tx", None),
        P("tx"),
        P("tx", None),
        P("tx", None),
        P("tx", None),
        P("tx", None),
        P("tx"),
        P("tx", None),
        P("tx", None),
    )
    fits = mesh.shape["ty"] == 4 and mesh.shape["tx"] == HEADS
    plan = on_device_fast if fits else on_device
    return jax.shard_map(
        plan, mesh=mesh, in_specs=in_specs, out_specs=out_specs, check_vma=False
    )
```

```python
import math

import jax
import jax.numpy as jnp
import numpy as np
from jax import lax
from jax.experimental import pallas as pl
from jax.experimental.pallas import tpu as pltpu
from jax.sharding import PartitionSpec as P

BANDS = 64
FEAT = 261
HEADS = 8


EPSILON = 1e-05
FLOAT = jnp.float32
BFLOAT = jnp.bfloat16


def layer_norm(values, scales):
    centre = jnp.mean(values, axis=-1, keepdims=True)
    shifted = values - centre
    spread = jnp.mean(shifted * shifted, axis=-1, keepdims=True)
    return shifted * lax.rsqrt(spread + EPSILON) * scales


def gelu_tanh(values):
    cubic = values + 0.044715 * values * values * values
    return 0.5 * values * (1.0 + jnp.tanh(0.7978845608028654 * cubic))


def linear(inputs, weight):
    return lax.dot_general(
        inputs, weight, (((inputs.ndim - 1,), (0,)), ((), ())), preferred_element_type=FLOAT
    )


def linear_back(upstream, weight):
    return lax.dot_general(
        upstream, weight, (((upstream.ndim - 1,), (1,)), ((), ())), preferred_element_type=FLOAT
    )


def weight_grad(inputs, upstream):
    flat_inputs = inputs.reshape(-1, inputs.shape[-1])
    flat_upstream = upstream.reshape(-1, upstream.shape[-1])
    return lax.dot_general(
        flat_inputs, flat_upstream, (((0,), (0,)), ((), ())), preferred_element_type=FLOAT
    )


def axis_tables(image_sizes, ids, coord_lane, first_lane):
    side = image_sizes.astype(FLOAT)[:, None]
    coord = -1.0 + 2.0 * ids.astype(FLOAT)[None, :] / (side - 1.0)
    band = jnp.arange(BANDS, dtype=jnp.int32).astype(FLOAT)
    frequency = 1.0 + band[None, :] * (side * 0.5 - 1.0) / (BANDS - 1)
    angle = math.pi * coord[:, :, None] * frequency[:, None, :]
    waves = jnp.concatenate([jnp.sin(angle), jnp.cos(angle)], axis=2)
    count, length = coord.shape
    lead = jnp.zeros((count, length, coord_lane), FLOAT)
    gap = jnp.zeros((count, length, first_lane - coord_lane - 1), FLOAT)
    tail = jnp.zeros((count, length, FEAT - first_lane - 2 * BANDS), FLOAT)
    table = jnp.concatenate([lead, coord[:, :, None], gap, waves, tail], axis=2)
    return table, coord, jnp.sum(waves, axis=2) + coord


MESH = pl.DeviceIdType.MESH


def send(src, dst, send_sem, recv_sem, where):
    copy = pltpu.make_async_remote_copy(
        src_ref=src, dst_ref=dst, send_sem=send_sem, recv_sem=recv_sem,
        device_id=where, device_id_type=MESH,
    )
    copy.start()
    return copy


def greet(places):
    barrier = pltpu.get_barrier_semaphore()
    for place in places:
        pl.semaphore_signal(barrier, inc=1, device_id=place, device_id_type=MESH)
    pl.semaphore_wait(barrier, len(places))


def outer(left, right):
    return lax.dot_general(left, right, (((0,), (0,)), ((), ())), preferred_element_type=FLOAT)


LANES = 384
CUBE = 0.044715
SLOPE = 0.7978845608028654


def norm_rows(rows):
    shifted = rows - jnp.mean(rows, axis=-1, keepdims=True)
    rate = lax.rsqrt(jnp.mean(shifted * shifted, axis=-1, keepdims=True) + EPSILON)
    return shifted * rate, rate


def norm_rows_back(upstream, gain, unit, rate):
    scaled = upstream * gain
    along = jnp.mean(scaled * unit, axis=-1, keepdims=True)
    grad = rate * (scaled - jnp.mean(scaled, axis=-1, keepdims=True) - unit * along)
    return grad, jnp.sum(upstream * unit, axis=0, keepdims=True)


def gelu_pair(values):
    square = values * values
    bend = jnp.tanh(SLOPE * (values + CUBE * values * square))
    half = 0.5 * (1.0 + bend)
    slope = half + 0.5 * values * (1.0 - bend * bend) * (SLOPE * (1.0 + 3.0 * CUBE * square))
    return values * half, slope


def dot_nt(left, right):
    return lax.dot_general(left, right, (((1,), (1,)), ((), ())), preferred_element_type=FLOAT)


def dot_nn(left, right):
    return lax.dot_general(left, right, (((1,), (0,)), ((), ())), preferred_element_type=FLOAT)


HALVES = 2
GROUP = 128
LOG2E = 1.0 / math.log(2.0)


def split_two(values):
    high = values.astype(BFLOAT)
    return high, (values - high.astype(FLOAT)).astype(BFLOAT)


def dot_wide(dot, values, high, low):
    first, second = split_two(values)
    return dot(first, high) + (dot(first, low) + dot(second, high))


def coefs_by_pixel(coefs, thigh_ref, tlow_ref, into):
    count = coefs.shape[0] // 2
    for b in range(2):
        wide = dot_wide(dot_nt, coefs[b * count : (b + 1) * count], thigh_ref[b], tlow_ref[b])
        for half in range(HALVES):
            at = pl.ds((half * 2 + b) * count, count)
            rows = wide[:, half * GROUP : (half + 1) * GROUP]
            for t in range(8):
                high, low = split_two(rows + wide[:, (2 + t) * GROUP : (3 + t) * GROUP])
                into[t, at, 0:GROUP] = high
                into[t, at, GROUP : 2 * GROUP] = low


def features_of(sums, scales, thigh_ref, tlow_ref):
    count = sums.shape[1] // 4
    blocks = [sums[t] if scales is None else sums[t] * scales[t] for t in range(8)]
    joined = blocks[0]
    for block in blocks[1:]:
        joined = joined + block
    outs = []
    for b in range(2):
        first, second = pl.ds(b * count, count), (2 + b) * count
        lo, hi = slice(b * count, (b + 1) * count), slice((2 + b) * count, (3 + b) * count)
        wide = jnp.concatenate(
            [joined[lo], joined[hi]] + [block[lo] + block[hi] for block in blocks], axis=1
        )
        outs.append(dot_wide(dot_nn, wide, thigh_ref[b], tlow_ref[b]))
    return jnp.concatenate(outs, axis=0)


def rate_and_bias(block, group):
    rate = block[group % 2 * 4 + group // 2 * 8 + 3 :][:1].astype(FLOAT)
    return rate, jnp.where(rate == 0.0, -1e30, 0.0)


class Ring:
    def __init__(self, places, send_sems, recv_sems):
        self.places, self.sems = places, (send_sems, recv_sems)

    def copy(self, i, d, src, dst):
        return pltpu.make_async_remote_copy(
            src_ref=src, dst_ref=dst, send_sem=self.sems[0].at[i, d], recv_sem=self.sems[1].at[i, d],
            device_id=self.places[d], device_id_type=MESH,
        )

    def start(self, i, sources, into):
        copies = [self.copy(i, d, sources(d), into(d)) for d in range(len(self.places))]
        for copy in copies:
            copy.start()
        return copies


def finish(*groups):
    for copies in groups:
        for copy in copies:
            copy.wait()


def sin_half_turns(turns):
    whole = jnp.floor(turns + 0.5)
    part = turns - whole
    odd = whole - 2.0 * jnp.floor(whole * 0.5)
    square = part * part
    total = jnp.full_like(square, SINE[-1])
    for term in SINE[-2::-1]:
        total = total * square + term
    return part * total * (1.0 - 2.0 * odd)


def axis_rows(axis, side, first, lanes):
    place = (lax.broadcasted_iota(jnp.int32, (48, 1), 0) + first).astype(FLOAT)
    coord = -1.0 + 2.0 * place / (side - 1.0)
    here = lanes[:, 128 * axis : 128 * axis + 256]
    rate = 1.0 + here[0:1] * (side * 0.5 - 1.0) * (1.0 / (BANDS - 1))
    waves = sin_half_turns(coord * rate + here[1:2]) * here[2 + axis : 3 + axis]
    empty = jnp.zeros((48, LANES - 256), FLOAT)
    table = jnp.concatenate([empty, waves] if axis else [waves, empty], axis=1)
    total = jnp.sum(waves, axis=1, keepdims=True) + coord
    table = table + coord * lanes[4 + axis : 5 + axis] - (total * (1.0 / FEAT)) * lanes[6:7]
    return table, coord, total


def main_kernel(sizes_ref, *refs):
    matrices = refs[15:25]
    result_ref, grad_ref, value_ref, key_ref, sums_ref = refs[25:30]
    (ws, msgs, pixcoefs, upcoefs, pixels, scores, ups, weights, sums, tops, totals, raw_all, qrows,
     part_out, part_in, half_out, half_in, up_sent, q_out, q_in, kv_out, kv_in, kv_more, probs, mixed_out, mixed_in, gm_out, gm_in,
     kvx_out, kvx_in, gq_in, gkv_in, up_ref, mix_all, gcross_out, gcross_all, gains_out, gains_all, gmix,
     x_out, x_all, g_out, g_all, own, held, relay_in, zsend, zrecv, last, nrest, nsend, nextra, nrecv, nmore,
     msg_rows, msg_ref, thigh_ref, tlow_ref, kproj_ref, vproj_ref, fgain_ref, result_v, grad_v, value_v, key_v,
     w_sem, l_sem, ty_s, ty_r, tx_s, tx_r, mate_s, mate_r, xg_s, xg_r, z_s, z_r, ac_s, ac_r, re_s, re_r, g_s, g_r,
     in_sem, out_sem,
     pix_v, mask_v, lat_ref, cot_ref, fgain_v, qgain_ref, hgain_ref, tgain_ref, ogain_ref,
     kraw_v, vraw_v, hot_ref, hotrow_ref, ids_ref, lanes_ref) = refs[30:]
    ty, tx = lax.axis_index("ty"), lax.axis_index("tx")
    z, y = tx // 2, lax.rem(tx, 2)
    tys = [{"ty": lax.rem(ty + d, 4), "tx": tx} for d in (1, 2, 3)]
    txs = [{"ty": ty, "tx": lax.rem(tx + d, 8)} for d in range(1, 8)]
    mate = {"ty": 2 * (ty // 2) + 1 - lax.rem(ty, 2), "tx": tx}
    beside = {"ty": ty, "tx": 2 * z + 1 - y}
    on_ty, on_tx = Ring(tys, ty_s, ty_r), Ring(txs, tx_s, tx_r)
    on_mate, across = Ring([mate], mate_s, mate_r), Ring([tys[1]], ac_s, ac_r)
    over = [{"ty": lax.rem(ty + d, 4), "tx": 2 * z + 1 - y} for d in range(4)]
    handing = Ring(tys + over, xg_s, xg_r)
    loads = []
    small = []
    for i, (source, into) in enumerate(zip(refs[:15], refs[-15:])):
        small.append(pltpu.make_async_copy(source, into, in_sem.at[i]))
        small[i].start()
    for i, w in enumerate(matrices):
        loads.append(pltpu.make_async_copy(w, ws.at[i], w_sem.at[i]))
    loads[0].start()
    cross, up, down, tq, tk, tv, tproj, fup, fdown = range(1, 10)
    partners = tys + txs + over[1:]
    barrier = pltpu.get_barrier_semaphore()
    for place in partners:
        pl.semaphore_signal(barrier, inc=1, device_id=place, device_id_type=MESH)
    ty_at = lambda d: lax.rem(ty + d + 1, 4)
    tx_at = lambda d: lax.rem(tx + d + 1, 8)

    def times(rows, i):
        return dot_nn(rows, ws[i])

    def times_back(rows, i):
        return dot_nt(rows, ws[i])

    def to_ty(i, src, into):
        return on_ty.start(i, lambda d: src, lambda d: into)

    def spread(i, out, into):
        copies = on_tx.start(i, lambda d: out.at[tx_at(d)], lambda d: into.at[tx])
        into[tx] = out[tx]
        return copies

    def over_ty(i, out, into):
        copies = on_ty.start(i, lambda d: out.at[ty_at(d)], lambda d: into.at[ty])
        into[ty] = out[ty]
        return copies

    xg = {}

    def handed(i, source, into):
        return [
            handing.copy(i, k, source(k), into(0 if k < 3 else 1)) for k in range(7)
        ]

    def give_x(i, rows):
        for c in range(8):
            x_out[i, c % 2, c // 2] = rows[:, 128 * c : 128 * c + 128]
        x_all[i, :, 0, ty] = x_out[i, y]
        xg["x", i] = handed(
            i, lambda k: x_out.at[i, y if k < 3 else 1 - y], lambda slot: x_all.at[i, :, slot, ty]
        )
        for copy in xg["x", i]:
            copy.start()

    def g_copies(w):
        return handed(
            6 + w, lambda k: g_out.at[w, lax.rem(ty + k + 1, 4)], lambda slot: g_all.at[w, slot, ty]
        )

    def give_g(w, rows):
        for h in range(4):
            g_out[w, h] = rows[:, 256 * h : 256 * h + 256]
        g_all[w, 0, ty] = g_out[w, ty]
        for copy in g_copies(w):
            copy.start()

    def slot_x(w):
        return min(w, 3) + max(w - 5, 0) if isinstance(w, int) else jnp.minimum(w, 3) + jnp.maximum(w - 5, 0)

    def zcopy(w, c):
        return pltpu.make_async_remote_copy(
            src_ref=zsend.at[w, c], dst_ref=zrecv.at[w, c], send_sem=z_s.at[w, c],
            recv_sem=z_r.at[w, c], device_id={"ty": ty, "tx": 2 * lax.rem(z + c + 1, 4) + y},
            device_id_type=MESH,
        )

    at_end = (z == 0) | (z == 3)

    def relay(w):
        return pltpu.make_async_remote_copy(
            src_ref=zsend.at[w, 1], dst_ref=relay_in.at[w], send_sem=re_s.at[w], recv_sem=re_r.at[w],
            device_id={"ty": ty, "tx": 2 * (1 + z // 2) + y}, device_id_type=MESH,
        )

    def stage_one(w):
        i = slot_x(w)
        if isinstance(w, int):
            finish(xg.pop(("x", i), ()))
        finish(g_copies(w))
        right = g_all[w].reshape(256, 256)

        def part(c):
            return outer(x_all[i, lax.rem(z + c + 1, 4)].reshape(256, 128), right)

        zsend[w, 1] = part(1).astype(BFLOAT)

        @pl.when(at_end)
        def _():
            relay(w).start()

        @pl.when(jnp.logical_not(at_end))
        def _():
            zcopy(w, 1).start()

        for c, middle in ((0, 1), (2, 2)):
            total = part(c)

            @pl.when(z == middle)
            def _():
                held[w] = total

            @pl.when(z != middle)
            def _():
                zsend[w, c] = total.astype(BFLOAT)
                zcopy(w, c).start()

        own[w] = part(3)

    def stage_two(w):
        for c, middle in ((0, 1), (2, 2)):
            @pl.when(z == middle)
            def _():
                relay(w).wait_recv()
                zsend[w, c] = (held[w] + relay_in[w].astype(FLOAT)).astype(BFLOAT)
                zcopy(w, c).start()

    def out_copies(w):
        return [
            on_mate.copy(2 + w, 0, last.at[w], sums_ref.at[w, ty]),
            across.copy(w, 0, last.at[w], sums_ref.at[w, ty]),
            pltpu.make_async_copy(last.at[w], sums_ref.at[w, ty], l_sem.at[w]),
        ]

    def stage_three(w):
        total = own[w]
        for c in (0, 2):
            zcopy(w, c).wait()
            total = total + zrecv[w, c].astype(FLOAT)
        own[w] = total

        @pl.when(at_end)
        def _():
            relay(w).wait_send()
            zcopy(w, 1).wait_recv()
            own[w] = own[w] + zrecv[w, 1].astype(FLOAT)

        @pl.when(jnp.logical_not(at_end))
        def _():
            zcopy(w, 1).wait_send()

        last[w] = own[w].astype(BFLOAT)
        for copy in out_copies(w):
            copy.start()

    def stage_four(w):
        across.copy(w, 0, last.at[w], sums_ref.at[w, ty]).wait()
        there = sums_ref.at[w, lax.rem(ty + 2, 4)]
        on_mate.copy(10 + w, 0, there, there).start()

    def stage_end(w):
        there = sums_ref.at[w, lax.rem(ty + 2, 4)]
        on_mate.copy(10 + w, 0, there, there).wait()
        on_mate.copy(2 + w, 0, last.at[w], sums_ref.at[w, ty]).wait()
        pltpu.make_async_copy(last.at[w], sums_ref.at[w, ty], l_sem.at[w]).wait()

    def product_main(i, left, right):
        product = outer(left, right)
        nsend[i] = product[0:256].astype(BFLOAT).reshape(8, 32, 256)
        nrest[i] = product[256:272]
        return on_tx.start(6 + 3 * i, lambda d: nsend.at[i, tx_at(d)], lambda d: nrecv.at[i, d])

    def product_rest(i, gains):
        row = lax.broadcasted_iota(jnp.int32, (16, 256), 0)
        more = nrest[i] + jnp.where(row < 8, 0.0, jnp.concatenate([gains, gains], axis=0))
        nextra[i] = more.astype(BFLOAT)
        return on_tx.start(7 + 3 * i, lambda d: nextra.at[i], lambda d: nmore.at[i, d])

    def product_join(i, copies, into):
        finish(copies)
        main = nsend[i, tx].astype(FLOAT)
        more = nextra[i].astype(FLOAT)
        for d in range(7):
            main = main + nrecv[i, d].astype(FLOAT)
            more = more + nmore[i, d].astype(FLOAT)
        mine = pl.ds(pl.multiple_of(tx * 32, 32), 32)
        into[ty, mine] = main.astype(BFLOAT)
        into[ty, 256:272] = more.astype(BFLOAT)
        return on_tx.start(8 + 3 * i, lambda d: into.at[ty, mine], lambda d: into.at[ty, mine])

    def hand_out(k, source, out):
        mine = pltpu.make_async_copy(source, out.at[ty], out_sem.at[k])
        mine.start()
        return on_mate.start(18 + k, lambda d: source, lambda d: out.at[ty]) + [mine], across.start(
            8 + k, lambda d: source, lambda d: out.at[ty]
        )

    def hand_on(k, copies, out):
        near, far = copies
        finish(far)
        there = out.at[lax.rem(ty + 2, 4)]
        return near + on_mate.start(22 + k, lambda d: there, lambda d: there)

    def block_end(copies, into, out):
        near, far, places = [], [], []
        for k in range(8):
            if k:
                copies[k - 1].wait()
            rows = pl.ds(pl.multiple_of(lax.rem(tx + 8 - k, 8) * 32, 32), 32)
            block = into.at[ty, rows]
            near += on_mate.start(26 + k, lambda d: block, lambda d: out.at[ty, rows])
            far += across.start(12 + k, lambda d: block, lambda d: out.at[ty, rows])
            mine = pltpu.make_async_copy(block, out.at[ty, rows], out_sem.at[4 + k])
            mine.start()
            near.append(mine)
            places.append(rows)
        rows = pl.ds(256, 16)
        block = into.at[ty, rows]
        near += on_mate.start(34, lambda d: block, lambda d: out.at[ty, rows])
        far += across.start(20, lambda d: block, lambda d: out.at[ty, rows])
        mine = pltpu.make_async_copy(block, out.at[ty, rows], out_sem.at[12])
        mine.start()
        return near + [mine], far, places + [rows]

    def block_on(state, out):
        near, far, places = state
        for k in range(9):
            far[k].wait()
            there = out.at[lax.rem(ty + 2, 4), places[k]]
            near += on_mate.start(35 + k, lambda d: there, lambda d: there)
        return near

    def product_end(i, copies, into, out):
        finish(copies)
        return hand_out(i, into.at[ty], out)

    def message(k, src, at, where):
        return pltpu.make_async_remote_copy(
            src_ref=src, dst_ref=msgs.at[at], send_sem=g_s.at[k], recv_sem=g_r.at[k],
            device_id=where, device_id_type=MESH,
        )

    def message_from(k):
        far = lax.rem(z + 8 - jnp.where(k < 5, k - 1, k - 4), 4)
        return jnp.where(
            k == 0, tx, jnp.where(k == 1, 2 * z + 1 - y, 2 * far + jnp.where(k < 5, y, 1 - y))
        )

    share, width = lat_ref.shape[1], lat_ref.shape[2]
    count = 2 * share
    high, wide = pix_v.shape[3] // HALVES, pix_v.shape[1]
    for copy in small:
        copy.wait()
    lanes = lanes_ref[...]
    ids = ids_ref[...]
    sides = [jnp.zeros((1, 1), FLOAT) + sizes_ref[b].astype(FLOAT) for b in range(2)]
    colours_in, live_in = pix_v[...].astype(FLOAT), jnp.where(mask_v[...] > 0, 1.0, 0.0)
    plane_rows = -(-wide // 8) * 8
    filler = [jnp.zeros((plane_rows - wide, HALVES * high), FLOAT)] if plane_rows > wide else []
    planes = []
    for b in range(2):
        for plane in [colours_in[c, :, b, :] for c in range(3)] + [live_in[:, b, :]]:
            planes += [plane] + filler
    planes = jnp.concatenate(planes, axis=0).astype(BFLOAT)
    flat = [dot_nn(planes, hotrow_ref[half]) for half in range(HALVES)]
    row_of = lax.broadcasted_iota(jnp.int32, (plane_rows, 1), 0).astype(FLOAT)
    pick = ids[1:2] == row_of

    def flatten(plane, half):
        rows = flat[half][plane * plane_rows : (plane + 1) * plane_rows]
        return jnp.sum(jnp.where(pick, rows, 0.0), axis=0, keepdims=True)

    def put_table(b, at, rows):
        high_part, low_part = split_two(rows)
        thigh_ref[b, at : at + rows.shape[0]] = high_part
        tlow_ref[b, at : at + rows.shape[0]] = low_part

    def by_pixel(total, coord, rows):
        square = coord * coord
        total_high, total_low = split_two(total)
        square_high, square_low = split_two(square)
        left = jnp.concatenate([total_high, total_low, square_high, square_low], axis=1)
        spread_out = outer(left, rows)
        return spread_out[0:1] + spread_out[1:2], spread_out[2:3] + spread_out[3:4]

    zeros = jnp.zeros((GROUP, LANES), BFLOAT)
    lane_at = lax.broadcasted_iota(jnp.int32, (16, LANES), 1)
    row_at = lax.broadcasted_iota(jnp.int32, (16, LANES), 0)
    for b in range(2):
        _, col_coord, col_total = axis_rows(1, sides[b], tx * wide, lanes)
        col_sum, col_square = by_pixel(col_total, col_coord, hot_ref[64:112])
        for half in range(HALVES):
            first = ty * (2 * high) + half * high
            table, coord, total = axis_rows(0, sides[b], first, lanes)
            row_sum, row_square = by_pixel(total, coord, hot_ref[16:64])
            put_table(b, half * GROUP + 16, table)
            thigh_ref[b, half * GROUP + 64 : half * GROUP + GROUP] = zeros[64:]
            tlow_ref[b, half * GROUP + 64 : half * GROUP + GROUP] = zeros[64:]
            channel = row_at - (half * 8 + b * 4)
            colour = (channel >= 0) & (channel < 3)
            value = jnp.where(channel == lane_at, 1.0, 0.0) - (1.0 / FEAT) * lanes[6:7]
            put_table(b, half * GROUP, jnp.where(colour, value, 0.0))
            colours = [flatten(b * 4 + c, half) for c in range(3)]
            mean = (colours[0] + colours[1] + colours[2] + row_sum + col_sum) * (1.0 / FEAT)
            square = sum(c * c for c in colours) + row_square + col_square + 2.0 * BANDS
            rate = lax.rsqrt(square * (1.0 / FEAT) - mean * mean + EPSILON)
            side = sides[b]
            first_row = jnp.zeros((1, 1), FLOAT) + first.astype(FLOAT)
            first_col = jnp.zeros((1, 1), FLOAT) + (tx * wide).astype(FLOAT)
            live = (
                (flatten(4 * b + 3, half) > 0.5)
                & (ids[0:1] + first_row < side)
                & (ids[1:2] + first_col < side)
            )
            for c, row in enumerate(colours + [jnp.where(live, rate, 0.0)]):
                at = half * 8 + b * 4 + c
                msg_rows[at : at + 1] = row
    msg_ref[...] = msg_rows[...].astype(BFLOAT)
    pl.semaphore_wait(barrier, len(partners))
    message(0, msg_ref, tx, beside).start()
    for d in range(3):
        message(1 + d, msg_ref, tx, {"ty": ty, "tx": 2 * lax.rem(z + 1 + d, 4) + y}).start()
    msgs[tx] = msg_ref[...]
    for load in loads[1:]:
        load.start()
    for b in range(2):
        for t in range(8):
            table, _, _ = axis_rows(1, sides[b], t * wide, lanes)
            at = (2 + t) * GROUP
            thigh_ref[b, at : at + 64] = zeros[:64]
            tlow_ref[b, at : at + 64] = zeros[:64]
            put_table(b, at + 64, table)
            thigh_ref[b, at + 112 : at + GROUP] = zeros[:16]
            tlow_ref[b, at + 112 : at + GROUP] = zeros[:16]
    for raw_ref, padded in ((kraw_v, kproj_ref), (vraw_v, vproj_ref)):
        padded[0:256] = raw_ref[0:256]
        padded[256:272] = jnp.concatenate(
            [raw_ref[256:FEAT].astype(FLOAT), jnp.zeros((272 - FEAT, width), FLOAT)], axis=0
        ).astype(BFLOAT)
        padded[272:LANES] = jnp.zeros((LANES - 272, width), BFLOAT)
    fgain_ref[...] = jnp.zeros_like(fgain_ref)
    fgain_ref[:, 0:FEAT] = fgain_v[...].reshape(1, FEAT)
    pixels[0:GROUP] = hot_ref[...]
    pixels[GROUP : 2 * GROUP] = hot_ref[...]
    gains_out[...] = jnp.zeros_like(gains_out)
    cot = cot_ref[ty]
    give_g(0, cot)
    fgain = fgain_ref[...]
    unit, _ = norm_rows(lat_ref[...].reshape(4 * share, width).astype(FLOAT))
    rows = (unit * qgain_ref[...]).astype(BFLOAT)
    qrows[...] = rows
    finish(loads[:1])
    queries = times(rows, 0).astype(BFLOAT)
    cross_scale = 1.0 / math.sqrt(width)
    raw = dot_nt(queries, kproj_ref[...]) * cross_scale
    raw_all[...] = raw.reshape(raw_all.shape)
    coefs_by_pixel(raw * (fgain * LOG2E), thigh_ref, tlow_ref, pixcoefs)

    def take_block(t):
        block = msgs[t]
        pixels[0:16] = block
        pixels[GROUP : GROUP + 16] = block
        scores[...] = dot_nn(pixcoefs[t], pixels[...])
        return block

    def front_step(k, _):
        t = message_from(k)

        @pl.when(k > 0)
        def _():
            message(k - 1, msg_ref, tx, beside).wait()

        @pl.when((k > 1) & (k < 5))
        def _():
            message(k + 2, msgs.at[t], t, beside).start()

        block = take_block(t)
        for group in range(4):
            at = pl.ds(group * count, count)
            rate, bias = rate_and_bias(block, group)
            s = scores[at] * rate + bias
            top = jnp.max(s, axis=1, keepdims=True)
            e = jnp.exp2(s - top)
            tops[t, at] = top
            totals[t, at] = jnp.sum(e, axis=1, keepdims=True)
            weights[at] = (e * rate).astype(BFLOAT)
        sums[t] = dot_nt(weights[...], pixels[0:GROUP])
        return 0

    lax.fori_loop(0, 8, front_step, 0)
    top = tops[0]
    for t in range(1, 8):
        top = jnp.maximum(top, tops[t])
    top = jnp.maximum(top[: 2 * count], top[2 * count :])
    both = jnp.concatenate([top, top], axis=0)
    scales = [jnp.exp2(tops[t] - both) for t in range(8)]
    total = sum(totals[t] * scales[t] for t in range(8))
    total = total[: 2 * count] + total[2 * count :]
    feats = features_of(sums, scales, thigh_ref, tlow_ref)
    lane = lax.broadcasted_iota(jnp.int32, feats.shape, 1)
    part_out[...] = jnp.where(
        lane < FEAT, feats, jnp.where(lane == FEAT, total, top)
    ).reshape(part_out.shape)

    copies = on_ty.start(0, lambda d: part_out.at[ty_at(d)], lambda d: part_in.at[d])
    latent = lat_ref[ty].astype(FLOAT)
    parts = [part_out[ty]]
    finish(copies)
    parts += [part_in[d] for d in range(3)]
    tops_in = [p[:, FEAT + 1 : FEAT + 2] for p in parts]
    top = jnp.maximum(
        jnp.maximum(tops_in[0], tops_in[1]), jnp.maximum(tops_in[2], tops_in[3])
    )
    joined = sum(p * jnp.exp2(t - top) for p, t in zip(parts, tops_in))
    total = joined[:, FEAT : FEAT + 1]
    raw_mix = joined / total
    shift = top + jnp.log2(total)
    mix = (raw_mix * fgain).astype(BFLOAT)
    mix_all[ty] = mix
    later = to_ty(1, mix_all.at[ty], mix_all.at[ty])
    attended = dot_nn(mix, vproj_ref[...])
    finish(loads[1:])
    one = latent + times(attended.astype(BFLOAT), cross)
    h_unit, h_rate = norm_rows(one)
    hidden = (h_unit * hgain_ref[...]).astype(BFLOAT)
    act, act_slope = gelu_pair(times(hidden, up))
    act = act.astype(BFLOAT)
    two = one + times(act, down)
    t_unit, t_rate = norm_rows(two)
    trows = (t_unit * tgain_ref[...]).astype(BFLOAT)
    for s, i in enumerate((tk, tv)):
        value = times(trows, i).astype(BFLOAT)
        for h in range(8):
            kv_out[h, 32 * s : 32 * s + 32] = value[:, 128 * h : 128 * h + 128]
    kv_copies = spread(1, kv_out, kv_in)
    value = times(trows, tq).astype(BFLOAT)
    for h in range(8):
        q_out[h] = value[:, 128 * h : 128 * h + 128]
    q_copies = spread(2, q_out, q_in)
    give_x(3, trows)
    back_four = times_back(cot, fdown)
    finish(kv_copies)
    copies = on_mate.start(0, lambda d: kv_in, lambda d: kv_more)
    finish(q_copies)
    q = q_in[...].reshape(8 * share, 128)
    k1 = kv_in[:, 0:32].reshape(8 * share, 128)
    v1 = kv_in[:, 32:64].reshape(8 * share, 128)
    scale = 1.0 / math.sqrt(128)
    s1 = dot_nt(q, k1) * scale
    finish(copies)
    k2 = kv_more[:, 0:32].reshape(8 * share, 128)
    v2 = kv_more[:, 32:64].reshape(8 * share, 128)
    s2 = dot_nt(q, k2) * scale
    stop = jnp.maximum(jnp.max(s1, axis=1, keepdims=True), jnp.max(s2, axis=1, keepdims=True))
    e1, e2 = jnp.exp(s1 - stop), jnp.exp(s2 - stop)
    rate = 1.0 / (jnp.sum(e1, axis=1, keepdims=True) + jnp.sum(e2, axis=1, keepdims=True))
    p1, p2 = e1 * rate, e2 * rate
    probs[0] = p1
    probs[1] = p2
    mixed_out[...] = (
        (dot_nn(p1.astype(BFLOAT), v1) + dot_nn(p2.astype(BFLOAT), v2))
        .astype(BFLOAT)
        .reshape(8, share, 128)
    )
    copies = spread(3, mixed_out, mixed_in)
    finish(copies)
    mixed = jnp.concatenate([mixed_in[h] for h in range(8)], axis=1)
    give_x(2, mixed)
    three = two + times(mixed, tproj)
    o_unit, o_rate = norm_rows(three)
    ogain = ogain_ref[...]
    frows = (o_unit * ogain).astype(BFLOAT)
    give_x(1, frows)
    fact, fact_slope = gelu_pair(times(frows, fup))
    fact = fact.astype(BFLOAT)

    def put_gain(row, grad):
        for h in range(4):
            gains_out[0, h, row : row + 1] = grad[:, 256 * h : 256 * h + 256]

    g_lift = (back_four * fact_slope).astype(BFLOAT)
    give_g(1, g_lift)
    g_three, o_grad = norm_rows_back(times_back(g_lift, fup), ogain, o_unit, o_rate)
    put_gain(2, o_grad)
    g_three = cot.astype(FLOAT) + g_three
    g_tower = g_three.astype(BFLOAT)
    g_mixed = times_back(g_tower, tproj).astype(BFLOAT)
    for h in range(8):
        gm_out[h] = g_mixed[:, 128 * h : 128 * h + 128]
    copies = spread(4, gm_out, gm_in)
    give_g(2, g_tower)
    result_v[...] = (three + times(fact, fdown)).astype(BFLOAT)
    result_copies = hand_out(2, result_v, result_ref)
    finish(copies)
    give_x(0, fact)
    gm = gm_in[...].reshape(8 * share, 128)
    q = q_in[...].reshape(8 * share, 128)
    k1 = kv_in[:, 0:32].reshape(8 * share, 128)
    v1 = kv_in[:, 32:64].reshape(8 * share, 128)
    k2 = kv_more[:, 0:32].reshape(8 * share, 128)
    v2 = kv_more[:, 32:64].reshape(8 * share, 128)
    p1, p2 = probs[0], probs[1]
    gp1, gp2 = dot_nt(gm, v1), dot_nt(gm, v2)
    away = jnp.sum(p1 * gp1, axis=1, keepdims=True) + jnp.sum(p2 * gp2, axis=1, keepdims=True)
    gs1 = (p1 * (gp1 - away)).astype(BFLOAT)
    gs2 = (p2 * (gp2 - away)).astype(BFLOAT)
    kvx_out[0] = (outer(gs2, q) * scale).astype(BFLOAT)
    kvx_out[1] = outer(p2.astype(BFLOAT), gm).astype(BFLOAT)
    copies = on_mate.start(1, lambda d: kvx_out, lambda d: kvx_in)
    gq = (dot_nn(gs1, k1) + dot_nn(gs2, k2)) * scale
    q_out[...] = gq.astype(BFLOAT).reshape(8, share, 128)
    q_copies = spread(5, q_out, gq_in)
    gk = outer(gs1, q) * scale
    gv = outer(p1.astype(BFLOAT), gm)
    finish(copies)
    kv_out[:, 0:32] = (gk + kvx_in[0].astype(FLOAT)).astype(BFLOAT).reshape(8, share, 128)
    kv_out[:, 32:64] = (gv + kvx_in[1].astype(FLOAT)).astype(BFLOAT).reshape(8, share, 128)
    kv_copies = spread(12, kv_out, gkv_in)
    stage_one(0)
    finish(q_copies)
    value = jnp.concatenate([gq_in[h] for h in range(8)], axis=1)
    give_g(3, value)
    g_trows = times_back(value, tq)
    finish(kv_copies)
    for s, i in enumerate((tk, tv)):
        value = jnp.concatenate([gkv_in[h, 32 * s : 32 * s + 32] for h in range(8)], axis=1)
        give_g(4 + s, value)
        g_trows = g_trows + times_back(value, i)
    g_two, t_grad = norm_rows_back(g_trows, tgain_ref[...], t_unit, t_rate)
    put_gain(1, t_grad)
    g_two = g_three + g_two
    g_hidden = g_two.astype(BFLOAT)
    stage_two(0)
    stage_one(1)
    g_hlift = (times_back(g_hidden, down) * act_slope).astype(BFLOAT)
    stage_two(1)
    stage_one(2)
    g_one, h_grad = norm_rows_back(times_back(g_hlift, up), hgain_ref[...], h_unit, h_rate)
    put_gain(0, h_grad)
    gain_copies = over_ty(3, gains_out.at[0], gains_all.at[0])
    g_one = g_two + g_one
    g_cross = g_one.astype(BFLOAT)
    for h in range(4):
        gcross_out[h] = g_cross[:, 256 * h : 256 * h + 256]
    gcross_copies = over_ty(4, gcross_out, gcross_all)
    g_att = times_back(g_cross, cross).astype(BFLOAT)
    raw_up = dot_nt(g_att, vproj_ref[...])
    feat_part = jnp.sum(raw_mix * raw_up, axis=0, keepdims=True)
    delta = jnp.sum(g_att.astype(FLOAT) * attended, axis=1, keepdims=True)
    lane = lax.broadcasted_iota(jnp.int32, raw_up.shape, 1)
    sent = raw_up * fgain
    for at, number in ((FEAT, delta), (FEAT + 3, shift)):
        for k in range(3):
            piece = number.astype(BFLOAT).astype(FLOAT)
            sent = jnp.where(lane == at + k, piece, sent)
            number = number - piece
    up_sent[ty] = sent.astype(BFLOAT)
    copies = to_ty(5, up_sent.at[ty], up_sent.at[ty])
    give_x(4, act)
    give_g(6, g_hidden)
    give_x(5, hidden)
    give_g(7, g_hlift)
    stage_two(2)
    stage_one(3)
    finish(later, gain_copies, gcross_copies)
    result_copies = hand_on(2, result_copies, result_ref)
    gain_rows = gains_all[0, 0] + gains_all[0, 1] + gains_all[0, 2] + gains_all[0, 3]
    ncopies = product_main(
        0, mix_all[...].reshape(4 * share, LANES), gcross_all[...].reshape(4 * share, 256)
    ) + product_rest(0, gain_rows)
    finish(copies)
    finish(xg.pop(("x", 3), ()))

    sent = up_sent[...].astype(FLOAT).reshape(4 * share, LANES)
    lane = lax.broadcasted_iota(jnp.int32, sent.shape, 1)
    delta, shift = [
        sent[:, at : at + 1] + sent[:, at + 1 : at + 2] + sent[:, at + 2 : at + 3]
        for at in (FEAT, FEAT + 3)
    ]
    up_ref[...] = jnp.where(
        lane < FEAT, sent, jnp.where(lane == FEAT, delta, shift)
    ).reshape(up_ref.shape)
    coefs_by_pixel(up_ref[...].reshape(4 * share, LANES), thigh_ref, tlow_ref, upcoefs)

    def back_step(t):
        block = take_block(t)
        ups[...] = dot_nn(upcoefs[t], pixels[...])
        for group in range(4):
            at = pl.ds(group * count, count)
            rate, bias = rate_and_bias(block, group)
            b = group % 2
            mine = up_ref[2 * b : 2 * b + 2].reshape(count, LANES)
            p = jnp.exp2(scores[at] * rate + (bias - mine[:, FEAT + 1 : FEAT + 2]))
            g = p * (ups[at] * rate - mine[:, FEAT : FEAT + 1])
            weights[at] = (g * rate).astype(BFLOAT)
        sums[t] = dot_nt(weights[...], pixels[0:GROUP])

    def first_steps(t, _):
        back_step(t)
        stage_two(3 + t)
        stage_one(4 + t)
        return 0

    def second_steps(t, _):
        back_step(t)
        stage_three(t - 4)
        return 0

    lax.fori_loop(0, 2, first_steps, 0)
    finish(xg.pop(("x", 4)), xg.pop(("x", 5)))
    lax.fori_loop(2, 3, first_steps, 0)
    ncopies = product_join(0, ncopies, value_v)
    back_step(3)
    stage_two(6)
    lax.fori_loop(4, 8, second_steps, 0)
    part_out[...] = features_of(sums, None, thigh_ref, tlow_ref).reshape(part_out.shape)
    half_out[...] = part_out[...].astype(BFLOAT)
    copies = on_ty.start(9, lambda d: half_out.at[ty_at(d)], lambda d: half_in.at[d])
    value_copies = product_end(0, ncopies, value_v, value_ref)
    unit, rate = norm_rows(lat_ref[ty].astype(FLOAT))
    raw_mix = part_out[ty]
    finish(copies)
    for d in range(3):
        raw_mix = raw_mix + half_in[d].astype(FLOAT)
    mix = (raw_mix * fgain).astype(BFLOAT)
    gmix[ty] = mix
    mcopies = to_ty(6, gmix.at[ty], gmix.at[ty])
    grad_q = (dot_nn(mix, kproj_ref[...]) * cross_scale).astype(BFLOAT)
    finish(mcopies)
    right = qrows[:, pl.ds(pl.multiple_of(ty * 256, 256), 256)]
    mcopies = product_main(1, gmix[...].reshape(4 * share, LANES), right)
    stage_one(7)
    grad, qgain_grad = norm_rows_back(times_back(grad_q, 0), qgain_ref[...], unit, rate)
    features = feat_part + jnp.sum(raw_mix * raw_all[ty], axis=0, keepdims=True)
    for h in range(4):
        gains_out[1, h, 0:1] = qgain_grad[:, 256 * h : 256 * h + 256]
    gains_out[1, 0, 1:2] = features[:, 0:256]
    gains_out[1, 1, 1:2, 0:128] = features[:, 256:384]
    gain_copies = over_ty(10, gains_out.at[1], gains_all.at[1])
    grad_v[...] = (g_one + grad).astype(BFLOAT)
    grad_copies = hand_out(3, grad_v, grad_ref)
    for w in range(4):
        stage_four(w)
    finish(gain_copies)
    gain_rows = gains_all[1, 0] + gains_all[1, 1] + gains_all[1, 2] + gains_all[1, 3]
    mcopies += product_rest(1, gain_rows)
    stage_three(4)
    stage_three(5)
    stage_two(7)
    mcopies = product_join(1, mcopies, key_v)
    value_copies = hand_on(0, value_copies, value_ref)
    grad_copies = hand_on(3, grad_copies, grad_ref)
    stage_three(6)
    stage_three(7)
    key_copies = block_end(mcopies, key_v, key_ref)
    for w in range(4, 6):
        stage_four(w)
    key_copies = block_on(key_copies, key_ref)
    for w in range(6, 8):
        stage_four(w)
    finish(result_copies, value_copies, grad_copies, key_copies)
    for w in range(8):
        stage_end(w)


SINE = tuple((-1) ** n * math.pi ** (2 * n + 1) / math.factorial(2 * n + 1) for n in range(7))


def pixel_constants(high, wide):
    length = -(-high * wide // 128) * 128
    hot = np.zeros((GROUP, length), np.float32)
    ids = np.full((8, length), 1e6, np.float32)
    for i in range(high):
        for j in range(wide):
            hot[16 + i, i * wide + j] = 1.0
            hot[64 + j, i * wide + j] = 1.0
            ids[0, i * wide + j], ids[1, i * wide + j] = i, j
    lanes = np.zeros((8, LANES), np.float32)
    for axis in range(2):
        first = 5 + 2 * BANDS * axis
        lanes[0, first : first + 2 * BANDS] = np.tile(np.arange(BANDS), 2)
        lanes[1, first + BANDS : first + 2 * BANDS] = 0.5
        lanes[2 + axis, first : first + 2 * BANDS] = 1.0
        lanes[4 + axis, 3 + axis] = 1.0
    lanes[6, :FEAT] = 1.0
    rows = np.zeros((HALVES, HALVES * high, length), np.float32)
    for half in range(HALVES):
        rows[half, half * high : (half + 1) * high] = hot[16 : 16 + high]
    return jnp.asarray(hot, BFLOAT), jnp.asarray(rows, BFLOAT), jnp.asarray(ids), jnp.asarray(lanes)


def main_call(sizes, inputs, matrices):
    pixels, mask, lat, cot = inputs[:4]
    _, share, width = lat.shape
    inputs = inputs + pixel_constants(pixels.shape[3] // HALVES, pixels.shape[1])
    rows, length = 8 * share, inputs[11].shape[1]
    dma = pltpu.SemaphoreType.DMA
    hbm = pl.BlockSpec(memory_space=pl.ANY)
    shape = jax.ShapeDtypeStruct
    half, full = (lambda *s: pltpu.VMEM(s, BFLOAT)), (lambda *s: pltpu.VMEM(s, FLOAT))
    return pl.pallas_call(
        main_kernel,
        out_shape=(
            shape((4, share, width), BFLOAT),
            shape((4, share, width), BFLOAT),
            shape((4, 272, 256), BFLOAT),
            shape((4, 272, 256), BFLOAT),
            shape((8, 4, 128, 256), BFLOAT),
        ),
        in_specs=[pl.BlockSpec(memory_space=pltpu.SMEM)] + [hbm] * 25,
        out_specs=(hbm,) * 5,
        scratch_shapes=[
            half(10, width, width), half(8, 16, length), half(8, rows, 2 * GROUP), half(8, rows, 2 * GROUP),
            half(2 * GROUP, length), full(rows, length), full(rows, length), half(rows, length),
            full(8, rows, GROUP), full(8, rows, 1), full(8, rows, 1), full(4, share, LANES), half(4 * share, width),
            full(4, share, LANES), full(3, share, LANES),
            half(4, share, LANES), half(3, share, LANES), half(4, share, LANES),
            half(8, share, 128), half(8, share, 128), half(8, 2 * share, 128), half(8, 2 * share, 128),
            half(8, 2 * share, 128), full(2, rows, rows), half(8, share, 128), half(8, share, 128),
            half(8, share, 128), half(8, share, 128), half(2, rows, 128), half(2, rows, 128),
            half(8, share, 128), half(8, 2 * share, 128),
            full(4, share, LANES), half(4, share, LANES), half(4, share, 256), half(4, share, 256),
            full(2, 4, 8, 256), full(2, 4, 8, 256), half(4, share, LANES),
            half(6, 2, 4, share, 128), half(6, 4, 2, 4, share, 128),
            half(8, 4, share, 256), half(8, 2, 4, share, 256), full(8, 128, 256), full(8, 128, 256), half(8, 128, 256),
            half(8, 3, 128, 256), half(8, 3, 128, 256), half(8, 128, 256),
            full(2, 16, 256), half(2, 8, 32, 256), half(2, 16, 256), half(2, 7, 32, 256), half(2, 7, 16, 256),
            full(16, length), half(16, length), half(2, 10 * GROUP, LANES), half(2, 10 * GROUP, LANES),
            half(LANES, width), half(LANES, width), full(1, LANES),
            half(share, width), half(share, width), half(4, 272, 256), half(4, 272, 256),
            dma((10,)), dma((8,)), dma((12, 3)), dma((12, 3)), dma((13, 7)), dma((13, 7)),
            dma((44, 1)), dma((44, 1)), dma((14, 7)), dma((14, 7)),
            dma((8, 3)), dma((8, 3)), dma((21, 1)), dma((21, 1)), dma((8,)), dma((8,)), dma((7,)), dma((7,)), dma((15,)), dma((13,)),
        ] + [pltpu.VMEM(v.shape, v.dtype) for v in inputs],
        compiler_params=pltpu.CompilerParams(
            collective_id=1, has_side_effects=True, vmem_limit_bytes=62 << 20
        ),
        name="main",
    )(sizes, *inputs, *matrices)


def finish_kernel(*refs):
    ins, outs, stage, held = refs[:9], refs[9:28], refs[28:37], refs[37:56]
    in_sem, out_sem = refs[56:]
    copies = [pltpu.make_async_copy(a, v, in_sem.at[i]) for i, (a, v) in enumerate(zip(ins, stage))]
    for i in (1, 5, 2, 6, 7, 8, 0, 4, 3):
        copies[i].start()
    tx = lax.axis_index("tx")
    sums_ref, cross_core_ref, query_core_ref, latent_ref, result_in_ref, cross_ref, query_ref, value_ref, key_ref = stage
    result_ref, latent_out, feat_out, qgain_out, query_out, key_out, value_out, cross_out = held[:8]
    written = []

    def write(*places):
        for i in places:
            written.append(pltpu.make_async_copy(held[i], outs[i], out_sem.at[i]))
            written[-1].start()

    here = pl.ds(pl.multiple_of(tx * 128, 128), 128)
    quarter = tx // 2
    inside = pl.ds(pl.multiple_of(lax.rem(tx, 2) * 128, 128), 128)
    scale = 1.0 / math.sqrt(query_ref.shape[0])
    copies[1].wait()
    copies[5].wait()
    cross_core = jnp.concatenate([cross_core_ref[h] for h in range(4)], axis=1)
    value_out[...] = dot_nt(cross_core, cross_ref[...])[:FEAT]
    write(6)
    copies[2].wait()
    copies[6].wait()
    query_core = jnp.concatenate([query_core_ref[h] for h in range(4)], axis=1)
    key_out[...] = (dot_nn(query_core, query_ref[...]) * scale)[:FEAT]
    write(5)
    copies[7].wait()
    cross_out[...] = outer(value_ref[:, here], cross_core[:FEAT])
    write(7)
    copies[8].wait()
    mine = query_core_ref[quarter, :, inside].astype(FLOAT)
    query_out[...] = outer(mine[:FEAT].astype(BFLOAT), key_ref[...]) * scale
    qgain_out[...] = mine[264:265]
    more = jnp.concatenate([query_core_ref[h, 256:272] for h in range(2)], axis=1).astype(FLOAT)
    feat_out[...] = more[9:10, 0:FEAT].reshape(FEAT)
    mine = cross_core_ref[quarter, 256:272, inside].astype(FLOAT)
    for i in range(3):
        held[16 + i][...] = mine[8 + i : 9 + i]
    write(4, 2, 3, 16, 17, 18)
    copies[0].wait()
    for w in range(8):
        for h in range(4):
            held[8 + w][:, 256 * h : 256 * h + 256] = sums_ref[w, h].astype(FLOAT)
        write(8 + w)
    copies[4].wait()
    copies[3].wait()
    result_ref[...] = result_in_ref[...]
    latent_out[...] = latent_ref[...].astype(FLOAT)
    write(0, 1)
    for copy in written:
        copy.wait()


def finish_call(*inputs):
    width = inputs[5].shape[0]
    shape = lambda *s: jax.ShapeDtypeStruct(s, FLOAT)
    rows = inputs[3].shape
    block = [shape(128, width)]
    hbm = pl.BlockSpec(memory_space=pl.ANY)
    outs = (
        [jax.ShapeDtypeStruct(rows, BFLOAT), shape(*rows), shape(FEAT), shape(1, 128)]
        + block + [shape(FEAT, width)] * 2 + block + block * 8 + [shape(1, 128)] * 3
    )
    return pl.pallas_call(
        finish_kernel,
        out_shape=outs,
        in_specs=[hbm] * 9,
        out_specs=[hbm] * 19,
        scratch_shapes=[pltpu.VMEM(v.shape, v.dtype) for v in list(inputs) + outs]
        + [pltpu.SemaphoreType.DMA((9,)), pltpu.SemaphoreType.DMA((19,))],
        compiler_params=pltpu.CompilerParams(vmem_limit_bytes=62 << 20),
        name="finish",
    )(*inputs)


def on_device_fast(
    pixels,
    pixel_mask,
    image_sizes,
    latents,
    cotangent,
    feature_gain,
    query_gain,
    query_proj,
    key_proj,
    value_proj,
    cross_proj,
    hidden_gain,
    hidden_up,
    hidden_down,
    tower_gain,
    tower_query,
    tower_key,
    tower_value,
    tower_proj,
    final_gain,
    final_up,
    final_down,
):
    item_count = pixels.shape[0]
    tile_height = pixels.shape[2]
    tile_width = pixels.shape[3]
    model_width = latents.shape[2]
    rows_here = latents.shape[1]
    share = item_count * rows_here // 4

    def in_shares(rows):
        return rows.reshape(4, share, rows.shape[-1])

    result, latent_grad, cross_core, query_core, sums = main_call(
        image_sizes,
        (jnp.transpose(pixels, (1, 3, 0, 2)), jnp.transpose(pixel_mask, (2, 0, 1)), in_shares(latents),
         in_shares(cotangent), feature_gain, query_gain[None],
         hidden_gain[None], tower_gain[None], final_gain[None], key_proj, value_proj),
        (query_proj, cross_proj, hidden_up, hidden_down, tower_query, tower_key, tower_value,
         tower_proj, final_up, final_down),
    )
    (result, latent_grad, feature_sum, query_sum, query_grad, key_grad, value_grad, cross_grad,
     final_down_grad, final_up_grad, tower_proj_grad, tower_query_grad, tower_key_grad,
     tower_value_grad, hidden_down_grad, hidden_up_grad, hidden_sum, tower_sum, final_sum) = finish_call(
        sums, cross_core, query_core, latent_grad, result, cross_proj, query_proj, value_proj, key_proj
    )
    return (
        result.reshape(latents.shape),
        latent_grad.reshape(latents.shape),
        feature_sum,
        query_sum[0],
        query_grad,
        key_grad,
        value_grad,
        cross_grad,
        hidden_sum[0],
        hidden_up_grad,
        hidden_down_grad,
        tower_sum[0],
        tower_query_grad,
        tower_key_grad,
        tower_value_grad,
        tower_proj_grad,
        final_sum[0],
        final_up_grad,
        final_down_grad,
    )


def on_device(
    pixels,
    pixel_mask,
    image_sizes,
    latents,
    cotangent,
    feature_gain,
    query_gain,
    query_proj,
    key_proj,
    value_proj,
    cross_proj,
    hidden_gain,
    hidden_up,
    hidden_down,
    tower_gain,
    tower_query,
    tower_key,
    tower_value,
    tower_proj,
    final_gain,
    final_up,
    final_down,
):
    item_count = pixels.shape[0]
    tile_height = pixels.shape[2]
    tile_width = pixels.shape[3]
    model_width = latents.shape[2]
    rows_here = latents.shape[1]
    head_count = HEADS
    head_size = model_width // head_count
    cross_scale = 1.0 / math.sqrt(model_width)
    tower_scale = 1.0 / math.sqrt(head_size)
    row_ids = lax.axis_index("ty") * tile_height + jnp.arange(tile_height, dtype=jnp.int32)
    col_ids = lax.axis_index("tx") * tile_width + jnp.arange(tile_width, dtype=jnp.int32)
    all_cols = jnp.arange(tile_width * lax.axis_size("tx"), dtype=jnp.int32)
    wide_pixels = lax.all_gather(pixels, "tx", axis=3, tiled=True).astype(FLOAT)
    wide_mask = lax.all_gather(pixel_mask, "tx", axis=2, tiled=True)
    side_sizes = image_sizes[:, None, None]
    live = (
        (wide_mask > 0)
        & (row_ids[None, :, None] < side_sizes)
        & (all_cols[None, None, :] < side_sizes)
    )[:, None]
    row_table, row_coord, row_sum = axis_tables(image_sizes, row_ids, 3, 5)
    col_table, col_coord, col_sum = axis_tables(image_sizes, all_cols, 4, 5 + 2 * BANDS)
    pixel_mean = (
        jnp.sum(wide_pixels, axis=1) + row_sum[:, :, None] + col_sum[:, None, :]
    ) / FEAT
    pixel_square = (
        jnp.sum(wide_pixels * wide_pixels, axis=1)
        + (row_coord * row_coord)[:, :, None]
        + (col_coord * col_coord)[:, None, :]
        + 2.0 * BANDS
    ) / FEAT
    pixel_rate = lax.rsqrt(pixel_square - pixel_mean * pixel_mean + EPSILON)
    exact = lax.Precision.HIGHEST

    def against_pixels(coefs):
        by_row = jnp.einsum("blf,bif->bli", coefs, row_table, precision=exact)
        by_col = jnp.einsum("blf,bjf->blj", coefs, col_table, precision=exact)
        total = by_row[:, :, :, None] + by_col[:, :, None, :]
        for c in range(3):
            total = total + coefs[:, :, c][:, :, None, None] * wide_pixels[:, None, c]
        total = total - jnp.sum(coefs, axis=2)[:, :, None, None] * pixel_mean[:, None]
        return total * pixel_rate[:, None]

    def over_pixels(weights):
        scaled = weights * pixel_rate[:, None]
        by_row = jnp.sum(scaled, axis=3)
        by_col = jnp.sum(scaled, axis=2)
        total = jnp.einsum("bli,bif->blf", by_row, row_table, precision=exact)
        total = total + jnp.einsum("blj,bjf->blf", by_col, col_table, precision=exact)
        colour = jnp.stack(
            [jnp.sum(scaled * wide_pixels[:, None, c], axis=(2, 3)) for c in range(3)], axis=2
        )
        total = total + jnp.pad(colour, ((0, 0), (0, 0), (0, FEAT - 3)))
        return total - jnp.sum(scaled * pixel_mean[:, None], axis=(2, 3))[:, :, None]

    latent_rows = latents.astype(FLOAT)
    query_normed, back_query_norm = jax.vjp(layer_norm, latent_rows, query_gain)
    query_input = query_normed.astype(BFLOAT)
    own_queries = linear(query_input, query_proj).astype(BFLOAT)
    raw_query = linear_back(own_queries, key_proj) * cross_scale
    scores = against_pixels(raw_query * feature_gain)
    row_top = jnp.max(jnp.where(live, scores, -1e30), axis=(2, 3))
    all_top = lax.pmax(row_top, "ty")
    row_exp = jnp.where(live, jnp.exp(scores - all_top[:, :, None, None]), 0.0)
    row_total = lax.psum(jnp.sum(row_exp, axis=(2, 3)), "ty")
    cross_exact = row_exp / row_total[:, :, None, None]
    raw_mix = lax.psum(over_pixels(cross_exact), "ty")
    mix = raw_mix * feature_gain
    attended = linear(mix.astype(BFLOAT), value_proj)
    attended_input = attended.astype(BFLOAT)
    resid_one = latent_rows + linear(attended_input, cross_proj)
    hidden_normed, back_hidden_norm = jax.vjp(layer_norm, resid_one, hidden_gain)
    hidden_input = hidden_normed.astype(BFLOAT)
    hidden_lifted, back_hidden_gelu = jax.vjp(gelu_tanh, linear(hidden_input, hidden_up))
    hidden_act = hidden_lifted.astype(BFLOAT)
    resid_two = resid_one + linear(hidden_act, hidden_down)
    tower_normed, back_tower_norm = jax.vjp(layer_norm, resid_two, tower_gain)
    tower_input = tower_normed.astype(BFLOAT)
    tower_q = linear(tower_input, tower_query).astype(BFLOAT)
    tower_k = linear(tower_input, tower_key).astype(BFLOAT)
    tower_v = linear(tower_input, tower_value).astype(BFLOAT)
    all_keys, all_values = (
        lax.all_gather(tower_k, "tx", axis=1, tiled=True),
        lax.all_gather(tower_v, "tx", axis=1, tiled=True),
    )
    split_q = tower_q.reshape(item_count, rows_here, head_count, head_size)
    split_k = all_keys.reshape(item_count, -1, head_count, head_size)
    split_v = all_values.reshape(item_count, -1, head_count, head_size)
    tower_scores = (
        jnp.einsum("bqhd,bkhd->bhqk", split_q, split_k, preferred_element_type=FLOAT) * tower_scale
    )
    tower_top = jnp.max(tower_scores, axis=3, keepdims=True)
    tower_exp = jnp.exp(tower_scores - tower_top)
    tower_total = jnp.sum(tower_exp, axis=3, keepdims=True)
    tower_exact = tower_exp / tower_total
    tower_probs = tower_exact.astype(BFLOAT)
    mixed = jnp.einsum(
        "bhqk,bkhd->bqhd", tower_probs, split_v, preferred_element_type=FLOAT
    ).reshape(item_count, rows_here, model_width)
    mixed_input = mixed.astype(BFLOAT)
    resid_three = resid_two + linear(mixed_input, tower_proj)
    final_normed, back_final_norm = jax.vjp(layer_norm, resid_three, final_gain)
    final_input = final_normed.astype(BFLOAT)
    final_lifted, back_final_gelu = jax.vjp(gelu_tanh, linear(final_input, final_up))
    final_act = final_lifted.astype(BFLOAT)
    resid_four = resid_three + linear(final_act, final_down)
    grad_four = cotangent.astype(FLOAT)
    final_down_grad = weight_grad(final_act, cotangent)
    grad_final_lift = back_final_gelu(linear_back(cotangent, final_down))[0].astype(BFLOAT)
    final_up_grad = weight_grad(final_input, grad_final_lift)
    grad_rows_three, final_gain_grad = back_final_norm(linear_back(grad_final_lift, final_up))
    grad_three = grad_four + grad_rows_three
    grad_tower_out = grad_three.astype(BFLOAT)
    tower_proj_grad = weight_grad(mixed_input, grad_tower_out)
    grad_mixed_flat = linear_back(grad_tower_out, tower_proj).astype(BFLOAT)
    grad_mixed = grad_mixed_flat.reshape(item_count, rows_here, head_count, head_size)
    grad_tower_p = jnp.einsum("bqhd,bkhd->bhqk", grad_mixed, split_v, preferred_element_type=FLOAT)
    tower_delta = jnp.sum(tower_exact * grad_tower_p, axis=3, keepdims=True)
    grad_tower_scores = (tower_exact * (grad_tower_p - tower_delta)).astype(BFLOAT)
    grad_tower_q = (
        (
            jnp.einsum("bhqk,bkhd->bqhd", grad_tower_scores, split_k, preferred_element_type=FLOAT)
            * tower_scale
        )
        .astype(BFLOAT)
        .reshape(item_count, rows_here, model_width)
    )
    value_part = jnp.einsum(
        "bhqk,bqhd->bkhd", tower_probs, grad_mixed, preferred_element_type=FLOAT
    )
    key_part = (
        jnp.einsum("bhqk,bqhd->bkhd", grad_tower_scores, split_q, preferred_element_type=FLOAT)
        * tower_scale
    )
    key_sums, value_sums = (
        lax.psum_scatter(
            key_part.reshape(item_count, -1, model_width), "tx", scatter_dimension=1, tiled=True
        ),
        lax.psum_scatter(
            value_part.reshape(item_count, -1, model_width), "tx", scatter_dimension=1, tiled=True
        ),
    )
    grad_tower_k = key_sums.astype(BFLOAT)
    grad_tower_v = value_sums.astype(BFLOAT)
    tower_query_grad = weight_grad(tower_input, grad_tower_q)
    tower_key_grad = weight_grad(tower_input, grad_tower_k)
    tower_value_grad = weight_grad(tower_input, grad_tower_v)
    grad_tower_rows = (
        linear_back(grad_tower_q, tower_query)
        + linear_back(grad_tower_k, tower_key)
        + linear_back(grad_tower_v, tower_value)
    )
    grad_rows_two, tower_gain_grad = back_tower_norm(grad_tower_rows)
    grad_two = grad_three + grad_rows_two
    grad_hidden_out = grad_two.astype(BFLOAT)
    hidden_down_grad = weight_grad(hidden_act, grad_hidden_out)
    grad_hidden_lift = back_hidden_gelu(linear_back(grad_hidden_out, hidden_down))[0].astype(BFLOAT)
    hidden_up_grad = weight_grad(hidden_input, grad_hidden_lift)
    grad_rows_one, hidden_gain_grad = back_hidden_norm(linear_back(grad_hidden_lift, hidden_up))
    grad_one = grad_two + grad_rows_one
    grad_cross_out = grad_one.astype(BFLOAT)
    cross_proj_grad = weight_grad(attended_input, grad_cross_out)
    grad_attended = linear_back(grad_cross_out, cross_proj).astype(BFLOAT)
    raw_up = linear_back(grad_attended, value_proj)
    grad_probs = against_pixels(raw_up * feature_gain)
    cross_delta = jnp.sum(grad_attended.astype(FLOAT) * attended, axis=2)
    grad_scores = cross_exact * (grad_probs - cross_delta[:, :, None, None])
    raw_grad_mix = lax.psum(over_pixels(grad_scores), "ty")
    grad_mix = (raw_grad_mix * feature_gain).astype(BFLOAT)
    grad_queries = (linear(grad_mix, key_proj) * cross_scale).astype(BFLOAT)
    key_proj_grad = weight_grad(grad_mix, own_queries) * cross_scale
    value_proj_grad = weight_grad(mix.astype(BFLOAT), grad_attended)
    feature_part = jnp.sum(raw_grad_mix * raw_query + raw_mix * raw_up, axis=(0, 1))
    pixel_sums = lax.psum((key_proj_grad, value_proj_grad, feature_part), "tx")
    query_proj_grad = weight_grad(query_input, grad_queries)
    grad_latent_rows, query_gain_grad = back_query_norm(linear_back(grad_queries, query_proj))
    latent_grad = grad_one + grad_latent_rows
    summed = (
        lax.psum_scatter(query_gain_grad, "tx", scatter_dimension=0, tiled=True),
        lax.psum_scatter(query_proj_grad, "tx", scatter_dimension=0, tiled=True),
        lax.psum_scatter(cross_proj_grad, "tx", scatter_dimension=0, tiled=True),
        lax.psum_scatter(hidden_gain_grad, "tx", scatter_dimension=0, tiled=True),
        lax.psum_scatter(hidden_up_grad, "tx", scatter_dimension=0, tiled=True),
        lax.psum_scatter(hidden_down_grad, "tx", scatter_dimension=0, tiled=True),
        lax.psum_scatter(tower_gain_grad, "tx", scatter_dimension=0, tiled=True),
        lax.psum_scatter(tower_query_grad, "tx", scatter_dimension=0, tiled=True),
        lax.psum_scatter(tower_key_grad, "tx", scatter_dimension=0, tiled=True),
        lax.psum_scatter(tower_value_grad, "tx", scatter_dimension=0, tiled=True),
        lax.psum_scatter(tower_proj_grad, "tx", scatter_dimension=0, tiled=True),
        lax.psum_scatter(final_gain_grad, "tx", scatter_dimension=0, tiled=True),
        lax.psum_scatter(final_up_grad, "tx", scatter_dimension=0, tiled=True),
        lax.psum_scatter(final_down_grad, "tx", scatter_dimension=0, tiled=True),
    )
    return (
        resid_four.astype(BFLOAT),
        latent_grad,
        pixel_sums[2],
        summed[0],
        summed[1],
        pixel_sums[0],
        pixel_sums[1],
        summed[2],
        summed[3],
        summed[4],
        summed[5],
        summed[6],
        summed[7],
        summed[8],
        summed[9],
        summed[10],
        summed[11],
        summed[12],
        summed[13],
    )


def solution(mesh):
    in_specs = (
        P(None, None, "ty", "tx"),
        P(None, "ty", "tx"),
        P(),
        P(None, "tx", None),
        P(None, "tx", None),
        P(),
        P(),
        P(),
        P(),
        P(),
        P(),
        P(),
        P(),
        P(),
        P(),
        P(),
        P(),
        P(),
        P(),
        P(),
        P(),
        P(),
    )
    out_specs = (
        P(None, "tx", None),
        P(None, "tx", None),
        P(),
        P("tx"),
        P("tx", None),
        P(),
        P(),
        P("tx", None),
        P("tx"),
        P("tx", None),
        P("tx", None),
        P("tx"),
        P("tx", None),
        P("tx", None),
        P("tx", None),
        P("tx", None),
        P("tx"),
        P("tx", None),
        P("tx", None),
    )
    fits = mesh.shape["ty"] == 4 and mesh.shape["tx"] == HEADS
    plan = on_device_fast if fits else on_device
    return jax.shard_map(
        plan, mesh=mesh, in_specs=in_specs, out_specs=out_specs, check_vma=False
    )
```
